128 devices in a mesh: ctx: 16 (over y, z_lo, core), fsdp: 8 (over z_hi, x).
Axes of the slice: x: 4, y: 4, z: 4 (z_hi: 2, z_lo: 2; z = z_hi * 2 + z_lo), core: 2. Of those that a mesh axis runs over, the one named last changes fastest.
Arguments:
- tokens: bfloat16 [8, 4096, 576], P('fsdp', 'ctx'), may hold values from -6 to 6
- block_order: int32 [32], replicated, may hold values from 0 to 31, as said below
- doc_ids: int32 [8, 4096], P('fsdp'), may hold values from 0 to 4, as said below
- norm_gains: bfloat16 [2, 2, 576], P(None, None, 'fsdp'), may hold values from 0.5 to 1.5
- w_qkv: bfloat16 [2, 576, 960], P(None, 'fsdp'), may hold values from -0.25 to 0.25
- w_out: bfloat16 [2, 576, 576], P(None, 'fsdp'), may hold values from -3 to 3
- w_gate_up: bfloat16 [2, 576, 3072], P(None, 'fsdp'), may hold values from -0.25 to 0.25
- w_down: bfloat16 [2, 1536, 576], P(None, 'fsdp'), may hold values from -0.15625 to 0.15625
- cotangent: bfloat16 [8, 4096, 576], P('fsdp', 'ctx'), may hold values from -6 to 6
Outputs:
- output: bfloat16 [8, 4096, 576], P('fsdp', 'ctx')
- input_grad: float32 [8, 4096, 576], P('fsdp', 'ctx')
- gain_grad: float32 [2, 2, 576], P(None, None, 'fsdp')
- qkv_grad: float32 [2, 576, 960], P(None, 'fsdp')
- out_proj_grad: float32 [2, 576, 576], P(None, 'fsdp')
- gate_up_grad: float32 [2, 576, 3072], P(None, 'fsdp')
- down_grad: float32 [2, 1536, 576], P(None, 'fsdp')
The draws below stay inside these ranges and needn't reach their ends.
Inputs may be any that keep to these rules, and one draw needn't show every extreme that they name: `block_order`: entries 2 c and 2 c + 1 add up to 31, and every block number appears once. `doc_ids`: non-decreasing along each sequence; document 0 covers at least the first 2176 positions; the last position has id 4.
All inputs are finite; a program needn't handle non-finite values.
Results may differ from the reference program's by a relative error of at most 0.025.
Values may be sent and summed in bfloat16 or wider, within the bound.
No kernel may reach another device: no remote copies, remote signals or barrier semaphores. Data moves between devices by JAX's collectives and lax.ppermute only.
A program may use at most 192 MiB of HBM per device.

```python
import jax
import jax.numpy as jnp
from jax import lax

D = 576
HEADS = 9
KV_HEADS = 3
HEAD_DIM = 64
FF = 1536
LAYERS = 2
BLK = 128
NBLK = 32
LEN = 4096
SEQS = 8


def draw_block_order(key, part):
    key = jax.random.fold_in(key, 11)
    pairs = jax.random.permutation(key, NBLK // 2).astype(jnp.int32)
    mirror = (NBLK - 1 - pairs).astype(jnp.int32)
    return jnp.stack([pairs, mirror], 1).reshape(NBLK).astype(jnp.int32)


def draw_doc_ids(key, part):
    key = jax.random.fold_in(key, 23)
    head_key, tail_key = jax.random.split(key)
    first_end = jax.random.randint(head_key, (SEQS, 1), LEN // 2 + BLK, LEN).astype(jnp.int32)
    offsets = jax.random.randint(tail_key, (SEQS, 3), 0, LEN).astype(jnp.int32)
    later = first_end + offsets % (LEN - first_end)
    bounds = jnp.concatenate([first_end, later], 1)
    places = jnp.arange(LEN, dtype=jnp.int32)
    return jnp.sum((places[None, :, None] >= bounds[:, None, :]).astype(jnp.int32), -1).astype(jnp.int32)


def level_of(rng, shape, cuts, least, top_value):
    gain = 1.0
    for position, parts in cuts:
        draws = jax.random.uniform(jax.random.fold_in(jax.random.fold_in(rng, 6), position), (parts,), jnp.float32, least / len(cuts), top_value / len(cuts))
        gain = gain * jnp.repeat(jnp.exp(draws), shape[position] // parts).reshape((-1,) + (1,) * (len(shape) - 1 - position))
    return gain


def noise(key, dims, deviation, bound, cuts=(), kind=jnp.bfloat16):
    array = jax.random.normal(key, dims, jnp.float32) * deviation
    if len(cuts) > 0:
        array = level_of(key, dims, cuts, -0.22, 0.18) * array
    return jnp.clip(array, min=-bound, max=bound).astype(kind)


def setup_inputs(seed: int = 0) -> dict:
    splits = jax.random.split(jax.random.key(seed), 10)
    tokens = noise(splits[0], (SEQS, LEN, D), 1.0, 6.0, ((0, 8), (1, 16)))
    block_order = draw_block_order(jax.random.fold_in(splits[9], 71), 0)
    doc_ids = draw_doc_ids(jax.random.fold_in(splits[9], 71), 0)
    norm_gains = jnp.clip(1.0 + 0.1 * jax.random.normal(splits[3], (LAYERS, 2, D), jnp.float32), 0.5, 1.5).astype(jnp.bfloat16)
    w_qkv = noise(splits[4], (LAYERS, D, (HEADS + 2 * KV_HEADS) * HEAD_DIM), D ** -0.5, 0.25, ((1, 8),))
    w_out = noise(splits[5], (LAYERS, HEADS * HEAD_DIM, D), (max(D // 128, 1)) ** -0.5, 3.0, ((1, 8),))
    w_gate_up = noise(splits[6], (LAYERS, D, 2 * FF), D ** -0.5, 0.25, ((1, 8),))
    w_down = noise(splits[7], (LAYERS, FF, D), FF ** -0.5, 0.15625, ((1, 8),))
    cotangent = noise(splits[8], (SEQS, LEN, D), 1.0, 6.0, ((0, 8), (1, 16)))
    return {"tokens": tokens, "block_order": block_order, "doc_ids": doc_ids, "norm_gains": norm_gains, "w_qkv": w_qkv, "w_out": w_out, "w_gate_up": w_gate_up, "w_down": w_down, "cotangent": cotangent}


EPS = 1e-05
THETA = 100000.0
NEG = -1e+30

@jax.custom_vjp
def low(v):
    return lax.optimization_barrier(v.astype(jnp.bfloat16)).astype(jnp.float32)

@jax.custom_vjp
def low_back(v):
    return v

def low_keep(v):
    return (low(v), None)

def low_pass(kept, grad):
    return (grad,)

def back_keep(v):
    return (v, None)

def back_low(kept, grad):
    return (low(grad),)
low.defvjp(low_keep, low_pass)
low_back.defvjp(back_keep, back_low)

def rope_tables(positions):
    half_dim = HEAD_DIM // 2
    freq_idx = jnp.arange(half_dim, dtype=jnp.float32)
    inv_freq = THETA ** (-freq_idx / half_dim)
    angles = positions.astype(jnp.float32)[:, None] * inv_freq[None, :]
    return (jnp.cos(angles), jnp.sin(angles))

def rotate(vectors, cosine, sine_t):
    half_dim = HEAD_DIM // 2
    lower_half = vectors[..., :half_dim]
    second = vectors[..., half_dim:]
    cos_b = cosine[:, None, :]
    sin_b = sine_t[:, None, :]
    return jnp.concatenate([lower_half * cos_b - second * sin_b, second * cos_b + lower_half * sin_b], -1)

def rms_scale(hidden):
    return hidden * lax.rsqrt(lax.optimization_barrier(jnp.mean(hidden * hidden, -1, keepdims=True)) + EPS)

def attend(queries, key_part, val_part, positions, doc_row):
    q_rows = min(512, LEN)
    q_steps = LEN // q_rows
    groups = HEADS // KV_HEADS
    q_blocks = queries.reshape(q_steps, q_rows, KV_HEADS, groups, HEAD_DIM)
    pos_blocks = positions.reshape(q_steps, q_rows)
    doc_blocks = doc_row.reshape(q_steps, q_rows)
    factor = HEAD_DIM ** (-0.5)

    def one_block(pieces):
        q_part, pos_part, doc_part = pieces
        scores = jnp.einsum('qkgd,nkd->kgqn', q_part, key_part, precision=lax.Precision.HIGHEST) * factor
        allowed = (doc_part[:, None] == doc_row[None, :]) & (positions[None, :] <= pos_part[:, None])
        scores = low_back(jnp.where(allowed[None, None], scores, NEG))
        prob_b = low(jax.nn.softmax(scores, -1))
        mixed = jnp.einsum('kgqn,nkd->qkgd', prob_b, val_part, precision=lax.Precision.HIGHEST)
        return mixed.reshape(q_rows, HEADS * HEAD_DIM)
    return lax.map(jax.checkpoint(one_block), (q_blocks, pos_blocks, doc_blocks)).reshape(LEN, HEADS * HEAD_DIM)

def layer_forward(hidden, gain_pair, wqkv, wout, wgu, wdown, cosine, sine_t, positions, doc_row):
    q_width = HEADS * HEAD_DIM
    kv_width = KV_HEADS * HEAD_DIM
    attn_in = low(rms_scale(hidden) * gain_pair[0])
    qkv = low_back(jnp.dot(attn_in, wqkv, precision=lax.Precision.HIGHEST))
    queries = low(rotate(qkv[:, :q_width].reshape(LEN, HEADS, HEAD_DIM), cosine, sine_t))
    key_part = low(rotate(qkv[:, q_width:q_width + kv_width].reshape(LEN, KV_HEADS, HEAD_DIM), cosine, sine_t))
    val_part = low(qkv[:, q_width + kv_width:].reshape(LEN, KV_HEADS, HEAD_DIM))
    attn_out = low_back(low(attend(queries, key_part, val_part, positions, doc_row)))
    mid_h = hidden + low_back(jnp.dot(attn_out, wout, precision=lax.Precision.HIGHEST))
    mlp_in = low(rms_scale(mid_h) * gain_pair[1])
    gate_up = low_back(jnp.dot(mlp_in, wgu, precision=lax.Precision.HIGHEST))
    inner_act = low(jax.nn.silu(gate_up[:, :FF]) * gate_up[:, FF:])
    return mid_h + low_back(jnp.dot(inner_act, wdown, precision=lax.Precision.HIGHEST))

def reference(tokens, block_order, doc_ids, norm_gains, w_qkv, w_out, w_gate_up, w_down, cotangent):
    places = jnp.arange(LEN, dtype=jnp.int32)
    positions = (block_order[places // BLK] * BLK + places % BLK).astype(jnp.int32)
    cosine, sine_t = rope_tables(positions)
    params = (norm_gains.astype(jnp.float32), w_qkv.astype(jnp.float32), w_out.astype(jnp.float32), w_gate_up.astype(jnp.float32), w_down.astype(jnp.float32))

    def forward(inputs, weights, doc_row):
        gains_all, wqkv_all, wout_all, wgu_all, wdown_all = weights
        hidden = inputs
        for layer_idx in range(LAYERS):
            hidden = layer_forward(hidden, gains_all[layer_idx], wqkv_all[layer_idx], wout_all[layer_idx], wgu_all[layer_idx], wdown_all[layer_idx], cosine, sine_t, positions, doc_row)
        return hidden

    def one_sequence(totals, pieces):
        inputs, doc_natural, cot_row = pieces
        doc_row = doc_natural[positions]
        result, pull = jax.vjp(lambda first_arg, weights: forward(first_arg, weights, doc_row), inputs, params)
        d_inputs, d_params = pull(cot_row)
        return (jax.tree.map(jnp.add, totals, d_params), (result.astype(jnp.bfloat16), d_inputs))
    zeros = jax.tree.map(jnp.zeros_like, params)
    totals, (outputs, d_tokens) = lax.scan(one_sequence, zeros, (tokens.astype(jnp.float32), doc_ids, cotangent.astype(jnp.float32)))
    return (outputs, d_tokens, totals[0], totals[1], totals[2], totals[3], totals[4])
```

```python
import functools

import jax
import jax.numpy as jnp
from jax import lax
from jax.experimental import pallas as pl
from jax.experimental.pallas import tpu as pltpu
from jax.sharding import PartitionSpec as P

D = 576
HEADS = 9
KV_HEADS = 3
GROUP = 3
HEAD_DIM = 64
FF = 1536
LAYERS = 2
BLK = 128
NBLK = 32
EPS = 1e-05
THETA = 100000.0
NEG = -1e30
F32 = jnp.float32
BF16 = jnp.bfloat16
LANES = GROUP * BLK
CTX = 16
FSDP = 8
SHARD = D // FSDP
HALF = FF // 2

PARTNER = [(i, i ^ 1) for i in range(CTX)]
SAME_CORE = [[2 * chip + core for chip in range(CTX // 2)] for core in range(2)]


def to_partner(x):
    return lax.ppermute(x, "ctx", PARTNER)


def over_chips(x):
    return lax.all_to_all(x, "ctx", 0, 0, axis_index_groups=SAME_CORE, tiled=True)


def over_fsdp(x):
    return lax.all_to_all(x, "fsdp", 0, 0, tiled=True)


def dot_tn(a, b):
    return lax.dot_general(a, b, (((0,), (0,)), ((), ())), preferred_element_type=F32)


def dot_nt(a, b):
    return lax.dot_general(a, b, (((1,), (1,)), ((), ())), preferred_element_type=F32)


def fill_keys(sc, own_ref, other_ref, kv_s):
    core = sc[2]
    for chip in range(CTX // 2):
        for half in range(2):
            lanes = slice(half * BLK, (half + 1) * BLK)
            block = sc[7 + 2 * (2 * chip + core) + half]
            kv_s[block] = own_ref[chip, :, 0, :, lanes]
            block = sc[7 + 2 * (2 * chip + 1 - core) + half]
            kv_s[block] = other_ref[chip, :, 0, :, lanes]


def fill_queries(sc, src_ref, dst):
    for half in range(2):
        lanes = slice(half * BLK, (half + 1) * BLK)
        which = jnp.bitwise_xor(half, sc[1])
        dst[which] = jnp.concatenate([src_ref[j, :, lanes] for j in range(GROUP)], axis=1)


def query_rows(sc, which):
    block = jnp.where(which == 0, sc[0], NBLK - 1 - sc[0])
    lane = lax.broadcasted_iota(jnp.int32, (1, LANES), 1)
    pos = block * BLK + jnp.bitwise_and(lane, BLK - 1)
    start = jnp.zeros((1, LANES), jnp.int32)
    for d in range(4):
        start = jnp.where(pos >= sc[3 + d], jnp.maximum(start, sc[3 + d]), start)
    return pos, start


def forward_kernel(sc, q_ref, own_ref, other_ref, o_ref, lse_ref, kv_s, q_s, o_s, acc_s, m_s, l_s):
    fill_keys(sc, own_ref, other_ref, kv_s)
    fill_queries(sc, q_ref, q_s)
    acc_s[...] = jnp.zeros_like(acc_s)
    m_s[...] = jnp.full_like(m_s, NEG)
    l_s[...] = jnp.zeros_like(l_s)
    low = sc[0]
    hi_doc0 = query_rows(sc, 1)[1] == 0
    sub = lax.broadcasted_iota(jnp.int32, (BLK, LANES), 0)

    def update(block, which, slot, valid):
        scores = dot_tn(kv_s[block, 0], q_s[which])
        scores = jnp.where(valid, scores, NEG)
        old = m_s[slot]
        new = jnp.maximum(old, jnp.max(scores, axis=0, keepdims=True))
        prob = jnp.exp(scores - new)
        shrink = jnp.exp(old - new)
        m_s[slot] = new
        l_s[slot] = l_s[slot] * shrink + jnp.sum(prob, axis=0, keepdims=True)
        acc_s[slot] = acc_s[slot] * shrink + jnp.dot(
            kv_s[block, 1], prob.astype(BF16), preferred_element_type=F32
        )

    def masked(block, which):
        pos, start = query_rows(sc, which)
        at = block * BLK + sub
        return (at >= start) & (at <= pos)

    def step(i, carry):
        update(i, 1, 2, hi_doc0)
        which = (i > low).astype(jnp.int32)
        block = jnp.where(i <= low, i, NBLK // 2 - 1 + i - low)
        update(block, which, which, masked(block, which))
        return carry

    lax.fori_loop(0, NBLK // 2, step, 0)
    update(NBLK - 1 - low, 1, 1, masked(NBLK - 1 - low, 1))
    top = jnp.maximum(m_s[1], m_s[2])
    w1, w2 = jnp.exp(m_s[1] - top), jnp.exp(m_s[2] - top)
    total = l_s[1] * w1 + l_s[2] * w2
    o_s[1] = (acc_s[1] * w1 + acc_s[2] * w2) / total
    lse_ref[0, 1] = top + jnp.log(total)
    o_s[0] = acc_s[0] / l_s[0]
    lse_ref[0, 0] = m_s[0] + jnp.log(l_s[0])
    for half in range(2):
        which = jnp.bitwise_xor(half, sc[1])
        mine = o_s[which]
        for j in range(GROUP):
            o_ref[j, :, half * BLK : (half + 1) * BLK] = mine[:, j * BLK : (j + 1) * BLK]


def backward_kernel(
    sc, q_ref, own_ref, other_ref, o_ref, do_ref, lse_ref,
    dq_ref, down_ref, dother_ref,
    kv_s, q_s, do_s, dq_s, dkv_s, delta_s,
):
    fill_keys(sc, own_ref, other_ref, kv_s)
    fill_queries(sc, q_ref, q_s)
    fill_queries(sc, do_ref, do_s)
    fill_queries(sc, o_ref, dq_s)
    for which in range(2):
        delta_s[which] = jnp.sum(dq_s[which] * do_s[which].astype(F32), axis=0, keepdims=True)
    dq_s[...] = jnp.zeros_like(dq_s)
    low = sc[0]
    hi_doc0 = query_rows(sc, 1)[1] == 0
    sub = lax.broadcasted_iota(jnp.int32, (BLK, LANES), 0)

    def tile(block, which, valid):
        key_t, val_t, q_t, do_t = kv_s[block, 0], kv_s[block, 1], q_s[which], do_s[which]
        scores = dot_tn(key_t, q_t)
        prob = jnp.where(valid, jnp.exp(scores - lse_ref[0, which]), 0.0)
        d_prob = dot_tn(val_t, do_t)
        d_score = (prob * (d_prob - delta_s[which])).astype(BF16)
        d_val = dot_nt(do_t, prob.astype(BF16))
        d_key = dot_nt(q_t, d_score)
        d_q = jnp.dot(key_t, d_score, preferred_element_type=F32)
        return d_key, d_val, d_q

    def masked(block, which):
        pos, start = query_rows(sc, which)
        at = block * BLK + sub
        return (at >= start) & (at <= pos)

    zero = jnp.zeros((NBLK // 2,) + dkv_s.shape[1:], F32)
    dkv_s[NBLK // 2 :] = zero

    def step(i, carry):
        d_key, d_val, d_q = tile(i, 1, hi_doc0)
        dq_s[2] = dq_s[2] + d_q
        dkv_s[i, 0] = d_key
        dkv_s[i, 1] = d_val
        which = (i > low).astype(jnp.int32)
        block = jnp.where(i <= low, i, NBLK // 2 - 1 + i - low)
        d_key, d_val, d_q = tile(block, which, masked(block, which))
        dq_s[which] = dq_s[which] + d_q
        dkv_s[block, 0] = dkv_s[block, 0] + d_key
        dkv_s[block, 1] = dkv_s[block, 1] + d_val
        return carry

    lax.fori_loop(0, NBLK // 2, step, 0)
    last = NBLK - 1 - low
    d_key, d_val, d_q = tile(last, 1, masked(last, 1))
    dkv_s[last, 0] = d_key
    dkv_s[last, 1] = d_val
    dq_s[1] = dq_s[1] + dq_s[2] + d_q
    core = sc[2]
    scale = HEAD_DIM**-0.5
    for half in range(2):
        lanes = slice(half * BLK, (half + 1) * BLK)
        which = jnp.bitwise_xor(half, sc[1])
        mine = dq_s[which] * scale
        for j in range(GROUP):
            dq_ref[j, :, lanes] = mine[:, j * BLK : (j + 1) * BLK]
        for chip in range(CTX // 2):
            block = sc[7 + 2 * (2 * chip + core) + half]
            down_ref[chip, :, 0, :, lanes] = dkv_s[block].astype(BF16)
            block = sc[7 + 2 * (2 * chip + 1 - core) + half]
            dother_ref[chip, :, 0, :, lanes] = dkv_s[block].astype(BF16)


ROWS = 2 * BLK
HEAD_SPEC = pl.BlockSpec((GROUP, HEAD_DIM, ROWS), lambda g, sc: (g, 0, 0))
KV_SPEC = pl.BlockSpec((CTX // 2, 2, 1, HEAD_DIM, ROWS), lambda g, sc: (0, 0, g, 0, 0))
LSE_SPEC = pl.BlockSpec((1, 2, 1, LANES), lambda g, sc: (g, 0, 0, 0))
HEAD_SHAPE = jax.ShapeDtypeStruct((HEADS, HEAD_DIM, ROWS), F32)
KV_SHAPE = jax.ShapeDtypeStruct((CTX // 2, 2, KV_HEADS, HEAD_DIM, ROWS), BF16)
LSE_SHAPE = jax.ShapeDtypeStruct((KV_HEADS, 2, 1, LANES), F32)
KERNEL_PARAMS = pltpu.CompilerParams(
    dimension_semantics=("arbitrary",), vmem_limit_bytes=40 * 2**20
)


def attention(scalars, q_t, own, other):
    return pl.pallas_call(
        forward_kernel,
        grid_spec=pltpu.PrefetchScalarGridSpec(
            num_scalar_prefetch=1,
            grid=(KV_HEADS,),
            in_specs=[HEAD_SPEC, KV_SPEC, KV_SPEC],
            out_specs=[HEAD_SPEC, LSE_SPEC],
            scratch_shapes=[
                pltpu.VMEM((NBLK, 2, HEAD_DIM, BLK), BF16),
                pltpu.VMEM((2, HEAD_DIM, LANES), BF16),
                pltpu.VMEM((2, HEAD_DIM, LANES), F32),
                pltpu.VMEM((3, HEAD_DIM, LANES), F32),
                pltpu.VMEM((3, 1, LANES), F32),
                pltpu.VMEM((3, 1, LANES), F32),
            ],
        ),
        out_shape=[HEAD_SHAPE, LSE_SHAPE],
        compiler_params=KERNEL_PARAMS,
        name="attention",
    )(scalars, q_t, own, other)


def attention_back(scalars, q_t, own, other, o_t, do_t, lse):
    return pl.pallas_call(
        backward_kernel,
        grid_spec=pltpu.PrefetchScalarGridSpec(
            num_scalar_prefetch=1,
            grid=(KV_HEADS,),
            in_specs=[HEAD_SPEC, KV_SPEC, KV_SPEC, HEAD_SPEC, HEAD_SPEC, LSE_SPEC],
            out_specs=[HEAD_SPEC, KV_SPEC, KV_SPEC],
            scratch_shapes=[
                pltpu.VMEM((NBLK, 2, HEAD_DIM, BLK), BF16),
                pltpu.VMEM((2, HEAD_DIM, LANES), BF16),
                pltpu.VMEM((2, HEAD_DIM, LANES), BF16),
                pltpu.VMEM((3, HEAD_DIM, LANES), F32),
                pltpu.VMEM((NBLK, 2, HEAD_DIM, BLK), F32),
                pltpu.VMEM((2, 1, LANES), F32),
            ],
        ),
        out_shape=[HEAD_SHAPE, KV_SHAPE, KV_SHAPE],
        compiler_params=KERNEL_PARAMS,
        name="attention_back",
    )(scalars, q_t, own, other, o_t, do_t, lse)


def rotate(x, cosine, sine):
    half = HEAD_DIM // 2
    first, second = x[:, :half], x[:, half:]
    return jnp.concatenate([first * cosine - second * sine, second * cosine + first * sine], 1)


def normed(hidden):
    inv_rms = lax.rsqrt(jnp.mean(hidden * hidden, -1, keepdims=True) + EPS)
    return hidden * inv_rms, inv_rms


def norm_back(d_unit, unit, inv_rms):
    return inv_rms * (d_unit - unit * jnp.mean(d_unit * unit, -1, keepdims=True))


def mm(a, b):
    return jnp.dot(a, b, preferred_element_type=F32)


def ein(spec, a, b):
    return jnp.einsum(spec, a, b, preferred_element_type=F32)


def local(tokens, block_order, doc_ids, norm_gains, w_qkv, w_out, w_gate_up, w_down, cotangent):
    place = lax.axis_index("ctx")
    core = jnp.bitwise_and(place, 1)
    first_core = core == 0
    kv_rows = 2 * KV_HEADS * HEAD_DIM
    q_rows = HEADS * HEAD_DIM

    gain_cols = jnp.transpose(norm_gains.reshape(2 * LAYERS, SHARD))
    proj = jnp.concatenate([w_qkv, w_out], 2)
    proj = jnp.concatenate([jnp.where(first_core, proj[0], proj[1]), gain_cols], 1)
    proj_own = over_fsdp(jnp.broadcast_to(proj[None], (FSDP,) + proj.shape)).reshape(D, -1)
    proj_other = to_partner(proj_own)
    proj_layer = [
        jnp.where(first_core, proj_own, proj_other),
        jnp.where(first_core, proj_other, proj_own),
    ]
    gains = jnp.transpose(proj_own[:, -2 * LAYERS :].astype(F32)).reshape(LAYERS, 2, D)
    wgu_cut = w_gate_up.reshape(LAYERS, SHARD, 2, FSDP, 2, FF // FSDP // 2)
    wgu_cut = jnp.where(first_core, wgu_cut[..., 0, :], wgu_cut[..., 1, :])
    wgu_cut = wgu_cut.reshape(LAYERS, SHARD, FF)
    wd_cut = w_down.reshape(LAYERS, 2, FF // FSDP // 2, D)
    wd_cut = jnp.where(first_core, wd_cut[:, 0], wd_cut[:, 1]).reshape(LAYERS, SHARD, HALF)
    mlp_cut = jnp.concatenate([wgu_cut, wd_cut], 2)
    mlp_own = [lax.all_gather(mlp_cut[l], "fsdp", axis=0, tiled=True) for l in range(LAYERS)]
    mlp_other = [to_partner(w) for w in mlp_own]

    def mlp_weights(layer):
        return [
            (w[:, :FF], w[:, FF:].reshape(HALF, D)) for w in (mlp_own[layer], mlp_other[layer])
        ]

    first_block = lax.dynamic_index_in_dim(block_order, 2 * place, 0, keepdims=False)
    low = jnp.minimum(first_block, NBLK - 1 - first_block)
    low_half = (first_block != low).astype(jnp.int32)
    starts = jnp.sum(
        (doc_ids[0][None, :] < jnp.arange(1, 5, dtype=jnp.int32)[:, None]).astype(jnp.int32), 1
    )
    scalars = jnp.concatenate([jnp.stack([low, low_half, core]), starts, block_order])
    lane = jnp.arange(ROWS, dtype=jnp.int32)
    pos = jnp.where(lane < BLK, first_block, NBLK - 2 - first_block) * BLK + lane
    inv_freq = THETA ** (-jnp.arange(HEAD_DIM // 2, dtype=F32) / (HEAD_DIM // 2))
    angles = pos.astype(F32)[None, :] * inv_freq[:, None]
    cosine, sine = jnp.cos(angles), jnp.sin(angles)

    hidden = tokens[0].astype(F32)
    saved = []
    for layer in range(LAYERS):
        wqkv = proj_layer[layer][:, : q_rows + kv_rows]
        wout = proj_layer[layer][:, q_rows + kv_rows : q_rows + kv_rows + D]
        unit_a, rms_a = normed(hidden)
        attn_in = (unit_a * gains[layer, 0]).astype(BF16)
        qkv_t = ein("de,td->et", wqkv, attn_in).reshape(-1, HEAD_DIM, ROWS)
        turned = rotate(qkv_t[: HEADS + KV_HEADS], cosine, sine)
        q_t = (turned[:HEADS] * HEAD_DIM**-0.5).astype(BF16)
        kv_t = jnp.concatenate([turned[HEADS:], qkv_t[HEADS + KV_HEADS :]], 0).astype(BF16)
        kv_t = kv_t.reshape(1, 2, KV_HEADS, HEAD_DIM, ROWS)
        kv_own = over_chips(jnp.broadcast_to(kv_t, (CTX // 2,) + kv_t.shape[1:]))
        kv_other = to_partner(kv_own)
        o_t, lse = attention(scalars, q_t, kv_own, kv_other)
        attn_out = o_t.astype(BF16).reshape(q_rows, ROWS)
        mid = hidden + ein("at,ad->td", attn_out, wout)
        unit_m, rms_m = normed(mid)
        mlp_in = (unit_m * gains[layer, 1]).astype(BF16)
        hidden = mid
        halves = []
        for wgu, wdown in mlp_weights(layer):
            gate_up = mm(mlp_in, wgu)
            inner = (jax.nn.silu(gate_up[:, :HALF]) * gate_up[:, HALF:]).astype(BF16)
            hidden = hidden + mm(inner, wdown)
            halves.append((wgu, wdown, gate_up, inner))
        saved.append(
            (wqkv, wout, unit_a, rms_a, attn_in, q_t, kv_own, kv_other, o_t, lse, attn_out,
             unit_m, rms_m, mlp_in, halves)
        )
    output = hidden.astype(BF16).reshape(1, ROWS, D)

    d_hidden = cotangent[0].astype(F32)
    mlp_shares = [None] * LAYERS
    proj_grads = [None] * LAYERS
    gain_grads = [None] * LAYERS
    for layer in reversed(range(LAYERS)):
        (wqkv, wout, unit_a, rms_a, attn_in, q_t, kv_own, kv_other, o_t, lse, attn_out,
         unit_m, rms_m, mlp_in, halves) = saved[layer]
        grad_b = d_hidden.astype(BF16)
        d_norm = 0.0
        packs = []
        for wgu, wdown, gate_up, inner in halves:
            d_inner = ein("td,fd->tf", grad_b, wdown)
            gate, up = gate_up[:, :HALF], gate_up[:, HALF:]
            sig = jax.nn.sigmoid(gate)
            d_gate = d_inner * up * sig * (1.0 + gate * (1.0 - sig))
            d_up = d_inner * (gate * sig)
            d_gu = jnp.concatenate([d_gate, d_up], 1).astype(BF16)
            d_norm = d_norm + ein("tf,df->td", d_gu, wgu)
            d_wdown = ein("tf,td->fd", inner, grad_b).astype(BF16)
            d_wgu = ein("td,tf->df", mlp_in, d_gu).astype(BF16)
            packs.append(jnp.concatenate([d_wgu, d_wdown.reshape(D, HALF)], 1))
        both = (packs[0].astype(F32) + to_partner(packs[1]).astype(F32)).astype(BF16)
        mlp_shares[layer] = lax.psum_scatter(both, "fsdp", scatter_dimension=0, tiled=True)
        d_gain_m = jnp.sum(d_norm * unit_m, 0)
        d_hidden = d_hidden + norm_back(d_norm * gains[layer, 1], unit_m, rms_m)
        grad_b = d_hidden.astype(BF16)
        d_wout = mm(attn_out, grad_b)
        do_t = ein("ad,td->at", wout, grad_b).astype(BF16).reshape(HEADS, HEAD_DIM, ROWS)
        dq_t, dkv_own, dkv_other = attention_back(scalars, q_t, kv_own, kv_other, o_t, do_t, lse)
        dkv = (dkv_own.astype(F32) + to_partner(dkv_other).astype(F32)).astype(BF16)
        dkv = jnp.sum(over_chips(dkv).astype(F32), 0)
        turned = jnp.concatenate([dq_t, dkv[0]], 0)
        d_qkv = jnp.concatenate([rotate(turned, cosine, -sine), dkv[1]], 0)
        d_qkv = d_qkv.astype(BF16).reshape(q_rows + kv_rows, ROWS)
        d_wqkv = ein("td,et->de", attn_in, d_qkv)
        d_norm = ein("et,de->td", d_qkv, wqkv)
        d_gain_a = jnp.sum(d_norm * unit_a, 0)
        d_hidden = d_hidden + norm_back(d_norm * gains[layer, 0], unit_a, rms_a)
        gain_grads[layer] = jnp.stack([d_gain_a, d_gain_m])
        proj_grads[layer] = jnp.concatenate([d_wqkv, d_wout], 1).astype(BF16)
    input_grad = d_hidden.reshape(1, ROWS, D)

    own = jnp.where(first_core, proj_grads[0], proj_grads[1])
    other = jnp.where(first_core, proj_grads[1], proj_grads[0])
    d_gains = jnp.transpose(jnp.stack(gain_grads).reshape(2 * LAYERS, D)).astype(BF16)
    own = own.astype(F32) + to_partner(other).astype(F32)
    own = jnp.concatenate([own.astype(BF16), d_gains], 1).reshape(FSDP, SHARD, -1)
    proj_share = jnp.sum(over_fsdp(own).astype(F32), 0)

    share = jnp.concatenate(
        [mlp_shares[0], mlp_shares[1], proj_share.astype(BF16)], 1
    )
    width = share.shape[1]
    pieces = over_chips(share.reshape(CTX // 2, SHARD // 8, width)).astype(F32)
    piece = jnp.sum(pieces.reshape(CTX // 2, SHARD // 8, width), 0).astype(BF16)
    total = over_chips(jnp.broadcast_to(piece[None], (CTX // 2,) + piece.shape)).reshape(SHARD, width)
    theirs = to_partner(total)
    d_gain = total[:, -2 * LAYERS :].astype(F32) + theirs[:, -2 * LAYERS :].astype(F32)
    gain_grad = jnp.transpose(d_gain).reshape(LAYERS, 2, SHARD)
    pair = (jnp.where(first_core, total, theirs), jnp.where(first_core, theirs, total))
    pw = FF + HALF
    proj = jnp.stack([t[:, 2 * pw : 2 * pw + 2 * q_rows + kv_rows] for t in pair]).astype(F32)
    qkv_grad, out_proj_grad = proj[..., : q_rows + kv_rows], proj[..., q_rows + kv_rows :]
    gate_up_grad, down_grad = [], []
    for layer in range(LAYERS):
        mine = [t[:, layer * pw : (layer + 1) * pw] for t in pair]
        cols = jnp.stack([t[:, :FF].reshape(SHARD, 2, FSDP, -1) for t in mine], 3)
        gate_up_grad.append(cols.reshape(SHARD, 2 * FF))
        rows = [t[:, FF:].reshape(FF // FSDP // 2, D) for t in mine]
        down_grad.append(jnp.concatenate(rows, 0))
    gate_up_grad = jnp.stack(gate_up_grad).astype(F32)
    down_grad = jnp.stack(down_grad).astype(F32)
    return (output, input_grad, gain_grad, qkv_grad, out_proj_grad, gate_up_grad, down_grad)


def solution(mesh):
    in_specs = (
        P("fsdp", "ctx", None),
        P(),
        P("fsdp", None),
        P(None, None, "fsdp"),
        P(None, "fsdp", None),
        P(None, "fsdp", None),
        P(None, "fsdp", None),
        P(None, "fsdp", None),
        P("fsdp", "ctx", None),
    )
    out_specs = (
        P("fsdp", "ctx", None),
        P("fsdp", "ctx", None),
        P(None, None, "fsdp"),
        P(None, "fsdp", None),
        P(None, "fsdp", None),
        P(None, "fsdp", None),
        P(None, "fsdp", None),
    )
    return jax.shard_map(local, mesh=mesh, in_specs=in_specs, out_specs=out_specs, check_vma=False)
```

```python
import functools

import jax
import jax.numpy as jnp
from jax import lax
from jax.experimental import pallas as pl
from jax.experimental.pallas import tpu as pltpu
from jax.sharding import PartitionSpec as P

D = 576
HEADS = 9
KV_HEADS = 3
GROUP = 3
HEAD_DIM = 64
FF = 1536
LAYERS = 2
BLK = 128
NBLK = 32
EPS = 1e-05
THETA = 100000.0
NEG = -1e30
F32 = jnp.float32
BF16 = jnp.bfloat16
LANES = GROUP * BLK
CTX = 16
FSDP = 8
SHARD = D // FSDP
HALF = FF // 2
Q_ROWS = HEADS * HEAD_DIM
KV_ROWS = 2 * KV_HEADS * HEAD_DIM

PARTNER = [(i, i ^ 1) for i in range(CTX)]
SAME_CORE = [[2 * chip + core for chip in range(CTX // 2)] for core in range(2)]


def to_partner(x):
    return lax.ppermute(x, "ctx", PARTNER)


def over_chips(x):
    return lax.all_to_all(x, "ctx", 0, 0, axis_index_groups=SAME_CORE, tiled=True)


def over_fsdp(x):
    return lax.all_to_all(x, "fsdp", 0, 0, tiled=True)


def gather_fsdp(x):
    return over_fsdp(jnp.broadcast_to(x[None], (FSDP,) + x.shape)).reshape(-1, x.shape[1])


def scatter_fsdp(x):
    parts = over_fsdp(x.reshape(FSDP, -1, x.shape[1]))
    return jnp.sum(parts.astype(F32), 0).astype(BF16)


def sum_pair(a, b):
    return (a.astype(F32) + b.astype(F32)).astype(BF16)


def sum_chips(x):
    for bit in (2, 4, 8):
        x = sum_pair(x, lax.ppermute(x, "ctx", [(i, i ^ bit) for i in range(CTX)]))
    return x


def dot_tn(a, b):
    return lax.dot_general(a, b, (((0,), (0,)), ((), ())), preferred_element_type=F32)


def dot_nt(a, b):
    return lax.dot_general(a, b, (((1,), (1,)), ((), ())), preferred_element_type=F32)


UNROLL_F = 9
UNROLL_B = 3
CHUNK = 4
KEYS = CHUNK * BLK
CHUNKS = NBLK // CHUNK


def fill_keys(sc, own_ref, other_ref, kv_s):
    core = sc[2]
    for chip in range(CTX // 2):
        for half in range(2):
            lanes = slice(half * BLK, (half + 1) * BLK)
            block = sc[7 + 2 * (2 * chip + core) + half]
            kv_s[block] = own_ref[chip, :, 0, :, lanes]
            block = sc[7 + 2 * (2 * chip + 1 - core) + half]
            kv_s[block] = other_ref[chip, :, 0, :, lanes]


def fill_queries(sc, src_ref, dst):
    for half in range(2):
        lanes = slice(half * BLK, (half + 1) * BLK)
        which = jnp.bitwise_xor(half, sc[1])
        dst[which] = jnp.concatenate([src_ref[j, :, lanes] for j in range(GROUP)], axis=1)


def query_rows(sc, which):
    block = jnp.where(which == 0, sc[0], NBLK - 1 - sc[0])
    lane = lax.broadcasted_iota(jnp.int32, (1, LANES), 1)
    pos = block * BLK + jnp.bitwise_and(lane, BLK - 1)
    start = jnp.zeros((1, LANES), jnp.int32)
    for d in range(4):
        start = jnp.where(pos >= sc[3 + d], jnp.maximum(start, sc[3 + d]), start)
    return pos, start


def chunk_of(sc, t):
    high = (NBLK - sc[0] + CHUNK - 1) // CHUNK
    which = (t < high).astype(jnp.int32)
    return which, jnp.where(t < high, t, t - high)


def keys_of(kv_s, chunk, kind):
    return jnp.concatenate([kv_s[chunk * CHUNK + j, kind] for j in range(CHUNK)], axis=1)


def seen(pos_s, which, chunk):
    at = lax.broadcasted_iota(jnp.int32, (KEYS, LANES), 0)
    base = chunk * KEYS
    return (at >= pos_s[which, 1:2] - base) & (at <= pos_s[which, 0:1] - base)


def fill_rows(sc, pos_s):
    for which in range(2):
        pos, start = query_rows(sc, which)
        pos_s[which, 0:1] = pos
        pos_s[which, 1:2] = start


def forward_kernel(sc, q_ref, own_ref, other_ref, o_ref, lse_ref, kv_s, q_s, acc_s, m_s, l_s, pos_s):
    fill_keys(sc, own_ref, other_ref, kv_s)
    fill_queries(sc, q_ref, q_s)
    fill_rows(sc, pos_s)
    acc_s[...] = jnp.zeros_like(acc_s)
    m_s[...] = jnp.full_like(m_s, NEG)
    l_s[...] = jnp.zeros_like(l_s)

    def step(t, carry):
        which, chunk = chunk_of(sc, t)
        scores = dot_tn(keys_of(kv_s, chunk, 0), q_s[which])
        scores = jnp.where(seen(pos_s, which, chunk), scores, NEG)
        old = m_s[which]
        new = jnp.maximum(old, jnp.max(scores, axis=0, keepdims=True))
        prob = jnp.exp(scores - new)
        shrink = jnp.exp(old - new)
        m_s[which] = new
        l_s[which] = l_s[which] * shrink + jnp.sum(prob, axis=0, keepdims=True)
        acc_s[which] = acc_s[which] * shrink + jnp.dot(
            keys_of(kv_s, chunk, 1), prob.astype(BF16), preferred_element_type=F32
        )
        return carry

    lax.fori_loop(0, CHUNKS + 1, step, 0, unroll=UNROLL_F)
    for which in range(2):
        acc_s[which] = acc_s[which] / l_s[which]
        lse_ref[0, which] = m_s[which] + jnp.log(l_s[which])
    for half in range(2):
        mine = acc_s[jnp.bitwise_xor(half, sc[1])]
        for j in range(GROUP):
            o_ref[j, :, half * BLK : (half + 1) * BLK] = mine[:, j * BLK : (j + 1) * BLK]


def backward_kernel(
    sc, q_ref, own_ref, other_ref, o_ref, do_ref, lse_ref,
    dq_ref, down_ref, dother_ref,
    kv_s, q_s, do_s, dq_s, dkv_s, delta_s, pos_s,
):
    fill_keys(sc, own_ref, other_ref, kv_s)
    fill_queries(sc, q_ref, q_s)
    fill_queries(sc, do_ref, do_s)
    fill_queries(sc, o_ref, dq_s)
    fill_rows(sc, pos_s)
    for which in range(2):
        delta_s[which] = jnp.sum(dq_s[which] * do_s[which].astype(F32), axis=0, keepdims=True)
    dq_s[...] = jnp.zeros_like(dq_s)
    dkv_s[...] = jnp.zeros_like(dkv_s)

    def step(t, carry):
        which, chunk = chunk_of(sc, t)
        key_t, val_t, q_t, do_t = keys_of(kv_s, chunk, 0), keys_of(kv_s, chunk, 1), q_s[which], do_s[which]
        scores = dot_tn(key_t, q_t)
        prob = jnp.where(seen(pos_s, which, chunk), jnp.exp(scores - lse_ref[0, which]), 0.0)
        d_prob = dot_tn(val_t, do_t)
        d_score = (prob * (d_prob - delta_s[which])).astype(BF16)
        d_val = dot_nt(do_t, prob.astype(BF16))
        d_key = dot_nt(q_t, d_score)
        dq_s[which] = dq_s[which] + jnp.dot(key_t, d_score, preferred_element_type=F32)
        for j in range(CHUNK):
            lanes = slice(j * BLK, (j + 1) * BLK)
            dkv_s[chunk * CHUNK + j, 0] = dkv_s[chunk * CHUNK + j, 0] + d_key[:, lanes]
            dkv_s[chunk * CHUNK + j, 1] = dkv_s[chunk * CHUNK + j, 1] + d_val[:, lanes]
        return carry

    lax.fori_loop(0, CHUNKS + 1, step, 0, unroll=UNROLL_B)
    core = sc[2]
    scale = HEAD_DIM**-0.5
    for half in range(2):
        lanes = slice(half * BLK, (half + 1) * BLK)
        mine = dq_s[jnp.bitwise_xor(half, sc[1])] * scale
        for j in range(GROUP):
            dq_ref[j, :, lanes] = mine[:, j * BLK : (j + 1) * BLK]
        for chip in range(CTX // 2):
            block = sc[7 + 2 * (2 * chip + core) + half]
            down_ref[chip, :, 0, :, lanes] = dkv_s[block].astype(BF16)
            block = sc[7 + 2 * (2 * chip + 1 - core) + half]
            dother_ref[chip, :, 0, :, lanes] = dkv_s[block].astype(BF16)


ROWS = 2 * BLK
HEAD_SPEC = pl.BlockSpec((GROUP, HEAD_DIM, ROWS), lambda g, sc: (g, 0, 0))
KV_SPEC = pl.BlockSpec((CTX // 2, 2, 1, HEAD_DIM, ROWS), lambda g, sc: (0, 0, g, 0, 0))
LSE_SPEC = pl.BlockSpec((1, 2, 1, LANES), lambda g, sc: (g, 0, 0, 0))
HEAD_SHAPE = jax.ShapeDtypeStruct((HEADS, HEAD_DIM, ROWS), F32)
KV_SHAPE = jax.ShapeDtypeStruct((CTX // 2, 2, KV_HEADS, HEAD_DIM, ROWS), BF16)
LSE_SHAPE = jax.ShapeDtypeStruct((KV_HEADS, 2, 1, LANES), F32)
KERNEL_PARAMS = pltpu.CompilerParams(
    dimension_semantics=("arbitrary",), vmem_limit_bytes=40 * 2**20
)


def attention(scalars, q_t, own, other):
    return pl.pallas_call(
        forward_kernel,
        grid_spec=pltpu.PrefetchScalarGridSpec(
            num_scalar_prefetch=1,
            grid=(KV_HEADS,),
            in_specs=[HEAD_SPEC, KV_SPEC, KV_SPEC],
            out_specs=[HEAD_SPEC, LSE_SPEC],
            scratch_shapes=[
                pltpu.VMEM((NBLK, 2, HEAD_DIM, BLK), BF16),
                pltpu.VMEM((2, HEAD_DIM, LANES), BF16),
                pltpu.VMEM((2, HEAD_DIM, LANES), F32),
                pltpu.VMEM((2, 1, LANES), F32),
                pltpu.VMEM((2, 1, LANES), F32),
                pltpu.VMEM((2, 8, LANES), jnp.int32),
            ],
        ),
        out_shape=[HEAD_SHAPE, LSE_SHAPE],
        compiler_params=KERNEL_PARAMS,
        name="attention",
    )(scalars, q_t, own, other)


def attention_back(scalars, q_t, own, other, o_t, do_t, lse):
    return pl.pallas_call(
        backward_kernel,
        grid_spec=pltpu.PrefetchScalarGridSpec(
            num_scalar_prefetch=1,
            grid=(KV_HEADS,),
            in_specs=[HEAD_SPEC, KV_SPEC, KV_SPEC, HEAD_SPEC, HEAD_SPEC, LSE_SPEC],
            out_specs=[HEAD_SPEC, KV_SPEC, KV_SPEC],
            scratch_shapes=[
                pltpu.VMEM((NBLK, 2, HEAD_DIM, BLK), BF16),
                pltpu.VMEM((2, HEAD_DIM, LANES), BF16),
                pltpu.VMEM((2, HEAD_DIM, LANES), BF16),
                pltpu.VMEM((2, HEAD_DIM, LANES), F32),
                pltpu.VMEM((NBLK, 2, HEAD_DIM, BLK), F32),
                pltpu.VMEM((2, 1, LANES), F32),
                pltpu.VMEM((2, 8, LANES), jnp.int32),
            ],
        ),
        out_shape=[HEAD_SHAPE, KV_SHAPE, KV_SHAPE],
        compiler_params=KERNEL_PARAMS,
        name="attention_back",
    )(scalars, q_t, own, other, o_t, do_t, lse)


def rotate(x, cosine, sine):
    half = HEAD_DIM // 2
    first, second = x[:, :half], x[:, half:]
    return jnp.concatenate([first * cosine - second * sine, second * cosine + first * sine], 1)


def normed(hidden):
    inv_rms = lax.rsqrt(jnp.mean(hidden * hidden, -1, keepdims=True) + EPS)
    return hidden * inv_rms, inv_rms


def norm_back(d_unit, unit, inv_rms):
    return inv_rms * (d_unit - unit * jnp.mean(d_unit * unit, -1, keepdims=True))


def mm(a, b):
    return jnp.dot(a, b, preferred_element_type=F32)


def ein(spec, a, b):
    return jnp.einsum(spec, a, b, preferred_element_type=F32)


def local(tokens, block_order, doc_ids, norm_gains, w_qkv, w_out, w_gate_up, w_down, cotangent):
    place = lax.axis_index("ctx")
    core = jnp.bitwise_and(place, 1)
    first_core = core == 0

    def my_half(left, right):
        return jnp.where(first_core, left, right)

    def in_order(own, other):
        return my_half(own, other), my_half(other, own)

    gain_cols = jnp.transpose(norm_gains.reshape(2 * LAYERS, SHARD))
    cut = (Q_ROWS + KV_ROWS + D) // 2
    wgu_cut = w_gate_up.reshape(LAYERS, SHARD, 2, FSDP, 2, FF // FSDP // 2)
    wgu_cut = my_half(wgu_cut[..., 0, :], wgu_cut[..., 1, :]).reshape(LAYERS, SHARD, FF)
    wd_cut = w_down.reshape(LAYERS, 2, FF // FSDP // 2, D)
    wd_cut = my_half(wd_cut[:, 0], wd_cut[:, 1])
    projs, mlps = [], []
    for layer in range(LAYERS):
        proj = jnp.concatenate([w_qkv[layer], w_out[layer]], 1)
        proj = my_half(proj[:, :cut], proj[:, cut:])
        if layer == 0:
            proj = jnp.concatenate([proj, gain_cols], 1)
        own = gather_fsdp(proj)
        if layer == 0:
            gains = jnp.transpose(own[:, cut:].astype(F32)).reshape(LAYERS, 2, D)
        pair = in_order(own, to_partner(own))
        projs.append(jnp.concatenate([half[:, :cut] for half in pair], 1))
        wgu, wdown = gather_fsdp(wgu_cut[layer]), gather_fsdp(wd_cut[layer])
        mlps.append([(wgu, wdown), (to_partner(wgu), to_partner(wdown))])

    first_block = lax.dynamic_index_in_dim(block_order, 2 * place, 0, keepdims=False)
    low = jnp.minimum(first_block, NBLK - 1 - first_block)
    low_half = (first_block != low).astype(jnp.int32)
    starts = jnp.sum(
        (doc_ids[0][None, :] < jnp.arange(1, 5, dtype=jnp.int32)[:, None]).astype(jnp.int32), 1
    )
    scalars = jnp.concatenate([jnp.stack([low, low_half, core]), starts, block_order])
    lane = jnp.arange(ROWS, dtype=jnp.int32)
    pos = jnp.where(lane < BLK, first_block, NBLK - 2 - first_block) * BLK + lane
    inv_freq = THETA ** (-jnp.arange(HEAD_DIM // 2, dtype=F32) / (HEAD_DIM // 2))
    angles = pos.astype(F32)[None, :] * inv_freq[:, None]
    cosine, sine = jnp.cos(angles), jnp.sin(angles)

    hidden = tokens[0].astype(F32)
    saved = []
    for layer in range(LAYERS):
        wqkv, wout = projs[layer][:, : Q_ROWS + KV_ROWS], projs[layer][:, Q_ROWS + KV_ROWS :]
        unit_a, rms_a = normed(hidden)
        attn_in = (unit_a * gains[layer, 0]).astype(BF16)
        qkv_t = ein("de,td->et", wqkv, attn_in).reshape(-1, HEAD_DIM, ROWS)
        turned = rotate(qkv_t[: HEADS + KV_HEADS], cosine, sine)
        q_t = (turned[:HEADS] * HEAD_DIM**-0.5).astype(BF16)
        kv_t = jnp.concatenate([turned[HEADS:], qkv_t[HEADS + KV_HEADS :]], 0).astype(BF16)
        kv_t = kv_t.reshape(1, 2, KV_HEADS, HEAD_DIM, ROWS)
        kv_own = over_chips(jnp.broadcast_to(kv_t, (CTX // 2,) + kv_t.shape[1:]))
        kv_other = to_partner(kv_own)
        o_t, lse = attention(scalars, q_t, kv_own, kv_other)
        attn_out = o_t.astype(BF16).reshape(Q_ROWS, ROWS)
        mid = hidden + ein("at,ad->td", attn_out, wout)
        unit_m, rms_m = normed(mid)
        mlp_in = (unit_m * gains[layer, 1]).astype(BF16)
        hidden = mid
        halves = []
        for wgu, wdown in mlps[layer]:
            gate_up = mm(mlp_in, wgu)
            inner = (jax.nn.silu(gate_up[:, :HALF]) * gate_up[:, HALF:]).astype(BF16)
            hidden = hidden + mm(inner, wdown)
            halves.append((wgu, wdown, gate_up, inner))
        saved.append(
            (wqkv, wout, unit_a, rms_a, attn_in, q_t, kv_own, kv_other, o_t, lse, attn_out,
             unit_m, rms_m, mlp_in, halves)
        )
    output = hidden.astype(BF16).reshape(1, ROWS, D)

    d_hidden = cotangent[0].astype(F32)
    shares = [None] * LAYERS
    gain_grads = [None] * LAYERS
    for layer in reversed(range(LAYERS)):
        (wqkv, wout, unit_a, rms_a, attn_in, q_t, kv_own, kv_other, o_t, lse, attn_out,
         unit_m, rms_m, mlp_in, halves) = saved[layer]
        grad_b = d_hidden.astype(BF16)
        d_norm = 0.0
        wgu_parts, wd_parts = [], []
        for wgu, wdown, gate_up, inner in halves:
            d_inner = ein("td,fd->tf", grad_b, wdown)
            gate, up = gate_up[:, :HALF], gate_up[:, HALF:]
            sig = jax.nn.sigmoid(gate)
            d_gate = d_inner * up * sig * (1.0 + gate * (1.0 - sig))
            d_up = d_inner * (gate * sig)
            d_gu = jnp.concatenate([d_gate, d_up], 1).astype(BF16)
            d_norm = d_norm + ein("tf,df->td", d_gu, wgu)
            wd_parts.append(ein("tf,td->fd", inner, grad_b).astype(BF16))
            wgu_parts.append(ein("td,tf->df", mlp_in, d_gu).astype(BF16))
        d_wgu = sum_pair(wgu_parts[0], to_partner(wgu_parts[1]))
        d_wdown = sum_pair(wd_parts[0], to_partner(wd_parts[1]))
        d_gain_m = jnp.sum(d_norm * unit_m, 0)
        d_hidden = d_hidden + norm_back(d_norm * gains[layer, 1], unit_m, rms_m)
        grad_b = d_hidden.astype(BF16)
        d_wout = mm(attn_out, grad_b)
        do_t = ein("ad,td->at", wout, grad_b).astype(BF16).reshape(HEADS, HEAD_DIM, ROWS)
        if layer == 0:
            do_t, d_wgu, d_wdown = lax.optimization_barrier((do_t, d_wgu, d_wdown))
        dq_t, dkv_own, dkv_other = attention_back(scalars, q_t, kv_own, kv_other, o_t, do_t, lse)
        dkv = (dkv_own.astype(F32) + to_partner(dkv_other).astype(F32)).astype(BF16)
        dkv = jnp.sum(over_chips(dkv).astype(F32), 0)
        turned = jnp.concatenate([dq_t, dkv[0]], 0)
        d_qkv = jnp.concatenate([rotate(turned, cosine, -sine), dkv[1]], 0)
        d_qkv = d_qkv.astype(BF16).reshape(Q_ROWS + KV_ROWS, ROWS)
        d_wqkv = ein("td,et->de", attn_in, d_qkv)
        d_norm = ein("et,de->td", d_qkv, wqkv)
        d_gain_a = jnp.sum(d_norm * unit_a, 0)
        d_hidden = d_hidden + norm_back(d_norm * gains[layer, 0], unit_a, rms_a)
        gain_grads[layer] = jnp.stack([d_gain_a, d_gain_m])
        d_proj = jnp.concatenate([d_wqkv, d_wout], 1).astype(BF16)
        mine, theirs = my_half(d_proj[:, :cut], d_proj[:, cut:]), my_half(d_proj[:, cut:], d_proj[:, :cut])
        d_proj = sum_pair(mine, to_partner(theirs))
        if layer == 0:
            d_gains = jnp.transpose(jnp.stack(gain_grads).reshape(2 * LAYERS, D)).astype(BF16)
            d_proj = jnp.concatenate([d_proj, d_gains], 1)
        mlp_share = jnp.concatenate(
            [scatter_fsdp(d_wgu), scatter_fsdp(d_wdown).reshape(SHARD, HALF)], 1
        )
        proj_share = scatter_fsdp(d_proj)
        if layer == 0:
            shares[layer] = sum_chips(mlp_share), sum_chips(proj_share)
        else:
            both = sum_chips(jnp.concatenate([mlp_share, proj_share], 1))
            shares[layer] = both[:, : FF + HALF], both[:, FF + HALF :]
    input_grad = d_hidden.reshape(1, ROWS, D)

    proj_grads, gate_up_grad, down_grad = [], [], []
    for layer in range(LAYERS):
        mlp_share, proj_share = shares[layer]
        pair = in_order(mlp_share, to_partner(mlp_share))
        cols = jnp.stack([half[:, :FF].reshape(SHARD, 2, FSDP, -1) for half in pair], 3)
        gate_up_grad.append(cols.reshape(SHARD, 2 * FF).astype(F32))
        rows = [half[:, FF:].reshape(FF // FSDP // 2, D) for half in pair]
        down_grad.append(jnp.concatenate(rows, 0).astype(F32))
        theirs = to_partner(proj_share)
        if layer == 0:
            d_gain = proj_share[:, cut:].astype(F32) + theirs[:, cut:].astype(F32)
            gain_grad = jnp.transpose(d_gain).reshape(LAYERS, 2, SHARD)
        pair = in_order(proj_share[:, :cut], theirs[:, :cut])
        proj_grads.append(jnp.concatenate(pair, 1).astype(F32))
    qkv_grad = jnp.stack([g[:, : Q_ROWS + KV_ROWS] for g in proj_grads])
    out_proj_grad = jnp.stack([g[:, Q_ROWS + KV_ROWS :] for g in proj_grads])
    gate_up_grad, down_grad = jnp.stack(gate_up_grad), jnp.stack(down_grad)
    return (output, input_grad, gain_grad, qkv_grad, out_proj_grad, gate_up_grad, down_grad)


def solution(mesh):
    in_specs = (
        P("fsdp", "ctx", None),
        P(),
        P("fsdp", None),
        P(None, None, "fsdp"),
        P(None, "fsdp", None),
        P(None, "fsdp", None),
        P(None, "fsdp", None),
        P(None, "fsdp", None),
        P("fsdp", "ctx", None),
    )
    out_specs = (
        P("fsdp", "ctx", None),
        P("fsdp", "ctx", None),
        P(None, None, "fsdp"),
        P(None, "fsdp", None),
        P(None, "fsdp", None),
        P(None, "fsdp", None),
        P(None, "fsdp", None),
    )
    return jax.shard_map(local, mesh=mesh, in_specs=in_specs, out_specs=out_specs, check_vma=False)
```

```python
import functools

import jax
import jax.numpy as jnp
from jax import lax
from jax.experimental import pallas as pl
from jax.experimental.pallas import tpu as pltpu
from jax.sharding import PartitionSpec as P

D = 576
HEADS = 9
KV_HEADS = 3
GROUP = 3
HEAD_DIM = 64
FF = 1536
LAYERS = 2
BLK = 128
NBLK = 32
EPS = 1e-05
THETA = 100000.0
NEG = -1e30
F32 = jnp.float32
BF16 = jnp.bfloat16
LANES = GROUP * BLK
CTX = 16
FSDP = 8
SHARD = D // FSDP
HALF = FF // 2
Q_ROWS = HEADS * HEAD_DIM
KV_ROWS = 2 * KV_HEADS * HEAD_DIM

PARTNER = [(i, i ^ 1) for i in range(CTX)]
SAME_CORE = [[2 * chip + core for chip in range(CTX // 2)] for core in range(2)]


def to_partner(x):
    return lax.ppermute(x, "ctx", PARTNER)


def over_chips(x):
    return lax.all_to_all(x, "ctx", 0, 0, axis_index_groups=SAME_CORE, tiled=True)


def over_fsdp(x):
    return lax.all_to_all(x, "fsdp", 0, 0, tiled=True)


def gather_fsdp(x):
    return over_fsdp(jnp.broadcast_to(x[None], (FSDP,) + x.shape)).reshape(-1, x.shape[1])


def scatter_fsdp(x):
    parts = over_fsdp(x.reshape(FSDP, -1, x.shape[1]))
    return jnp.sum(parts.astype(F32), 0).astype(BF16)


def sum_pair(a, b):
    return (a.astype(F32) + b.astype(F32)).astype(BF16)


def sum_chips(x):
    for bit in (2, 4, 8):
        x = sum_pair(x, lax.ppermute(x, "ctx", [(i, i ^ bit) for i in range(CTX)]))
    return x


def dot_tn(a, b):
    return lax.dot_general(a, b, (((0,), (0,)), ((), ())), preferred_element_type=F32)


def dot_nt(a, b):
    return lax.dot_general(a, b, (((1,), (1,)), ((), ())), preferred_element_type=F32)


UNROLL_F = 9
UNROLL_B = 3
CHUNK = 4
KEYS = CHUNK * BLK
CHUNKS = NBLK // CHUNK


def fill_keys(sc, own_ref, other_ref, kv_s):
    core = sc[2]
    for chip in range(CTX // 2):
        for half in range(2):
            lanes = slice(half * BLK, (half + 1) * BLK)
            block = sc[7 + 2 * (2 * chip + core) + half]
            kv_s[block] = own_ref[chip, :, 0, :, lanes]
            block = sc[7 + 2 * (2 * chip + 1 - core) + half]
            kv_s[block] = other_ref[chip, :, 0, :, lanes]


def fill_queries(sc, src_ref, dst):
    for half in range(2):
        lanes = slice(half * BLK, (half + 1) * BLK)
        which = jnp.bitwise_xor(half, sc[1])
        dst[which] = jnp.concatenate([src_ref[j, :, lanes] for j in range(GROUP)], axis=1)


def query_rows(sc, which):
    block = jnp.where(which == 0, sc[0], NBLK - 1 - sc[0])
    lane = lax.broadcasted_iota(jnp.int32, (1, LANES), 1)
    pos = block * BLK + jnp.bitwise_and(lane, BLK - 1)
    start = jnp.zeros((1, LANES), jnp.int32)
    for d in range(4):
        start = jnp.where(pos >= sc[3 + d], jnp.maximum(start, sc[3 + d]), start)
    return pos, start


def chunk_of(sc, t):
    high = (NBLK - sc[0] + CHUNK - 1) // CHUNK
    which = (t < high).astype(jnp.int32)
    return which, jnp.where(t < high, t, t - high)


def keys_of(kv_s, chunk, kind):
    return jnp.concatenate([kv_s[chunk * CHUNK + j, kind] for j in range(CHUNK)], axis=1)


def seen(pos_s, which, chunk):
    at = lax.broadcasted_iota(jnp.int32, (KEYS, LANES), 0)
    base = chunk * KEYS
    return (at >= pos_s[which, 1:2] - base) & (at <= pos_s[which, 0:1] - base)


def fill_rows(sc, pos_s):
    for which in range(2):
        pos, start = query_rows(sc, which)
        pos_s[which, 0:1] = pos
        pos_s[which, 1:2] = start


def forward_kernel(sc, q_ref, own_ref, other_ref, o_ref, lse_ref, kv_s, q_s, acc_s, m_s, l_s, pos_s):
    fill_keys(sc, own_ref, other_ref, kv_s)
    fill_queries(sc, q_ref, q_s)
    fill_rows(sc, pos_s)
    acc_s[...] = jnp.zeros_like(acc_s)
    m_s[...] = jnp.full_like(m_s, NEG)
    l_s[...] = jnp.zeros_like(l_s)

    def step(t, carry):
        which, chunk = chunk_of(sc, t)
        scores = dot_tn(keys_of(kv_s, chunk, 0), q_s[which])
        scores = jnp.where(seen(pos_s, which, chunk), scores, NEG)
        old = m_s[which]
        new = jnp.maximum(old, jnp.max(scores, axis=0, keepdims=True))
        prob = jnp.exp(scores - new)
        shrink = jnp.exp(old - new)
        m_s[which] = new
        l_s[which] = l_s[which] * shrink + jnp.sum(prob, axis=0, keepdims=True)
        acc_s[which] = acc_s[which] * shrink + jnp.dot(
            keys_of(kv_s, chunk, 1), prob.astype(BF16), preferred_element_type=F32
        )
        return carry

    lax.fori_loop(0, CHUNKS + 1, step, 0, unroll=UNROLL_F)
    for which in range(2):
        acc_s[which] = acc_s[which] / l_s[which]
        lse_ref[0, which] = m_s[which] + jnp.log(l_s[which])
    for half in range(2):
        mine = acc_s[jnp.bitwise_xor(half, sc[1])]
        for j in range(GROUP):
            o_ref[j, :, half * BLK : (half + 1) * BLK] = mine[:, j * BLK : (j + 1) * BLK]


def backward_kernel(
    sc, q_ref, own_ref, other_ref, o_ref, do_ref, lse_ref,
    dq_ref, down_ref, dother_ref,
    kv_s, q_s, do_s, dq_s, dkv_s, delta_s, pos_s,
):
    fill_keys(sc, own_ref, other_ref, kv_s)
    fill_queries(sc, q_ref, q_s)
    fill_queries(sc, do_ref, do_s)
    fill_queries(sc, o_ref, dq_s)
    fill_rows(sc, pos_s)
    for which in range(2):
        delta_s[which] = jnp.sum(dq_s[which] * do_s[which].astype(F32), axis=0, keepdims=True)
    dq_s[...] = jnp.zeros_like(dq_s)
    dkv_s[...] = jnp.zeros_like(dkv_s)

    def step(t, carry):
        which, chunk = chunk_of(sc, t)
        key_t, val_t, q_t, do_t = keys_of(kv_s, chunk, 0), keys_of(kv_s, chunk, 1), q_s[which], do_s[which]
        scores = dot_tn(key_t, q_t)
        prob = jnp.where(seen(pos_s, which, chunk), jnp.exp(scores - lse_ref[0, which]), 0.0)
        d_prob = dot_tn(val_t, do_t)
        d_score = (prob * (d_prob - delta_s[which])).astype(BF16)
        d_val = dot_nt(do_t, prob.astype(BF16))
        d_key = dot_nt(q_t, d_score)
        dq_s[which] = dq_s[which] + jnp.dot(key_t, d_score, preferred_element_type=F32)
        for j in range(CHUNK):
            lanes = slice(j * BLK, (j + 1) * BLK)
            dkv_s[chunk * CHUNK + j, 0] = dkv_s[chunk * CHUNK + j, 0] + d_key[:, lanes]
            dkv_s[chunk * CHUNK + j, 1] = dkv_s[chunk * CHUNK + j, 1] + d_val[:, lanes]
        return carry

    lax.fori_loop(0, CHUNKS + 1, step, 0, unroll=UNROLL_B)
    core = sc[2]
    scale = HEAD_DIM**-0.5
    for half in range(2):
        lanes = slice(half * BLK, (half + 1) * BLK)
        mine = dq_s[jnp.bitwise_xor(half, sc[1])] * scale
        for j in range(GROUP):
            dq_ref[j, :, lanes] = mine[:, j * BLK : (j + 1) * BLK]
        for chip in range(CTX // 2):
            block = sc[7 + 2 * (2 * chip + core) + half]
            down_ref[chip, :, 0, :, lanes] = dkv_s[block].astype(BF16)
            block = sc[7 + 2 * (2 * chip + 1 - core) + half]
            dother_ref[chip, :, 0, :, lanes] = dkv_s[block].astype(BF16)


ROWS = 2 * BLK
HEAD_SPEC = pl.BlockSpec((GROUP, HEAD_DIM, ROWS), lambda g, sc: (g, 0, 0))
KV_SPEC = pl.BlockSpec((CTX // 2, 2, 1, HEAD_DIM, ROWS), lambda g, sc: (0, 0, g, 0, 0))
LSE_SPEC = pl.BlockSpec((1, 2, 1, LANES), lambda g, sc: (g, 0, 0, 0))
HEAD_SHAPE = jax.ShapeDtypeStruct((HEADS, HEAD_DIM, ROWS), F32)
KV_SHAPE = jax.ShapeDtypeStruct((CTX // 2, 2, KV_HEADS, HEAD_DIM, ROWS), BF16)
LSE_SHAPE = jax.ShapeDtypeStruct((KV_HEADS, 2, 1, LANES), F32)
KERNEL_PARAMS = pltpu.CompilerParams(
    dimension_semantics=("arbitrary",), vmem_limit_bytes=40 * 2**20
)


def attention(scalars, q_t, own, other):
    return pl.pallas_call(
        forward_kernel,
        grid_spec=pltpu.PrefetchScalarGridSpec(
            num_scalar_prefetch=1,
            grid=(KV_HEADS,),
            in_specs=[HEAD_SPEC, KV_SPEC, KV_SPEC],
            out_specs=[HEAD_SPEC, LSE_SPEC],
            scratch_shapes=[
                pltpu.VMEM((NBLK, 2, HEAD_DIM, BLK), BF16),
                pltpu.VMEM((2, HEAD_DIM, LANES), BF16),
                pltpu.VMEM((2, HEAD_DIM, LANES), F32),
                pltpu.VMEM((2, 1, LANES), F32),
                pltpu.VMEM((2, 1, LANES), F32),
                pltpu.VMEM((2, 8, LANES), jnp.int32),
            ],
        ),
        out_shape=[HEAD_SHAPE, LSE_SHAPE],
        compiler_params=KERNEL_PARAMS,
        name="attention",
    )(scalars, q_t, own, other)


def attention_back(scalars, q_t, own, other, o_t, do_t, lse):
    return pl.pallas_call(
        backward_kernel,
        grid_spec=pltpu.PrefetchScalarGridSpec(
            num_scalar_prefetch=1,
            grid=(KV_HEADS,),
            in_specs=[HEAD_SPEC, KV_SPEC, KV_SPEC, HEAD_SPEC, HEAD_SPEC, LSE_SPEC],
            out_specs=[HEAD_SPEC, KV_SPEC, KV_SPEC],
            scratch_shapes=[
                pltpu.VMEM((NBLK, 2, HEAD_DIM, BLK), BF16),
                pltpu.VMEM((2, HEAD_DIM, LANES), BF16),
                pltpu.VMEM((2, HEAD_DIM, LANES), BF16),
                pltpu.VMEM((2, HEAD_DIM, LANES), F32),
                pltpu.VMEM((NBLK, 2, HEAD_DIM, BLK), F32),
                pltpu.VMEM((2, 1, LANES), F32),
                pltpu.VMEM((2, 8, LANES), jnp.int32),
            ],
        ),
        out_shape=[HEAD_SHAPE, KV_SHAPE, KV_SHAPE],
        compiler_params=KERNEL_PARAMS,
        name="attention_back",
    )(scalars, q_t, own, other, o_t, do_t, lse)


def rotate(x, cosine, sine):
    half = HEAD_DIM // 2
    first, second = x[:, :half], x[:, half:]
    return jnp.concatenate([first * cosine - second * sine, second * cosine + first * sine], 1)


def normed(hidden):
    inv_rms = lax.rsqrt(jnp.mean(hidden * hidden, -1, keepdims=True) + EPS)
    return hidden * inv_rms, inv_rms


def norm_back(d_unit, unit, inv_rms):
    return inv_rms * (d_unit - unit * jnp.mean(d_unit * unit, -1, keepdims=True))


def mm(a, b):
    return jnp.dot(a, b, preferred_element_type=F32)


def ein(spec, a, b):
    return jnp.einsum(spec, a, b, preferred_element_type=F32)


def local(tokens, block_order, doc_ids, norm_gains, w_qkv, w_out, w_gate_up, w_down, cotangent):
    place = lax.axis_index("ctx")
    core = jnp.bitwise_and(place, 1)
    first_core = core == 0

    def my_half(left, right):
        return jnp.where(first_core, left, right)

    def in_order(own, other):
        return my_half(own, other), my_half(other, own)

    gain_cols = jnp.transpose(norm_gains.reshape(2 * LAYERS, SHARD))
    cut = (Q_ROWS + KV_ROWS + D) // 2
    wgu_cut = w_gate_up.reshape(LAYERS, SHARD, 2, FSDP, 2, FF // FSDP // 2)
    wgu_cut = my_half(wgu_cut[..., 0, :], wgu_cut[..., 1, :]).reshape(LAYERS, SHARD, FF)
    wd_cut = w_down.reshape(LAYERS, 2, FF // FSDP // 2, D)
    wd_cut = my_half(wd_cut[:, 0], wd_cut[:, 1]).reshape(LAYERS, SHARD, HALF)
    proj_cut = jnp.concatenate([w_qkv, w_out], 2)
    proj_cut = my_half(proj_cut[..., :cut], proj_cut[..., cut:])
    first = jnp.concatenate([proj_cut[0], gain_cols], 1)
    packs = [
        jnp.concatenate([wgu_cut[0], wd_cut[0]], 1),
        jnp.concatenate([wgu_cut[1], wd_cut[1], proj_cut[1]], 1),
    ]
    packs[0], first = lax.optimization_barrier((packs[0], first))
    packs = [lax.all_gather(p, "fsdp", axis=0, tiled=True) for p in packs]
    first = gather_fsdp(first)
    gains = jnp.transpose(first[:, cut:].astype(F32)).reshape(LAYERS, 2, D)
    projs = [first[:, :cut], packs[1][:, FF + HALF :]]
    projs = [jnp.concatenate(in_order(own, to_partner(own)), 1) for own in projs]
    mlps = []
    for pack in packs:
        wgu, wdown = pack[:, :FF], pack[:, FF : FF + HALF].reshape(HALF, D)
        mlps.append([(wgu, wdown), (to_partner(wgu), to_partner(wdown))])

    first_block = lax.dynamic_index_in_dim(block_order, 2 * place, 0, keepdims=False)
    low = jnp.minimum(first_block, NBLK - 1 - first_block)
    low_half = (first_block != low).astype(jnp.int32)
    starts = jnp.sum(
        (doc_ids[0][None, :] < jnp.arange(1, 5, dtype=jnp.int32)[:, None]).astype(jnp.int32), 1
    )
    scalars = jnp.concatenate([jnp.stack([low, low_half, core]), starts, block_order])
    lane = jnp.arange(ROWS, dtype=jnp.int32)
    pos = jnp.where(lane < BLK, first_block, NBLK - 2 - first_block) * BLK + lane
    inv_freq = THETA ** (-jnp.arange(HEAD_DIM // 2, dtype=F32) / (HEAD_DIM // 2))
    angles = pos.astype(F32)[None, :] * inv_freq[:, None]
    cosine, sine = jnp.cos(angles), jnp.sin(angles)

    hidden = tokens[0].astype(F32)
    saved = []
    for layer in range(LAYERS):
        wqkv, wout = projs[layer][:, : Q_ROWS + KV_ROWS], projs[layer][:, Q_ROWS + KV_ROWS :]
        unit_a, rms_a = normed(hidden)
        attn_in = (unit_a * gains[layer, 0]).astype(BF16)
        qkv_t = ein("de,td->et", wqkv, attn_in).reshape(-1, HEAD_DIM, ROWS)
        turned = rotate(qkv_t[: HEADS + KV_HEADS], cosine, sine)
        q_t = (turned[:HEADS] * HEAD_DIM**-0.5).astype(BF16)
        kv_t = jnp.concatenate([turned[HEADS:], qkv_t[HEADS + KV_HEADS :]], 0).astype(BF16)
        kv_t = kv_t.reshape(1, 2, KV_HEADS, HEAD_DIM, ROWS)
        kv_own = over_chips(jnp.broadcast_to(kv_t, (CTX // 2,) + kv_t.shape[1:]))
        kv_other = to_partner(kv_own)
        o_t, lse = attention(scalars, q_t, kv_own, kv_other)
        attn_out = o_t.astype(BF16).reshape(Q_ROWS, ROWS)
        mid = hidden + ein("at,ad->td", attn_out, wout)
        unit_m, rms_m = normed(mid)
        mlp_in = (unit_m * gains[layer, 1]).astype(BF16)
        hidden = mid
        halves = []
        for wgu, wdown in mlps[layer]:
            gate_up = mm(mlp_in, wgu)
            inner = (jax.nn.silu(gate_up[:, :HALF]) * gate_up[:, HALF:]).astype(BF16)
            hidden = hidden + mm(inner, wdown)
            halves.append((wgu, wdown, gate_up, inner))
        saved.append(
            (wqkv, wout, unit_a, rms_a, attn_in, q_t, kv_own, kv_other, o_t, lse, attn_out,
             unit_m, rms_m, mlp_in, halves)
        )
    output = hidden.astype(BF16).reshape(1, ROWS, D)

    d_hidden = cotangent[0].astype(F32)
    shares = [None] * LAYERS
    gain_grads = [None] * LAYERS
    for layer in reversed(range(LAYERS)):
        (wqkv, wout, unit_a, rms_a, attn_in, q_t, kv_own, kv_other, o_t, lse, attn_out,
         unit_m, rms_m, mlp_in, halves) = saved[layer]
        grad_b = d_hidden.astype(BF16)
        d_norm = 0.0
        wgu_parts, wd_parts = [], []
        for wgu, wdown, gate_up, inner in halves:
            d_inner = ein("td,fd->tf", grad_b, wdown)
            gate, up = gate_up[:, :HALF], gate_up[:, HALF:]
            sig = jax.nn.sigmoid(gate)
            d_gate = d_inner * up * sig * (1.0 + gate * (1.0 - sig))
            d_up = d_inner * (gate * sig)
            d_gu = jnp.concatenate([d_gate, d_up], 1).astype(BF16)
            d_norm = d_norm + ein("tf,df->td", d_gu, wgu)
            wd_parts.append(ein("tf,td->fd", inner, grad_b).astype(BF16))
            wgu_parts.append(ein("td,tf->df", mlp_in, d_gu).astype(BF16))
        d_wgu = sum_pair(wgu_parts[0], to_partner(wgu_parts[1]))
        d_wdown = sum_pair(wd_parts[0], to_partner(wd_parts[1])).reshape(D, HALF)
        d_mlp = jnp.concatenate([d_wgu, d_wdown], 1)
        d_gain_m = jnp.sum(d_norm * unit_m, 0)
        d_hidden = d_hidden + norm_back(d_norm * gains[layer, 1], unit_m, rms_m)
        grad_b = d_hidden.astype(BF16)
        d_wout = mm(attn_out, grad_b)
        do_t = ein("ad,td->at", wout, grad_b).astype(BF16).reshape(HEADS, HEAD_DIM, ROWS)
        if layer == 0:
            do_t, d_mlp = lax.optimization_barrier((do_t, d_mlp))
        mlp_share = lax.psum_scatter(d_mlp, "fsdp", scatter_dimension=0, tiled=True)
        dq_t, dkv_own, dkv_other = attention_back(scalars, q_t, kv_own, kv_other, o_t, do_t, lse)
        dkv = (dkv_own.astype(F32) + to_partner(dkv_other).astype(F32)).astype(BF16)
        dkv = jnp.sum(over_chips(dkv).astype(F32), 0)
        turned = jnp.concatenate([dq_t, dkv[0]], 0)
        d_qkv = jnp.concatenate([rotate(turned, cosine, -sine), dkv[1]], 0)
        d_qkv = d_qkv.astype(BF16).reshape(Q_ROWS + KV_ROWS, ROWS)
        d_wqkv = ein("td,et->de", attn_in, d_qkv)
        d_norm = ein("et,de->td", d_qkv, wqkv)
        d_gain_a = jnp.sum(d_norm * unit_a, 0)
        d_hidden = d_hidden + norm_back(d_norm * gains[layer, 0], unit_a, rms_a)
        gain_grads[layer] = jnp.stack([d_gain_a, d_gain_m])
        d_proj = jnp.concatenate([d_wqkv, d_wout], 1).astype(BF16)
        mine, theirs = my_half(d_proj[:, :cut], d_proj[:, cut:]), my_half(d_proj[:, cut:], d_proj[:, :cut])
        d_proj = sum_pair(mine, to_partner(theirs))
        if layer == 0:
            d_gains = jnp.transpose(jnp.stack(gain_grads).reshape(2 * LAYERS, D)).astype(BF16)
            d_proj = jnp.concatenate([d_proj, d_gains], 1)
        shares[layer] = sum_chips(mlp_share), sum_chips(scatter_fsdp(d_proj))
    input_grad = d_hidden.reshape(1, ROWS, D)

    proj_grads, gate_up_grad, down_grad = [], [], []
    for layer in range(LAYERS):
        mlp_share, proj_share = shares[layer]
        pair = in_order(mlp_share, to_partner(mlp_share))
        cols = jnp.stack([half[:, :FF].reshape(SHARD, 2, FSDP, -1) for half in pair], 3)
        gate_up_grad.append(cols.reshape(SHARD, 2 * FF).astype(F32))
        rows = [half[:, FF:].reshape(FF // FSDP // 2, D) for half in pair]
        down_grad.append(jnp.concatenate(rows, 0).astype(F32))
        theirs = to_partner(proj_share)
        if layer == 0:
            d_gain = proj_share[:, cut:].astype(F32) + theirs[:, cut:].astype(F32)
            gain_grad = jnp.transpose(d_gain).reshape(LAYERS, 2, SHARD)
        pair = in_order(proj_share[:, :cut], theirs[:, :cut])
        proj_grads.append(jnp.concatenate(pair, 1).astype(F32))
    qkv_grad = jnp.stack([g[:, : Q_ROWS + KV_ROWS] for g in proj_grads])
    out_proj_grad = jnp.stack([g[:, Q_ROWS + KV_ROWS :] for g in proj_grads])
    gate_up_grad, down_grad = jnp.stack(gate_up_grad), jnp.stack(down_grad)
    return (output, input_grad, gain_grad, qkv_grad, out_proj_grad, gate_up_grad, down_grad)


def solution(mesh):
    in_specs = (
        P("fsdp", "ctx", None),
        P(),
        P("fsdp", None),
        P(None, None, "fsdp"),
        P(None, "fsdp", None),
        P(None, "fsdp", None),
        P(None, "fsdp", None),
        P(None, "fsdp", None),
        P("fsdp", "ctx", None),
    )
    out_specs = (
        P("fsdp", "ctx", None),
        P("fsdp", "ctx", None),
        P(None, None, "fsdp"),
        P(None, "fsdp", None),
        P(None, "fsdp", None),
        P(None, "fsdp", None),
        P(None, "fsdp", None),
    )
    return jax.shard_map(local, mesh=mesh, in_specs=in_specs, out_specs=out_specs, check_vma=False)
```

```python
import functools

import jax
import jax.numpy as jnp
from jax import lax
from jax.experimental import pallas as pl
from jax.experimental.pallas import tpu as pltpu
from jax.sharding import PartitionSpec as P

D = 576
HEADS = 9
KV_HEADS = 3
GROUP = 3
HEAD_DIM = 64
FF = 1536
LAYERS = 2
BLK = 128
NBLK = 32
EPS = 1e-05
THETA = 100000.0
NEG = -1e30
F32 = jnp.float32
BF16 = jnp.bfloat16
LANES = GROUP * BLK
CTX = 16
FSDP = 8
SHARD = D // FSDP
HALF = FF // 2
Q_ROWS = HEADS * HEAD_DIM
KV_ROWS = 2 * KV_HEADS * HEAD_DIM

PARTNER = [(i, i ^ 1) for i in range(CTX)]
SAME_CORE = [[2 * chip + core for chip in range(CTX // 2)] for core in range(2)]


def to_partner(x):
    return lax.ppermute(x, "ctx", PARTNER)


def over_chips(x):
    return lax.all_to_all(x, "ctx", 0, 0, axis_index_groups=SAME_CORE, tiled=True)


def over_fsdp(x):
    return lax.all_to_all(x, "fsdp", 0, 0, tiled=True)


def gather_fsdp(x):
    return over_fsdp(jnp.broadcast_to(x[None], (FSDP,) + x.shape)).reshape(-1, x.shape[1])


def scatter_fsdp(x):
    parts = over_fsdp(x.reshape(FSDP, -1, x.shape[1]))
    return jnp.sum(parts.astype(F32), 0).astype(BF16)


def sum_pair(a, b):
    return (a.astype(F32) + b.astype(F32)).astype(BF16)


def sum_chips(x):
    for bit in (2, 4, 8):
        x = sum_pair(x, lax.ppermute(x, "ctx", [(i, i ^ bit) for i in range(CTX)]))
    return x


def dot_tn(a, b):
    return lax.dot_general(a, b, (((0,), (0,)), ((), ())), preferred_element_type=F32)


def dot_nt(a, b):
    return lax.dot_general(a, b, (((1,), (1,)), ((), ())), preferred_element_type=F32)


UNROLL_F = 9
UNROLL_B = 3
CHUNK = 4
KEYS = CHUNK * BLK
CHUNKS = NBLK // CHUNK


def fill_keys(sc, own_ref, other_ref, kv_s):
    core = sc[2]
    for chip in range(CTX // 2):
        for half in range(2):
            lanes = slice(half * BLK, (half + 1) * BLK)
            block = sc[7 + 2 * (2 * chip + core) + half]
            kv_s[block] = own_ref[chip, :, 0, :, lanes]
            block = sc[7 + 2 * (2 * chip + 1 - core) + half]
            kv_s[block] = other_ref[chip, :, 0, :, lanes]


def fill_queries(sc, src_ref, dst):
    for half in range(2):
        lanes = slice(half * BLK, (half + 1) * BLK)
        which = jnp.bitwise_xor(half, sc[1])
        dst[which] = jnp.concatenate([src_ref[j, :, lanes] for j in range(GROUP)], axis=1)


def query_rows(sc, which):
    block = jnp.where(which == 0, sc[0], NBLK - 1 - sc[0])
    lane = lax.broadcasted_iota(jnp.int32, (1, LANES), 1)
    pos = block * BLK + jnp.bitwise_and(lane, BLK - 1)
    start = jnp.zeros((1, LANES), jnp.int32)
    for d in range(4):
        start = jnp.where(pos >= sc[3 + d], jnp.maximum(start, sc[3 + d]), start)
    return pos, start


def chunk_of(sc, t):
    high = (NBLK - sc[0] + CHUNK - 1) // CHUNK
    which = (t < high).astype(jnp.int32)
    return which, jnp.where(t < high, t, t - high)


def keys_of(kv_s, chunk, kind):
    return jnp.concatenate([kv_s[chunk * CHUNK + j, kind] for j in range(CHUNK)], axis=1)


def seen(pos_s, which, chunk):
    at = lax.broadcasted_iota(jnp.int32, (KEYS, LANES), 0)
    base = chunk * KEYS
    return (at >= pos_s[which, 1:2] - base) & (at <= pos_s[which, 0:1] - base)


def fill_rows(sc, pos_s):
    for which in range(2):
        pos, start = query_rows(sc, which)
        pos_s[which, 0:1] = pos
        pos_s[which, 1:2] = start


def forward_kernel(sc, q_ref, own_ref, other_ref, o_ref, lse_ref, kv_s, q_s, acc_s, m_s, l_s, pos_s):
    fill_keys(sc, own_ref, other_ref, kv_s)
    fill_queries(sc, q_ref, q_s)
    fill_rows(sc, pos_s)
    acc_s[...] = jnp.zeros_like(acc_s)
    m_s[...] = jnp.full_like(m_s, NEG)
    l_s[...] = jnp.zeros_like(l_s)

    def step(t, carry):
        which, chunk = chunk_of(sc, t)
        scores = dot_tn(keys_of(kv_s, chunk, 0), q_s[which])
        scores = jnp.where(seen(pos_s, which, chunk), scores, NEG)
        old = m_s[which]
        new = jnp.maximum(old, jnp.max(scores, axis=0, keepdims=True))
        prob = jnp.exp(scores - new)
        shrink = jnp.exp(old - new)
        m_s[which] = new
        l_s[which] = l_s[which] * shrink + jnp.sum(prob, axis=0, keepdims=True)
        acc_s[which] = acc_s[which] * shrink + jnp.dot(
            keys_of(kv_s, chunk, 1), prob.astype(BF16), preferred_element_type=F32
        )
        return carry

    lax.fori_loop(0, CHUNKS + 1, step, 0, unroll=UNROLL_F)
    for which in range(2):
        acc_s[which] = acc_s[which] / l_s[which]
        lse_ref[0, which] = m_s[which] + jnp.log(l_s[which])
    for half in range(2):
        mine = acc_s[jnp.bitwise_xor(half, sc[1])]
        for j in range(GROUP):
            o_ref[j, :, half * BLK : (half + 1) * BLK] = mine[:, j * BLK : (j + 1) * BLK]


def backward_kernel(
    sc, q_ref, own_ref, other_ref, o_ref, do_ref, lse_ref,
    dq_ref, down_ref, dother_ref,
    kv_s, q_s, do_s, dq_s, dkv_s, delta_s, pos_s,
):
    fill_keys(sc, own_ref, other_ref, kv_s)
    fill_queries(sc, q_ref, q_s)
    fill_queries(sc, do_ref, do_s)
    fill_queries(sc, o_ref, dq_s)
    fill_rows(sc, pos_s)
    for which in range(2):
        delta_s[which] = jnp.sum(dq_s[which] * do_s[which].astype(F32), axis=0, keepdims=True)
    dq_s[...] = jnp.zeros_like(dq_s)
    dkv_s[...] = jnp.zeros_like(dkv_s)

    def step(t, carry):
        which, chunk = chunk_of(sc, t)
        key_t, val_t, q_t, do_t = keys_of(kv_s, chunk, 0), keys_of(kv_s, chunk, 1), q_s[which], do_s[which]
        scores = dot_tn(key_t, q_t)
        prob = jnp.where(seen(pos_s, which, chunk), jnp.exp(scores - lse_ref[0, which]), 0.0)
        d_prob = dot_tn(val_t, do_t)
        d_score = (prob * (d_prob - delta_s[which])).astype(BF16)
        d_val = dot_nt(do_t, prob.astype(BF16))
        d_key = dot_nt(q_t, d_score)
        dq_s[which] = dq_s[which] + jnp.dot(key_t, d_score, preferred_element_type=F32)
        for j in range(CHUNK):
            lanes = slice(j * BLK, (j + 1) * BLK)
            dkv_s[chunk * CHUNK + j, 0] = dkv_s[chunk * CHUNK + j, 0] + d_key[:, lanes]
            dkv_s[chunk * CHUNK + j, 1] = dkv_s[chunk * CHUNK + j, 1] + d_val[:, lanes]
        return carry

    lax.fori_loop(0, CHUNKS + 1, step, 0, unroll=UNROLL_B)
    core = sc[2]
    scale = HEAD_DIM**-0.5
    for half in range(2):
        lanes = slice(half * BLK, (half + 1) * BLK)
        mine = dq_s[jnp.bitwise_xor(half, sc[1])] * scale
        for j in range(GROUP):
            dq_ref[j, :, lanes] = mine[:, j * BLK : (j + 1) * BLK]
        for chip in range(CTX // 2):
            block = sc[7 + 2 * (2 * chip + core) + half]
            down_ref[chip, :, 0, :, lanes] = dkv_s[block].astype(BF16)
            block = sc[7 + 2 * (2 * chip + 1 - core) + half]
            dother_ref[chip, :, 0, :, lanes] = dkv_s[block].astype(BF16)


ROWS = 2 * BLK
HEAD_SPEC = pl.BlockSpec((GROUP, HEAD_DIM, ROWS), lambda g, sc: (g, 0, 0))
KV_SPEC = pl.BlockSpec((CTX // 2, 2, 1, HEAD_DIM, ROWS), lambda g, sc: (0, 0, g, 0, 0))
LSE_SPEC = pl.BlockSpec((1, 2, 1, LANES), lambda g, sc: (g, 0, 0, 0))
HEAD_SHAPE = jax.ShapeDtypeStruct((HEADS, HEAD_DIM, ROWS), F32)
KV_SHAPE = jax.ShapeDtypeStruct((CTX // 2, 2, KV_HEADS, HEAD_DIM, ROWS), BF16)
LSE_SHAPE = jax.ShapeDtypeStruct((KV_HEADS, 2, 1, LANES), F32)
KERNEL_PARAMS = pltpu.CompilerParams(
    dimension_semantics=("arbitrary",), vmem_limit_bytes=40 * 2**20
)


def attention(scalars, q_t, own, other):
    return pl.pallas_call(
        forward_kernel,
        grid_spec=pltpu.PrefetchScalarGridSpec(
            num_scalar_prefetch=1,
            grid=(KV_HEADS,),
            in_specs=[HEAD_SPEC, KV_SPEC, KV_SPEC],
            out_specs=[HEAD_SPEC, LSE_SPEC],
            scratch_shapes=[
                pltpu.VMEM((NBLK, 2, HEAD_DIM, BLK), BF16),
                pltpu.VMEM((2, HEAD_DIM, LANES), BF16),
                pltpu.VMEM((2, HEAD_DIM, LANES), F32),
                pltpu.VMEM((2, 1, LANES), F32),
                pltpu.VMEM((2, 1, LANES), F32),
                pltpu.VMEM((2, 8, LANES), jnp.int32),
            ],
        ),
        out_shape=[HEAD_SHAPE, LSE_SHAPE],
        compiler_params=KERNEL_PARAMS,
        name="attention",
    )(scalars, q_t, own, other)


def attention_back(scalars, q_t, own, other, o_t, do_t, lse):
    return pl.pallas_call(
        backward_kernel,
        grid_spec=pltpu.PrefetchScalarGridSpec(
            num_scalar_prefetch=1,
            grid=(KV_HEADS,),
            in_specs=[HEAD_SPEC, KV_SPEC, KV_SPEC, HEAD_SPEC, HEAD_SPEC, LSE_SPEC],
            out_specs=[HEAD_SPEC, KV_SPEC, KV_SPEC],
            scratch_shapes=[
                pltpu.VMEM((NBLK, 2, HEAD_DIM, BLK), BF16),
                pltpu.VMEM((2, HEAD_DIM, LANES), BF16),
                pltpu.VMEM((2, HEAD_DIM, LANES), BF16),
                pltpu.VMEM((2, HEAD_DIM, LANES), F32),
                pltpu.VMEM((NBLK, 2, HEAD_DIM, BLK), F32),
                pltpu.VMEM((2, 1, LANES), F32),
                pltpu.VMEM((2, 8, LANES), jnp.int32),
            ],
        ),
        out_shape=[HEAD_SHAPE, KV_SHAPE, KV_SHAPE],
        compiler_params=KERNEL_PARAMS,
        name="attention_back",
    )(scalars, q_t, own, other, o_t, do_t, lse)


ANY_SPEC = pl.BlockSpec(memory_space=pl.ANY)


def arrange_kernel(me, *refs):
    pieces, outs, sems = refs[:FSDP], refs[FSDP:-1], refs[-1]
    copies, at = [], 0
    for k, out in enumerate(outs):
        width = out.shape[2]
        for d, piece in enumerate(pieces):
            copies.append(
                pltpu.make_async_copy(
                    piece.at[:, pl.ds(at, width)], out.at[jnp.bitwise_xor(me[0], d)], sems.at[k, d]
                )
            )
        at += width
    for copy in copies:
        copy.start()
    for copy in copies:
        copy.wait()


def arrange(me, pieces, widths):
    rows = pieces[0].shape[0]
    return pl.pallas_call(
        arrange_kernel,
        grid_spec=pltpu.PrefetchScalarGridSpec(
            num_scalar_prefetch=1,
            grid=(),
            in_specs=[ANY_SPEC] * FSDP,
            out_specs=[ANY_SPEC] * len(widths),
            scratch_shapes=[pltpu.SemaphoreType.DMA((len(widths), FSDP))],
        ),
        out_shape=[jax.ShapeDtypeStruct((FSDP, rows, w), BF16) for w in widths],
        name="arrange",
    )(me, *pieces)


def dispatch_kernel(me, x_ref, *refs):
    outs, sems = refs[:FSDP], refs[FSDP]
    copies = [
        pltpu.make_async_copy(x_ref.at[jnp.bitwise_xor(me[0], d)], outs[d], sems.at[d])
        for d in range(FSDP)
    ]
    for copy in copies:
        copy.start()
    for copy in copies:
        copy.wait()


def dispatch(me, x):
    return pl.pallas_call(
        dispatch_kernel,
        grid_spec=pltpu.PrefetchScalarGridSpec(
            num_scalar_prefetch=1,
            grid=(),
            in_specs=[ANY_SPEC],
            out_specs=[ANY_SPEC] * FSDP,
            scratch_shapes=[pltpu.SemaphoreType.DMA((FSDP,))],
        ),
        out_shape=[jax.ShapeDtypeStruct(x.shape[1:], BF16)] * FSDP,
        name="dispatch",
    )(me, x)


def across(x, d):
    return lax.ppermute(x, "fsdp", [(i, i ^ d) for i in range(FSDP)]) if d else x


UNITS = FF // FSDP // 2


def unpack_kernel(sc, *refs):
    mlp0, mlp0_p, qkv0, qkv0_p, all1, all1_p, qkv_ref, out_ref, gu_ref = refs

    def layer_out(layer, halves, qkv_halves, qkv_at, wout_at):
        for half in range(2):
            mlp = halves[half]
            for k in range(2):
                for i in range(FSDP):
                    src = k * HALF + i * UNITS
                    dst = k * FF + i * 2 * UNITS + half * UNITS
                    gu_ref[layer, :, dst : dst + UNITS] = mlp[:, src : src + UNITS].astype(F32)
            cut = (Q_ROWS + KV_ROWS) // 2
            qkv_ref[layer, :, half * cut : (half + 1) * cut] = (
                qkv_halves[half][:, qkv_at : qkv_at + cut].astype(F32)
            )
            cut = D // 2
            out_ref[layer, :, half * cut : (half + 1) * cut] = (
                mlp[:, wout_at : wout_at + cut].astype(F32)
            )

    def both(order):
        m0, q0, a1 = [mlp0, mlp0_p][::order], [qkv0, qkv0_p][::order], [all1, all1_p][::order]
        layer_out(0, m0, q0, 0, FF + HALF)
        layer_out(1, a1, a1, FF + HALF + D // 2, FF + HALF)

    @pl.when(sc[0] == 0)
    def _():
        both(1)

    @pl.when(sc[0] != 0)
    def _():
        both(-1)


def unpack(core, mlp0, mlp0_p, qkv0, qkv0_p, all1, all1_p):
    return pl.pallas_call(
        unpack_kernel,
        grid_spec=pltpu.PrefetchScalarGridSpec(
            num_scalar_prefetch=1,
            grid=(),
            in_specs=[pl.BlockSpec(memory_space=pltpu.VMEM)] * 6,
            out_specs=[pl.BlockSpec(memory_space=pltpu.VMEM)] * 3,
        ),
        out_shape=[
            jax.ShapeDtypeStruct((LAYERS, SHARD, Q_ROWS + KV_ROWS), F32),
            jax.ShapeDtypeStruct((LAYERS, SHARD, D), F32),
            jax.ShapeDtypeStruct((LAYERS, SHARD, 2 * FF), F32),
        ],
        compiler_params=pltpu.CompilerParams(vmem_limit_bytes=40 * 2**20),
        name="unpack",
    )(core, mlp0, mlp0_p, qkv0, qkv0_p, all1, all1_p)


def rotate(x, cosine, sine):
    half = HEAD_DIM // 2
    first, second = x[:, :half], x[:, half:]
    return jnp.concatenate([first * cosine - second * sine, second * cosine + first * sine], 1)


def normed(hidden):
    inv_rms = lax.rsqrt(jnp.mean(hidden * hidden, -1, keepdims=True) + EPS)
    return hidden * inv_rms, inv_rms


def norm_back(d_unit, unit, inv_rms):
    return inv_rms * (d_unit - unit * jnp.mean(d_unit * unit, -1, keepdims=True))


def mm(a, b):
    return jnp.dot(a, b, preferred_element_type=F32)


def ein(spec, a, b):
    return jnp.einsum(spec, a, b, preferred_element_type=F32)


def local(tokens, block_order, doc_ids, norm_gains, w_qkv, w_out, w_gate_up, w_down, cotangent):
    place = lax.axis_index("ctx")
    core = jnp.bitwise_and(place, 1)
    first_core = core == 0
    me = lax.axis_index("fsdp").reshape(1)

    def my_half(left, right):
        return jnp.where(first_core, left, right)

    def in_order(own, other):
        return my_half(own, other), my_half(other, own)

    gain_cols = jnp.transpose(norm_gains.reshape(2 * LAYERS, SHARD))
    cut = (Q_ROWS + KV_ROWS + D) // 2
    wgu_cut = w_gate_up.reshape(LAYERS, SHARD, 2, FSDP, 2, FF // FSDP // 2)
    wgu_cut = my_half(wgu_cut[..., 0, :], wgu_cut[..., 1, :]).reshape(LAYERS, SHARD, FF)
    wd_cut = w_down.reshape(LAYERS, 2, FF // FSDP // 2, D)
    wd_cut = my_half(wd_cut[:, 0], wd_cut[:, 1]).reshape(LAYERS, SHARD, HALF)
    proj_cut = jnp.concatenate([w_qkv, w_out], 2)
    proj_cut = my_half(proj_cut[..., :cut], proj_cut[..., cut:])
    first = jnp.concatenate([proj_cut[0], gain_cols], 1)
    packs = [jnp.concatenate([wgu_cut[l], wd_cut[l]], 1) for l in range(LAYERS)]
    first = gather_fsdp(first)
    pieces = [across(packs[0], d) for d in range(FSDP)]
    pack1 = lax.all_gather(packs[1], "fsdp", axis=0, tiled=True)
    gains = jnp.transpose(first[:, cut:].astype(F32)).reshape(LAYERS, 2, D)

    def whole_proj(own):
        return jnp.concatenate(in_order(own, to_partner(own)), 1)

    def both_halves(wgu, wdown):
        return [(wgu, wdown), (to_partner(wgu), to_partner(wdown))]

    projs, mlps = [whole_proj(first[:, :cut])], []

    first_block = lax.dynamic_index_in_dim(block_order, 2 * place, 0, keepdims=False)
    low = jnp.minimum(first_block, NBLK - 1 - first_block)
    low_half = (first_block != low).astype(jnp.int32)
    starts = jnp.sum(
        (doc_ids[0][None, :] < jnp.arange(1, 5, dtype=jnp.int32)[:, None]).astype(jnp.int32), 1
    )
    scalars = jnp.concatenate([jnp.stack([low, low_half, core]), starts, block_order])
    lane = jnp.arange(ROWS, dtype=jnp.int32)
    pos = jnp.where(lane < BLK, first_block, NBLK - 2 - first_block) * BLK + lane
    inv_freq = THETA ** (-jnp.arange(HEAD_DIM // 2, dtype=F32) / (HEAD_DIM // 2))
    angles = pos.astype(F32)[None, :] * inv_freq[:, None]
    cosine, sine = jnp.cos(angles), jnp.sin(angles)

    hidden = tokens[0].astype(F32)
    saved = []
    for layer in range(LAYERS):
        wqkv, wout = projs[layer][:, : Q_ROWS + KV_ROWS], projs[layer][:, Q_ROWS + KV_ROWS :]
        unit_a, rms_a = normed(hidden)
        attn_in = (unit_a * gains[layer, 0]).astype(BF16)
        qkv_t = ein("de,td->et", wqkv, attn_in).reshape(-1, HEAD_DIM, ROWS)
        turned = rotate(qkv_t[: HEADS + KV_HEADS], cosine, sine)
        q_t = (turned[:HEADS] * HEAD_DIM**-0.5).astype(BF16)
        kv_t = jnp.concatenate([turned[HEADS:], qkv_t[HEADS + KV_HEADS :]], 0).astype(BF16)
        kv_t = kv_t.reshape(1, 2, KV_HEADS, HEAD_DIM, ROWS)
        kv_own = over_chips(jnp.broadcast_to(kv_t, (CTX // 2,) + kv_t.shape[1:]))
        if layer == 0:
            kv_own, pieces, late = lax.optimization_barrier((kv_own, pieces, proj_cut[1]))
            wgu, wdown = arrange(me, pieces, (FF, HALF))
            mlps.append(both_halves(wgu.reshape(D, FF), wdown.reshape(HALF, D)))
            late = gather_fsdp(late)
        else:
            mlps.append(both_halves(pack1[:, :FF], pack1[:, FF:].reshape(HALF, D)))
        kv_other = to_partner(kv_own)
        o_t, lse = attention(scalars, q_t, kv_own, kv_other)
        if layer == 0:
            projs.append(whole_proj(late))
        attn_out = o_t.astype(BF16).reshape(Q_ROWS, ROWS)
        mid = hidden + ein("at,ad->td", attn_out, wout)
        unit_m, rms_m = normed(mid)
        mlp_in = (unit_m * gains[layer, 1]).astype(BF16)
        hidden = mid
        halves = []
        for wgu, wdown in mlps[layer]:
            gate_up = mm(mlp_in, wgu)
            inner = (jax.nn.silu(gate_up[:, :HALF]) * gate_up[:, HALF:]).astype(BF16)
            hidden = hidden + mm(inner, wdown)
            halves.append((wgu, wdown, gate_up, inner))
        saved.append(
            (wqkv, wout, unit_a, rms_a, attn_in, q_t, kv_own, kv_other, o_t, lse, attn_out,
             unit_m, rms_m, mlp_in, halves)
        )
    output = hidden.astype(BF16).reshape(1, ROWS, D)

    d_hidden = cotangent[0].astype(F32)
    shares = []
    gain_grads = [None] * LAYERS
    for layer in reversed(range(LAYERS)):
        (wqkv, wout, unit_a, rms_a, attn_in, q_t, kv_own, kv_other, o_t, lse, attn_out,
         unit_m, rms_m, mlp_in, halves) = saved[layer]
        grad_b = d_hidden.astype(BF16)
        d_norm = 0.0
        wgu_parts, wd_parts = [], []
        for wgu, wdown, gate_up, inner in halves:
            d_inner = ein("td,fd->tf", grad_b, wdown)
            gate, up = gate_up[:, :HALF], gate_up[:, HALF:]
            sig = jax.nn.sigmoid(gate)
            d_gate = d_inner * up * sig * (1.0 + gate * (1.0 - sig))
            d_up = d_inner * (gate * sig)
            d_gu = jnp.concatenate([d_gate, d_up], 1).astype(BF16)
            d_norm = d_norm + ein("tf,df->td", d_gu, wgu)
            wd_parts.append(ein("tf,td->fd", inner, grad_b).astype(BF16))
            wgu_parts.append(ein("td,tf->df", mlp_in, d_gu).astype(BF16))
        d_gain_m = jnp.sum(d_norm * unit_m, 0)
        d_hidden = d_hidden + norm_back(d_norm * gains[layer, 1], unit_m, rms_m)
        grad_b = d_hidden.astype(BF16)
        d_wout = mm(attn_out, grad_b)
        do_t = ein("ad,td->at", wout, grad_b).astype(BF16).reshape(HEADS, HEAD_DIM, ROWS)
        if layer == 0:
            do_t, wgu_parts, wd_parts = lax.optimization_barrier((do_t, wgu_parts, wd_parts))
        wout_half = D // 2
        d_wout = d_wout.astype(BF16)
        wout_mine = my_half(d_wout[:, :wout_half], d_wout[:, wout_half:])
        wout_theirs = my_half(d_wout[:, wout_half:], d_wout[:, :wout_half])
        d_mlp = [
            sum_pair(wgu_parts[0], to_partner(wgu_parts[1])),
            sum_pair(wd_parts[0], to_partner(wd_parts[1])).reshape(D, HALF),
            sum_pair(wout_mine, to_partner(wout_theirs)),
        ]
        if layer == 0:
            d_mlp = jnp.concatenate(d_mlp, 1).reshape(FSDP, SHARD, -1)
            parts = [across(p, d) for d, p in enumerate(dispatch(me, d_mlp))]
            share = sum_chips(sum(p.astype(F32) for p in parts).astype(BF16))
            shares += [share, to_partner(share)]
        dq_t, dkv_own, dkv_other = attention_back(scalars, q_t, kv_own, kv_other, o_t, do_t, lse)
        dkv = (dkv_own.astype(F32) + to_partner(dkv_other).astype(F32)).astype(BF16)
        dkv = jnp.sum(over_chips(dkv).astype(F32), 0)
        turned = jnp.concatenate([dq_t, dkv[0]], 0)
        d_qkv = jnp.concatenate([rotate(turned, cosine, -sine), dkv[1]], 0)
        d_qkv = d_qkv.astype(BF16).reshape(Q_ROWS + KV_ROWS, ROWS)
        d_wqkv = ein("td,et->de", attn_in, d_qkv)
        d_norm = ein("et,de->td", d_qkv, wqkv)
        d_gain_a = jnp.sum(d_norm * unit_a, 0)
        d_hidden = d_hidden + norm_back(d_norm * gains[layer, 0], unit_a, rms_a)
        gain_grads[layer] = jnp.stack([d_gain_a, d_gain_m])
        d_wqkv = d_wqkv.astype(BF16)
        half = (Q_ROWS + KV_ROWS) // 2
        mine = my_half(d_wqkv[:, :half], d_wqkv[:, half:])
        theirs = my_half(d_wqkv[:, half:], d_wqkv[:, :half])
        d_wqkv = sum_pair(mine, to_partner(theirs))
        if layer == 0:
            d_gains = jnp.transpose(jnp.stack(gain_grads).reshape(2 * LAYERS, D)).astype(BF16)
            share = sum_chips(scatter_fsdp(jnp.concatenate([d_wqkv, d_gains], 1)))
        else:
            share = jnp.concatenate(d_mlp + [d_wqkv], 1)
            share = sum_chips(lax.psum_scatter(share, "fsdp", scatter_dimension=0, tiled=True))
        shares += [share, to_partner(share)]
    input_grad = d_hidden.reshape(1, ROWS, D)

    all1, all1_p, mlp0, mlp0_p, qkv0, qkv0_p = shares
    d_gain = qkv0[:, half:].astype(F32) + qkv0_p[:, half:].astype(F32)
    gain_grad = jnp.transpose(d_gain).reshape(LAYERS, 2, SHARD)
    qkv_grad, out_proj_grad, gate_up_grad = unpack(
        core.reshape(1), mlp0, mlp0_p, qkv0, qkv0_p, all1, all1_p
    )
    down_grad = []
    for own, theirs in ((mlp0, mlp0_p), (all1, all1_p)):
        rows = [x[:, FF : FF + HALF].reshape(UNITS, D) for x in in_order(own, theirs)]
        down_grad.append(jnp.concatenate(rows, 0))
    down_grad = jnp.stack(down_grad).astype(F32)
    return (output, input_grad, gain_grad, qkv_grad, out_proj_grad, gate_up_grad, down_grad)


def solution(mesh):
    in_specs = (
        P("fsdp", "ctx", None),
        P(),
        P("fsdp", None),
        P(None, None, "fsdp"),
        P(None, "fsdp", None),
        P(None, "fsdp", None),
        P(None, "fsdp", None),
        P(None, "fsdp", None),
        P("fsdp", "ctx", None),
    )
    out_specs = (
        P("fsdp", "ctx", None),
        P("fsdp", "ctx", None),
        P(None, None, "fsdp"),
        P(None, "fsdp", None),
        P(None, "fsdp", None),
        P(None, "fsdp", None),
        P(None, "fsdp", None),
    )
    return jax.shard_map(local, mesh=mesh, in_specs=in_specs, out_specs=out_specs, check_vma=False)
```

```python
import functools

import jax
import jax.numpy as jnp
from jax import lax
from jax.experimental import pallas as pl
from jax.experimental.pallas import tpu as pltpu
from jax.sharding import PartitionSpec as P

D = 576
HEADS = 9
KV_HEADS = 3
GROUP = 3
HEAD_DIM = 64
FF = 1536
LAYERS = 2
BLK = 128
NBLK = 32
EPS = 1e-05
THETA = 100000.0
NEG = -1e30
F32 = jnp.float32
BF16 = jnp.bfloat16
LANES = GROUP * BLK
CTX = 16
FSDP = 8
SHARD = D // FSDP
HALF = FF // 2
Q_ROWS = HEADS * HEAD_DIM
KV_ROWS = 2 * KV_HEADS * HEAD_DIM

PARTNER = [(i, i ^ 1) for i in range(CTX)]
SAME_CORE = [[2 * chip + core for chip in range(CTX // 2)] for core in range(2)]


def to_partner(x):
    return lax.ppermute(x, "ctx", PARTNER)


def over_chips(x):
    return lax.all_to_all(x, "ctx", 0, 0, axis_index_groups=SAME_CORE, tiled=True)


def over_fsdp(x):
    return lax.all_to_all(x, "fsdp", 0, 0, tiled=True)


def gather_fsdp(x):
    return over_fsdp(jnp.broadcast_to(x[None], (FSDP,) + x.shape)).reshape(-1, x.shape[1])


def scatter_fsdp(x):
    parts = over_fsdp(x.reshape(FSDP, -1, x.shape[1]))
    return jnp.sum(parts.astype(F32), 0).astype(BF16)


def sum_pair(a, b):
    return (a.astype(F32) + b.astype(F32)).astype(BF16)


def sum_chips(x):
    for bit in (2, 4, 8):
        x = sum_pair(x, lax.ppermute(x, "ctx", [(i, i ^ bit) for i in range(CTX)]))
    return x


def dot_tn(a, b):
    return lax.dot_general(a, b, (((0,), (0,)), ((), ())), preferred_element_type=F32)


def dot_nt(a, b):
    return lax.dot_general(a, b, (((1,), (1,)), ((), ())), preferred_element_type=F32)


UNROLL_F = 9
UNROLL_B = 3
CHUNK = 4
KEYS = CHUNK * BLK
CHUNKS = NBLK // CHUNK


def fill_keys(sc, own_ref, other_ref, kv_s):
    core = sc[2]
    for chip in range(CTX // 2):
        for half in range(2):
            lanes = slice(half * BLK, (half + 1) * BLK)
            block = sc[7 + 2 * (2 * chip + core) + half]
            kv_s[block] = own_ref[chip, :, 0, :, lanes]
            block = sc[7 + 2 * (2 * chip + 1 - core) + half]
            kv_s[block] = other_ref[chip, :, 0, :, lanes]


def fill_queries(sc, src_ref, dst):
    for half in range(2):
        lanes = slice(half * BLK, (half + 1) * BLK)
        which = jnp.bitwise_xor(half, sc[1])
        dst[which] = jnp.concatenate([src_ref[j, :, lanes] for j in range(GROUP)], axis=1)


def query_rows(sc, which):
    block = jnp.where(which == 0, sc[0], NBLK - 1 - sc[0])
    lane = lax.broadcasted_iota(jnp.int32, (1, LANES), 1)
    pos = block * BLK + jnp.bitwise_and(lane, BLK - 1)
    start = jnp.zeros((1, LANES), jnp.int32)
    for d in range(4):
        start = jnp.where(pos >= sc[3 + d], jnp.maximum(start, sc[3 + d]), start)
    return pos, start


def chunk_of(sc, t):
    high = (NBLK - sc[0] + CHUNK - 1) // CHUNK
    which = (t < high).astype(jnp.int32)
    return which, jnp.where(t < high, t, t - high)


def keys_of(kv_s, chunk, kind):
    return jnp.concatenate([kv_s[chunk * CHUNK + j, kind] for j in range(CHUNK)], axis=1)


def seen(pos_s, which, chunk):
    at = lax.broadcasted_iota(jnp.int32, (KEYS, LANES), 0)
    base = chunk * KEYS
    return (at >= pos_s[which, 1:2] - base) & (at <= pos_s[which, 0:1] - base)


def fill_rows(sc, pos_s):
    for which in range(2):
        pos, start = query_rows(sc, which)
        pos_s[which, 0:1] = pos
        pos_s[which, 1:2] = start


def forward_kernel(sc, q_ref, own_ref, other_ref, o_ref, lse_ref, kv_s, q_s, acc_s, m_s, l_s, pos_s):
    fill_keys(sc, own_ref, other_ref, kv_s)
    fill_queries(sc, q_ref, q_s)
    fill_rows(sc, pos_s)
    acc_s[...] = jnp.zeros_like(acc_s)
    m_s[...] = jnp.full_like(m_s, NEG)
    l_s[...] = jnp.zeros_like(l_s)

    def step(t, carry):
        which, chunk = chunk_of(sc, t)
        scores = dot_tn(keys_of(kv_s, chunk, 0), q_s[which])
        scores = jnp.where(seen(pos_s, which, chunk), scores, NEG)
        old = m_s[which]
        new = jnp.maximum(old, jnp.max(scores, axis=0, keepdims=True))
        prob = jnp.exp(scores - new)
        shrink = jnp.exp(old - new)
        m_s[which] = new
        l_s[which] = l_s[which] * shrink + jnp.sum(prob, axis=0, keepdims=True)
        acc_s[which] = acc_s[which] * shrink + jnp.dot(
            keys_of(kv_s, chunk, 1), prob.astype(BF16), preferred_element_type=F32
        )
        return carry

    lax.fori_loop(0, CHUNKS + 1, step, 0, unroll=UNROLL_F)
    for which in range(2):
        acc_s[which] = acc_s[which] / l_s[which]
        lse_ref[0, which] = m_s[which] + jnp.log(l_s[which])
    for half in range(2):
        mine = acc_s[jnp.bitwise_xor(half, sc[1])]
        for j in range(GROUP):
            o_ref[j, :, half * BLK : (half + 1) * BLK] = mine[:, j * BLK : (j + 1) * BLK]


def backward_kernel(
    sc, q_ref, own_ref, other_ref, o_ref, do_ref, lse_ref,
    dq_ref, down_ref, dother_ref,
    kv_s, q_s, do_s, dq_s, dkv_s, delta_s, pos_s,
):
    fill_keys(sc, own_ref, other_ref, kv_s)
    fill_queries(sc, q_ref, q_s)
    fill_queries(sc, do_ref, do_s)
    fill_queries(sc, o_ref, dq_s)
    fill_rows(sc, pos_s)
    for which in range(2):
        delta_s[which] = jnp.sum(dq_s[which] * do_s[which].astype(F32), axis=0, keepdims=True)
    dq_s[...] = jnp.zeros_like(dq_s)
    dkv_s[...] = jnp.zeros_like(dkv_s)

    def step(t, carry):
        which, chunk = chunk_of(sc, t)
        key_t, val_t, q_t, do_t = keys_of(kv_s, chunk, 0), keys_of(kv_s, chunk, 1), q_s[which], do_s[which]
        scores = dot_tn(key_t, q_t)
        prob = jnp.where(seen(pos_s, which, chunk), jnp.exp(scores - lse_ref[0, which]), 0.0)
        d_prob = dot_tn(val_t, do_t)
        d_score = (prob * (d_prob - delta_s[which])).astype(BF16)
        d_val = dot_nt(do_t, prob.astype(BF16))
        d_key = dot_nt(q_t, d_score)
        dq_s[which] = dq_s[which] + jnp.dot(key_t, d_score, preferred_element_type=F32)
        for j in range(CHUNK):
            lanes = slice(j * BLK, (j + 1) * BLK)
            dkv_s[chunk * CHUNK + j, 0] = dkv_s[chunk * CHUNK + j, 0] + d_key[:, lanes]
            dkv_s[chunk * CHUNK + j, 1] = dkv_s[chunk * CHUNK + j, 1] + d_val[:, lanes]
        return carry

    lax.fori_loop(0, CHUNKS + 1, step, 0, unroll=UNROLL_B)
    core = sc[2]
    scale = HEAD_DIM**-0.5
    for half in range(2):
        lanes = slice(half * BLK, (half + 1) * BLK)
        mine = dq_s[jnp.bitwise_xor(half, sc[1])] * scale
        for j in range(GROUP):
            dq_ref[j, :, lanes] = mine[:, j * BLK : (j + 1) * BLK]
        for chip in range(CTX // 2):
            block = sc[7 + 2 * (2 * chip + core) + half]
            down_ref[chip, :, 0, :, lanes] = dkv_s[block].astype(BF16)
            block = sc[7 + 2 * (2 * chip + 1 - core) + half]
            dother_ref[chip, :, 0, :, lanes] = dkv_s[block].astype(BF16)


ROWS = 2 * BLK
HEAD_SPEC = pl.BlockSpec((GROUP, HEAD_DIM, ROWS), lambda g, sc: (g, 0, 0))
KV_SPEC = pl.BlockSpec((CTX // 2, 2, 1, HEAD_DIM, ROWS), lambda g, sc: (0, 0, g, 0, 0))
LSE_SPEC = pl.BlockSpec((1, 2, 1, LANES), lambda g, sc: (g, 0, 0, 0))
HEAD_SHAPE = jax.ShapeDtypeStruct((HEADS, HEAD_DIM, ROWS), F32)
KV_SHAPE = jax.ShapeDtypeStruct((CTX // 2, 2, KV_HEADS, HEAD_DIM, ROWS), BF16)
LSE_SHAPE = jax.ShapeDtypeStruct((KV_HEADS, 2, 1, LANES), F32)
KERNEL_PARAMS = pltpu.CompilerParams(
    dimension_semantics=("arbitrary",), vmem_limit_bytes=40 * 2**20
)


def attention(scalars, q_t, own, other):
    return pl.pallas_call(
        forward_kernel,
        grid_spec=pltpu.PrefetchScalarGridSpec(
            num_scalar_prefetch=1,
            grid=(KV_HEADS,),
            in_specs=[HEAD_SPEC, KV_SPEC, KV_SPEC],
            out_specs=[HEAD_SPEC, LSE_SPEC],
            scratch_shapes=[
                pltpu.VMEM((NBLK, 2, HEAD_DIM, BLK), BF16),
                pltpu.VMEM((2, HEAD_DIM, LANES), BF16),
                pltpu.VMEM((2, HEAD_DIM, LANES), F32),
                pltpu.VMEM((2, 1, LANES), F32),
                pltpu.VMEM((2, 1, LANES), F32),
                pltpu.VMEM((2, 8, LANES), jnp.int32),
            ],
        ),
        out_shape=[HEAD_SHAPE, LSE_SHAPE],
        compiler_params=KERNEL_PARAMS,
        name="attention",
    )(scalars, q_t, own, other)


def attention_back(scalars, q_t, own, other, o_t, do_t, lse):
    return pl.pallas_call(
        backward_kernel,
        grid_spec=pltpu.PrefetchScalarGridSpec(
            num_scalar_prefetch=1,
            grid=(KV_HEADS,),
            in_specs=[HEAD_SPEC, KV_SPEC, KV_SPEC, HEAD_SPEC, HEAD_SPEC, LSE_SPEC],
            out_specs=[HEAD_SPEC, KV_SPEC, KV_SPEC],
            scratch_shapes=[
                pltpu.VMEM((NBLK, 2, HEAD_DIM, BLK), BF16),
                pltpu.VMEM((2, HEAD_DIM, LANES), BF16),
                pltpu.VMEM((2, HEAD_DIM, LANES), BF16),
                pltpu.VMEM((2, HEAD_DIM, LANES), F32),
                pltpu.VMEM((NBLK, 2, HEAD_DIM, BLK), F32),
                pltpu.VMEM((2, 1, LANES), F32),
                pltpu.VMEM((2, 8, LANES), jnp.int32),
            ],
        ),
        out_shape=[HEAD_SHAPE, KV_SHAPE, KV_SHAPE],
        compiler_params=KERNEL_PARAMS,
        name="attention_back",
    )(scalars, q_t, own, other, o_t, do_t, lse)


VMEM_SPEC = pl.BlockSpec(memory_space=pltpu.VMEM)


def arrange_kernel(me, *refs):
    pieces, outs = refs[:FSDP], refs[FSDP:]
    at = 0
    for out in outs:
        width = out.shape[2]
        for d, piece in enumerate(pieces):
            out[jnp.bitwise_xor(me[0], d)] = piece[:, at : at + width]
        at += width


def arrange(me, pieces, widths):
    rows = pieces[0].shape[0]
    return pl.pallas_call(
        arrange_kernel,
        grid_spec=pltpu.PrefetchScalarGridSpec(
            num_scalar_prefetch=1,
            grid=(),
            in_specs=[VMEM_SPEC] * FSDP,
            out_specs=[VMEM_SPEC] * len(widths),
        ),
        out_shape=[jax.ShapeDtypeStruct((FSDP, rows, w), BF16) for w in widths],
        compiler_params=pltpu.CompilerParams(vmem_limit_bytes=40 * 2**20),
        name="arrange",
    )(me, *pieces)


def dispatch_kernel(me, x_ref, *outs):
    for d, out in enumerate(outs):
        out[...] = x_ref[jnp.bitwise_xor(me[0], d)]


def dispatch(me, x):
    return pl.pallas_call(
        dispatch_kernel,
        grid_spec=pltpu.PrefetchScalarGridSpec(
            num_scalar_prefetch=1,
            grid=(),
            in_specs=[VMEM_SPEC],
            out_specs=[VMEM_SPEC] * FSDP,
        ),
        out_shape=[jax.ShapeDtypeStruct(x.shape[1:], BF16)] * FSDP,
        compiler_params=pltpu.CompilerParams(vmem_limit_bytes=40 * 2**20),
        name="dispatch",
    )(me, x)


def across(x, d):
    return lax.ppermute(x, "fsdp", [(i, i ^ d) for i in range(FSDP)]) if d else x


UNITS = FF // FSDP // 2


def unpack_kernel(sc, *refs):
    mlp0, mlp0_p, qkv0, qkv0_p, all1, all1_p, qkv_ref, out_ref, gu_ref = refs

    def layer_out(layer, halves, qkv_halves, qkv_at, wout_at):
        for half in range(2):
            mlp = halves[half]
            for k in range(2):
                for i in range(FSDP):
                    src = k * HALF + i * UNITS
                    dst = k * FF + i * 2 * UNITS + half * UNITS
                    gu_ref[layer, :, dst : dst + UNITS] = mlp[:, src : src + UNITS].astype(F32)
            cut = (Q_ROWS + KV_ROWS) // 2
            qkv_ref[layer, :, half * cut : (half + 1) * cut] = (
                qkv_halves[half][:, qkv_at : qkv_at + cut].astype(F32)
            )
            cut = D // 2
            out_ref[layer, :, half * cut : (half + 1) * cut] = (
                mlp[:, wout_at : wout_at + cut].astype(F32)
            )

    def both(order):
        m0, q0, a1 = [mlp0, mlp0_p][::order], [qkv0, qkv0_p][::order], [all1, all1_p][::order]
        layer_out(0, m0, q0, 0, FF + HALF)
        layer_out(1, a1, a1, FF + HALF + D // 2, FF + HALF)

    @pl.when(sc[0] == 0)
    def _():
        both(1)

    @pl.when(sc[0] != 0)
    def _():
        both(-1)


def unpack(core, mlp0, mlp0_p, qkv0, qkv0_p, all1, all1_p):
    return pl.pallas_call(
        unpack_kernel,
        grid_spec=pltpu.PrefetchScalarGridSpec(
            num_scalar_prefetch=1,
            grid=(),
            in_specs=[pl.BlockSpec(memory_space=pltpu.VMEM)] * 6,
            out_specs=[pl.BlockSpec(memory_space=pltpu.VMEM)] * 3,
        ),
        out_shape=[
            jax.ShapeDtypeStruct((LAYERS, SHARD, Q_ROWS + KV_ROWS), F32),
            jax.ShapeDtypeStruct((LAYERS, SHARD, D), F32),
            jax.ShapeDtypeStruct((LAYERS, SHARD, 2 * FF), F32),
        ],
        compiler_params=pltpu.CompilerParams(vmem_limit_bytes=40 * 2**20),
        name="unpack",
    )(core, mlp0, mlp0_p, qkv0, qkv0_p, all1, all1_p)


def rotate(x, cosine, sine):
    half = HEAD_DIM // 2
    first, second = x[:, :half], x[:, half:]
    return jnp.concatenate([first * cosine - second * sine, second * cosine + first * sine], 1)


def normed(hidden):
    inv_rms = lax.rsqrt(jnp.mean(hidden * hidden, -1, keepdims=True) + EPS)
    return hidden * inv_rms, inv_rms


def norm_back(d_unit, unit, inv_rms):
    return inv_rms * (d_unit - unit * jnp.mean(d_unit * unit, -1, keepdims=True))


def mm(a, b):
    return jnp.dot(a, b, preferred_element_type=F32)


def ein(spec, a, b):
    return jnp.einsum(spec, a, b, preferred_element_type=F32)


def local(tokens, block_order, doc_ids, norm_gains, w_qkv, w_out, w_gate_up, w_down, cotangent):
    place = lax.axis_index("ctx")
    core = jnp.bitwise_and(place, 1)
    first_core = core == 0
    me = lax.axis_index("fsdp").reshape(1)

    def my_half(left, right):
        return jnp.where(first_core, left, right)

    def in_order(own, other):
        return my_half(own, other), my_half(other, own)

    gain_cols = jnp.transpose(norm_gains.reshape(2 * LAYERS, SHARD))
    cut = (Q_ROWS + KV_ROWS + D) // 2
    wgu_cut = w_gate_up.reshape(LAYERS, SHARD, 2, FSDP, 2, FF // FSDP // 2)
    wgu_cut = my_half(wgu_cut[..., 0, :], wgu_cut[..., 1, :]).reshape(LAYERS, SHARD, FF)
    wd_cut = w_down.reshape(LAYERS, 2, FF // FSDP // 2, D)
    wd_cut = my_half(wd_cut[:, 0], wd_cut[:, 1]).reshape(LAYERS, SHARD, HALF)
    proj_cut = jnp.concatenate([w_qkv, w_out], 2)
    proj_cut = my_half(proj_cut[..., :cut], proj_cut[..., cut:])
    first = jnp.concatenate([proj_cut[0], gain_cols], 1)
    packs = [jnp.concatenate([wgu_cut[l], wd_cut[l]], 1) for l in range(LAYERS)]
    first = gather_fsdp(first)
    pieces = [across(packs[0], d) for d in range(FSDP)]
    pack1 = lax.all_gather(packs[1], "fsdp", axis=0, tiled=True)
    gains = jnp.transpose(first[:, cut:].astype(F32)).reshape(LAYERS, 2, D)

    def whole_proj(own):
        return jnp.concatenate(in_order(own, to_partner(own)), 1)

    def both_halves(wgu, wdown):
        return [(wgu, wdown), (to_partner(wgu), to_partner(wdown))]

    projs, mlps = [whole_proj(first[:, :cut])], []

    first_block = lax.dynamic_index_in_dim(block_order, 2 * place, 0, keepdims=False)
    low = jnp.minimum(first_block, NBLK - 1 - first_block)
    low_half = (first_block != low).astype(jnp.int32)
    starts = jnp.sum(
        (doc_ids[0][None, :] < jnp.arange(1, 5, dtype=jnp.int32)[:, None]).astype(jnp.int32), 1
    )
    scalars = jnp.concatenate([jnp.stack([low, low_half, core]), starts, block_order])
    lane = jnp.arange(ROWS, dtype=jnp.int32)
    pos = jnp.where(lane < BLK, first_block, NBLK - 2 - first_block) * BLK + lane
    inv_freq = THETA ** (-jnp.arange(HEAD_DIM // 2, dtype=F32) / (HEAD_DIM // 2))
    angles = pos.astype(F32)[None, :] * inv_freq[:, None]
    cosine, sine = jnp.cos(angles), jnp.sin(angles)

    hidden = tokens[0].astype(F32)
    saved = []
    for layer in range(LAYERS):
        wqkv, wout = projs[layer][:, : Q_ROWS + KV_ROWS], projs[layer][:, Q_ROWS + KV_ROWS :]
        unit_a, rms_a = normed(hidden)
        attn_in = (unit_a * gains[layer, 0]).astype(BF16)
        qkv_t = ein("de,td->et", wqkv, attn_in).reshape(-1, HEAD_DIM, ROWS)
        turned = rotate(qkv_t[: HEADS + KV_HEADS], cosine, sine)
        q_t = (turned[:HEADS] * HEAD_DIM**-0.5).astype(BF16)
        kv_t = jnp.concatenate([turned[HEADS:], qkv_t[HEADS + KV_HEADS :]], 0).astype(BF16)
        kv_t = kv_t.reshape(1, 2, KV_HEADS, HEAD_DIM, ROWS)
        kv_own = over_chips(jnp.broadcast_to(kv_t, (CTX // 2,) + kv_t.shape[1:]))
        if layer == 0:
            kv_own, late = lax.optimization_barrier((kv_own, proj_cut[1]))
            late = gather_fsdp(late)
        kv_other = to_partner(kv_own)
        o_t, lse = attention(scalars, q_t, kv_own, kv_other)
        if layer == 0:
            o_t, pieces, late = lax.optimization_barrier((o_t, pieces, late))
            wgu, wdown = arrange(me, pieces, (FF, HALF))
            mlps.append(both_halves(wgu.reshape(D, FF), wdown.reshape(HALF, D)))
            projs.append(whole_proj(late))
        else:
            mlps.append(both_halves(pack1[:, :FF], pack1[:, FF:].reshape(HALF, D)))
        attn_out = o_t.astype(BF16).reshape(Q_ROWS, ROWS)
        mid = hidden + ein("at,ad->td", attn_out, wout)
        unit_m, rms_m = normed(mid)
        mlp_in = (unit_m * gains[layer, 1]).astype(BF16)
        hidden = mid
        halves = []
        for wgu, wdown in mlps[layer]:
            gate_up = mm(mlp_in, wgu)
            inner = (jax.nn.silu(gate_up[:, :HALF]) * gate_up[:, HALF:]).astype(BF16)
            hidden = hidden + mm(inner, wdown)
            halves.append((wgu, wdown, gate_up, inner))
        saved.append(
            (wqkv, wout, unit_a, rms_a, attn_in, q_t, kv_own, kv_other, o_t, lse, attn_out,
             unit_m, rms_m, mlp_in, halves)
        )
    output = hidden.astype(BF16).reshape(1, ROWS, D)

    d_hidden = cotangent[0].astype(F32)
    shares = []
    gain_grads = [None] * LAYERS
    for layer in reversed(range(LAYERS)):
        (wqkv, wout, unit_a, rms_a, attn_in, q_t, kv_own, kv_other, o_t, lse, attn_out,
         unit_m, rms_m, mlp_in, halves) = saved[layer]
        grad_b = d_hidden.astype(BF16)
        d_norm = 0.0
        wgu_parts, wd_parts = [], []
        for wgu, wdown, gate_up, inner in halves:
            d_inner = ein("td,fd->tf", grad_b, wdown)
            gate, up = gate_up[:, :HALF], gate_up[:, HALF:]
            sig = jax.nn.sigmoid(gate)
            d_gate = d_inner * up * sig * (1.0 + gate * (1.0 - sig))
            d_up = d_inner * (gate * sig)
            d_gu = jnp.concatenate([d_gate, d_up], 1).astype(BF16)
            d_norm = d_norm + ein("tf,df->td", d_gu, wgu)
            wd_parts.append(ein("tf,td->fd", inner, grad_b).astype(BF16))
            wgu_parts.append(ein("td,tf->df", mlp_in, d_gu).astype(BF16))
        d_gain_m = jnp.sum(d_norm * unit_m, 0)
        d_hidden = d_hidden + norm_back(d_norm * gains[layer, 1], unit_m, rms_m)
        grad_b = d_hidden.astype(BF16)
        d_wout = mm(attn_out, grad_b)
        do_t = ein("ad,td->at", wout, grad_b).astype(BF16).reshape(HEADS, HEAD_DIM, ROWS)
        if layer == 0:
            do_t, wgu_parts, wd_parts = lax.optimization_barrier((do_t, wgu_parts, wd_parts))
        wout_half = D // 2
        d_wout = d_wout.astype(BF16)
        wout_mine = my_half(d_wout[:, :wout_half], d_wout[:, wout_half:])
        wout_theirs = my_half(d_wout[:, wout_half:], d_wout[:, :wout_half])
        d_mlp = [
            sum_pair(wgu_parts[0], to_partner(wgu_parts[1])),
            sum_pair(wd_parts[0], to_partner(wd_parts[1])).reshape(D, HALF),
            sum_pair(wout_mine, to_partner(wout_theirs)),
        ]
        if layer == 0:
            d_mlp = jnp.concatenate(d_mlp, 1).reshape(FSDP, SHARD, -1)
            parts = [across(p, d) for d, p in enumerate(dispatch(me, d_mlp))]
            share = sum_chips(sum(p.astype(F32) for p in parts).astype(BF16))
            shares += [share, to_partner(share)]
        dq_t, dkv_own, dkv_other = attention_back(scalars, q_t, kv_own, kv_other, o_t, do_t, lse)
        dkv = (dkv_own.astype(F32) + to_partner(dkv_other).astype(F32)).astype(BF16)
        dkv = jnp.sum(over_chips(dkv).astype(F32), 0)
        turned = jnp.concatenate([dq_t, dkv[0]], 0)
        d_qkv = jnp.concatenate([rotate(turned, cosine, -sine), dkv[1]], 0)
        d_qkv = d_qkv.astype(BF16).reshape(Q_ROWS + KV_ROWS, ROWS)
        d_wqkv = ein("td,et->de", attn_in, d_qkv)
        d_norm = ein("et,de->td", d_qkv, wqkv)
        d_gain_a = jnp.sum(d_norm * unit_a, 0)
        d_hidden = d_hidden + norm_back(d_norm * gains[layer, 0], unit_a, rms_a)
        gain_grads[layer] = jnp.stack([d_gain_a, d_gain_m])
        d_wqkv = d_wqkv.astype(BF16)
        half = (Q_ROWS + KV_ROWS) // 2
        mine = my_half(d_wqkv[:, :half], d_wqkv[:, half:])
        theirs = my_half(d_wqkv[:, half:], d_wqkv[:, :half])
        d_wqkv = sum_pair(mine, to_partner(theirs))
        if layer == 0:
            d_gains = jnp.transpose(jnp.stack(gain_grads).reshape(2 * LAYERS, D)).astype(BF16)
            share = sum_chips(scatter_fsdp(jnp.concatenate([d_wqkv, d_gains], 1)))
        else:
            share = jnp.concatenate(d_mlp + [d_wqkv], 1)
            share = sum_chips(lax.psum_scatter(share, "fsdp", scatter_dimension=0, tiled=True))
        shares += [share, to_partner(share)]
    input_grad = d_hidden.reshape(1, ROWS, D)

    all1, all1_p, mlp0, mlp0_p, qkv0, qkv0_p = shares
    d_gain = qkv0[:, half:].astype(F32) + qkv0_p[:, half:].astype(F32)
    gain_grad = jnp.transpose(d_gain).reshape(LAYERS, 2, SHARD)
    qkv_grad, out_proj_grad, gate_up_grad = unpack(
        core.reshape(1), mlp0, mlp0_p, qkv0, qkv0_p, all1, all1_p
    )
    down_grad = []
    for own, theirs in ((mlp0, mlp0_p), (all1, all1_p)):
        rows = [x[:, FF : FF + HALF].reshape(UNITS, D) for x in in_order(own, theirs)]
        down_grad.append(jnp.concatenate(rows, 0))
    down_grad = jnp.stack(down_grad).astype(F32)
    return (output, input_grad, gain_grad, qkv_grad, out_proj_grad, gate_up_grad, down_grad)


def solution(mesh):
    in_specs = (
        P("fsdp", "ctx", None),
        P(),
        P("fsdp", None),
        P(None, None, "fsdp"),
        P(None, "fsdp", None),
        P(None, "fsdp", None),
        P(None, "fsdp", None),
        P(None, "fsdp", None),
        P("fsdp", "ctx", None),
    )
    out_specs = (
        P("fsdp", "ctx", None),
        P("fsdp", "ctx", None),
        P(None, None, "fsdp"),
        P(None, "fsdp", None),
        P(None, "fsdp", None),
        P(None, "fsdp", None),
        P(None, "fsdp", None),
    )
    return jax.shard_map(local, mesh=mesh, in_specs=in_specs, out_specs=out_specs, check_vma=False)
```

```python
import functools

import jax
import jax.numpy as jnp
from jax import lax
from jax.experimental import pallas as pl
from jax.experimental.pallas import tpu as pltpu
from jax.sharding import PartitionSpec as P

D = 576
HEADS = 9
KV_HEADS = 3
GROUP = 3
HEAD_DIM = 64
FF = 1536
LAYERS = 2
BLK = 128
NBLK = 32
EPS = 1e-05
THETA = 100000.0
NEG = -1e30
F32 = jnp.float32
BF16 = jnp.bfloat16
LANES = GROUP * BLK
CTX = 16
FSDP = 8
SHARD = D // FSDP
HALF = FF // 2
Q_ROWS = HEADS * HEAD_DIM
KV_ROWS = 2 * KV_HEADS * HEAD_DIM

PARTNER = [(i, i ^ 1) for i in range(CTX)]
SAME_CORE = [[2 * chip + core for chip in range(CTX // 2)] for core in range(2)]


def to_partner(x):
    return lax.ppermute(x, "ctx", PARTNER)


def over_chips(x):
    return lax.all_to_all(x, "ctx", 0, 0, axis_index_groups=SAME_CORE, tiled=True)


def over_fsdp(x):
    return lax.all_to_all(x, "fsdp", 0, 0, tiled=True)


def gather_fsdp(x):
    return over_fsdp(jnp.broadcast_to(x[None], (FSDP,) + x.shape)).reshape(-1, x.shape[1])


def scatter_fsdp(x):
    parts = over_fsdp(x.reshape(FSDP, -1, x.shape[1]))
    return jnp.sum(parts.astype(F32), 0).astype(BF16)


def sum_pair(a, b):
    return (a.astype(F32) + b.astype(F32)).astype(BF16)


def sum_chips(x):
    for bit in (2, 4, 8):
        x = sum_pair(x, lax.ppermute(x, "ctx", [(i, i ^ bit) for i in range(CTX)]))
    return x


def dot_tn(a, b):
    return lax.dot_general(a, b, (((0,), (0,)), ((), ())), preferred_element_type=F32)


def dot_nt(a, b):
    return lax.dot_general(a, b, (((1,), (1,)), ((), ())), preferred_element_type=F32)


UNROLL_F = 9
UNROLL_B = 3
CHUNK = 4
KEYS = CHUNK * BLK
CHUNKS = NBLK // CHUNK


def fill_keys(sc, own_ref, other_ref, kv_s):
    core = sc[2]
    for chip in range(CTX // 2):
        for half in range(2):
            lanes = slice(half * BLK, (half + 1) * BLK)
            block = sc[7 + 2 * (2 * chip + core) + half]
            kv_s[block] = own_ref[chip, :, 0, :, lanes]
            block = sc[7 + 2 * (2 * chip + 1 - core) + half]
            kv_s[block] = other_ref[chip, :, 0, :, lanes]


def fill_queries(sc, src_ref, dst):
    for half in range(2):
        lanes = slice(half * BLK, (half + 1) * BLK)
        which = jnp.bitwise_xor(half, sc[1])
        dst[which] = jnp.concatenate([src_ref[j, :, lanes] for j in range(GROUP)], axis=1)


def query_rows(sc, which):
    block = jnp.where(which == 0, sc[0], NBLK - 1 - sc[0])
    lane = lax.broadcasted_iota(jnp.int32, (1, LANES), 1)
    pos = block * BLK + jnp.bitwise_and(lane, BLK - 1)
    start = jnp.zeros((1, LANES), jnp.int32)
    for d in range(4):
        start = jnp.where(pos >= sc[3 + d], jnp.maximum(start, sc[3 + d]), start)
    return pos, start


def chunk_of(sc, t):
    high = (NBLK - sc[0] + CHUNK - 1) // CHUNK
    which = (t < high).astype(jnp.int32)
    return which, jnp.where(t < high, t, t - high)


def keys_of(kv_s, chunk, kind):
    return jnp.concatenate([kv_s[chunk * CHUNK + j, kind] for j in range(CHUNK)], axis=1)


def seen(pos_s, which, chunk):
    at = lax.broadcasted_iota(jnp.int32, (KEYS, LANES), 0)
    base = chunk * KEYS
    return (at >= pos_s[which, 1:2] - base) & (at <= pos_s[which, 0:1] - base)


def fill_rows(sc, pos_s):
    for which in range(2):
        pos, start = query_rows(sc, which)
        pos_s[which, 0:1] = pos
        pos_s[which, 1:2] = start


def forward_kernel(sc, q_ref, own_ref, other_ref, o_ref, lse_ref, kv_s, q_s, acc_s, m_s, l_s, pos_s):
    fill_keys(sc, own_ref, other_ref, kv_s)
    fill_queries(sc, q_ref, q_s)
    fill_rows(sc, pos_s)
    acc_s[...] = jnp.zeros_like(acc_s)
    m_s[...] = jnp.full_like(m_s, NEG)
    l_s[...] = jnp.zeros_like(l_s)

    def step(t, carry):
        which, chunk = chunk_of(sc, t)
        scores = dot_tn(keys_of(kv_s, chunk, 0), q_s[which])
        scores = jnp.where(seen(pos_s, which, chunk), scores, NEG)
        old = m_s[which]
        new = jnp.maximum(old, jnp.max(scores, axis=0, keepdims=True))
        prob = jnp.exp(scores - new)
        shrink = jnp.exp(old - new)
        m_s[which] = new
        l_s[which] = l_s[which] * shrink + jnp.sum(prob, axis=0, keepdims=True)
        acc_s[which] = acc_s[which] * shrink + jnp.dot(
            keys_of(kv_s, chunk, 1), prob.astype(BF16), preferred_element_type=F32
        )
        return carry

    lax.fori_loop(0, CHUNKS + 1, step, 0, unroll=UNROLL_F)
    for which in range(2):
        acc_s[which] = acc_s[which] / l_s[which]
        lse_ref[0, which] = m_s[which] + jnp.log(l_s[which])
    for half in range(2):
        mine = acc_s[jnp.bitwise_xor(half, sc[1])]
        for j in range(GROUP):
            o_ref[j, :, half * BLK : (half + 1) * BLK] = mine[:, j * BLK : (j + 1) * BLK]


def backward_kernel(
    sc, q_ref, own_ref, other_ref, o_ref, do_ref, lse_ref,
    dq_ref, down_ref, dother_ref,
    kv_s, q_s, do_s, dq_s, dkv_s, delta_s, pos_s,
):
    fill_keys(sc, own_ref, other_ref, kv_s)
    fill_queries(sc, q_ref, q_s)
    fill_queries(sc, do_ref, do_s)
    fill_queries(sc, o_ref, dq_s)
    fill_rows(sc, pos_s)
    for which in range(2):
        delta_s[which] = jnp.sum(dq_s[which] * do_s[which].astype(F32), axis=0, keepdims=True)
    dq_s[...] = jnp.zeros_like(dq_s)
    dkv_s[...] = jnp.zeros_like(dkv_s)

    def step(t, carry):
        which, chunk = chunk_of(sc, t)
        key_t, val_t, q_t, do_t = keys_of(kv_s, chunk, 0), keys_of(kv_s, chunk, 1), q_s[which], do_s[which]
        scores = dot_tn(key_t, q_t)
        prob = jnp.where(seen(pos_s, which, chunk), jnp.exp(scores - lse_ref[0, which]), 0.0)
        d_prob = dot_tn(val_t, do_t)
        d_score = (prob * (d_prob - delta_s[which])).astype(BF16)
        d_val = dot_nt(do_t, prob.astype(BF16))
        d_key = dot_nt(q_t, d_score)
        dq_s[which] = dq_s[which] + jnp.dot(key_t, d_score, preferred_element_type=F32)
        for j in range(CHUNK):
            lanes = slice(j * BLK, (j + 1) * BLK)
            dkv_s[chunk * CHUNK + j, 0] = dkv_s[chunk * CHUNK + j, 0] + d_key[:, lanes]
            dkv_s[chunk * CHUNK + j, 1] = dkv_s[chunk * CHUNK + j, 1] + d_val[:, lanes]
        return carry

    lax.fori_loop(0, CHUNKS + 1, step, 0, unroll=UNROLL_B)
    core = sc[2]
    scale = HEAD_DIM**-0.5
    for half in range(2):
        lanes = slice(half * BLK, (half + 1) * BLK)
        mine = dq_s[jnp.bitwise_xor(half, sc[1])] * scale
        for j in range(GROUP):
            dq_ref[j, :, lanes] = mine[:, j * BLK : (j + 1) * BLK]
        for chip in range(CTX // 2):
            block = sc[7 + 2 * (2 * chip + core) + half]
            down_ref[chip, :, 0, :, lanes] = dkv_s[block].astype(BF16)
            block = sc[7 + 2 * (2 * chip + 1 - core) + half]
            dother_ref[chip, :, 0, :, lanes] = dkv_s[block].astype(BF16)


ROWS = 2 * BLK
HEAD_SPEC = pl.BlockSpec((GROUP, HEAD_DIM, ROWS), lambda g, sc: (g, 0, 0))
KV_SPEC = pl.BlockSpec((CTX // 2, 2, 1, HEAD_DIM, ROWS), lambda g, sc: (0, 0, g, 0, 0))
LSE_SPEC = pl.BlockSpec((1, 2, 1, LANES), lambda g, sc: (g, 0, 0, 0))
HEAD_SHAPE = jax.ShapeDtypeStruct((HEADS, HEAD_DIM, ROWS), F32)
KV_SHAPE = jax.ShapeDtypeStruct((CTX // 2, 2, KV_HEADS, HEAD_DIM, ROWS), BF16)
LSE_SHAPE = jax.ShapeDtypeStruct((KV_HEADS, 2, 1, LANES), F32)
KERNEL_PARAMS = pltpu.CompilerParams(
    dimension_semantics=("arbitrary",), vmem_limit_bytes=40 * 2**20
)


def attention(scalars, q_t, own, other):
    return pl.pallas_call(
        forward_kernel,
        grid_spec=pltpu.PrefetchScalarGridSpec(
            num_scalar_prefetch=1,
            grid=(KV_HEADS,),
            in_specs=[HEAD_SPEC, KV_SPEC, KV_SPEC],
            out_specs=[HEAD_SPEC, LSE_SPEC],
            scratch_shapes=[
                pltpu.VMEM((NBLK, 2, HEAD_DIM, BLK), BF16),
                pltpu.VMEM((2, HEAD_DIM, LANES), BF16),
                pltpu.VMEM((2, HEAD_DIM, LANES), F32),
                pltpu.VMEM((2, 1, LANES), F32),
                pltpu.VMEM((2, 1, LANES), F32),
                pltpu.VMEM((2, 8, LANES), jnp.int32),
            ],
        ),
        out_shape=[HEAD_SHAPE, LSE_SHAPE],
        compiler_params=KERNEL_PARAMS,
        name="attention",
    )(scalars, q_t, own, other)


def attention_back(scalars, q_t, own, other, o_t, do_t, lse):
    return pl.pallas_call(
        backward_kernel,
        grid_spec=pltpu.PrefetchScalarGridSpec(
            num_scalar_prefetch=1,
            grid=(KV_HEADS,),
            in_specs=[HEAD_SPEC, KV_SPEC, KV_SPEC, HEAD_SPEC, HEAD_SPEC, LSE_SPEC],
            out_specs=[HEAD_SPEC, KV_SPEC, KV_SPEC],
            scratch_shapes=[
                pltpu.VMEM((NBLK, 2, HEAD_DIM, BLK), BF16),
                pltpu.VMEM((2, HEAD_DIM, LANES), BF16),
                pltpu.VMEM((2, HEAD_DIM, LANES), BF16),
                pltpu.VMEM((2, HEAD_DIM, LANES), F32),
                pltpu.VMEM((NBLK, 2, HEAD_DIM, BLK), F32),
                pltpu.VMEM((2, 1, LANES), F32),
                pltpu.VMEM((2, 8, LANES), jnp.int32),
            ],
        ),
        out_shape=[HEAD_SHAPE, KV_SHAPE, KV_SHAPE],
        compiler_params=KERNEL_PARAMS,
        name="attention_back",
    )(scalars, q_t, own, other, o_t, do_t, lse)


VMEM_SPEC = pl.BlockSpec(memory_space=pltpu.VMEM)


UNITS = FF // FSDP // 2


def unpack_kernel(sc, *refs):
    mlp0, mlp0_p, qkv0, qkv0_p, all1, all1_p, qkv_ref, out_ref, gu_ref = refs

    def layer_out(layer, halves, qkv_halves, qkv_at, wout_at):
        for half in range(2):
            mlp = halves[half]
            for k in range(2):
                for i in range(FSDP):
                    src = k * HALF + i * UNITS
                    dst = k * FF + i * 2 * UNITS + half * UNITS
                    gu_ref[layer, :, dst : dst + UNITS] = mlp[:, src : src + UNITS].astype(F32)
            cut = (Q_ROWS + KV_ROWS) // 2
            qkv_ref[layer, :, half * cut : (half + 1) * cut] = (
                qkv_halves[half][:, qkv_at : qkv_at + cut].astype(F32)
            )
            cut = D // 2
            out_ref[layer, :, half * cut : (half + 1) * cut] = (
                mlp[:, wout_at : wout_at + cut].astype(F32)
            )

    def both(order):
        m0, q0, a1 = [mlp0, mlp0_p][::order], [qkv0, qkv0_p][::order], [all1, all1_p][::order]
        layer_out(0, m0, q0, 0, FF + HALF)
        layer_out(1, a1, a1, FF + HALF + D // 2, FF + HALF)

    @pl.when(sc[0] == 0)
    def _():
        both(1)

    @pl.when(sc[0] != 0)
    def _():
        both(-1)


def unpack(core, mlp0, mlp0_p, qkv0, qkv0_p, all1, all1_p):
    return pl.pallas_call(
        unpack_kernel,
        grid_spec=pltpu.PrefetchScalarGridSpec(
            num_scalar_prefetch=1,
            grid=(),
            in_specs=[VMEM_SPEC] * 6,
            out_specs=[VMEM_SPEC] * 3,
        ),
        out_shape=[
            jax.ShapeDtypeStruct((LAYERS, SHARD, Q_ROWS + KV_ROWS), F32),
            jax.ShapeDtypeStruct((LAYERS, SHARD, D), F32),
            jax.ShapeDtypeStruct((LAYERS, SHARD, 2 * FF), F32),
        ],
        compiler_params=pltpu.CompilerParams(vmem_limit_bytes=40 * 2**20),
        name="unpack",
    )(core, mlp0, mlp0_p, qkv0, qkv0_p, all1, all1_p)


def rotate(x, cosine, sine):
    half = HEAD_DIM // 2
    first, second = x[:, :half], x[:, half:]
    return jnp.concatenate([first * cosine - second * sine, second * cosine + first * sine], 1)


def normed(hidden):
    inv_rms = lax.rsqrt(jnp.mean(hidden * hidden, -1, keepdims=True) + EPS)
    return hidden * inv_rms, inv_rms


def norm_back(d_unit, unit, inv_rms):
    return inv_rms * (d_unit - unit * jnp.mean(d_unit * unit, -1, keepdims=True))


def mm(a, b):
    return jnp.dot(a, b, preferred_element_type=F32)


def ein(spec, a, b):
    return jnp.einsum(spec, a, b, preferred_element_type=F32)


def local(tokens, block_order, doc_ids, norm_gains, w_qkv, w_out, w_gate_up, w_down, cotangent):
    place = lax.axis_index("ctx")
    core = jnp.bitwise_and(place, 1)
    first_core = core == 0

    def my_half(left, right):
        return jnp.where(first_core, left, right)

    def in_order(own, other):
        return my_half(own, other), my_half(other, own)

    gain_cols = jnp.transpose(norm_gains.reshape(2 * LAYERS, SHARD))
    cut = (Q_ROWS + KV_ROWS + D) // 2

    def mlp_pack(layer):
        wgu = w_gate_up[layer].reshape(SHARD, 2, FSDP, 2, UNITS)
        wgu = my_half(wgu[..., 0, :], wgu[..., 1, :]).reshape(SHARD, FF)
        wdown = my_half(w_down[layer, :UNITS], w_down[layer, UNITS:]).reshape(SHARD, HALF)
        return jnp.concatenate([wgu, wdown], 1)

    def proj_pack(layer):
        proj = jnp.concatenate([w_qkv[layer], w_out[layer]], 1)
        return my_half(proj[:, :cut], proj[:, cut:])

    pack0, first = lax.optimization_barrier(
        (mlp_pack(0), jnp.concatenate([proj_pack(0), gain_cols], 1))
    )
    pack0 = lax.all_gather(pack0, "fsdp", axis=0, tiled=True)
    first = gather_fsdp(first)
    pack1 = lax.all_gather(mlp_pack(1), "fsdp", axis=0, tiled=True)
    gains = jnp.transpose(first[:, cut:].astype(F32)).reshape(LAYERS, 2, D)

    def whole_proj(own):
        return jnp.concatenate(in_order(own, to_partner(own)), 1)

    def mlp_halves(pack):
        wgu, wdown = pack[:, :FF], pack[:, FF:].reshape(HALF, D)
        return [(wgu, wdown), (to_partner(wgu), to_partner(wdown))]

    projs, mlps = [whole_proj(first[:, :cut])], []

    first_block = lax.dynamic_index_in_dim(block_order, 2 * place, 0, keepdims=False)
    low = jnp.minimum(first_block, NBLK - 1 - first_block)
    low_half = (first_block != low).astype(jnp.int32)
    starts = jnp.sum(
        (doc_ids[0][None, :] < jnp.arange(1, 5, dtype=jnp.int32)[:, None]).astype(jnp.int32), 1
    )
    scalars = jnp.concatenate([jnp.stack([low, low_half, core]), starts, block_order])
    lane = jnp.arange(ROWS, dtype=jnp.int32)
    pos = jnp.where(lane < BLK, first_block, NBLK - 2 - first_block) * BLK + lane
    inv_freq = THETA ** (-jnp.arange(HEAD_DIM // 2, dtype=F32) / (HEAD_DIM // 2))
    angles = pos.astype(F32)[None, :] * inv_freq[:, None]
    cosine, sine = jnp.cos(angles), jnp.sin(angles)

    hidden = tokens[0].astype(F32)
    saved = []
    for layer in range(LAYERS):
        wqkv, wout = projs[layer][:, : Q_ROWS + KV_ROWS], projs[layer][:, Q_ROWS + KV_ROWS :]
        unit_a, rms_a = normed(hidden)
        attn_in = (unit_a * gains[layer, 0]).astype(BF16)
        qkv_t = ein("de,td->et", wqkv, attn_in).reshape(-1, HEAD_DIM, ROWS)
        turned = rotate(qkv_t[: HEADS + KV_HEADS], cosine, sine)
        q_t = (turned[:HEADS] * HEAD_DIM**-0.5).astype(BF16)
        kv_t = jnp.concatenate([turned[HEADS:], qkv_t[HEADS + KV_HEADS :]], 0).astype(BF16)
        kv_t = kv_t.reshape(1, 2, KV_HEADS, HEAD_DIM, ROWS)
        kv_own = over_chips(jnp.broadcast_to(kv_t, (CTX // 2,) + kv_t.shape[1:]))
        if layer == 0:
            kv_own, late = lax.optimization_barrier((kv_own, proj_pack(1)))
            late = gather_fsdp(late)
        else:
            mlps.append(mlp_halves(pack1))
        kv_other = to_partner(kv_own)
        o_t, lse = attention(scalars, q_t, kv_own, kv_other)
        if layer == 0:
            o_t, pack0, late = lax.optimization_barrier((o_t, pack0, late))
            mlps.append(mlp_halves(pack0))
            projs.append(whole_proj(late))
        attn_out = o_t.astype(BF16).reshape(Q_ROWS, ROWS)
        mid = hidden + ein("at,ad->td", attn_out, wout)
        unit_m, rms_m = normed(mid)
        mlp_in = (unit_m * gains[layer, 1]).astype(BF16)
        hidden = mid
        halves = []
        for wgu, wdown in mlps[layer]:
            gate_up = mm(mlp_in, wgu)
            inner = (jax.nn.silu(gate_up[:, :HALF]) * gate_up[:, HALF:]).astype(BF16)
            hidden = hidden + mm(inner, wdown)
            halves.append((wgu, wdown, gate_up, inner))
        saved.append(
            (wqkv, wout, unit_a, rms_a, attn_in, q_t, kv_own, kv_other, o_t, lse, attn_out,
             unit_m, rms_m, mlp_in, halves)
        )
    output = hidden.astype(BF16).reshape(1, ROWS, D)

    d_hidden = cotangent[0].astype(F32)
    gain_grads = [None] * LAYERS
    for layer in reversed(range(LAYERS)):
        (wqkv, wout, unit_a, rms_a, attn_in, q_t, kv_own, kv_other, o_t, lse, attn_out,
         unit_m, rms_m, mlp_in, halves) = saved[layer]
        grad_b = d_hidden.astype(BF16)
        d_norm = 0.0
        wgu_parts, wd_parts = [], []
        for wgu, wdown, gate_up, inner in halves:
            d_inner = ein("td,fd->tf", grad_b, wdown)
            gate, up = gate_up[:, :HALF], gate_up[:, HALF:]
            sig = jax.nn.sigmoid(gate)
            d_gate = d_inner * up * sig * (1.0 + gate * (1.0 - sig))
            d_up = d_inner * (gate * sig)
            d_gu = jnp.concatenate([d_gate, d_up], 1).astype(BF16)
            d_norm = d_norm + ein("tf,df->td", d_gu, wgu)
            wd_parts.append(ein("tf,td->fd", inner, grad_b).astype(BF16))
            wgu_parts.append(ein("td,tf->df", mlp_in, d_gu).astype(BF16))
        d_gain_m = jnp.sum(d_norm * unit_m, 0)
        d_hidden = d_hidden + norm_back(d_norm * gains[layer, 1], unit_m, rms_m)
        grad_b = d_hidden.astype(BF16)
        d_wout = mm(attn_out, grad_b)
        do_t = ein("ad,td->at", wout, grad_b).astype(BF16).reshape(HEADS, HEAD_DIM, ROWS)
        if layer == 0:
            do_t, wgu_parts, wd_parts, late = lax.optimization_barrier(
                (do_t, wgu_parts, wd_parts, late)
            )
            late = scatter_fsdp(late)
        wout_half = D // 2
        d_wout = d_wout.astype(BF16)
        wout_mine = my_half(d_wout[:, :wout_half], d_wout[:, wout_half:])
        wout_theirs = my_half(d_wout[:, wout_half:], d_wout[:, :wout_half])
        d_mlp = [
            sum_pair(wgu_parts[0], to_partner(wgu_parts[1])),
            sum_pair(wd_parts[0], to_partner(wd_parts[1])).reshape(D, HALF),
            sum_pair(wout_mine, to_partner(wout_theirs)),
        ]
        share = lax.psum_scatter(
            jnp.concatenate(d_mlp, 1), "fsdp", scatter_dimension=0, tiled=True
        )
        if layer == 1:
            share1 = share
        else:
            share0 = share
        dq_t, dkv_own, dkv_other = attention_back(scalars, q_t, kv_own, kv_other, o_t, do_t, lse)
        dkv = (dkv_own.astype(F32) + to_partner(dkv_other).astype(F32)).astype(BF16)
        if layer == 0:
            dkv, late = lax.optimization_barrier((dkv, late))
            share1 = lax.optimization_barrier((share1, late, dkv))[0]
            share1 = sum_chips(jnp.concatenate([share1, late], 1))
        dkv = jnp.sum(over_chips(dkv).astype(F32), 0)
        turned = jnp.concatenate([dq_t, dkv[0]], 0)
        d_qkv = jnp.concatenate([rotate(turned, cosine, -sine), dkv[1]], 0)
        d_qkv = d_qkv.astype(BF16).reshape(Q_ROWS + KV_ROWS, ROWS)
        d_wqkv = ein("td,et->de", attn_in, d_qkv)
        d_norm = ein("et,de->td", d_qkv, wqkv)
        d_gain_a = jnp.sum(d_norm * unit_a, 0)
        d_hidden = d_hidden + norm_back(d_norm * gains[layer, 0], unit_a, rms_a)
        gain_grads[layer] = jnp.stack([d_gain_a, d_gain_m])
        d_wqkv = d_wqkv.astype(BF16)
        half = (Q_ROWS + KV_ROWS) // 2
        mine = my_half(d_wqkv[:, :half], d_wqkv[:, half:])
        theirs = my_half(d_wqkv[:, half:], d_wqkv[:, :half])
        d_wqkv = sum_pair(mine, to_partner(theirs))
        if layer == 0:
            d_gains = jnp.transpose(jnp.stack(gain_grads).reshape(2 * LAYERS, D)).astype(BF16)
            share_qkv = sum_chips(scatter_fsdp(jnp.concatenate([d_wqkv, d_gains], 1)))
        else:
            late = d_wqkv
    input_grad = d_hidden.reshape(1, ROWS, D)

    share0 = sum_chips(share0)
    mlp0, mlp0_p, qkv0, qkv0_p = share0, to_partner(share0), share_qkv, to_partner(share_qkv)
    all1, all1_p = share1, to_partner(share1)
    d_gain = qkv0[:, half:].astype(F32) + qkv0_p[:, half:].astype(F32)
    gain_grad = jnp.transpose(d_gain).reshape(LAYERS, 2, SHARD)
    qkv_grad, out_proj_grad, gate_up_grad = unpack(
        core.reshape(1), mlp0, mlp0_p, qkv0, qkv0_p, all1, all1_p
    )
    down_grad = []
    for own, theirs in ((mlp0, mlp0_p), (all1, all1_p)):
        rows = [x[:, FF : FF + HALF].reshape(UNITS, D) for x in in_order(own, theirs)]
        down_grad.append(jnp.concatenate(rows, 0))
    down_grad = jnp.stack(down_grad).astype(F32)
    return (output, input_grad, gain_grad, qkv_grad, out_proj_grad, gate_up_grad, down_grad)


def solution(mesh):
    in_specs = (
        P("fsdp", "ctx", None),
        P(),
        P("fsdp", None),
        P(None, None, "fsdp"),
        P(None, "fsdp", None),
        P(None, "fsdp", None),
        P(None, "fsdp", None),
        P(None, "fsdp", None),
        P("fsdp", "ctx", None),
    )
    out_specs = (
        P("fsdp", "ctx", None),
        P("fsdp", "ctx", None),
        P(None, None, "fsdp"),
        P(None, "fsdp", None),
        P(None, "fsdp", None),
        P(None, "fsdp", None),
        P(None, "fsdp", None),
    )
    return jax.shard_map(local, mesh=mesh, in_specs=in_specs, out_specs=out_specs, check_vma=False)
```

```python
import functools

import jax
import jax.numpy as jnp
from jax import lax
from jax.experimental import pallas as pl
from jax.experimental.pallas import tpu as pltpu
from jax.sharding import PartitionSpec as P

D = 576
HEADS = 9
KV_HEADS = 3
GROUP = 3
HEAD_DIM = 64
FF = 1536
LAYERS = 2
BLK = 128
NBLK = 32
EPS = 1e-05
THETA = 100000.0
NEG = -1e30
F32 = jnp.float32
BF16 = jnp.bfloat16
LANES = GROUP * BLK
CTX = 16
FSDP = 8
SHARD = D // FSDP
HALF = FF // 2
Q_ROWS = HEADS * HEAD_DIM
KV_ROWS = 2 * KV_HEADS * HEAD_DIM

PARTNER = [(i, i ^ 1) for i in range(CTX)]
SAME_CORE = [[2 * chip + core for chip in range(CTX // 2)] for core in range(2)]


def to_partner(x):
    return lax.ppermute(x, "ctx", PARTNER)


def over_chips(x):
    return lax.all_to_all(x, "ctx", 0, 0, axis_index_groups=SAME_CORE, tiled=True)


def over_fsdp(x):
    return lax.all_to_all(x, "fsdp", 0, 0, tiled=True)


def gather_fsdp(x):
    return over_fsdp(jnp.broadcast_to(x[None], (FSDP,) + x.shape)).reshape(-1, x.shape[1])


def scatter_fsdp(x):
    parts = over_fsdp(x.reshape(FSDP, -1, x.shape[1]))
    return jnp.sum(parts.astype(F32), 0).astype(BF16)


def sum_pair(a, b):
    return (a.astype(F32) + b.astype(F32)).astype(BF16)


def sum_chips(x):
    for bit in (2, 4, 8):
        x = sum_pair(x, lax.ppermute(x, "ctx", [(i, i ^ bit) for i in range(CTX)]))
    return x


def dot_tn(a, b):
    return lax.dot_general(a, b, (((0,), (0,)), ((), ())), preferred_element_type=F32)


def dot_nt(a, b):
    return lax.dot_general(a, b, (((1,), (1,)), ((), ())), preferred_element_type=F32)


UNROLL_F = 9
UNROLL_B = 3
CHUNK = 4
KEYS = CHUNK * BLK
CHUNKS = NBLK // CHUNK


def fill_keys(sc, own_ref, other_ref, kv_s):
    core = sc[2]
    for chip in range(CTX // 2):
        for half in range(2):
            lanes = slice(half * BLK, (half + 1) * BLK)
            block = sc[7 + 2 * (2 * chip + core) + half]
            kv_s[block] = own_ref[chip, :, 0, :, lanes]
            block = sc[7 + 2 * (2 * chip + 1 - core) + half]
            kv_s[block] = other_ref[chip, :, 0, :, lanes]


def fill_queries(sc, src_ref, dst):
    for half in range(2):
        lanes = slice(half * BLK, (half + 1) * BLK)
        which = jnp.bitwise_xor(half, sc[1])
        dst[which] = jnp.concatenate([src_ref[j, :, lanes] for j in range(GROUP)], axis=1)


def query_rows(sc, which):
    block = jnp.where(which == 0, sc[0], NBLK - 1 - sc[0])
    lane = lax.broadcasted_iota(jnp.int32, (1, LANES), 1)
    pos = block * BLK + jnp.bitwise_and(lane, BLK - 1)
    start = jnp.zeros((1, LANES), jnp.int32)
    for d in range(4):
        start = jnp.where(pos >= sc[3 + d], jnp.maximum(start, sc[3 + d]), start)
    return pos, start


def chunk_of(sc, t):
    high = (NBLK - sc[0] + CHUNK - 1) // CHUNK
    which = (t < high).astype(jnp.int32)
    return which, jnp.where(t < high, t, t - high)


def keys_of(kv_s, chunk, kind):
    return jnp.concatenate([kv_s[chunk * CHUNK + j, kind] for j in range(CHUNK)], axis=1)


def seen(pos_s, which, chunk):
    at = lax.broadcasted_iota(jnp.int32, (KEYS, LANES), 0)
    base = chunk * KEYS
    return (at >= pos_s[which, 1:2] - base) & (at <= pos_s[which, 0:1] - base)


def fill_rows(sc, pos_s):
    for which in range(2):
        pos, start = query_rows(sc, which)
        pos_s[which, 0:1] = pos
        pos_s[which, 1:2] = start


def forward_kernel(sc, q_ref, own_ref, other_ref, o_ref, lse_ref, kv_s, q_s, acc_s, m_s, l_s, pos_s):
    fill_keys(sc, own_ref, other_ref, kv_s)
    fill_queries(sc, q_ref, q_s)
    fill_rows(sc, pos_s)
    acc_s[...] = jnp.zeros_like(acc_s)
    m_s[...] = jnp.full_like(m_s, NEG)
    l_s[...] = jnp.zeros_like(l_s)

    def step(t, carry):
        which, chunk = chunk_of(sc, t)
        scores = dot_tn(keys_of(kv_s, chunk, 0), q_s[which])
        scores = jnp.where(seen(pos_s, which, chunk), scores, NEG)
        old = m_s[which]
        new = jnp.maximum(old, jnp.max(scores, axis=0, keepdims=True))
        prob = jnp.exp(scores - new)
        shrink = jnp.exp(old - new)
        m_s[which] = new
        l_s[which] = l_s[which] * shrink + jnp.sum(prob, axis=0, keepdims=True)
        acc_s[which] = acc_s[which] * shrink + jnp.dot(
            keys_of(kv_s, chunk, 1), prob.astype(BF16), preferred_element_type=F32
        )
        return carry

    lax.fori_loop(0, CHUNKS + 1, step, 0, unroll=UNROLL_F)
    for which in range(2):
        acc_s[which] = acc_s[which] / l_s[which]
        lse_ref[0, which] = m_s[which] + jnp.log(l_s[which])
    for half in range(2):
        mine = acc_s[jnp.bitwise_xor(half, sc[1])]
        for j in range(GROUP):
            o_ref[j, :, half * BLK : (half + 1) * BLK] = mine[:, j * BLK : (j + 1) * BLK]


def backward_kernel(
    sc, q_ref, own_ref, other_ref, o_ref, do_ref, lse_ref,
    dq_ref, down_ref, dother_ref,
    kv_s, q_s, do_s, dq_s, dkv_s, delta_s, pos_s,
):
    fill_keys(sc, own_ref, other_ref, kv_s)
    fill_queries(sc, q_ref, q_s)
    fill_queries(sc, do_ref, do_s)
    fill_queries(sc, o_ref, dq_s)
    fill_rows(sc, pos_s)
    for which in range(2):
        delta_s[which] = jnp.sum(dq_s[which] * do_s[which].astype(F32), axis=0, keepdims=True)
    dq_s[...] = jnp.zeros_like(dq_s)
    dkv_s[...] = jnp.zeros_like(dkv_s)

    def step(t, carry):
        which, chunk = chunk_of(sc, t)
        key_t, val_t, q_t, do_t = keys_of(kv_s, chunk, 0), keys_of(kv_s, chunk, 1), q_s[which], do_s[which]
        scores = dot_tn(key_t, q_t)
        prob = jnp.where(seen(pos_s, which, chunk), jnp.exp(scores - lse_ref[0, which]), 0.0)
        d_prob = dot_tn(val_t, do_t)
        d_score = (prob * (d_prob - delta_s[which])).astype(BF16)
        d_val = dot_nt(do_t, prob.astype(BF16))
        d_key = dot_nt(q_t, d_score)
        dq_s[which] = dq_s[which] + jnp.dot(key_t, d_score, preferred_element_type=F32)
        for j in range(CHUNK):
            lanes = slice(j * BLK, (j + 1) * BLK)
            dkv_s[chunk * CHUNK + j, 0] = dkv_s[chunk * CHUNK + j, 0] + d_key[:, lanes]
            dkv_s[chunk * CHUNK + j, 1] = dkv_s[chunk * CHUNK + j, 1] + d_val[:, lanes]
        return carry

    lax.fori_loop(0, CHUNKS + 1, step, 0, unroll=UNROLL_B)
    core = sc[2]
    scale = HEAD_DIM**-0.5
    for half in range(2):
        lanes = slice(half * BLK, (half + 1) * BLK)
        mine = dq_s[jnp.bitwise_xor(half, sc[1])] * scale
        for j in range(GROUP):
            dq_ref[j, :, lanes] = mine[:, j * BLK : (j + 1) * BLK]
        for chip in range(CTX // 2):
            block = sc[7 + 2 * (2 * chip + core) + half]
            down_ref[chip, :, 0, :, lanes] = dkv_s[block].astype(BF16)
            block = sc[7 + 2 * (2 * chip + 1 - core) + half]
            dother_ref[chip, :, 0, :, lanes] = dkv_s[block].astype(BF16)


ROWS = 2 * BLK
HEAD_SPEC = pl.BlockSpec((GROUP, HEAD_DIM, ROWS), lambda g, sc: (g, 0, 0))
KV_SPEC = pl.BlockSpec((CTX // 2, 2, 1, HEAD_DIM, ROWS), lambda g, sc: (0, 0, g, 0, 0))
LSE_SPEC = pl.BlockSpec((1, 2, 1, LANES), lambda g, sc: (g, 0, 0, 0))
HEAD_SHAPE = jax.ShapeDtypeStruct((HEADS, HEAD_DIM, ROWS), F32)
KV_SHAPE = jax.ShapeDtypeStruct((CTX // 2, 2, KV_HEADS, HEAD_DIM, ROWS), BF16)
LSE_SHAPE = jax.ShapeDtypeStruct((KV_HEADS, 2, 1, LANES), F32)
KERNEL_PARAMS = pltpu.CompilerParams(
    dimension_semantics=("arbitrary",), vmem_limit_bytes=40 * 2**20
)


def attention(scalars, q_t, own, other):
    return pl.pallas_call(
        forward_kernel,
        grid_spec=pltpu.PrefetchScalarGridSpec(
            num_scalar_prefetch=1,
            grid=(KV_HEADS,),
            in_specs=[HEAD_SPEC, KV_SPEC, KV_SPEC],
            out_specs=[HEAD_SPEC, LSE_SPEC],
            scratch_shapes=[
                pltpu.VMEM((NBLK, 2, HEAD_DIM, BLK), BF16),
                pltpu.VMEM((2, HEAD_DIM, LANES), BF16),
                pltpu.VMEM((2, HEAD_DIM, LANES), F32),
                pltpu.VMEM((2, 1, LANES), F32),
                pltpu.VMEM((2, 1, LANES), F32),
                pltpu.VMEM((2, 8, LANES), jnp.int32),
            ],
        ),
        out_shape=[HEAD_SHAPE, LSE_SHAPE],
        compiler_params=KERNEL_PARAMS,
        cost_estimate=pl.CostEstimate(
            flops=4 * 36 * BLK * HEADS * BLK * 256, transcendentals=36 * BLK * HEADS * BLK, bytes_accessed=50 * 10**6
        ),
        name="attention",
    )(scalars, q_t, own, other)


def attention_back(scalars, q_t, own, other, o_t, do_t, lse):
    return pl.pallas_call(
        backward_kernel,
        grid_spec=pltpu.PrefetchScalarGridSpec(
            num_scalar_prefetch=1,
            grid=(KV_HEADS,),
            in_specs=[HEAD_SPEC, KV_SPEC, KV_SPEC, HEAD_SPEC, HEAD_SPEC, LSE_SPEC],
            out_specs=[HEAD_SPEC, KV_SPEC, KV_SPEC],
            scratch_shapes=[
                pltpu.VMEM((NBLK, 2, HEAD_DIM, BLK), BF16),
                pltpu.VMEM((2, HEAD_DIM, LANES), BF16),
                pltpu.VMEM((2, HEAD_DIM, LANES), BF16),
                pltpu.VMEM((2, HEAD_DIM, LANES), F32),
                pltpu.VMEM((NBLK, 2, HEAD_DIM, BLK), F32),
                pltpu.VMEM((2, 1, LANES), F32),
                pltpu.VMEM((2, 8, LANES), jnp.int32),
            ],
        ),
        out_shape=[HEAD_SHAPE, KV_SHAPE, KV_SHAPE],
        compiler_params=KERNEL_PARAMS,
        cost_estimate=pl.CostEstimate(
            flops=10 * 36 * BLK * HEADS * BLK * 256, transcendentals=36 * BLK * HEADS * BLK, bytes_accessed=75 * 10**6
        ),
        name="attention_back",
    )(scalars, q_t, own, other, o_t, do_t, lse)


VMEM_SPEC = pl.BlockSpec(memory_space=pltpu.VMEM)


UNITS = FF // FSDP // 2


def unpack_kernel(sc, *refs):
    mlp0, mlp0_p, qkv0, qkv0_p, all1, all1_p, qkv_ref, out_ref, gu_ref = refs

    def layer_out(layer, halves, qkv_halves, qkv_at, wout_at):
        for half in range(2):
            mlp = halves[half]
            for k in range(2):
                for i in range(FSDP):
                    src = k * HALF + i * UNITS
                    dst = k * FF + i * 2 * UNITS + half * UNITS
                    gu_ref[layer, :, dst : dst + UNITS] = mlp[:, src : src + UNITS].astype(F32)
            cut = (Q_ROWS + KV_ROWS) // 2
            qkv_ref[layer, :, half * cut : (half + 1) * cut] = (
                qkv_halves[half][:, qkv_at : qkv_at + cut].astype(F32)
            )
            cut = D // 2
            out_ref[layer, :, half * cut : (half + 1) * cut] = (
                mlp[:, wout_at : wout_at + cut].astype(F32)
            )

    def both(order):
        m0, q0, a1 = [mlp0, mlp0_p][::order], [qkv0, qkv0_p][::order], [all1, all1_p][::order]
        layer_out(0, m0, q0, 0, FF + HALF)
        layer_out(1, a1, a1, FF + HALF + D // 2, FF + HALF)

    @pl.when(sc[0] == 0)
    def _():
        both(1)

    @pl.when(sc[0] != 0)
    def _():
        both(-1)


def unpack(core, mlp0, mlp0_p, qkv0, qkv0_p, all1, all1_p):
    return pl.pallas_call(
        unpack_kernel,
        grid_spec=pltpu.PrefetchScalarGridSpec(
            num_scalar_prefetch=1,
            grid=(),
            in_specs=[VMEM_SPEC] * 6,
            out_specs=[VMEM_SPEC] * 3,
        ),
        out_shape=[
            jax.ShapeDtypeStruct((LAYERS, SHARD, Q_ROWS + KV_ROWS), F32),
            jax.ShapeDtypeStruct((LAYERS, SHARD, D), F32),
            jax.ShapeDtypeStruct((LAYERS, SHARD, 2 * FF), F32),
        ],
        compiler_params=pltpu.CompilerParams(vmem_limit_bytes=40 * 2**20),
        name="unpack",
    )(core, mlp0, mlp0_p, qkv0, qkv0_p, all1, all1_p)


def rotate(x, cosine, sine):
    half = HEAD_DIM // 2
    first, second = x[:, :half], x[:, half:]
    return jnp.concatenate([first * cosine - second * sine, second * cosine + first * sine], 1)


def normed(hidden):
    inv_rms = lax.rsqrt(jnp.mean(hidden * hidden, -1, keepdims=True) + EPS)
    return hidden * inv_rms, inv_rms


def norm_back(d_unit, unit, inv_rms):
    return inv_rms * (d_unit - unit * jnp.mean(d_unit * unit, -1, keepdims=True))


def mm(a, b):
    return jnp.dot(a, b, preferred_element_type=F32)


def ein(spec, a, b):
    return jnp.einsum(spec, a, b, preferred_element_type=F32)


def local(tokens, block_order, doc_ids, norm_gains, w_qkv, w_out, w_gate_up, w_down, cotangent):
    place = lax.axis_index("ctx")
    core = jnp.bitwise_and(place, 1)
    first_core = core == 0

    def my_half(left, right):
        return jnp.where(first_core, left, right)

    def in_order(own, other):
        return my_half(own, other), my_half(other, own)

    gain_cols = jnp.transpose(norm_gains.reshape(2 * LAYERS, SHARD))
    cut = (Q_ROWS + KV_ROWS + D) // 2

    def mlp_pack(layer):
        wgu = w_gate_up[layer].reshape(SHARD, 2, FSDP, 2, UNITS)
        wgu = my_half(wgu[..., 0, :], wgu[..., 1, :]).reshape(SHARD, FF)
        wdown = my_half(w_down[layer, :UNITS], w_down[layer, UNITS:]).reshape(SHARD, HALF)
        return jnp.concatenate([wgu, wdown], 1)

    def proj_pack(layer):
        proj = jnp.concatenate([w_qkv[layer], w_out[layer]], 1)
        return my_half(proj[:, :cut], proj[:, cut:])

    pack0, first = lax.optimization_barrier(
        (mlp_pack(0), jnp.concatenate([proj_pack(0), gain_cols], 1))
    )
    pack0 = lax.all_gather(pack0, "fsdp", axis=0, tiled=True)
    first = gather_fsdp(first)
    pack1 = lax.all_gather(mlp_pack(1), "fsdp", axis=0, tiled=True)
    gains = jnp.transpose(first[:, cut:].astype(F32)).reshape(LAYERS, 2, D)

    def whole_proj(own):
        return jnp.concatenate(in_order(own, to_partner(own)), 1)

    def mlp_halves(pack):
        wgu, wdown = pack[:, :FF], pack[:, FF:].reshape(HALF, D)
        return [(wgu, wdown), (to_partner(wgu), to_partner(wdown))]

    projs, mlps = [whole_proj(first[:, :cut])], []

    first_block = lax.dynamic_index_in_dim(block_order, 2 * place, 0, keepdims=False)
    low = jnp.minimum(first_block, NBLK - 1 - first_block)
    low_half = (first_block != low).astype(jnp.int32)
    starts = jnp.sum(
        (doc_ids[0][None, :] < jnp.arange(1, 5, dtype=jnp.int32)[:, None]).astype(jnp.int32), 1
    )
    scalars = jnp.concatenate([jnp.stack([low, low_half, core]), starts, block_order])
    lane = jnp.arange(ROWS, dtype=jnp.int32)
    pos = jnp.where(lane < BLK, first_block, NBLK - 2 - first_block) * BLK + lane
    inv_freq = THETA ** (-jnp.arange(HEAD_DIM // 2, dtype=F32) / (HEAD_DIM // 2))
    angles = pos.astype(F32)[None, :] * inv_freq[:, None]
    cosine, sine = jnp.cos(angles), jnp.sin(angles)

    hidden = tokens[0].astype(F32)
    saved = []
    for layer in range(LAYERS):
        wqkv, wout = projs[layer][:, : Q_ROWS + KV_ROWS], projs[layer][:, Q_ROWS + KV_ROWS :]
        unit_a, rms_a = normed(hidden)
        attn_in = (unit_a * gains[layer, 0]).astype(BF16)
        qkv_t = ein("de,td->et", wqkv, attn_in).reshape(-1, HEAD_DIM, ROWS)
        turned = rotate(qkv_t[: HEADS + KV_HEADS], cosine, sine)
        q_t = (turned[:HEADS] * HEAD_DIM**-0.5).astype(BF16)
        kv_t = jnp.concatenate([turned[HEADS:], qkv_t[HEADS + KV_HEADS :]], 0).astype(BF16)
        kv_t = kv_t.reshape(1, 2, KV_HEADS, HEAD_DIM, ROWS)
        kv_own = over_chips(jnp.broadcast_to(kv_t, (CTX // 2,) + kv_t.shape[1:]))
        if layer == 0:
            kv_own, late = lax.optimization_barrier((kv_own, proj_pack(1)))
            late = gather_fsdp(late)
        kv_other = to_partner(kv_own)
        o_t, lse = attention(scalars, q_t, kv_own, kv_other)
        if layer == 0:
            o_t, pack0, late = lax.optimization_barrier((o_t, pack0, late))
            mlps.append(mlp_halves(pack0))
            projs.append(whole_proj(late))
        else:
            o_t, pack1 = lax.optimization_barrier((o_t, pack1))
            mlps.append(mlp_halves(pack1))
        attn_out = o_t.astype(BF16).reshape(Q_ROWS, ROWS)
        mid = hidden + ein("at,ad->td", attn_out, wout)
        unit_m, rms_m = normed(mid)
        mlp_in = (unit_m * gains[layer, 1]).astype(BF16)
        hidden = mid
        halves = []
        for wgu, wdown in mlps[layer]:
            gate_up = mm(mlp_in, wgu)
            inner = (jax.nn.silu(gate_up[:, :HALF]) * gate_up[:, HALF:]).astype(BF16)
            hidden = hidden + mm(inner, wdown)
            halves.append((wgu, wdown, gate_up, inner))
        saved.append(
            (wqkv, wout, unit_a, rms_a, attn_in, q_t, kv_own, kv_other, o_t, lse, attn_out,
             unit_m, rms_m, mlp_in, halves)
        )
    output = hidden.astype(BF16).reshape(1, ROWS, D)

    d_hidden = cotangent[0].astype(F32)
    gain_grads = [None] * LAYERS
    for layer in reversed(range(LAYERS)):
        (wqkv, wout, unit_a, rms_a, attn_in, q_t, kv_own, kv_other, o_t, lse, attn_out,
         unit_m, rms_m, mlp_in, halves) = saved[layer]
        grad_b = d_hidden.astype(BF16)
        d_norm = 0.0
        wgu_parts, wd_parts = [], []
        for wgu, wdown, gate_up, inner in halves:
            d_inner = ein("td,fd->tf", grad_b, wdown)
            gate, up = gate_up[:, :HALF], gate_up[:, HALF:]
            sig = jax.nn.sigmoid(gate)
            d_gate = d_inner * up * sig * (1.0 + gate * (1.0 - sig))
            d_up = d_inner * (gate * sig)
            d_gu = jnp.concatenate([d_gate, d_up], 1).astype(BF16)
            d_norm = d_norm + ein("tf,df->td", d_gu, wgu)
            wd_parts.append(ein("tf,td->fd", inner, grad_b).astype(BF16))
            wgu_parts.append(ein("td,tf->df", mlp_in, d_gu).astype(BF16))
        d_gain_m = jnp.sum(d_norm * unit_m, 0)
        d_hidden = d_hidden + norm_back(d_norm * gains[layer, 1], unit_m, rms_m)
        grad_b = d_hidden.astype(BF16)
        d_wout = mm(attn_out, grad_b)
        do_t = ein("ad,td->at", wout, grad_b).astype(BF16).reshape(HEADS, HEAD_DIM, ROWS)
        if layer == 0:
            do_t, wgu_parts, wd_parts, late = lax.optimization_barrier(
                (do_t, wgu_parts, wd_parts, late)
            )
            late = scatter_fsdp(late)
        wout_half = D // 2
        d_wout = d_wout.astype(BF16)
        wout_mine = my_half(d_wout[:, :wout_half], d_wout[:, wout_half:])
        wout_theirs = my_half(d_wout[:, wout_half:], d_wout[:, :wout_half])
        d_mlp = [
            sum_pair(wgu_parts[0], to_partner(wgu_parts[1])),
            sum_pair(wd_parts[0], to_partner(wd_parts[1])).reshape(D, HALF),
            sum_pair(wout_mine, to_partner(wout_theirs)),
        ]
        if layer == 1:
            do_t, d_mlp = lax.optimization_barrier((do_t, d_mlp))
        share = lax.psum_scatter(
            jnp.concatenate(d_mlp, 1), "fsdp", scatter_dimension=0, tiled=True
        )
        if layer == 1:
            share1 = share
        else:
            share0 = share
        dq_t, dkv_own, dkv_other = attention_back(scalars, q_t, kv_own, kv_other, o_t, do_t, lse)
        dkv = (dkv_own.astype(F32) + to_partner(dkv_other).astype(F32)).astype(BF16)
        if layer == 0:
            dkv, late = lax.optimization_barrier((dkv, late))
            share1 = lax.optimization_barrier((share1, late, dkv))[0]
            share1 = sum_chips(jnp.concatenate([share1, late], 1))
        dkv = jnp.sum(over_chips(dkv).astype(F32), 0)
        turned = jnp.concatenate([dq_t, dkv[0]], 0)
        d_qkv = jnp.concatenate([rotate(turned, cosine, -sine), dkv[1]], 0)
        d_qkv = d_qkv.astype(BF16).reshape(Q_ROWS + KV_ROWS, ROWS)
        d_wqkv = ein("td,et->de", attn_in, d_qkv)
        d_norm = ein("et,de->td", d_qkv, wqkv)
        d_gain_a = jnp.sum(d_norm * unit_a, 0)
        d_hidden = d_hidden + norm_back(d_norm * gains[layer, 0], unit_a, rms_a)
        gain_grads[layer] = jnp.stack([d_gain_a, d_gain_m])
        d_wqkv = d_wqkv.astype(BF16)
        half = (Q_ROWS + KV_ROWS) // 2
        mine = my_half(d_wqkv[:, :half], d_wqkv[:, half:])
        theirs = my_half(d_wqkv[:, half:], d_wqkv[:, :half])
        d_wqkv = sum_pair(mine, to_partner(theirs))
        if layer == 0:
            d_gains = jnp.transpose(jnp.stack(gain_grads).reshape(2 * LAYERS, D)).astype(BF16)
            share_qkv = sum_chips(scatter_fsdp(jnp.concatenate([d_wqkv, d_gains], 1)))
        else:
            late = d_wqkv
    input_grad = d_hidden.reshape(1, ROWS, D)

    share0 = sum_chips(share0)
    mlp0, mlp0_p, qkv0, qkv0_p = share0, to_partner(share0), share_qkv, to_partner(share_qkv)
    all1, all1_p = share1, to_partner(share1)
    d_gain = qkv0[:, half:].astype(F32) + qkv0_p[:, half:].astype(F32)
    gain_grad = jnp.transpose(d_gain).reshape(LAYERS, 2, SHARD)
    qkv_grad, out_proj_grad, gate_up_grad = unpack(
        core.reshape(1), mlp0, mlp0_p, qkv0, qkv0_p, all1, all1_p
    )
    down_grad = []
    for own, theirs in ((mlp0, mlp0_p), (all1, all1_p)):
        rows = [x[:, FF : FF + HALF].reshape(UNITS, D) for x in in_order(own, theirs)]
        down_grad.append(jnp.concatenate(rows, 0))
    down_grad = jnp.stack(down_grad).astype(F32)
    return (output, input_grad, gain_grad, qkv_grad, out_proj_grad, gate_up_grad, down_grad)


def solution(mesh):
    in_specs = (
        P("fsdp", "ctx", None),
        P(),
        P("fsdp", None),
        P(None, None, "fsdp"),
        P(None, "fsdp", None),
        P(None, "fsdp", None),
        P(None, "fsdp", None),
        P(None, "fsdp", None),
        P("fsdp", "ctx", None),
    )
    out_specs = (
        P("fsdp", "ctx", None),
        P("fsdp", "ctx", None),
        P(None, None, "fsdp"),
        P(None, "fsdp", None),
        P(None, "fsdp", None),
        P(None, "fsdp", None),
        P(None, "fsdp", None),
    )
    return jax.shard_map(local, mesh=mesh, in_specs=in_specs, out_specs=out_specs, check_vma=False)
```

```python
import functools

import jax
import jax.numpy as jnp
from jax import lax
from jax.experimental import pallas as pl
from jax.experimental.pallas import tpu as pltpu
from jax.sharding import PartitionSpec as P

D = 576
HEADS = 9
KV_HEADS = 3
GROUP = 3
HEAD_DIM = 64
FF = 1536
LAYERS = 2
BLK = 128
NBLK = 32
EPS = 1e-05
THETA = 100000.0
NEG = -1e30
F32 = jnp.float32
BF16 = jnp.bfloat16
LANES = GROUP * BLK
CTX = 16
FSDP = 8
SHARD = D // FSDP
HALF = FF // 2
Q_ROWS = HEADS * HEAD_DIM
KV_ROWS = 2 * KV_HEADS * HEAD_DIM

PARTNER = [(i, i ^ 1) for i in range(CTX)]
SAME_CORE = [[2 * chip + core for chip in range(CTX // 2)] for core in range(2)]


def to_partner(x):
    return lax.ppermute(x, "ctx", PARTNER)


def over_chips(x):
    return lax.all_to_all(x, "ctx", 0, 0, axis_index_groups=SAME_CORE, tiled=True)


def over_fsdp(x):
    return lax.all_to_all(x, "fsdp", 0, 0, tiled=True)


def gather_fsdp(x):
    return over_fsdp(jnp.broadcast_to(x[None], (FSDP,) + x.shape)).reshape(-1, x.shape[1])


def scatter_fsdp(x):
    parts = over_fsdp(x.reshape(FSDP, -1, x.shape[1]))
    return jnp.sum(parts.astype(F32), 0).astype(BF16)


def sum_pair(a, b):
    return (a.astype(F32) + b.astype(F32)).astype(BF16)


def sum_chips(x):
    for bit in (2, 4, 8):
        x = sum_pair(x, lax.ppermute(x, "ctx", [(i, i ^ bit) for i in range(CTX)]))
    return x


def dot_tn(a, b):
    return lax.dot_general(a, b, (((0,), (0,)), ((), ())), preferred_element_type=F32)


def dot_nt(a, b):
    return lax.dot_general(a, b, (((1,), (1,)), ((), ())), preferred_element_type=F32)


UNROLL_F = 9
UNROLL_B = 3
CHUNK = 4
KEYS = CHUNK * BLK
CHUNKS = NBLK // CHUNK


def fill_keys(sc, own_ref, other_ref, kv_s):
    core = sc[2]
    for chip in range(CTX // 2):
        for half in range(2):
            lanes = slice(half * BLK, (half + 1) * BLK)
            block = sc[7 + 2 * (2 * chip + core) + half]
            kv_s[block] = own_ref[chip, :, 0, :, lanes]
            block = sc[7 + 2 * (2 * chip + 1 - core) + half]
            kv_s[block] = other_ref[chip, :, 0, :, lanes]


def fill_queries(sc, src_ref, dst):
    for half in range(2):
        lanes = slice(half * BLK, (half + 1) * BLK)
        which = jnp.bitwise_xor(half, sc[1])
        dst[which] = jnp.concatenate([src_ref[j, :, lanes] for j in range(GROUP)], axis=1)


def query_rows(sc, which):
    block = jnp.where(which == 0, sc[0], NBLK - 1 - sc[0])
    lane = lax.broadcasted_iota(jnp.int32, (1, LANES), 1)
    pos = block * BLK + jnp.bitwise_and(lane, BLK - 1)
    start = jnp.zeros((1, LANES), jnp.int32)
    for d in range(4):
        start = jnp.where(pos >= sc[3 + d], jnp.maximum(start, sc[3 + d]), start)
    return pos, start


def chunk_of(sc, t):
    high = (NBLK - sc[0] + CHUNK - 1) // CHUNK
    which = (t < high).astype(jnp.int32)
    return which, jnp.where(t < high, t, t - high)


def keys_of(kv_s, chunk, kind):
    return jnp.concatenate([kv_s[chunk * CHUNK + j, kind] for j in range(CHUNK)], axis=1)


def seen(pos_s, which, chunk):
    at = lax.broadcasted_iota(jnp.int32, (KEYS, LANES), 0)
    base = chunk * KEYS
    return (at >= pos_s[which, 1:2] - base) & (at <= pos_s[which, 0:1] - base)


def fill_rows(sc, pos_s):
    for which in range(2):
        pos, start = query_rows(sc, which)
        pos_s[which, 0:1] = pos
        pos_s[which, 1:2] = start


def forward_kernel(sc, q_ref, own_ref, other_ref, o_ref, lse_ref, kv_s, q_s, acc_s, m_s, l_s, pos_s):
    fill_keys(sc, own_ref, other_ref, kv_s)
    fill_queries(sc, q_ref, q_s)
    fill_rows(sc, pos_s)
    acc_s[...] = jnp.zeros_like(acc_s)
    m_s[...] = jnp.full_like(m_s, NEG)
    l_s[...] = jnp.zeros_like(l_s)

    def step(t, carry):
        which, chunk = chunk_of(sc, t)
        scores = dot_tn(keys_of(kv_s, chunk, 0), q_s[which])
        scores = jnp.where(seen(pos_s, which, chunk), scores, NEG)
        old = m_s[which]
        new = jnp.maximum(old, jnp.max(scores, axis=0, keepdims=True))
        prob = jnp.exp(scores - new)
        shrink = jnp.exp(old - new)
        m_s[which] = new
        l_s[which] = l_s[which] * shrink + jnp.sum(prob, axis=0, keepdims=True)
        acc_s[which] = acc_s[which] * shrink + jnp.dot(
            keys_of(kv_s, chunk, 1), prob.astype(BF16), preferred_element_type=F32
        )
        return carry

    lax.fori_loop(0, CHUNKS + 1, step, 0, unroll=UNROLL_F)
    for which in range(2):
        acc_s[which] = acc_s[which] / l_s[which]
        lse_ref[0, which] = m_s[which] + jnp.log(l_s[which])
    for half in range(2):
        mine = acc_s[jnp.bitwise_xor(half, sc[1])]
        for j in range(GROUP):
            o_ref[j, :, half * BLK : (half + 1) * BLK] = mine[:, j * BLK : (j + 1) * BLK]


def backward_kernel(
    sc, q_ref, own_ref, other_ref, o_ref, do_ref, lse_ref,
    dq_ref, down_ref, dother_ref,
    kv_s, q_s, do_s, dq_s, dkv_s, delta_s, pos_s,
):
    fill_keys(sc, own_ref, other_ref, kv_s)
    fill_queries(sc, q_ref, q_s)
    fill_queries(sc, do_ref, do_s)
    fill_queries(sc, o_ref, dq_s)
    fill_rows(sc, pos_s)
    for which in range(2):
        delta_s[which] = jnp.sum(dq_s[which] * do_s[which].astype(F32), axis=0, keepdims=True)
    dq_s[...] = jnp.zeros_like(dq_s)
    dkv_s[...] = jnp.zeros_like(dkv_s)

    def step(t, carry):
        which, chunk = chunk_of(sc, t)
        key_t, val_t, q_t, do_t = keys_of(kv_s, chunk, 0), keys_of(kv_s, chunk, 1), q_s[which], do_s[which]
        scores = dot_tn(key_t, q_t)
        prob = jnp.where(seen(pos_s, which, chunk), jnp.exp(scores - lse_ref[0, which]), 0.0)
        d_prob = dot_tn(val_t, do_t)
        d_score = (prob * (d_prob - delta_s[which])).astype(BF16)
        d_val = dot_nt(do_t, prob.astype(BF16))
        d_key = dot_nt(q_t, d_score)
        dq_s[which] = dq_s[which] + jnp.dot(key_t, d_score, preferred_element_type=F32)
        for j in range(CHUNK):
            lanes = slice(j * BLK, (j + 1) * BLK)
            dkv_s[chunk * CHUNK + j, 0] = dkv_s[chunk * CHUNK + j, 0] + d_key[:, lanes]
            dkv_s[chunk * CHUNK + j, 1] = dkv_s[chunk * CHUNK + j, 1] + d_val[:, lanes]
        return carry

    lax.fori_loop(0, CHUNKS + 1, step, 0, unroll=UNROLL_B)
    core = sc[2]
    scale = HEAD_DIM**-0.5
    for half in range(2):
        lanes = slice(half * BLK, (half + 1) * BLK)
        mine = dq_s[jnp.bitwise_xor(half, sc[1])] * scale
        for j in range(GROUP):
            dq_ref[j, :, lanes] = mine[:, j * BLK : (j + 1) * BLK]
        for chip in range(CTX // 2):
            block = sc[7 + 2 * (2 * chip + core) + half]
            down_ref[chip, :, 0, :, lanes] = dkv_s[block].astype(BF16)
            block = sc[7 + 2 * (2 * chip + 1 - core) + half]
            dother_ref[chip, :, 0, :, lanes] = dkv_s[block].astype(BF16)


ROWS = 2 * BLK
HEAD_SPEC = pl.BlockSpec((GROUP, HEAD_DIM, ROWS), lambda g, sc: (g, 0, 0))
KV_SPEC = pl.BlockSpec((CTX // 2, 2, 1, HEAD_DIM, ROWS), lambda g, sc: (0, 0, g, 0, 0))
LSE_SPEC = pl.BlockSpec((1, 2, 1, LANES), lambda g, sc: (g, 0, 0, 0))
HEAD_SHAPE = jax.ShapeDtypeStruct((HEADS, HEAD_DIM, ROWS), F32)
KV_SHAPE = jax.ShapeDtypeStruct((CTX // 2, 2, KV_HEADS, HEAD_DIM, ROWS), BF16)
LSE_SHAPE = jax.ShapeDtypeStruct((KV_HEADS, 2, 1, LANES), F32)
KERNEL_PARAMS = pltpu.CompilerParams(
    dimension_semantics=("arbitrary",), vmem_limit_bytes=40 * 2**20
)


def attention(scalars, q_t, own, other):
    return pl.pallas_call(
        forward_kernel,
        grid_spec=pltpu.PrefetchScalarGridSpec(
            num_scalar_prefetch=1,
            grid=(KV_HEADS,),
            in_specs=[HEAD_SPEC, KV_SPEC, KV_SPEC],
            out_specs=[HEAD_SPEC, LSE_SPEC],
            scratch_shapes=[
                pltpu.VMEM((NBLK, 2, HEAD_DIM, BLK), BF16),
                pltpu.VMEM((2, HEAD_DIM, LANES), BF16),
                pltpu.VMEM((2, HEAD_DIM, LANES), F32),
                pltpu.VMEM((2, 1, LANES), F32),
                pltpu.VMEM((2, 1, LANES), F32),
                pltpu.VMEM((2, 8, LANES), jnp.int32),
            ],
        ),
        out_shape=[HEAD_SHAPE, LSE_SHAPE],
        compiler_params=KERNEL_PARAMS,
        cost_estimate=pl.CostEstimate(
            flops=4 * 36 * BLK * HEADS * BLK * 256, transcendentals=36 * BLK * HEADS * BLK, bytes_accessed=50 * 10**6
        ),
        name="attention",
    )(scalars, q_t, own, other)


def attention_back(scalars, q_t, own, other, o_t, do_t, lse):
    return pl.pallas_call(
        backward_kernel,
        grid_spec=pltpu.PrefetchScalarGridSpec(
            num_scalar_prefetch=1,
            grid=(KV_HEADS,),
            in_specs=[HEAD_SPEC, KV_SPEC, KV_SPEC, HEAD_SPEC, HEAD_SPEC, LSE_SPEC],
            out_specs=[HEAD_SPEC, KV_SPEC, KV_SPEC],
            scratch_shapes=[
                pltpu.VMEM((NBLK, 2, HEAD_DIM, BLK), BF16),
                pltpu.VMEM((2, HEAD_DIM, LANES), BF16),
                pltpu.VMEM((2, HEAD_DIM, LANES), BF16),
                pltpu.VMEM((2, HEAD_DIM, LANES), F32),
                pltpu.VMEM((NBLK, 2, HEAD_DIM, BLK), F32),
                pltpu.VMEM((2, 1, LANES), F32),
                pltpu.VMEM((2, 8, LANES), jnp.int32),
            ],
        ),
        out_shape=[HEAD_SHAPE, KV_SHAPE, KV_SHAPE],
        compiler_params=KERNEL_PARAMS,
        cost_estimate=pl.CostEstimate(
            flops=10 * 36 * BLK * HEADS * BLK * 256, transcendentals=36 * BLK * HEADS * BLK, bytes_accessed=75 * 10**6
        ),
        name="attention_back",
    )(scalars, q_t, own, other, o_t, do_t, lse)


VMEM_SPEC = pl.BlockSpec(memory_space=pltpu.VMEM)


UNITS = FF // FSDP // 2


def unpack_kernel(sc, *refs):
    mlp0, mlp0_p, mlp1, mlp1_p, qkv, qkv_p, qkv_ref, out_ref, gu_ref = refs

    def write(order):
        for layer, pair in enumerate(((mlp0, mlp0_p), (mlp1, mlp1_p))):
            for half, mlp in enumerate(pair[::order]):
                for k in range(2):
                    for i in range(FSDP):
                        src = k * HALF + i * UNITS
                        dst = k * FF + i * 2 * UNITS + half * UNITS
                        gu_ref[layer, :, dst : dst + UNITS] = mlp[:, src : src + UNITS].astype(F32)
                cut = D // 2
                out_ref[layer, :, half * cut : (half + 1) * cut] = (
                    mlp[:, FF + HALF : FF + HALF + cut].astype(F32)
                )
        for layer, src in enumerate((qkv, qkv_p)[::order]):
            qkv_ref[layer] = src[:, : Q_ROWS + KV_ROWS].astype(F32)

    @pl.when(sc[0] == 0)
    def _():
        write(1)

    @pl.when(sc[0] != 0)
    def _():
        write(-1)


def unpack(core, *shares):
    return pl.pallas_call(
        unpack_kernel,
        grid_spec=pltpu.PrefetchScalarGridSpec(
            num_scalar_prefetch=1,
            grid=(),
            in_specs=[VMEM_SPEC] * 6,
            out_specs=[VMEM_SPEC] * 3,
        ),
        out_shape=[
            jax.ShapeDtypeStruct((LAYERS, SHARD, Q_ROWS + KV_ROWS), F32),
            jax.ShapeDtypeStruct((LAYERS, SHARD, D), F32),
            jax.ShapeDtypeStruct((LAYERS, SHARD, 2 * FF), F32),
        ],
        compiler_params=pltpu.CompilerParams(vmem_limit_bytes=40 * 2**20),
        name="unpack",
    )(core, *shares)


def rotate(x, cosine, sine):
    half = HEAD_DIM // 2
    first, second = x[:, :half], x[:, half:]
    return jnp.concatenate([first * cosine - second * sine, second * cosine + first * sine], 1)


def normed(hidden):
    inv_rms = lax.rsqrt(jnp.mean(hidden * hidden, -1, keepdims=True) + EPS)
    return hidden * inv_rms, inv_rms


def norm_back(d_unit, unit, inv_rms):
    return inv_rms * (d_unit - unit * jnp.mean(d_unit * unit, -1, keepdims=True))


def mm(a, b):
    return jnp.dot(a, b, preferred_element_type=F32)


def ein(spec, a, b):
    return jnp.einsum(spec, a, b, preferred_element_type=F32)


def local(tokens, block_order, doc_ids, norm_gains, w_qkv, w_out, w_gate_up, w_down, cotangent):
    place = lax.axis_index("ctx")
    core = jnp.bitwise_and(place, 1)
    first_core = core == 0

    def my_half(left, right):
        return jnp.where(first_core, left, right)

    def in_order(own, other):
        return my_half(own, other), my_half(other, own)

    gain_cols = jnp.transpose(norm_gains.reshape(2 * LAYERS, SHARD))
    cut = (Q_ROWS + KV_ROWS + D) // 2

    def mlp_pack(layer):
        wgu = w_gate_up[layer].reshape(SHARD, 2, FSDP, 2, UNITS)
        wgu = my_half(wgu[..., 0, :], wgu[..., 1, :]).reshape(SHARD, FF)
        wdown = my_half(w_down[layer, :UNITS], w_down[layer, UNITS:]).reshape(SHARD, HALF)
        return jnp.concatenate([wgu, wdown], 1)

    def proj_pack(layer):
        proj = jnp.concatenate([w_qkv[layer], w_out[layer]], 1)
        return my_half(proj[:, :cut], proj[:, cut:])

    first = jnp.concatenate([proj_pack(0), gain_cols], 1)
    first = jnp.broadcast_to(first[None], (FSDP,) + first.shape)
    first, w_gate_up, w_down = lax.optimization_barrier((first, w_gate_up, w_down))
    first = over_fsdp(first).reshape(D, -1)
    pack0 = lax.all_gather(mlp_pack(0), "fsdp", axis=0, tiled=True)
    pack1 = lax.all_gather(mlp_pack(1), "fsdp", axis=0, tiled=True)
    gains = jnp.transpose(first[:, cut:].astype(F32)).reshape(LAYERS, 2, D)

    def whole_proj(own):
        return jnp.concatenate(in_order(own, to_partner(own)), 1)

    def mlp_weights(pack):
        return pack[:, :FF], pack[:, FF:].reshape(HALF, D)

    projs, mlps = [whole_proj(first[:, :cut])], []

    first_block = lax.dynamic_index_in_dim(block_order, 2 * place, 0, keepdims=False)
    low = jnp.minimum(first_block, NBLK - 1 - first_block)
    low_half = (first_block != low).astype(jnp.int32)
    starts = jnp.sum(
        (doc_ids[0][None, :] < jnp.arange(1, 5, dtype=jnp.int32)[:, None]).astype(jnp.int32), 1
    )
    scalars = jnp.concatenate([jnp.stack([low, low_half, core]), starts, block_order])
    lane = jnp.arange(ROWS, dtype=jnp.int32)
    pos = jnp.where(lane < BLK, first_block, NBLK - 2 - first_block) * BLK + lane
    inv_freq = THETA ** (-jnp.arange(HEAD_DIM // 2, dtype=F32) / (HEAD_DIM // 2))
    angles = pos.astype(F32)[None, :] * inv_freq[:, None]
    cosine, sine = jnp.cos(angles), jnp.sin(angles)

    hidden = tokens[0].astype(F32)
    saved = []
    for layer in range(LAYERS):
        wqkv, wout = projs[layer][:, : Q_ROWS + KV_ROWS], projs[layer][:, Q_ROWS + KV_ROWS :]
        unit_a, rms_a = normed(hidden)
        attn_in = (unit_a * gains[layer, 0]).astype(BF16)
        qkv_t = ein("de,td->et", wqkv, attn_in).reshape(-1, HEAD_DIM, ROWS)
        turned = rotate(qkv_t[: HEADS + KV_HEADS], cosine, sine)
        q_t = (turned[:HEADS] * HEAD_DIM**-0.5).astype(BF16)
        kv_t = jnp.concatenate([turned[HEADS:], qkv_t[HEADS + KV_HEADS :]], 0).astype(BF16)
        kv_t = kv_t.reshape(1, 2, KV_HEADS, HEAD_DIM, ROWS)
        kv_own = over_chips(jnp.broadcast_to(kv_t, (CTX // 2,) + kv_t.shape[1:]))
        if layer == 0:
            kv_own, late = lax.optimization_barrier((kv_own, proj_pack(1)))
            late = gather_fsdp(late)
        kv_other = to_partner(kv_own)
        o_t, lse = attention(scalars, q_t, kv_own, kv_other)
        if layer == 0:
            o_t, pack0, late = lax.optimization_barrier((o_t, pack0, late))
            mlps.append(mlp_weights(pack0))
            projs.append(whole_proj(late))
        else:
            o_t, pack1 = lax.optimization_barrier((o_t, pack1))
            mlps.append(mlp_weights(pack1))
        attn_out = o_t.astype(BF16).reshape(Q_ROWS, ROWS)
        mid = hidden + ein("at,ad->td", attn_out, wout)
        unit_m, rms_m = normed(mid)
        mlp_in = (unit_m * gains[layer, 1]).astype(BF16)
        wgu, wdown = mlps[layer]
        both_in = jnp.concatenate([mlp_in, to_partner(mlp_in)], 0)
        gate_up = mm(both_in, wgu)
        inner = (jax.nn.silu(gate_up[:, :HALF]) * gate_up[:, HALF:]).astype(BF16)
        part = mm(inner, wdown)
        hidden = mid + part[:ROWS] + to_partner(part[ROWS:].astype(BF16)).astype(F32)
        saved.append(
            (wqkv, wout, unit_a, rms_a, attn_in, q_t, kv_own, kv_other, o_t, lse, attn_out,
             unit_m, rms_m, both_in, gate_up, inner, wgu, wdown)
        )
    output = hidden.astype(BF16).reshape(1, ROWS, D)

    d_hidden = cotangent[0].astype(F32)
    gain_grads, qkv_grads = [None] * LAYERS, [None] * LAYERS
    for layer in reversed(range(LAYERS)):
        (wqkv, wout, unit_a, rms_a, attn_in, q_t, kv_own, kv_other, o_t, lse, attn_out,
         unit_m, rms_m, both_in, gate_up, inner, wgu, wdown) = saved[layer]
        grad_b = d_hidden.astype(BF16)
        both_grad = jnp.concatenate([grad_b, to_partner(grad_b)], 0)
        d_inner = ein("td,fd->tf", both_grad, wdown)
        gate, up = gate_up[:, :HALF], gate_up[:, HALF:]
        sig = jax.nn.sigmoid(gate)
        d_gate = d_inner * up * sig * (1.0 + gate * (1.0 - sig))
        d_up = d_inner * (gate * sig)
        d_gu = jnp.concatenate([d_gate, d_up], 1).astype(BF16)
        part = ein("tf,df->td", d_gu, wgu)
        d_norm = part[:ROWS] + to_partner(part[ROWS:].astype(BF16)).astype(F32)
        d_wdown = ein("tf,td->fd", inner, both_grad).astype(BF16)
        d_wgu = ein("td,tf->df", both_in, d_gu).astype(BF16)
        d_gain_m = jnp.sum(d_norm * unit_m, 0)
        d_hidden = d_hidden + norm_back(d_norm * gains[layer, 1], unit_m, rms_m)
        grad_b = d_hidden.astype(BF16)
        d_wout = mm(attn_out, grad_b)
        do_t = ein("ad,td->at", wout, grad_b).astype(BF16).reshape(HEADS, HEAD_DIM, ROWS)
        wout_half = D // 2
        d_wout = d_wout.astype(BF16)
        wout_mine = my_half(d_wout[:, :wout_half], d_wout[:, wout_half:])
        wout_theirs = my_half(d_wout[:, wout_half:], d_wout[:, :wout_half])
        d_mlp = [d_wgu, d_wdown.reshape(D, HALF), sum_pair(wout_mine, to_partner(wout_theirs))]
        do_t, d_mlp = lax.optimization_barrier((do_t, jnp.concatenate(d_mlp, 1)))
        share = lax.psum_scatter(d_mlp, "fsdp", scatter_dimension=0, tiled=True)
        if layer == 1:
            share1 = share
        else:
            share0 = share
        dq_t, dkv_own, dkv_other = attention_back(scalars, q_t, kv_own, kv_other, o_t, do_t, lse)
        dkv = (dkv_own.astype(F32) + to_partner(dkv_other).astype(F32)).astype(BF16)
        if layer == 0:
            share1 = sum_chips(lax.optimization_barrier((share1, dkv))[0])
        dkv = jnp.sum(over_chips(dkv).astype(F32), 0)
        turned = jnp.concatenate([dq_t, dkv[0]], 0)
        d_qkv = jnp.concatenate([rotate(turned, cosine, -sine), dkv[1]], 0)
        d_qkv = d_qkv.astype(BF16).reshape(Q_ROWS + KV_ROWS, ROWS)
        d_wqkv = ein("td,et->de", attn_in, d_qkv)
        d_norm = ein("et,de->td", d_qkv, wqkv)
        d_gain_a = jnp.sum(d_norm * unit_a, 0)
        d_hidden = d_hidden + norm_back(d_norm * gains[layer, 0], unit_a, rms_a)
        gain_grads[layer] = jnp.stack([d_gain_a, d_gain_m])
        qkv_grads[layer] = d_wqkv.astype(BF16)
    input_grad = d_hidden.reshape(1, ROWS, D)

    mine, theirs = in_order(*qkv_grads)
    d_gains = jnp.transpose(jnp.stack(gain_grads).reshape(2 * LAYERS, D)).astype(BF16)
    d_wqkv = jnp.concatenate([sum_pair(mine, to_partner(theirs)), d_gains], 1)
    qkv = sum_chips(scatter_fsdp(d_wqkv))
    qkv_p = to_partner(qkv)

    share0 = sum_chips(share0)
    mlp0, mlp0_p, mlp1, mlp1_p = share0, to_partner(share0), share1, to_partner(share1)
    half = Q_ROWS + KV_ROWS
    d_gain = qkv[:, half:].astype(F32) + qkv_p[:, half:].astype(F32)
    gain_grad = jnp.transpose(d_gain).reshape(LAYERS, 2, SHARD)
    qkv_grad, out_proj_grad, gate_up_grad = unpack(
        core.reshape(1), mlp0, mlp0_p, mlp1, mlp1_p, qkv, qkv_p
    )
    down_grad = []
    for own, theirs in ((mlp0, mlp0_p), (mlp1, mlp1_p)):
        rows = [x[:, FF : FF + HALF].reshape(UNITS, D) for x in in_order(own, theirs)]
        down_grad.append(jnp.concatenate(rows, 0))
    down_grad = jnp.stack(down_grad).astype(F32)
    return (output, input_grad, gain_grad, qkv_grad, out_proj_grad, gate_up_grad, down_grad)


def solution(mesh):
    in_specs = (
        P("fsdp", "ctx", None),
        P(),
        P("fsdp", None),
        P(None, None, "fsdp"),
        P(None, "fsdp", None),
        P(None, "fsdp", None),
        P(None, "fsdp", None),
        P(None, "fsdp", None),
        P("fsdp", "ctx", None),
    )
    out_specs = (
        P("fsdp", "ctx", None),
        P("fsdp", "ctx", None),
        P(None, None, "fsdp"),
        P(None, "fsdp", None),
        P(None, "fsdp", None),
        P(None, "fsdp", None),
        P(None, "fsdp", None),
    )
    return jax.shard_map(local, mesh=mesh, in_specs=in_specs, out_specs=out_specs, check_vma=False)
```

```python
import functools

import jax
import jax.numpy as jnp
from jax import lax
from jax.experimental import pallas as pl
from jax.experimental.pallas import tpu as pltpu
from jax.sharding import PartitionSpec as P

D = 576
HEADS = 9
KV_HEADS = 3
GROUP = 3
HEAD_DIM = 64
FF = 1536
LAYERS = 2
BLK = 128
NBLK = 32
EPS = 1e-05
THETA = 100000.0
NEG = -1e30
F32 = jnp.float32
BF16 = jnp.bfloat16
LANES = GROUP * BLK
CTX = 16
FSDP = 8
SHARD = D // FSDP
HALF = FF // 2
Q_ROWS = HEADS * HEAD_DIM
KV_ROWS = 2 * KV_HEADS * HEAD_DIM

PARTNER = [(i, i ^ 1) for i in range(CTX)]
SAME_CORE = [[2 * chip + core for chip in range(CTX // 2)] for core in range(2)]


def to_partner(x):
    return lax.ppermute(x, "ctx", PARTNER)


def over_chips(x):
    return lax.all_to_all(x, "ctx", 0, 0, axis_index_groups=SAME_CORE, tiled=True)


def over_fsdp(x):
    return lax.all_to_all(x, "fsdp", 0, 0, tiled=True)


def gather_fsdp(x):
    return over_fsdp(jnp.broadcast_to(x[None], (FSDP,) + x.shape)).reshape(-1, x.shape[1])


def scatter_fsdp(x):
    parts = over_fsdp(x.reshape(FSDP, -1, x.shape[1]))
    return jnp.sum(parts.astype(F32), 0).astype(BF16)


def sum_pair(a, b):
    return (a.astype(F32) + b.astype(F32)).astype(BF16)


def sum_chips(x):
    for bit in (2, 4, 8):
        x = sum_pair(x, lax.ppermute(x, "ctx", [(i, i ^ bit) for i in range(CTX)]))
    return x


def dot_tn(a, b):
    return lax.dot_general(a, b, (((0,), (0,)), ((), ())), preferred_element_type=F32)


def dot_nt(a, b):
    return lax.dot_general(a, b, (((1,), (1,)), ((), ())), preferred_element_type=F32)


UNROLL_F = 9
UNROLL_B = 3
CHUNK = 4
KEYS = CHUNK * BLK
CHUNKS = NBLK // CHUNK


def fill_keys(sc, own_ref, other_ref, kv_s):
    core = sc[2]
    for chip in range(CTX // 2):
        for half in range(2):
            lanes = slice(half * BLK, (half + 1) * BLK)
            block = sc[7 + 2 * (2 * chip + core) + half]
            kv_s[block] = own_ref[chip, :, 0, :, lanes]
            block = sc[7 + 2 * (2 * chip + 1 - core) + half]
            kv_s[block] = other_ref[chip, :, 0, :, lanes]


def fill_queries(sc, src_ref, dst):
    for half in range(2):
        lanes = slice(half * BLK, (half + 1) * BLK)
        which = jnp.bitwise_xor(half, sc[1])
        dst[which] = jnp.concatenate([src_ref[j, :, lanes] for j in range(GROUP)], axis=1)


def query_rows(sc, which):
    block = jnp.where(which == 0, sc[0], NBLK - 1 - sc[0])
    lane = lax.broadcasted_iota(jnp.int32, (1, LANES), 1)
    pos = block * BLK + jnp.bitwise_and(lane, BLK - 1)
    start = jnp.zeros((1, LANES), jnp.int32)
    for d in range(4):
        start = jnp.where(pos >= sc[3 + d], jnp.maximum(start, sc[3 + d]), start)
    return pos, start


def chunk_of(sc, t):
    high = (NBLK - sc[0] + CHUNK - 1) // CHUNK
    which = (t < high).astype(jnp.int32)
    return which, jnp.where(t < high, t, t - high)


def keys_of(kv_s, chunk, kind):
    return jnp.concatenate([kv_s[chunk * CHUNK + j, kind] for j in range(CHUNK)], axis=1)


def seen(pos_s, which, chunk):
    at = lax.broadcasted_iota(jnp.int32, (KEYS, LANES), 0)
    base = chunk * KEYS
    return (at >= pos_s[which, 1:2] - base) & (at <= pos_s[which, 0:1] - base)


def fill_rows(sc, pos_s):
    for which in range(2):
        pos, start = query_rows(sc, which)
        pos_s[which, 0:1] = pos
        pos_s[which, 1:2] = start


def forward_kernel(sc, q_ref, own_ref, other_ref, o_ref, lse_ref, kv_s, q_s, acc_s, m_s, l_s, pos_s):
    fill_keys(sc, own_ref, other_ref, kv_s)
    fill_queries(sc, q_ref, q_s)
    fill_rows(sc, pos_s)
    acc_s[...] = jnp.zeros_like(acc_s)
    m_s[...] = jnp.full_like(m_s, NEG)
    l_s[...] = jnp.zeros_like(l_s)

    def step(t, carry):
        which, chunk = chunk_of(sc, t)
        scores = dot_tn(keys_of(kv_s, chunk, 0), q_s[which])
        scores = jnp.where(seen(pos_s, which, chunk), scores, NEG)
        old = m_s[which]
        new = jnp.maximum(old, jnp.max(scores, axis=0, keepdims=True))
        prob = jnp.exp(scores - new)
        shrink = jnp.exp(old - new)
        m_s[which] = new
        l_s[which] = l_s[which] * shrink + jnp.sum(prob, axis=0, keepdims=True)
        acc_s[which] = acc_s[which] * shrink + jnp.dot(
            keys_of(kv_s, chunk, 1), prob.astype(BF16), preferred_element_type=F32
        )
        return carry

    lax.fori_loop(0, CHUNKS + 1, step, 0, unroll=UNROLL_F)
    for which in range(2):
        acc_s[which] = acc_s[which] / l_s[which]
        lse_ref[0, which] = m_s[which] + jnp.log(l_s[which])
    for half in range(2):
        mine = acc_s[jnp.bitwise_xor(half, sc[1])]
        for j in range(GROUP):
            o_ref[j, :, half * BLK : (half + 1) * BLK] = mine[:, j * BLK : (j + 1) * BLK]


def backward_kernel(
    sc, q_ref, own_ref, other_ref, o_ref, do_ref, lse_ref,
    dq_ref, down_ref, dother_ref,
    kv_s, q_s, do_s, dq_s, dkv_s, delta_s, pos_s,
):
    fill_keys(sc, own_ref, other_ref, kv_s)
    fill_queries(sc, q_ref, q_s)
    fill_queries(sc, do_ref, do_s)
    fill_queries(sc, o_ref, dq_s)
    fill_rows(sc, pos_s)
    for which in range(2):
        delta_s[which] = jnp.sum(dq_s[which] * do_s[which].astype(F32), axis=0, keepdims=True)
    dq_s[...] = jnp.zeros_like(dq_s)
    dkv_s[...] = jnp.zeros_like(dkv_s)

    def step(t, carry):
        which, chunk = chunk_of(sc, t)
        key_t, val_t, q_t, do_t = keys_of(kv_s, chunk, 0), keys_of(kv_s, chunk, 1), q_s[which], do_s[which]
        scores = dot_tn(key_t, q_t)
        prob = jnp.where(seen(pos_s, which, chunk), jnp.exp(scores - lse_ref[0, which]), 0.0)
        d_prob = dot_tn(val_t, do_t)
        d_score = (prob * (d_prob - delta_s[which])).astype(BF16)
        d_val = dot_nt(do_t, prob.astype(BF16))
        d_key = dot_nt(q_t, d_score)
        dq_s[which] = dq_s[which] + jnp.dot(key_t, d_score, preferred_element_type=F32)
        for j in range(CHUNK):
            lanes = slice(j * BLK, (j + 1) * BLK)
            dkv_s[chunk * CHUNK + j, 0] = dkv_s[chunk * CHUNK + j, 0] + d_key[:, lanes]
            dkv_s[chunk * CHUNK + j, 1] = dkv_s[chunk * CHUNK + j, 1] + d_val[:, lanes]
        return carry

    lax.fori_loop(0, CHUNKS + 1, step, 0, unroll=UNROLL_B)
    core = sc[2]
    scale = HEAD_DIM**-0.5
    for half in range(2):
        lanes = slice(half * BLK, (half + 1) * BLK)
        mine = dq_s[jnp.bitwise_xor(half, sc[1])] * scale
        for j in range(GROUP):
            dq_ref[j, :, lanes] = mine[:, j * BLK : (j + 1) * BLK]
        for chip in range(CTX // 2):
            block = sc[7 + 2 * (2 * chip + core) + half]
            down_ref[chip, :, 0, :, lanes] = dkv_s[block].astype(BF16)
            block = sc[7 + 2 * (2 * chip + 1 - core) + half]
            dother_ref[chip, :, 0, :, lanes] = dkv_s[block].astype(BF16)


ROWS = 2 * BLK
HEAD_SPEC = pl.BlockSpec((GROUP, HEAD_DIM, ROWS), lambda g, sc: (g, 0, 0))
KV_SPEC = pl.BlockSpec((CTX // 2, 2, 1, HEAD_DIM, ROWS), lambda g, sc: (0, 0, g, 0, 0))
LSE_SPEC = pl.BlockSpec((1, 2, 1, LANES), lambda g, sc: (g, 0, 0, 0))
HEAD_SHAPE = jax.ShapeDtypeStruct((HEADS, HEAD_DIM, ROWS), F32)
KV_SHAPE = jax.ShapeDtypeStruct((CTX // 2, 2, KV_HEADS, HEAD_DIM, ROWS), BF16)
LSE_SHAPE = jax.ShapeDtypeStruct((KV_HEADS, 2, 1, LANES), F32)
KERNEL_PARAMS = pltpu.CompilerParams(
    dimension_semantics=("arbitrary",), vmem_limit_bytes=40 * 2**20
)


def attention(scalars, q_t, own, other):
    return pl.pallas_call(
        forward_kernel,
        grid_spec=pltpu.PrefetchScalarGridSpec(
            num_scalar_prefetch=1,
            grid=(KV_HEADS,),
            in_specs=[HEAD_SPEC, KV_SPEC, KV_SPEC],
            out_specs=[HEAD_SPEC, LSE_SPEC],
            scratch_shapes=[
                pltpu.VMEM((NBLK, 2, HEAD_DIM, BLK), BF16),
                pltpu.VMEM((2, HEAD_DIM, LANES), BF16),
                pltpu.VMEM((2, HEAD_DIM, LANES), F32),
                pltpu.VMEM((2, 1, LANES), F32),
                pltpu.VMEM((2, 1, LANES), F32),
                pltpu.VMEM((2, 8, LANES), jnp.int32),
            ],
        ),
        out_shape=[HEAD_SHAPE, LSE_SHAPE],
        compiler_params=KERNEL_PARAMS,
        name="attention",
    )(scalars, q_t, own, other)


def attention_back(scalars, q_t, own, other, o_t, do_t, lse):
    return pl.pallas_call(
        backward_kernel,
        grid_spec=pltpu.PrefetchScalarGridSpec(
            num_scalar_prefetch=1,
            grid=(KV_HEADS,),
            in_specs=[HEAD_SPEC, KV_SPEC, KV_SPEC, HEAD_SPEC, HEAD_SPEC, LSE_SPEC],
            out_specs=[HEAD_SPEC, KV_SPEC, KV_SPEC],
            scratch_shapes=[
                pltpu.VMEM((NBLK, 2, HEAD_DIM, BLK), BF16),
                pltpu.VMEM((2, HEAD_DIM, LANES), BF16),
                pltpu.VMEM((2, HEAD_DIM, LANES), BF16),
                pltpu.VMEM((2, HEAD_DIM, LANES), F32),
                pltpu.VMEM((NBLK, 2, HEAD_DIM, BLK), F32),
                pltpu.VMEM((2, 1, LANES), F32),
                pltpu.VMEM((2, 8, LANES), jnp.int32),
            ],
        ),
        out_shape=[HEAD_SHAPE, KV_SHAPE, KV_SHAPE],
        compiler_params=KERNEL_PARAMS,
        name="attention_back",
    )(scalars, q_t, own, other, o_t, do_t, lse)


VMEM_SPEC = pl.BlockSpec(memory_space=pltpu.VMEM)


UNITS = FF // FSDP // 2


def unpack_kernel(sc, *refs):
    mlp0, mlp0_p, mlp1, mlp1_p, qkv, qkv_p, qkv_ref, out_ref, gu_ref = refs

    def write(order):
        for layer, pair in enumerate(((mlp0, mlp0_p), (mlp1, mlp1_p))):
            for half, mlp in enumerate(pair[::order]):
                for k in range(2):
                    for i in range(FSDP):
                        src = k * HALF + i * UNITS
                        dst = k * FF + i * 2 * UNITS + half * UNITS
                        gu_ref[layer, :, dst : dst + UNITS] = mlp[:, src : src + UNITS].astype(F32)
                cut = D // 2
                out_ref[layer, :, half * cut : (half + 1) * cut] = (
                    mlp[:, FF + HALF : FF + HALF + cut].astype(F32)
                )
        for layer, src in enumerate((qkv, qkv_p)[::order]):
            qkv_ref[layer] = src[:, : Q_ROWS + KV_ROWS].astype(F32)

    @pl.when(sc[0] == 0)
    def _():
        write(1)

    @pl.when(sc[0] != 0)
    def _():
        write(-1)


def unpack(core, *shares):
    return pl.pallas_call(
        unpack_kernel,
        grid_spec=pltpu.PrefetchScalarGridSpec(
            num_scalar_prefetch=1,
            grid=(),
            in_specs=[VMEM_SPEC] * 6,
            out_specs=[VMEM_SPEC] * 3,
        ),
        out_shape=[
            jax.ShapeDtypeStruct((LAYERS, SHARD, Q_ROWS + KV_ROWS), F32),
            jax.ShapeDtypeStruct((LAYERS, SHARD, D), F32),
            jax.ShapeDtypeStruct((LAYERS, SHARD, 2 * FF), F32),
        ],
        compiler_params=pltpu.CompilerParams(vmem_limit_bytes=40 * 2**20),
        name="unpack",
    )(core, *shares)


def rotate(x, cosine, sine):
    half = HEAD_DIM // 2
    first, second = x[:, :half], x[:, half:]
    return jnp.concatenate([first * cosine - second * sine, second * cosine + first * sine], 1)


def normed(hidden):
    inv_rms = lax.rsqrt(jnp.mean(hidden * hidden, -1, keepdims=True) + EPS)
    return hidden * inv_rms, inv_rms


def norm_back(d_unit, unit, inv_rms):
    return inv_rms * (d_unit - unit * jnp.mean(d_unit * unit, -1, keepdims=True))


def mm(a, b):
    return jnp.dot(a, b, preferred_element_type=F32)


def ein(spec, a, b):
    return jnp.einsum(spec, a, b, preferred_element_type=F32)


def local(tokens, block_order, doc_ids, norm_gains, w_qkv, w_out, w_gate_up, w_down, cotangent):
    place = lax.axis_index("ctx")
    core = jnp.bitwise_and(place, 1)
    first_core = core == 0

    def my_half(left, right):
        return jnp.where(first_core, left, right)

    def in_order(own, other):
        return my_half(own, other), my_half(other, own)

    gain_cols = jnp.transpose(norm_gains.reshape(2 * LAYERS, SHARD))
    cut = (Q_ROWS + KV_ROWS + D) // 2

    def mlp_pack(layer):
        wgu = w_gate_up[layer].reshape(SHARD, 2, FSDP, 2, UNITS)
        wgu = my_half(wgu[..., 0, :], wgu[..., 1, :]).reshape(SHARD, FF)
        wdown = my_half(w_down[layer, :UNITS], w_down[layer, UNITS:]).reshape(SHARD, HALF)
        return jnp.concatenate([wgu, wdown], 1)

    def proj_pack(layer):
        proj = jnp.concatenate([w_qkv[layer], w_out[layer]], 1)
        return my_half(proj[:, :cut], proj[:, cut:])

    first = jnp.concatenate([proj_pack(0), gain_cols], 1)
    first = jnp.broadcast_to(first[None], (FSDP,) + first.shape)
    first, w_gate_up, w_down = lax.optimization_barrier((first, w_gate_up, w_down))
    first = over_fsdp(first).reshape(D, -1)
    pack0 = lax.all_gather(mlp_pack(0), "fsdp", axis=0, tiled=True)
    pack1 = lax.all_gather(mlp_pack(1), "fsdp", axis=0, tiled=True)
    gains = jnp.transpose(first[:, cut:].astype(F32)).reshape(LAYERS, 2, D)

    def whole_proj(own):
        return jnp.concatenate(in_order(own, to_partner(own)), 1)

    def mlp_weights(pack):
        return pack[:, :FF], pack[:, FF:].reshape(HALF, D)

    projs, mlps = [whole_proj(first[:, :cut])], []

    first_block = lax.dynamic_index_in_dim(block_order, 2 * place, 0, keepdims=False)
    low = jnp.minimum(first_block, NBLK - 1 - first_block)
    low_half = (first_block != low).astype(jnp.int32)
    starts = jnp.sum(
        (doc_ids[0][None, :] < jnp.arange(1, 5, dtype=jnp.int32)[:, None]).astype(jnp.int32), 1
    )
    scalars = jnp.concatenate([jnp.stack([low, low_half, core]), starts, block_order])
    lane = jnp.arange(ROWS, dtype=jnp.int32)
    pos = jnp.where(lane < BLK, first_block, NBLK - 2 - first_block) * BLK + lane
    inv_freq = THETA ** (-jnp.arange(HEAD_DIM // 2, dtype=F32) / (HEAD_DIM // 2))
    angles = pos.astype(F32)[None, :] * inv_freq[:, None]
    cosine, sine = jnp.cos(angles), jnp.sin(angles)

    hidden = tokens[0].astype(F32)
    saved = []
    for layer in range(LAYERS):
        wqkv, wout = projs[layer][:, : Q_ROWS + KV_ROWS], projs[layer][:, Q_ROWS + KV_ROWS :]
        unit_a, rms_a = normed(hidden)
        attn_in = (unit_a * gains[layer, 0]).astype(BF16)
        qkv_t = ein("de,td->et", wqkv, attn_in).reshape(-1, HEAD_DIM, ROWS)
        turned = rotate(qkv_t[: HEADS + KV_HEADS], cosine, sine)
        q_t = (turned[:HEADS] * HEAD_DIM**-0.5).astype(BF16)
        kv_t = jnp.concatenate([turned[HEADS:], qkv_t[HEADS + KV_HEADS :]], 0).astype(BF16)
        kv_t = kv_t.reshape(1, 2, KV_HEADS, HEAD_DIM, ROWS)
        kv_own = over_chips(jnp.broadcast_to(kv_t, (CTX // 2,) + kv_t.shape[1:]))
        if layer == 0:
            kv_own, late = lax.optimization_barrier((kv_own, proj_pack(1)))
            late = gather_fsdp(late)
        kv_other = to_partner(kv_own)
        o_t, lse = attention(scalars, q_t, kv_own, kv_other)
        if layer == 0:
            o_t, pack0, late = lax.optimization_barrier((o_t, pack0, late))
            mlps.append(mlp_weights(pack0))
            projs.append(whole_proj(late))
        else:
            o_t, pack1 = lax.optimization_barrier((o_t, pack1))
            mlps.append(mlp_weights(pack1))
        attn_out = o_t.astype(BF16).reshape(Q_ROWS, ROWS)
        mid = hidden + ein("at,ad->td", attn_out, wout)
        unit_m, rms_m = normed(mid)
        mlp_in = (unit_m * gains[layer, 1]).astype(BF16)
        wgu, wdown = mlps[layer]
        both_in = jnp.concatenate([mlp_in, to_partner(mlp_in)], 0)
        gate_up = mm(both_in, wgu)
        inner = (jax.nn.silu(gate_up[:, :HALF]) * gate_up[:, HALF:]).astype(BF16)
        part = mm(inner, wdown)
        hidden = mid + part[:ROWS] + to_partner(part[ROWS:].astype(BF16)).astype(F32)
        saved.append(
            (wqkv, wout, unit_a, rms_a, attn_in, q_t, kv_own, kv_other, o_t, lse, attn_out,
             unit_m, rms_m, both_in, gate_up, inner, wgu, wdown)
        )
    output = hidden.astype(BF16).reshape(1, ROWS, D)

    d_hidden = cotangent[0].astype(F32)
    gain_grads, qkv_grads = [None] * LAYERS, [None] * LAYERS
    for layer in reversed(range(LAYERS)):
        (wqkv, wout, unit_a, rms_a, attn_in, q_t, kv_own, kv_other, o_t, lse, attn_out,
         unit_m, rms_m, both_in, gate_up, inner, wgu, wdown) = saved[layer]
        grad_b = d_hidden.astype(BF16)
        both_grad = jnp.concatenate([grad_b, to_partner(grad_b)], 0)
        d_inner = ein("td,fd->tf", both_grad, wdown)
        gate, up = gate_up[:, :HALF], gate_up[:, HALF:]
        sig = jax.nn.sigmoid(gate)
        d_gate = d_inner * up * sig * (1.0 + gate * (1.0 - sig))
        d_up = d_inner * (gate * sig)
        d_gu = jnp.concatenate([d_gate, d_up], 1).astype(BF16)
        part = ein("tf,df->td", d_gu, wgu)
        d_norm = part[:ROWS] + to_partner(part[ROWS:].astype(BF16)).astype(F32)
        d_wdown = ein("tf,td->fd", inner, both_grad).astype(BF16)
        d_wgu = ein("td,tf->df", both_in, d_gu).astype(BF16)
        d_gain_m = jnp.sum(d_norm * unit_m, 0)
        d_hidden = d_hidden + norm_back(d_norm * gains[layer, 1], unit_m, rms_m)
        grad_b = d_hidden.astype(BF16)
        d_wout = mm(attn_out, grad_b)
        do_t = ein("ad,td->at", wout, grad_b).astype(BF16).reshape(HEADS, HEAD_DIM, ROWS)
        wout_half = D // 2
        d_wout = d_wout.astype(BF16)
        wout_mine = my_half(d_wout[:, :wout_half], d_wout[:, wout_half:])
        wout_theirs = my_half(d_wout[:, wout_half:], d_wout[:, :wout_half])
        d_mlp = [d_wgu, d_wdown.reshape(D, HALF), sum_pair(wout_mine, to_partner(wout_theirs))]
        do_t, d_mlp = lax.optimization_barrier((do_t, jnp.concatenate(d_mlp, 1)))
        share = lax.psum_scatter(d_mlp, "fsdp", scatter_dimension=0, tiled=True)
        if layer == 1:
            share1 = share
        else:
            share0 = share
        dq_t, dkv_own, dkv_other = attention_back(scalars, q_t, kv_own, kv_other, o_t, do_t, lse)
        dkv = (dkv_own.astype(F32) + to_partner(dkv_other).astype(F32)).astype(BF16)
        if layer == 0:
            share1 = sum_chips(lax.optimization_barrier((share1, dkv))[0])
        dkv = jnp.sum(over_chips(dkv).astype(F32), 0)
        turned = jnp.concatenate([dq_t, dkv[0]], 0)
        d_qkv = jnp.concatenate([rotate(turned, cosine, -sine), dkv[1]], 0)
        d_qkv = d_qkv.astype(BF16).reshape(Q_ROWS + KV_ROWS, ROWS)
        d_wqkv = ein("td,et->de", attn_in, d_qkv)
        d_norm = ein("et,de->td", d_qkv, wqkv)
        d_gain_a = jnp.sum(d_norm * unit_a, 0)
        d_hidden = d_hidden + norm_back(d_norm * gains[layer, 0], unit_a, rms_a)
        gain_grads[layer] = jnp.stack([d_gain_a, d_gain_m])
        qkv_grads[layer] = d_wqkv.astype(BF16)
    input_grad = d_hidden.reshape(1, ROWS, D)

    mine, theirs = in_order(*qkv_grads)
    d_gains = jnp.transpose(jnp.stack(gain_grads).reshape(2 * LAYERS, D)).astype(BF16)
    d_wqkv = jnp.concatenate([sum_pair(mine, to_partner(theirs)), d_gains], 1)
    qkv = sum_chips(scatter_fsdp(d_wqkv))
    qkv_p = to_partner(qkv)

    share0 = sum_chips(share0)
    mlp0, mlp0_p, mlp1, mlp1_p = share0, to_partner(share0), share1, to_partner(share1)
    half = Q_ROWS + KV_ROWS
    d_gain = qkv[:, half:].astype(F32) + qkv_p[:, half:].astype(F32)
    gain_grad = jnp.transpose(d_gain).reshape(LAYERS, 2, SHARD)
    qkv_grad, out_proj_grad, gate_up_grad = unpack(
        core.reshape(1), mlp0, mlp0_p, mlp1, mlp1_p, qkv, qkv_p
    )
    down_grad = []
    for own, theirs in ((mlp0, mlp0_p), (mlp1, mlp1_p)):
        rows = [x[:, FF : FF + HALF].reshape(UNITS, D) for x in in_order(own, theirs)]
        down_grad.append(jnp.concatenate(rows, 0))
    down_grad = jnp.stack(down_grad).astype(F32)
    return (output, input_grad, gain_grad, qkv_grad, out_proj_grad, gate_up_grad, down_grad)


def solution(mesh):
    in_specs = (
        P("fsdp", "ctx", None),
        P(),
        P("fsdp", None),
        P(None, None, "fsdp"),
        P(None, "fsdp", None),
        P(None, "fsdp", None),
        P(None, "fsdp", None),
        P(None, "fsdp", None),
        P("fsdp", "ctx", None),
    )
    out_specs = (
        P("fsdp", "ctx", None),
        P("fsdp", "ctx", None),
        P(None, None, "fsdp"),
        P(None, "fsdp", None),
        P(None, "fsdp", None),
        P(None, "fsdp", None),
        P(None, "fsdp", None),
    )
    return jax.shard_map(local, mesh=mesh, in_specs=in_specs, out_specs=out_specs, check_vma=False)
```

```python
import functools

import jax
import jax.numpy as jnp
from jax import lax
from jax.experimental import pallas as pl
from jax.experimental.pallas import tpu as pltpu
from jax.sharding import PartitionSpec as P

D = 576
HEADS = 9
KV_HEADS = 3
GROUP = 3
HEAD_DIM = 64
FF = 1536
LAYERS = 2
BLK = 128
NBLK = 32
EPS = 1e-05
THETA = 100000.0
NEG = -1e30
F32 = jnp.float32
BF16 = jnp.bfloat16
LANES = GROUP * BLK
CTX = 16
FSDP = 8
SHARD = D // FSDP
HALF = FF // 2
Q_ROWS = HEADS * HEAD_DIM
KV_ROWS = 2 * KV_HEADS * HEAD_DIM

PARTNER = [(i, i ^ 1) for i in range(CTX)]
SAME_CORE = [[2 * chip + core for chip in range(CTX // 2)] for core in range(2)]


def to_partner(x):
    return lax.ppermute(x, "ctx", PARTNER)


def over_chips(x):
    return lax.all_to_all(x, "ctx", 0, 0, axis_index_groups=SAME_CORE, tiled=True)


def over_fsdp(x):
    return lax.all_to_all(x, "fsdp", 0, 0, tiled=True)


def gather_fsdp(x):
    return over_fsdp(jnp.broadcast_to(x[None], (FSDP,) + x.shape)).reshape(-1, x.shape[1])


def scatter_fsdp(x):
    parts = over_fsdp(x.reshape(FSDP, -1, x.shape[1]))
    return jnp.sum(parts.astype(F32), 0).astype(BF16)


def sum_pair(a, b):
    return (a.astype(F32) + b.astype(F32)).astype(BF16)


def sum_chips(x):
    for bit in (2, 4, 8):
        x = sum_pair(x, lax.ppermute(x, "ctx", [(i, i ^ bit) for i in range(CTX)]))
    return x


def dot_tn(a, b):
    return lax.dot_general(a, b, (((0,), (0,)), ((), ())), preferred_element_type=F32)


def dot_nt(a, b):
    return lax.dot_general(a, b, (((1,), (1,)), ((), ())), preferred_element_type=F32)


UNROLL_F = 9
UNROLL_B = 3
CHUNK = 4
KEYS = CHUNK * BLK
CHUNKS = NBLK // CHUNK


def fill_keys(sc, own_ref, other_ref, kv_s):
    core = sc[2]
    for chip in range(CTX // 2):
        for half in range(2):
            lanes = slice(half * BLK, (half + 1) * BLK)
            block = sc[7 + 2 * (2 * chip + core) + half]
            kv_s[block] = own_ref[chip, :, 0, :, lanes]
            block = sc[7 + 2 * (2 * chip + 1 - core) + half]
            kv_s[block] = other_ref[chip, :, 0, :, lanes]


def fill_queries(sc, src_ref, dst):
    for half in range(2):
        lanes = slice(half * BLK, (half + 1) * BLK)
        which = jnp.bitwise_xor(half, sc[1])
        dst[which] = jnp.concatenate([src_ref[j, :, lanes] for j in range(GROUP)], axis=1)


def query_rows(sc, which):
    block = jnp.where(which == 0, sc[0], NBLK - 1 - sc[0])
    lane = lax.broadcasted_iota(jnp.int32, (1, LANES), 1)
    pos = block * BLK + jnp.bitwise_and(lane, BLK - 1)
    start = jnp.zeros((1, LANES), jnp.int32)
    for d in range(4):
        start = jnp.where(pos >= sc[3 + d], jnp.maximum(start, sc[3 + d]), start)
    return pos, start


def chunk_of(sc, t):
    high = (NBLK - sc[0] + CHUNK - 1) // CHUNK
    which = (t < high).astype(jnp.int32)
    return which, jnp.where(t < high, t, t - high)


def keys_of(kv_s, chunk, kind):
    return jnp.concatenate([kv_s[chunk * CHUNK + j, kind] for j in range(CHUNK)], axis=1)


def seen(pos_s, which, chunk):
    at = lax.broadcasted_iota(jnp.int32, (KEYS, LANES), 0)
    base = chunk * KEYS
    return (at >= pos_s[which, 1:2] - base) & (at <= pos_s[which, 0:1] - base)


def fill_rows(sc, pos_s):
    for which in range(2):
        pos, start = query_rows(sc, which)
        pos_s[which, 0:1] = pos
        pos_s[which, 1:2] = start


def forward_kernel(sc, q_ref, own_ref, other_ref, o_ref, lse_ref, kv_s, q_s, acc_s, m_s, l_s, pos_s):
    fill_keys(sc, own_ref, other_ref, kv_s)
    fill_queries(sc, q_ref, q_s)
    fill_rows(sc, pos_s)
    acc_s[...] = jnp.zeros_like(acc_s)
    m_s[...] = jnp.full_like(m_s, NEG)
    l_s[...] = jnp.zeros_like(l_s)

    def step(t, carry):
        which, chunk = chunk_of(sc, t)
        scores = dot_tn(keys_of(kv_s, chunk, 0), q_s[which])
        scores = jnp.where(seen(pos_s, which, chunk), scores, NEG)
        old = m_s[which]
        new = jnp.maximum(old, jnp.max(scores, axis=0, keepdims=True))
        prob = jnp.exp(scores - new)
        shrink = jnp.exp(old - new)
        m_s[which] = new
        l_s[which] = l_s[which] * shrink + jnp.sum(prob, axis=0, keepdims=True)
        acc_s[which] = acc_s[which] * shrink + jnp.dot(
            keys_of(kv_s, chunk, 1), prob.astype(BF16), preferred_element_type=F32
        )
        return carry

    lax.fori_loop(0, CHUNKS + 1, step, 0, unroll=UNROLL_F)
    for which in range(2):
        acc_s[which] = acc_s[which] / l_s[which]
        lse_ref[0, which] = m_s[which] + jnp.log(l_s[which])
    for half in range(2):
        mine = acc_s[jnp.bitwise_xor(half, sc[1])]
        for j in range(GROUP):
            o_ref[j, :, half * BLK : (half + 1) * BLK] = mine[:, j * BLK : (j + 1) * BLK]


def backward_kernel(
    sc, q_ref, own_ref, other_ref, o_ref, do_ref, lse_ref,
    dq_ref, down_ref, dother_ref,
    kv_s, q_s, do_s, dq_s, dkv_s, delta_s, pos_s,
):
    fill_keys(sc, own_ref, other_ref, kv_s)
    fill_queries(sc, q_ref, q_s)
    fill_queries(sc, do_ref, do_s)
    fill_queries(sc, o_ref, dq_s)
    fill_rows(sc, pos_s)
    for which in range(2):
        delta_s[which] = jnp.sum(dq_s[which] * do_s[which].astype(F32), axis=0, keepdims=True)
    dq_s[...] = jnp.zeros_like(dq_s)
    dkv_s[...] = jnp.zeros_like(dkv_s)

    def step(t, carry):
        which, chunk = chunk_of(sc, t)
        key_t, val_t, q_t, do_t = keys_of(kv_s, chunk, 0), keys_of(kv_s, chunk, 1), q_s[which], do_s[which]
        scores = dot_tn(key_t, q_t)
        prob = jnp.where(seen(pos_s, which, chunk), jnp.exp(scores - lse_ref[0, which]), 0.0)
        d_prob = dot_tn(val_t, do_t)
        d_score = (prob * (d_prob - delta_s[which])).astype(BF16)
        d_val = dot_nt(do_t, prob.astype(BF16))
        d_key = dot_nt(q_t, d_score)
        dq_s[which] = dq_s[which] + jnp.dot(key_t, d_score, preferred_element_type=F32)
        for j in range(CHUNK):
            lanes = slice(j * BLK, (j + 1) * BLK)
            dkv_s[chunk * CHUNK + j, 0] = dkv_s[chunk * CHUNK + j, 0] + d_key[:, lanes]
            dkv_s[chunk * CHUNK + j, 1] = dkv_s[chunk * CHUNK + j, 1] + d_val[:, lanes]
        return carry

    lax.fori_loop(0, CHUNKS + 1, step, 0, unroll=UNROLL_B)
    core = sc[2]
    scale = HEAD_DIM**-0.5
    for half in range(2):
        lanes = slice(half * BLK, (half + 1) * BLK)
        mine = dq_s[jnp.bitwise_xor(half, sc[1])] * scale
        for j in range(GROUP):
            dq_ref[j, :, lanes] = mine[:, j * BLK : (j + 1) * BLK]
        for chip in range(CTX // 2):
            block = sc[7 + 2 * (2 * chip + core) + half]
            down_ref[chip, :, 0, :, lanes] = dkv_s[block].astype(BF16)
            block = sc[7 + 2 * (2 * chip + 1 - core) + half]
            dother_ref[chip, :, 0, :, lanes] = dkv_s[block].astype(BF16)


ROWS = 2 * BLK
HEAD_SPEC = pl.BlockSpec((GROUP, HEAD_DIM, ROWS), lambda g, sc: (g, 0, 0))
KV_SPEC = pl.BlockSpec((CTX // 2, 2, 1, HEAD_DIM, ROWS), lambda g, sc: (0, 0, g, 0, 0))
LSE_SPEC = pl.BlockSpec((1, 2, 1, LANES), lambda g, sc: (g, 0, 0, 0))
HEAD_SHAPE = jax.ShapeDtypeStruct((HEADS, HEAD_DIM, ROWS), F32)
KV_SHAPE = jax.ShapeDtypeStruct((CTX // 2, 2, KV_HEADS, HEAD_DIM, ROWS), BF16)
LSE_SHAPE = jax.ShapeDtypeStruct((KV_HEADS, 2, 1, LANES), F32)
KERNEL_PARAMS = pltpu.CompilerParams(
    dimension_semantics=("arbitrary",), vmem_limit_bytes=40 * 2**20
)


def attention(scalars, q_t, own, other):
    return pl.pallas_call(
        forward_kernel,
        grid_spec=pltpu.PrefetchScalarGridSpec(
            num_scalar_prefetch=1,
            grid=(KV_HEADS,),
            in_specs=[HEAD_SPEC, KV_SPEC, KV_SPEC],
            out_specs=[HEAD_SPEC, LSE_SPEC],
            scratch_shapes=[
                pltpu.VMEM((NBLK, 2, HEAD_DIM, BLK), BF16),
                pltpu.VMEM((2, HEAD_DIM, LANES), BF16),
                pltpu.VMEM((2, HEAD_DIM, LANES), F32),
                pltpu.VMEM((2, 1, LANES), F32),
                pltpu.VMEM((2, 1, LANES), F32),
                pltpu.VMEM((2, 8, LANES), jnp.int32),
            ],
        ),
        out_shape=[HEAD_SHAPE, LSE_SHAPE],
        compiler_params=KERNEL_PARAMS,
        name="attention",
    )(scalars, q_t, own, other)


def attention_back(scalars, q_t, own, other, o_t, do_t, lse):
    return pl.pallas_call(
        backward_kernel,
        grid_spec=pltpu.PrefetchScalarGridSpec(
            num_scalar_prefetch=1,
            grid=(KV_HEADS,),
            in_specs=[HEAD_SPEC, KV_SPEC, KV_SPEC, HEAD_SPEC, HEAD_SPEC, LSE_SPEC],
            out_specs=[HEAD_SPEC, KV_SPEC, KV_SPEC],
            scratch_shapes=[
                pltpu.VMEM((NBLK, 2, HEAD_DIM, BLK), BF16),
                pltpu.VMEM((2, HEAD_DIM, LANES), BF16),
                pltpu.VMEM((2, HEAD_DIM, LANES), BF16),
                pltpu.VMEM((2, HEAD_DIM, LANES), F32),
                pltpu.VMEM((NBLK, 2, HEAD_DIM, BLK), F32),
                pltpu.VMEM((2, 1, LANES), F32),
                pltpu.VMEM((2, 8, LANES), jnp.int32),
            ],
        ),
        out_shape=[HEAD_SHAPE, KV_SHAPE, KV_SHAPE],
        compiler_params=KERNEL_PARAMS,
        name="attention_back",
    )(scalars, q_t, own, other, o_t, do_t, lse)


VMEM_SPEC = pl.BlockSpec(memory_space=pltpu.VMEM)


def dispatch_kernel(me, x_ref, *outs):
    for dx, out in enumerate(outs):
        for dz in range(2):
            out[dz] = x_ref[jnp.bitwise_xor(me[0], 4 * dz + dx)]


def dispatch(me, x):
    return pl.pallas_call(
        dispatch_kernel,
        grid_spec=pltpu.PrefetchScalarGridSpec(
            num_scalar_prefetch=1,
            grid=(),
            in_specs=[VMEM_SPEC],
            out_specs=[VMEM_SPEC] * 4,
        ),
        out_shape=[jax.ShapeDtypeStruct((2,) + x.shape[1:], BF16)] * 4,
        compiler_params=pltpu.CompilerParams(vmem_limit_bytes=40 * 2**20),
        name="dispatch",
    )(me, x)


def across(x, d):
    return lax.ppermute(x, "fsdp", [(i, i ^ d) for i in range(FSDP)])


def scatter_by_permutes(me, x):
    parts = dispatch(me, x.reshape(FSDP, -1, x.shape[1]))
    total = parts[0].astype(F32)
    for dx in range(1, 4):
        total = total + across(parts[dx], dx).astype(F32)
    return (total[0] + across(total[1].astype(BF16), 4).astype(F32)).astype(BF16)


UNITS = FF // FSDP // 2


def unpack_kernel(sc, *refs):
    mlp0, mlp0_p, mlp1, mlp1_p, qkv, qkv_p, qkv_ref, out_ref, gu_ref = refs

    def write(order):
        for layer, pair in enumerate(((mlp0, mlp0_p), (mlp1, mlp1_p))):
            for half, mlp in enumerate(pair[::order]):
                for k in range(2):
                    for i in range(FSDP):
                        src = k * HALF + i * UNITS
                        dst = k * FF + i * 2 * UNITS + half * UNITS
                        gu_ref[layer, :, dst : dst + UNITS] = mlp[:, src : src + UNITS].astype(F32)
                cut = D // 2
                out_ref[layer, :, half * cut : (half + 1) * cut] = (
                    mlp[:, FF + HALF : FF + HALF + cut].astype(F32)
                )
        for layer, src in enumerate((qkv, qkv_p)[::order]):
            qkv_ref[layer] = src[:, : Q_ROWS + KV_ROWS].astype(F32)

    @pl.when(sc[0] == 0)
    def _():
        write(1)

    @pl.when(sc[0] != 0)
    def _():
        write(-1)


def unpack(core, *shares):
    return pl.pallas_call(
        unpack_kernel,
        grid_spec=pltpu.PrefetchScalarGridSpec(
            num_scalar_prefetch=1,
            grid=(),
            in_specs=[VMEM_SPEC] * 6,
            out_specs=[VMEM_SPEC] * 3,
        ),
        out_shape=[
            jax.ShapeDtypeStruct((LAYERS, SHARD, Q_ROWS + KV_ROWS), F32),
            jax.ShapeDtypeStruct((LAYERS, SHARD, D), F32),
            jax.ShapeDtypeStruct((LAYERS, SHARD, 2 * FF), F32),
        ],
        compiler_params=pltpu.CompilerParams(vmem_limit_bytes=40 * 2**20),
        name="unpack",
    )(core, *shares)


def rotate(x, cosine, sine):
    half = HEAD_DIM // 2
    first, second = x[:, :half], x[:, half:]
    return jnp.concatenate([first * cosine - second * sine, second * cosine + first * sine], 1)


def normed(hidden):
    inv_rms = lax.rsqrt(jnp.mean(hidden * hidden, -1, keepdims=True) + EPS)
    return hidden * inv_rms, inv_rms


def norm_back(d_unit, unit, inv_rms):
    return inv_rms * (d_unit - unit * jnp.mean(d_unit * unit, -1, keepdims=True))


def mm(a, b):
    return jnp.dot(a, b, preferred_element_type=F32)


def ein(spec, a, b):
    return jnp.einsum(spec, a, b, preferred_element_type=F32)


def local(tokens, block_order, doc_ids, norm_gains, w_qkv, w_out, w_gate_up, w_down, cotangent):
    place = lax.axis_index("ctx")
    core = jnp.bitwise_and(place, 1)
    first_core = core == 0
    me = lax.axis_index("fsdp").reshape(1)

    def my_half(left, right):
        return jnp.where(first_core, left, right)

    def in_order(own, other):
        return my_half(own, other), my_half(other, own)

    gain_cols = jnp.transpose(norm_gains.reshape(2 * LAYERS, SHARD))
    cut = (Q_ROWS + KV_ROWS + D) // 2

    def mlp_pack(layer):
        wgu = w_gate_up[layer].reshape(SHARD, 2, FSDP, 2, UNITS)
        wgu = my_half(wgu[..., 0, :], wgu[..., 1, :]).reshape(SHARD, FF)
        wdown = my_half(w_down[layer, :UNITS], w_down[layer, UNITS:]).reshape(SHARD, HALF)
        return jnp.concatenate([wgu, wdown], 1)

    def proj_pack(layer):
        proj = jnp.concatenate([w_qkv[layer], w_out[layer]], 1)
        return my_half(proj[:, :cut], proj[:, cut:])

    first = jnp.concatenate([proj_pack(0), gain_cols], 1)
    first = jnp.broadcast_to(first[None], (FSDP,) + first.shape)
    first, w_gate_up, w_down = lax.optimization_barrier((first, w_gate_up, w_down))
    first = over_fsdp(first).reshape(D, -1)
    pack0 = lax.all_gather(mlp_pack(0), "fsdp", axis=0, tiled=True)
    pack1 = lax.all_gather(mlp_pack(1), "fsdp", axis=0, tiled=True)
    gains = jnp.transpose(first[:, cut:].astype(F32)).reshape(LAYERS, 2, D)

    def whole_proj(own):
        return jnp.concatenate(in_order(own, to_partner(own)), 1)

    def mlp_weights(pack):
        return pack[:, :FF], pack[:, FF:].reshape(HALF, D)

    projs, mlps = [whole_proj(first[:, :cut])], []

    first_block = lax.dynamic_index_in_dim(block_order, 2 * place, 0, keepdims=False)
    low = jnp.minimum(first_block, NBLK - 1 - first_block)
    low_half = (first_block != low).astype(jnp.int32)
    starts = jnp.sum(
        (doc_ids[0][None, :] < jnp.arange(1, 5, dtype=jnp.int32)[:, None]).astype(jnp.int32), 1
    )
    scalars = jnp.concatenate([jnp.stack([low, low_half, core]), starts, block_order])
    lane = jnp.arange(ROWS, dtype=jnp.int32)
    pos = jnp.where(lane < BLK, first_block, NBLK - 2 - first_block) * BLK + lane
    inv_freq = THETA ** (-jnp.arange(HEAD_DIM // 2, dtype=F32) / (HEAD_DIM // 2))
    angles = pos.astype(F32)[None, :] * inv_freq[:, None]
    cosine, sine = jnp.cos(angles), jnp.sin(angles)

    hidden = tokens[0].astype(F32)
    saved = []
    for layer in range(LAYERS):
        wqkv, wout = projs[layer][:, : Q_ROWS + KV_ROWS], projs[layer][:, Q_ROWS + KV_ROWS :]
        unit_a, rms_a = normed(hidden)
        attn_in = (unit_a * gains[layer, 0]).astype(BF16)
        qkv_t = ein("de,td->et", wqkv, attn_in).reshape(-1, HEAD_DIM, ROWS)
        turned = rotate(qkv_t[: HEADS + KV_HEADS], cosine, sine)
        q_t = (turned[:HEADS] * HEAD_DIM**-0.5).astype(BF16)
        kv_t = jnp.concatenate([turned[HEADS:], qkv_t[HEADS + KV_HEADS :]], 0).astype(BF16)
        kv_t = kv_t.reshape(1, 2, KV_HEADS, HEAD_DIM, ROWS)
        kv_own = over_chips(jnp.broadcast_to(kv_t, (CTX // 2,) + kv_t.shape[1:]))
        if layer == 0:
            kv_own, late = lax.optimization_barrier((kv_own, proj_pack(1)))
            late = gather_fsdp(late)
        kv_other = to_partner(kv_own)
        o_t, lse = attention(scalars, q_t, kv_own, kv_other)
        if layer == 0:
            o_t, pack0, late = lax.optimization_barrier((o_t, pack0, late))
            mlps.append(mlp_weights(pack0))
            projs.append(whole_proj(late))
        else:
            o_t, pack1 = lax.optimization_barrier((o_t, pack1))
            mlps.append(mlp_weights(pack1))
        attn_out = o_t.astype(BF16).reshape(Q_ROWS, ROWS)
        mid = hidden + ein("at,ad->td", attn_out, wout)
        unit_m, rms_m = normed(mid)
        mlp_in = (unit_m * gains[layer, 1]).astype(BF16)
        wgu, wdown = mlps[layer]
        both_in = jnp.concatenate([mlp_in, to_partner(mlp_in)], 0)
        gate_up = mm(both_in, wgu)
        inner = (jax.nn.silu(gate_up[:, :HALF]) * gate_up[:, HALF:]).astype(BF16)
        part = mm(inner, wdown)
        hidden = mid + part[:ROWS] + to_partner(part[ROWS:].astype(BF16)).astype(F32)
        saved.append(
            (wqkv, wout, unit_a, rms_a, attn_in, q_t, kv_own, kv_other, o_t, lse, attn_out,
             unit_m, rms_m, both_in, gate_up, inner, wgu, wdown)
        )
    output = hidden.astype(BF16).reshape(1, ROWS, D)

    d_hidden = cotangent[0].astype(F32)
    gain_grads, qkv_grads = [None] * LAYERS, [None] * LAYERS
    for layer in reversed(range(LAYERS)):
        (wqkv, wout, unit_a, rms_a, attn_in, q_t, kv_own, kv_other, o_t, lse, attn_out,
         unit_m, rms_m, both_in, gate_up, inner, wgu, wdown) = saved[layer]
        grad_b = d_hidden.astype(BF16)
        both_grad = jnp.concatenate([grad_b, to_partner(grad_b)], 0)
        d_inner = ein("td,fd->tf", both_grad, wdown)
        gate, up = gate_up[:, :HALF], gate_up[:, HALF:]
        sig = jax.nn.sigmoid(gate)
        d_gate = d_inner * up * sig * (1.0 + gate * (1.0 - sig))
        d_up = d_inner * (gate * sig)
        d_gu = jnp.concatenate([d_gate, d_up], 1).astype(BF16)
        part = ein("tf,df->td", d_gu, wgu)
        d_norm = part[:ROWS] + to_partner(part[ROWS:].astype(BF16)).astype(F32)
        d_gain_m = jnp.sum(d_norm * unit_m, 0)
        d_hidden = d_hidden + norm_back(d_norm * gains[layer, 1], unit_m, rms_m)
        grad_b = d_hidden.astype(BF16)
        do_t = ein("ad,td->at", wout, grad_b).astype(BF16).reshape(HEADS, HEAD_DIM, ROWS)
        dq_t, dkv_own, dkv_other = attention_back(scalars, q_t, kv_own, kv_other, o_t, do_t, lse)
        dkv = (dkv_own.astype(F32) + to_partner(dkv_other).astype(F32)).astype(BF16)
        d_gu, late_in, late_grad, _ = lax.optimization_barrier((d_gu, both_in, grad_b, dkv))
        d_wgu = ein("td,tf->df", late_in, d_gu).astype(BF16)
        d_wdown = ein("tf,td->fd", inner, both_grad).astype(BF16)
        d_wout = mm(attn_out, late_grad).astype(BF16)
        wout_half = D // 2
        wout_mine = my_half(d_wout[:, :wout_half], d_wout[:, wout_half:])
        wout_theirs = my_half(d_wout[:, wout_half:], d_wout[:, :wout_half])
        d_mlp = [d_wgu, d_wdown.reshape(D, HALF), sum_pair(wout_mine, to_partner(wout_theirs))]
        d_mlp = jnp.concatenate(d_mlp, 1)
        if layer == 1:
            share1 = lax.psum_scatter(d_mlp, "fsdp", scatter_dimension=0, tiled=True)
        else:
            share0 = scatter_by_permutes(me, d_mlp)
            share1 = sum_chips(lax.optimization_barrier((share1, dkv))[0])
        dkv = jnp.sum(over_chips(dkv).astype(F32), 0)
        turned = jnp.concatenate([dq_t, dkv[0]], 0)
        d_qkv = jnp.concatenate([rotate(turned, cosine, -sine), dkv[1]], 0)
        d_qkv = d_qkv.astype(BF16).reshape(Q_ROWS + KV_ROWS, ROWS)
        d_wqkv = ein("td,et->de", attn_in, d_qkv)
        d_norm = ein("et,de->td", d_qkv, wqkv)
        d_gain_a = jnp.sum(d_norm * unit_a, 0)
        d_hidden = d_hidden + norm_back(d_norm * gains[layer, 0], unit_a, rms_a)
        gain_grads[layer] = jnp.stack([d_gain_a, d_gain_m])
        qkv_grads[layer] = d_wqkv.astype(BF16)
    input_grad = d_hidden.reshape(1, ROWS, D)

    mine, theirs = in_order(*qkv_grads)
    d_gains = jnp.transpose(jnp.stack(gain_grads).reshape(2 * LAYERS, D)).astype(BF16)
    d_wqkv = jnp.concatenate([sum_pair(mine, to_partner(theirs)), d_gains], 1)
    qkv = sum_chips(scatter_fsdp(d_wqkv))
    qkv_p = to_partner(qkv)

    share0 = sum_chips(share0)
    mlp0, mlp0_p, mlp1, mlp1_p = share0, to_partner(share0), share1, to_partner(share1)
    half = Q_ROWS + KV_ROWS
    d_gain = qkv[:, half:].astype(F32) + qkv_p[:, half:].astype(F32)
    gain_grad = jnp.transpose(d_gain).reshape(LAYERS, 2, SHARD)
    qkv_grad, out_proj_grad, gate_up_grad = unpack(
        core.reshape(1), mlp0, mlp0_p, mlp1, mlp1_p, qkv, qkv_p
    )
    down_grad = []
    for own, theirs in ((mlp0, mlp0_p), (mlp1, mlp1_p)):
        rows = [x[:, FF : FF + HALF].reshape(UNITS, D) for x in in_order(own, theirs)]
        down_grad.append(jnp.concatenate(rows, 0))
    down_grad = jnp.stack(down_grad).astype(F32)
    return (output, input_grad, gain_grad, qkv_grad, out_proj_grad, gate_up_grad, down_grad)


def solution(mesh):
    in_specs = (
        P("fsdp", "ctx", None),
        P(),
        P("fsdp", None),
        P(None, None, "fsdp"),
        P(None, "fsdp", None),
        P(None, "fsdp", None),
        P(None, "fsdp", None),
        P(None, "fsdp", None),
        P("fsdp", "ctx", None),
    )
    out_specs = (
        P("fsdp", "ctx", None),
        P("fsdp", "ctx", None),
        P(None, None, "fsdp"),
        P(None, "fsdp", None),
        P(None, "fsdp", None),
        P(None, "fsdp", None),
        P(None, "fsdp", None),
    )
    return jax.shard_map(local, mesh=mesh, in_specs=in_specs, out_specs=out_specs, check_vma=False)
```

```python
import functools

import jax
import jax.numpy as jnp
from jax import lax
from jax.experimental import pallas as pl
from jax.experimental.pallas import tpu as pltpu
from jax.sharding import PartitionSpec as P

D = 576
HEADS = 9
KV_HEADS = 3
GROUP = 3
HEAD_DIM = 64
FF = 1536
LAYERS = 2
BLK = 128
NBLK = 32
EPS = 1e-05
THETA = 100000.0
NEG = -1e30
F32 = jnp.float32
BF16 = jnp.bfloat16
LANES = GROUP * BLK
CTX = 16
FSDP = 8
SHARD = D // FSDP
HALF = FF // 2
Q_ROWS = HEADS * HEAD_DIM
KV_ROWS = 2 * KV_HEADS * HEAD_DIM

PARTNER = [(i, i ^ 1) for i in range(CTX)]
SAME_CORE = [[2 * chip + core for chip in range(CTX // 2)] for core in range(2)]


def to_partner(x):
    return lax.ppermute(x, "ctx", PARTNER)


def over_chips(x):
    return lax.all_to_all(x, "ctx", 0, 0, axis_index_groups=SAME_CORE, tiled=True)


def over_fsdp(x):
    return lax.all_to_all(x, "fsdp", 0, 0, tiled=True)


def gather_fsdp(x):
    return over_fsdp(jnp.broadcast_to(x[None], (FSDP,) + x.shape)).reshape(-1, x.shape[1])


def scatter_fsdp(x):
    parts = over_fsdp(x.reshape(FSDP, -1, x.shape[1]))
    return jnp.sum(parts.astype(F32), 0).astype(BF16)


def sum_pair(a, b):
    return (a.astype(F32) + b.astype(F32)).astype(BF16)


def sum_chips(x):
    for bit in (2, 4, 8):
        x = sum_pair(x, lax.ppermute(x, "ctx", [(i, i ^ bit) for i in range(CTX)]))
    return x


def dot_tn(a, b):
    return lax.dot_general(a, b, (((0,), (0,)), ((), ())), preferred_element_type=F32)


def dot_nt(a, b):
    return lax.dot_general(a, b, (((1,), (1,)), ((), ())), preferred_element_type=F32)


UNROLL_F = 9
UNROLL_B = 3
CHUNK = 4
KEYS = CHUNK * BLK
CHUNKS = NBLK // CHUNK


def fill_keys(sc, own_ref, other_ref, kv_s):
    core = sc[2]
    for chip in range(CTX // 2):
        for half in range(2):
            lanes = slice(half * BLK, (half + 1) * BLK)
            block = sc[7 + 2 * (2 * chip + core) + half]
            kv_s[block] = own_ref[chip, :, 0, :, lanes]
            block = sc[7 + 2 * (2 * chip + 1 - core) + half]
            kv_s[block] = other_ref[chip, :, 0, :, lanes]


def fill_queries(sc, src_ref, dst):
    for half in range(2):
        lanes = slice(half * BLK, (half + 1) * BLK)
        which = jnp.bitwise_xor(half, sc[1])
        dst[which] = jnp.concatenate([src_ref[j, :, lanes] for j in range(GROUP)], axis=1)


def query_rows(sc, which):
    block = jnp.where(which == 0, sc[0], NBLK - 1 - sc[0])
    lane = lax.broadcasted_iota(jnp.int32, (1, LANES), 1)
    pos = block * BLK + jnp.bitwise_and(lane, BLK - 1)
    start = jnp.zeros((1, LANES), jnp.int32)
    for d in range(4):
        start = jnp.where(pos >= sc[3 + d], jnp.maximum(start, sc[3 + d]), start)
    return pos, start


def chunk_of(sc, t):
    high = (NBLK - sc[0] + CHUNK - 1) // CHUNK
    which = (t < high).astype(jnp.int32)
    return which, jnp.where(t < high, t, t - high)


def keys_of(kv_s, chunk, kind):
    return jnp.concatenate([kv_s[chunk * CHUNK + j, kind] for j in range(CHUNK)], axis=1)


def seen(pos_s, which, chunk):
    at = lax.broadcasted_iota(jnp.int32, (KEYS, LANES), 0)
    base = chunk * KEYS
    return (at >= pos_s[which, 1:2] - base) & (at <= pos_s[which, 0:1] - base)


def fill_rows(sc, pos_s):
    for which in range(2):
        pos, start = query_rows(sc, which)
        pos_s[which, 0:1] = pos
        pos_s[which, 1:2] = start


def forward_kernel(sc, q_ref, own_ref, other_ref, o_ref, lse_ref, kv_s, q_s, acc_s, m_s, l_s, pos_s):
    fill_keys(sc, own_ref, other_ref, kv_s)
    fill_queries(sc, q_ref, q_s)
    fill_rows(sc, pos_s)
    acc_s[...] = jnp.zeros_like(acc_s)
    m_s[...] = jnp.full_like(m_s, NEG)
    l_s[...] = jnp.zeros_like(l_s)

    def step(t, carry):
        which, chunk = chunk_of(sc, t)
        scores = dot_tn(keys_of(kv_s, chunk, 0), q_s[which])
        scores = jnp.where(seen(pos_s, which, chunk), scores, NEG)
        old = m_s[which]
        new = jnp.maximum(old, jnp.max(scores, axis=0, keepdims=True))
        prob = jnp.exp(scores - new)
        shrink = jnp.exp(old - new)
        m_s[which] = new
        l_s[which] = l_s[which] * shrink + jnp.sum(prob, axis=0, keepdims=True)
        acc_s[which] = acc_s[which] * shrink + jnp.dot(
            keys_of(kv_s, chunk, 1), prob.astype(BF16), preferred_element_type=F32
        )
        return carry

    lax.fori_loop(0, CHUNKS + 1, step, 0, unroll=UNROLL_F)
    for which in range(2):
        acc_s[which] = acc_s[which] / l_s[which]
        lse_ref[0, which] = m_s[which] + jnp.log(l_s[which])
    for half in range(2):
        mine = acc_s[jnp.bitwise_xor(half, sc[1])]
        for j in range(GROUP):
            o_ref[j, :, half * BLK : (half + 1) * BLK] = mine[:, j * BLK : (j + 1) * BLK]


def backward_kernel(
    sc, q_ref, own_ref, other_ref, o_ref, do_ref, lse_ref,
    dq_ref, down_ref, dother_ref,
    kv_s, q_s, do_s, dq_s, dkv_s, delta_s, pos_s,
):
    fill_keys(sc, own_ref, other_ref, kv_s)
    fill_queries(sc, q_ref, q_s)
    fill_queries(sc, do_ref, do_s)
    fill_queries(sc, o_ref, dq_s)
    fill_rows(sc, pos_s)
    for which in range(2):
        delta_s[which] = jnp.sum(dq_s[which] * do_s[which].astype(F32), axis=0, keepdims=True)
    dq_s[...] = jnp.zeros_like(dq_s)
    dkv_s[...] = jnp.zeros_like(dkv_s)

    def step(t, carry):
        which, chunk = chunk_of(sc, t)
        key_t, val_t, q_t, do_t = keys_of(kv_s, chunk, 0), keys_of(kv_s, chunk, 1), q_s[which], do_s[which]
        scores = dot_tn(key_t, q_t)
        prob = jnp.where(seen(pos_s, which, chunk), jnp.exp(scores - lse_ref[0, which]), 0.0)
        d_prob = dot_tn(val_t, do_t)
        d_score = (prob * (d_prob - delta_s[which])).astype(BF16)
        d_val = dot_nt(do_t, prob.astype(BF16))
        d_key = dot_nt(q_t, d_score)
        dq_s[which] = dq_s[which] + jnp.dot(key_t, d_score, preferred_element_type=F32)
        for j in range(CHUNK):
            lanes = slice(j * BLK, (j + 1) * BLK)
            dkv_s[chunk * CHUNK + j, 0] = dkv_s[chunk * CHUNK + j, 0] + d_key[:, lanes]
            dkv_s[chunk * CHUNK + j, 1] = dkv_s[chunk * CHUNK + j, 1] + d_val[:, lanes]
        return carry

    lax.fori_loop(0, CHUNKS + 1, step, 0, unroll=UNROLL_B)
    core = sc[2]
    scale = HEAD_DIM**-0.5
    for half in range(2):
        lanes = slice(half * BLK, (half + 1) * BLK)
        mine = dq_s[jnp.bitwise_xor(half, sc[1])] * scale
        for j in range(GROUP):
            dq_ref[j, :, lanes] = mine[:, j * BLK : (j + 1) * BLK]
        for chip in range(CTX // 2):
            block = sc[7 + 2 * (2 * chip + core) + half]
            down_ref[chip, :, 0, :, lanes] = dkv_s[block].astype(BF16)
            block = sc[7 + 2 * (2 * chip + 1 - core) + half]
            dother_ref[chip, :, 0, :, lanes] = dkv_s[block].astype(BF16)


ROWS = 2 * BLK
HEAD_SPEC = pl.BlockSpec((GROUP, HEAD_DIM, ROWS), lambda g, sc: (g, 0, 0))
KV_SPEC = pl.BlockSpec((CTX // 2, 2, 1, HEAD_DIM, ROWS), lambda g, sc: (0, 0, g, 0, 0))
LSE_SPEC = pl.BlockSpec((1, 2, 1, LANES), lambda g, sc: (g, 0, 0, 0))
HEAD_SHAPE = jax.ShapeDtypeStruct((HEADS, HEAD_DIM, ROWS), F32)
KV_SHAPE = jax.ShapeDtypeStruct((CTX // 2, 2, KV_HEADS, HEAD_DIM, ROWS), BF16)
LSE_SHAPE = jax.ShapeDtypeStruct((KV_HEADS, 2, 1, LANES), F32)
KERNEL_PARAMS = pltpu.CompilerParams(
    dimension_semantics=("arbitrary",), vmem_limit_bytes=40 * 2**20
)


def attention(scalars, q_t, own, other):
    return pl.pallas_call(
        forward_kernel,
        grid_spec=pltpu.PrefetchScalarGridSpec(
            num_scalar_prefetch=1,
            grid=(KV_HEADS,),
            in_specs=[HEAD_SPEC, KV_SPEC, KV_SPEC],
            out_specs=[HEAD_SPEC, LSE_SPEC],
            scratch_shapes=[
                pltpu.VMEM((NBLK, 2, HEAD_DIM, BLK), BF16),
                pltpu.VMEM((2, HEAD_DIM, LANES), BF16),
                pltpu.VMEM((2, HEAD_DIM, LANES), F32),
                pltpu.VMEM((2, 1, LANES), F32),
                pltpu.VMEM((2, 1, LANES), F32),
                pltpu.VMEM((2, 8, LANES), jnp.int32),
            ],
        ),
        out_shape=[HEAD_SHAPE, LSE_SHAPE],
        compiler_params=KERNEL_PARAMS,
        name="attention",
    )(scalars, q_t, own, other)


def attention_back(scalars, q_t, own, other, o_t, do_t, lse):
    return pl.pallas_call(
        backward_kernel,
        grid_spec=pltpu.PrefetchScalarGridSpec(
            num_scalar_prefetch=1,
            grid=(KV_HEADS,),
            in_specs=[HEAD_SPEC, KV_SPEC, KV_SPEC, HEAD_SPEC, HEAD_SPEC, LSE_SPEC],
            out_specs=[HEAD_SPEC, KV_SPEC, KV_SPEC],
            scratch_shapes=[
                pltpu.VMEM((NBLK, 2, HEAD_DIM, BLK), BF16),
                pltpu.VMEM((2, HEAD_DIM, LANES), BF16),
                pltpu.VMEM((2, HEAD_DIM, LANES), BF16),
                pltpu.VMEM((2, HEAD_DIM, LANES), F32),
                pltpu.VMEM((NBLK, 2, HEAD_DIM, BLK), F32),
                pltpu.VMEM((2, 1, LANES), F32),
                pltpu.VMEM((2, 8, LANES), jnp.int32),
            ],
        ),
        out_shape=[HEAD_SHAPE, KV_SHAPE, KV_SHAPE],
        compiler_params=KERNEL_PARAMS,
        name="attention_back",
    )(scalars, q_t, own, other, o_t, do_t, lse)


VMEM_SPEC = pl.BlockSpec(memory_space=pltpu.VMEM)


def dispatch_kernel(me, x_ref, *outs):
    for dx, out in enumerate(outs):
        for dz in range(2):
            out[dz] = x_ref[jnp.bitwise_xor(me[0], 4 * dz + dx)]


def dispatch(me, x):
    return pl.pallas_call(
        dispatch_kernel,
        grid_spec=pltpu.PrefetchScalarGridSpec(
            num_scalar_prefetch=1,
            grid=(),
            in_specs=[VMEM_SPEC],
            out_specs=[VMEM_SPEC] * 4,
        ),
        out_shape=[jax.ShapeDtypeStruct((2,) + x.shape[1:], BF16)] * 4,
        compiler_params=pltpu.CompilerParams(vmem_limit_bytes=40 * 2**20),
        name="dispatch",
    )(me, x)


def across(x, d):
    return lax.ppermute(x, "fsdp", [(i, i ^ d) for i in range(FSDP)])


def scatter_by_permutes(me, x):
    parts = dispatch(me, x.reshape(FSDP, -1, x.shape[1]))
    total = parts[0].astype(F32)
    for dx in range(1, 4):
        total = total + across(parts[dx], dx).astype(F32)
    return (total[0] + across(total[1].astype(BF16), 4).astype(F32)).astype(BF16)


UNITS = FF // FSDP // 2


def unpack_kernel(sc, *refs):
    mlp0, mlp0_p, mlp1, mlp1_p, qkv, qkv_p, qkv_ref, out_ref, gu_ref = refs

    def write(order):
        for layer, pair in enumerate(((mlp0, mlp0_p), (mlp1, mlp1_p))):
            for half, mlp in enumerate(pair[::order]):
                for k in range(2):
                    for i in range(FSDP):
                        src = k * HALF + i * UNITS
                        dst = k * FF + i * 2 * UNITS + half * UNITS
                        gu_ref[layer, :, dst : dst + UNITS] = mlp[:, src : src + UNITS].astype(F32)
                cut = D // 2
                out_ref[layer, :, half * cut : (half + 1) * cut] = (
                    mlp[:, FF + HALF : FF + HALF + cut].astype(F32)
                )
        for layer, src in enumerate((qkv, qkv_p)[::order]):
            qkv_ref[layer] = src[:, : Q_ROWS + KV_ROWS].astype(F32)

    @pl.when(sc[0] == 0)
    def _():
        write(1)

    @pl.when(sc[0] != 0)
    def _():
        write(-1)


def unpack(core, *shares):
    return pl.pallas_call(
        unpack_kernel,
        grid_spec=pltpu.PrefetchScalarGridSpec(
            num_scalar_prefetch=1,
            grid=(),
            in_specs=[VMEM_SPEC] * 6,
            out_specs=[VMEM_SPEC] * 3,
        ),
        out_shape=[
            jax.ShapeDtypeStruct((LAYERS, SHARD, Q_ROWS + KV_ROWS), F32),
            jax.ShapeDtypeStruct((LAYERS, SHARD, D), F32),
            jax.ShapeDtypeStruct((LAYERS, SHARD, 2 * FF), F32),
        ],
        compiler_params=pltpu.CompilerParams(vmem_limit_bytes=40 * 2**20),
        name="unpack",
    )(core, *shares)


def rotate(x, cosine, sine):
    half = HEAD_DIM // 2
    first, second = x[:, :half], x[:, half:]
    return jnp.concatenate([first * cosine - second * sine, second * cosine + first * sine], 1)


def normed(hidden):
    inv_rms = lax.rsqrt(jnp.mean(hidden * hidden, -1, keepdims=True) + EPS)
    return hidden * inv_rms, inv_rms


def norm_back(d_unit, unit, inv_rms):
    return inv_rms * (d_unit - unit * jnp.mean(d_unit * unit, -1, keepdims=True))


def mm(a, b):
    return jnp.dot(a, b, preferred_element_type=F32)


def ein(spec, a, b):
    return jnp.einsum(spec, a, b, preferred_element_type=F32)


def local(tokens, block_order, doc_ids, norm_gains, w_qkv, w_out, w_gate_up, w_down, cotangent):
    place = lax.axis_index("ctx")
    core = jnp.bitwise_and(place, 1)
    first_core = core == 0
    me = lax.axis_index("fsdp").reshape(1)

    def my_half(left, right):
        return jnp.where(first_core, left, right)

    def in_order(own, other):
        return my_half(own, other), my_half(other, own)

    gain_cols = jnp.transpose(norm_gains.reshape(2 * LAYERS, SHARD))
    cut = (Q_ROWS + KV_ROWS + D) // 2

    def wgu_pack(layer):
        wgu = w_gate_up[layer].reshape(SHARD, 2, FSDP, 2, UNITS)
        return my_half(wgu[..., 0, :], wgu[..., 1, :]).reshape(SHARD, FF)

    def wd_pack(layer):
        return my_half(w_down[layer, :UNITS], w_down[layer, UNITS:]).reshape(SHARD, HALF)

    def proj_pack(layer):
        proj = jnp.concatenate([w_qkv[layer], w_out[layer]], 1)
        return my_half(proj[:, :cut], proj[:, cut:])

    first = jnp.concatenate([proj_pack(0), gain_cols], 1)
    first = jnp.broadcast_to(first[None], (FSDP,) + first.shape)
    first, w_gate_up, w_down = lax.optimization_barrier((first, w_gate_up, w_down))
    first = over_fsdp(first).reshape(D, -1)
    pack0 = jnp.concatenate([wgu_pack(0), wd_pack(0), wd_pack(1)], 1)
    pack0 = lax.all_gather(pack0, "fsdp", axis=0, tiled=True)
    pack1 = lax.all_gather(wgu_pack(1), "fsdp", axis=0, tiled=True)
    gains = jnp.transpose(first[:, cut:].astype(F32)).reshape(LAYERS, 2, D)

    def whole_proj(own):
        return jnp.concatenate(in_order(own, to_partner(own)), 1)

    projs, mlps = [whole_proj(first[:, :cut])], []

    first_block = lax.dynamic_index_in_dim(block_order, 2 * place, 0, keepdims=False)
    low = jnp.minimum(first_block, NBLK - 1 - first_block)
    low_half = (first_block != low).astype(jnp.int32)
    starts = jnp.sum(
        (doc_ids[0][None, :] < jnp.arange(1, 5, dtype=jnp.int32)[:, None]).astype(jnp.int32), 1
    )
    scalars = jnp.concatenate([jnp.stack([low, low_half, core]), starts, block_order])
    lane = jnp.arange(ROWS, dtype=jnp.int32)
    pos = jnp.where(lane < BLK, first_block, NBLK - 2 - first_block) * BLK + lane
    inv_freq = THETA ** (-jnp.arange(HEAD_DIM // 2, dtype=F32) / (HEAD_DIM // 2))
    angles = pos.astype(F32)[None, :] * inv_freq[:, None]
    cosine, sine = jnp.cos(angles), jnp.sin(angles)

    hidden = tokens[0].astype(F32)
    saved = []
    for layer in range(LAYERS):
        wqkv, wout = projs[layer][:, : Q_ROWS + KV_ROWS], projs[layer][:, Q_ROWS + KV_ROWS :]
        unit_a, rms_a = normed(hidden)
        attn_in = (unit_a * gains[layer, 0]).astype(BF16)
        qkv_t = ein("de,td->et", wqkv, attn_in).reshape(-1, HEAD_DIM, ROWS)
        turned = rotate(qkv_t[: HEADS + KV_HEADS], cosine, sine)
        q_t = (turned[:HEADS] * HEAD_DIM**-0.5).astype(BF16)
        kv_t = jnp.concatenate([turned[HEADS:], qkv_t[HEADS + KV_HEADS :]], 0).astype(BF16)
        kv_t = kv_t.reshape(1, 2, KV_HEADS, HEAD_DIM, ROWS)
        kv_own = over_chips(jnp.broadcast_to(kv_t, (CTX // 2,) + kv_t.shape[1:]))
        if layer == 0:
            kv_own, late = lax.optimization_barrier((kv_own, proj_pack(1)))
            late = gather_fsdp(late)
        kv_other = to_partner(kv_own)
        o_t, lse = attention(scalars, q_t, kv_own, kv_other)
        if layer == 0:
            o_t, pack0, late = lax.optimization_barrier((o_t, pack0, late))
            mlps.append((pack0[:, :FF], pack0[:, FF : FF + HALF].reshape(HALF, D)))
            projs.append(whole_proj(late))
        else:
            o_t, pack1 = lax.optimization_barrier((o_t, pack1))
            mlps.append((pack1, pack0[:, FF + HALF :].reshape(HALF, D)))
        attn_out = o_t.astype(BF16).reshape(Q_ROWS, ROWS)
        mid = hidden + ein("at,ad->td", attn_out, wout)
        unit_m, rms_m = normed(mid)
        mlp_in = (unit_m * gains[layer, 1]).astype(BF16)
        wgu, wdown = mlps[layer]
        both_in = jnp.concatenate([mlp_in, to_partner(mlp_in)], 0)
        gate_up = mm(both_in, wgu)
        inner = (jax.nn.silu(gate_up[:, :HALF]) * gate_up[:, HALF:]).astype(BF16)
        part = mm(inner, wdown)
        hidden = mid + part[:ROWS] + to_partner(part[ROWS:].astype(BF16)).astype(F32)
        saved.append(
            (wqkv, wout, unit_a, rms_a, attn_in, q_t, kv_own, kv_other, o_t, lse, attn_out,
             unit_m, rms_m, both_in, gate_up, inner, wgu, wdown)
        )
    output = hidden.astype(BF16).reshape(1, ROWS, D)

    d_hidden = cotangent[0].astype(F32)
    gain_grads, qkv_grads = [None] * LAYERS, [None] * LAYERS
    for layer in reversed(range(LAYERS)):
        (wqkv, wout, unit_a, rms_a, attn_in, q_t, kv_own, kv_other, o_t, lse, attn_out,
         unit_m, rms_m, both_in, gate_up, inner, wgu, wdown) = saved[layer]
        grad_b = d_hidden.astype(BF16)
        both_grad = jnp.concatenate([grad_b, to_partner(grad_b)], 0)
        d_inner = ein("td,fd->tf", both_grad, wdown)
        gate, up = gate_up[:, :HALF], gate_up[:, HALF:]
        sig = jax.nn.sigmoid(gate)
        d_gate = d_inner * up * sig * (1.0 + gate * (1.0 - sig))
        d_up = d_inner * (gate * sig)
        d_gu = jnp.concatenate([d_gate, d_up], 1).astype(BF16)
        part = ein("tf,df->td", d_gu, wgu)
        d_norm = part[:ROWS] + to_partner(part[ROWS:].astype(BF16)).astype(F32)
        d_gain_m = jnp.sum(d_norm * unit_m, 0)
        d_hidden = d_hidden + norm_back(d_norm * gains[layer, 1], unit_m, rms_m)
        grad_b = d_hidden.astype(BF16)
        do_t = ein("ad,td->at", wout, grad_b).astype(BF16).reshape(HEADS, HEAD_DIM, ROWS)
        dq_t, dkv_own, dkv_other = attention_back(scalars, q_t, kv_own, kv_other, o_t, do_t, lse)
        dkv = (dkv_own.astype(F32) + to_partner(dkv_other).astype(F32)).astype(BF16)
        d_gu, late_in, late_grad, _ = lax.optimization_barrier((d_gu, both_in, grad_b, dkv))
        d_wgu = ein("td,tf->df", late_in, d_gu).astype(BF16)
        d_wdown = ein("tf,td->fd", inner, both_grad).astype(BF16)
        d_wout = mm(attn_out, late_grad).astype(BF16)
        wout_half = D // 2
        wout_mine = my_half(d_wout[:, :wout_half], d_wout[:, wout_half:])
        wout_theirs = my_half(d_wout[:, wout_half:], d_wout[:, :wout_half])
        d_mlp = [d_wgu, d_wdown.reshape(D, HALF), sum_pair(wout_mine, to_partner(wout_theirs))]
        d_mlp = jnp.concatenate(d_mlp, 1)
        if layer == 0:
            share1 = sum_chips(lax.optimization_barrier((share1, dkv))[0])
        dkv = jnp.sum(over_chips(dkv).astype(F32), 0)
        dkv, d_mlp = lax.optimization_barrier((dkv, d_mlp))
        if layer == 1:
            share1 = lax.psum_scatter(d_mlp, "fsdp", scatter_dimension=0, tiled=True)
        else:
            share0 = scatter_by_permutes(me, d_mlp)
        turned = jnp.concatenate([dq_t, dkv[0]], 0)
        d_qkv = jnp.concatenate([rotate(turned, cosine, -sine), dkv[1]], 0)
        d_qkv = d_qkv.astype(BF16).reshape(Q_ROWS + KV_ROWS, ROWS)
        d_wqkv = ein("td,et->de", attn_in, d_qkv)
        d_norm = ein("et,de->td", d_qkv, wqkv)
        d_gain_a = jnp.sum(d_norm * unit_a, 0)
        d_hidden = d_hidden + norm_back(d_norm * gains[layer, 0], unit_a, rms_a)
        gain_grads[layer] = jnp.stack([d_gain_a, d_gain_m])
        qkv_grads[layer] = d_wqkv.astype(BF16)
    input_grad = d_hidden.reshape(1, ROWS, D)

    mine, theirs = in_order(*qkv_grads)
    d_gains = jnp.transpose(jnp.stack(gain_grads).reshape(2 * LAYERS, D)).astype(BF16)
    d_wqkv = jnp.concatenate([sum_pair(mine, to_partner(theirs)), d_gains], 1)
    qkv = sum_chips(scatter_fsdp(d_wqkv))
    qkv_p = to_partner(qkv)

    share0 = sum_chips(share0)
    mlp0, mlp0_p, mlp1, mlp1_p = share0, to_partner(share0), share1, to_partner(share1)
    half = Q_ROWS + KV_ROWS
    d_gain = qkv[:, half:].astype(F32) + qkv_p[:, half:].astype(F32)
    gain_grad = jnp.transpose(d_gain).reshape(LAYERS, 2, SHARD)
    qkv_grad, out_proj_grad, gate_up_grad = unpack(
        core.reshape(1), mlp0, mlp0_p, mlp1, mlp1_p, qkv, qkv_p
    )
    down_grad = []
    for own, theirs in ((mlp0, mlp0_p), (mlp1, mlp1_p)):
        rows = [x[:, FF : FF + HALF].reshape(UNITS, D) for x in in_order(own, theirs)]
        down_grad.append(jnp.concatenate(rows, 0))
    down_grad = jnp.stack(down_grad).astype(F32)
    return (output, input_grad, gain_grad, qkv_grad, out_proj_grad, gate_up_grad, down_grad)


def solution(mesh):
    in_specs = (
        P("fsdp", "ctx", None),
        P(),
        P("fsdp", None),
        P(None, None, "fsdp"),
        P(None, "fsdp", None),
        P(None, "fsdp", None),
        P(None, "fsdp", None),
        P(None, "fsdp", None),
        P("fsdp", "ctx", None),
    )
    out_specs = (
        P("fsdp", "ctx", None),
        P("fsdp", "ctx", None),
        P(None, None, "fsdp"),
        P(None, "fsdp", None),
        P(None, "fsdp", None),
        P(None, "fsdp", None),
        P(None, "fsdp", None),
    )
    return jax.shard_map(local, mesh=mesh, in_specs=in_specs, out_specs=out_specs, check_vma=False)
```

```python
import functools

import jax
import jax.numpy as jnp
from jax import lax
from jax.experimental import pallas as pl
from jax.experimental.pallas import tpu as pltpu
from jax.sharding import PartitionSpec as P

D = 576
HEADS = 9
KV_HEADS = 3
GROUP = 3
HEAD_DIM = 64
FF = 1536
LAYERS = 2
BLK = 128
NBLK = 32
EPS = 1e-05
THETA = 100000.0
NEG = -1e30
F32 = jnp.float32
BF16 = jnp.bfloat16
LANES = GROUP * BLK
CTX = 16
FSDP = 8
SHARD = D // FSDP
HALF = FF // 2
Q_ROWS = HEADS * HEAD_DIM
KV_ROWS = 2 * KV_HEADS * HEAD_DIM

PARTNER = [(i, i ^ 1) for i in range(CTX)]
SAME_CORE = [[2 * chip + core for chip in range(CTX // 2)] for core in range(2)]


def to_partner(x):
    return lax.ppermute(x, "ctx", PARTNER)


def over_chips(x):
    return lax.all_to_all(x, "ctx", 0, 0, axis_index_groups=SAME_CORE, tiled=True)


def over_fsdp(x):
    return lax.all_to_all(x, "fsdp", 0, 0, tiled=True)


def gather_fsdp(x):
    return over_fsdp(jnp.broadcast_to(x[None], (FSDP,) + x.shape)).reshape(-1, x.shape[1])


def scatter_fsdp(x):
    parts = over_fsdp(x.reshape(FSDP, -1, x.shape[1]))
    return jnp.sum(parts.astype(F32), 0).astype(BF16)


def sum_pair(a, b):
    return (a.astype(F32) + b.astype(F32)).astype(BF16)


def sum_chips(x):
    for bit in (2, 4, 8):
        x = sum_pair(x, lax.ppermute(x, "ctx", [(i, i ^ bit) for i in range(CTX)]))
    return x


def dot_tn(a, b):
    return lax.dot_general(a, b, (((0,), (0,)), ((), ())), preferred_element_type=F32)


def dot_nt(a, b):
    return lax.dot_general(a, b, (((1,), (1,)), ((), ())), preferred_element_type=F32)


UNROLL_F = 9
UNROLL_B = 3
CHUNK = 4
KEYS = CHUNK * BLK
CHUNKS = NBLK // CHUNK


def fill_keys(sc, own_ref, other_ref, kv_s):
    core = sc[2]
    for chip in range(CTX // 2):
        for half in range(2):
            lanes = slice(half * BLK, (half + 1) * BLK)
            block = sc[7 + 2 * (2 * chip + core) + half]
            kv_s[block] = own_ref[chip, :, 0, :, lanes]
            block = sc[7 + 2 * (2 * chip + 1 - core) + half]
            kv_s[block] = other_ref[chip, :, 0, :, lanes]


def fill_queries(sc, src_ref, dst):
    for half in range(2):
        lanes = slice(half * BLK, (half + 1) * BLK)
        which = jnp.bitwise_xor(half, sc[1])
        dst[which] = jnp.concatenate([src_ref[j, :, lanes] for j in range(GROUP)], axis=1)


def query_rows(sc, which):
    block = jnp.where(which == 0, sc[0], NBLK - 1 - sc[0])
    lane = lax.broadcasted_iota(jnp.int32, (1, LANES), 1)
    pos = block * BLK + jnp.bitwise_and(lane, BLK - 1)
    start = jnp.zeros((1, LANES), jnp.int32)
    for d in range(4):
        start = jnp.where(pos >= sc[3 + d], jnp.maximum(start, sc[3 + d]), start)
    return pos, start


def chunk_of(sc, t):
    high = (NBLK - sc[0] + CHUNK - 1) // CHUNK
    which = (t < high).astype(jnp.int32)
    return which, jnp.where(t < high, t, t - high)


def keys_of(kv_s, chunk, kind):
    return jnp.concatenate([kv_s[chunk * CHUNK + j, kind] for j in range(CHUNK)], axis=1)


def seen(pos_s, which, chunk):
    at = lax.broadcasted_iota(jnp.int32, (KEYS, LANES), 0)
    base = chunk * KEYS
    return (at >= pos_s[which, 1:2] - base) & (at <= pos_s[which, 0:1] - base)


def fill_rows(sc, pos_s):
    for which in range(2):
        pos, start = query_rows(sc, which)
        pos_s[which, 0:1] = pos
        pos_s[which, 1:2] = start


def forward_kernel(sc, q_ref, own_ref, other_ref, o_ref, lse_ref, kv_s, q_s, acc_s, m_s, l_s, pos_s):
    fill_keys(sc, own_ref, other_ref, kv_s)
    fill_queries(sc, q_ref, q_s)
    fill_rows(sc, pos_s)
    acc_s[...] = jnp.zeros_like(acc_s)
    m_s[...] = jnp.full_like(m_s, NEG)
    l_s[...] = jnp.zeros_like(l_s)

    def step(t, carry):
        which, chunk = chunk_of(sc, t)
        scores = dot_tn(keys_of(kv_s, chunk, 0), q_s[which])
        scores = jnp.where(seen(pos_s, which, chunk), scores, NEG)
        old = m_s[which]
        new = jnp.maximum(old, jnp.max(scores, axis=0, keepdims=True))
        prob = jnp.exp(scores - new)
        shrink = jnp.exp(old - new)
        m_s[which] = new
        l_s[which] = l_s[which] * shrink + jnp.sum(prob, axis=0, keepdims=True)
        acc_s[which] = acc_s[which] * shrink + jnp.dot(
            keys_of(kv_s, chunk, 1), prob.astype(BF16), preferred_element_type=F32
        )
        return carry

    lax.fori_loop(0, CHUNKS + 1, step, 0, unroll=UNROLL_F)
    for which in range(2):
        acc_s[which] = acc_s[which] / l_s[which]
        lse_ref[0, which] = m_s[which] + jnp.log(l_s[which])
    for half in range(2):
        mine = acc_s[jnp.bitwise_xor(half, sc[1])]
        for j in range(GROUP):
            o_ref[j, :, half * BLK : (half + 1) * BLK] = mine[:, j * BLK : (j + 1) * BLK]


def backward_kernel(
    sc, q_ref, own_ref, other_ref, o_ref, do_ref, lse_ref,
    dq_ref, down_ref, dother_ref,
    kv_s, q_s, do_s, dq_s, dkv_s, delta_s, pos_s,
):
    fill_keys(sc, own_ref, other_ref, kv_s)
    fill_queries(sc, q_ref, q_s)
    fill_queries(sc, do_ref, do_s)
    fill_queries(sc, o_ref, dq_s)
    fill_rows(sc, pos_s)
    for which in range(2):
        delta_s[which] = jnp.sum(dq_s[which] * do_s[which].astype(F32), axis=0, keepdims=True)
    dq_s[...] = jnp.zeros_like(dq_s)
    dkv_s[...] = jnp.zeros_like(dkv_s)

    def step(t, carry):
        which, chunk = chunk_of(sc, t)
        key_t, val_t, q_t, do_t = keys_of(kv_s, chunk, 0), keys_of(kv_s, chunk, 1), q_s[which], do_s[which]
        scores = dot_tn(key_t, q_t)
        prob = jnp.where(seen(pos_s, which, chunk), jnp.exp(scores - lse_ref[0, which]), 0.0)
        d_prob = dot_tn(val_t, do_t)
        d_score = (prob * (d_prob - delta_s[which])).astype(BF16)
        d_val = dot_nt(do_t, prob.astype(BF16))
        d_key = dot_nt(q_t, d_score)
        dq_s[which] = dq_s[which] + jnp.dot(key_t, d_score, preferred_element_type=F32)
        for j in range(CHUNK):
            lanes = slice(j * BLK, (j + 1) * BLK)
            dkv_s[chunk * CHUNK + j, 0] = dkv_s[chunk * CHUNK + j, 0] + d_key[:, lanes]
            dkv_s[chunk * CHUNK + j, 1] = dkv_s[chunk * CHUNK + j, 1] + d_val[:, lanes]
        return carry

    lax.fori_loop(0, CHUNKS + 1, step, 0, unroll=UNROLL_B)
    core = sc[2]
    scale = HEAD_DIM**-0.5
    for half in range(2):
        lanes = slice(half * BLK, (half + 1) * BLK)
        mine = dq_s[jnp.bitwise_xor(half, sc[1])] * scale
        for j in range(GROUP):
            dq_ref[j, :, lanes] = mine[:, j * BLK : (j + 1) * BLK]
        for chip in range(CTX // 2):
            block = sc[7 + 2 * (2 * chip + core) + half]
            down_ref[chip, :, 0, :, lanes] = dkv_s[block].astype(BF16)
            block = sc[7 + 2 * (2 * chip + 1 - core) + half]
            dother_ref[chip, :, 0, :, lanes] = dkv_s[block].astype(BF16)


ROWS = 2 * BLK
HEAD_SPEC = pl.BlockSpec((GROUP, HEAD_DIM, ROWS), lambda g, sc: (g, 0, 0))
KV_SPEC = pl.BlockSpec((CTX // 2, 2, 1, HEAD_DIM, ROWS), lambda g, sc: (0, 0, g, 0, 0))
LSE_SPEC = pl.BlockSpec((1, 2, 1, LANES), lambda g, sc: (g, 0, 0, 0))
HEAD_SHAPE = jax.ShapeDtypeStruct((HEADS, HEAD_DIM, ROWS), F32)
KV_SHAPE = jax.ShapeDtypeStruct((CTX // 2, 2, KV_HEADS, HEAD_DIM, ROWS), BF16)
LSE_SHAPE = jax.ShapeDtypeStruct((KV_HEADS, 2, 1, LANES), F32)
KERNEL_PARAMS = pltpu.CompilerParams(
    dimension_semantics=("arbitrary",), vmem_limit_bytes=40 * 2**20
)


def attention(scalars, q_t, own, other):
    return pl.pallas_call(
        forward_kernel,
        grid_spec=pltpu.PrefetchScalarGridSpec(
            num_scalar_prefetch=1,
            grid=(KV_HEADS,),
            in_specs=[HEAD_SPEC, KV_SPEC, KV_SPEC],
            out_specs=[HEAD_SPEC, LSE_SPEC],
            scratch_shapes=[
                pltpu.VMEM((NBLK, 2, HEAD_DIM, BLK), BF16),
                pltpu.VMEM((2, HEAD_DIM, LANES), BF16),
                pltpu.VMEM((2, HEAD_DIM, LANES), F32),
                pltpu.VMEM((2, 1, LANES), F32),
                pltpu.VMEM((2, 1, LANES), F32),
                pltpu.VMEM((2, 8, LANES), jnp.int32),
            ],
        ),
        out_shape=[HEAD_SHAPE, LSE_SHAPE],
        compiler_params=KERNEL_PARAMS,
        name="attention",
    )(scalars, q_t, own, other)


def attention_back(scalars, q_t, own, other, o_t, do_t, lse):
    return pl.pallas_call(
        backward_kernel,
        grid_spec=pltpu.PrefetchScalarGridSpec(
            num_scalar_prefetch=1,
            grid=(KV_HEADS,),
            in_specs=[HEAD_SPEC, KV_SPEC, KV_SPEC, HEAD_SPEC, HEAD_SPEC, LSE_SPEC],
            out_specs=[HEAD_SPEC, KV_SPEC, KV_SPEC],
            scratch_shapes=[
                pltpu.VMEM((NBLK, 2, HEAD_DIM, BLK), BF16),
                pltpu.VMEM((2, HEAD_DIM, LANES), BF16),
                pltpu.VMEM((2, HEAD_DIM, LANES), BF16),
                pltpu.VMEM((2, HEAD_DIM, LANES), F32),
                pltpu.VMEM((NBLK, 2, HEAD_DIM, BLK), F32),
                pltpu.VMEM((2, 1, LANES), F32),
                pltpu.VMEM((2, 8, LANES), jnp.int32),
            ],
        ),
        out_shape=[HEAD_SHAPE, KV_SHAPE, KV_SHAPE],
        compiler_params=KERNEL_PARAMS,
        name="attention_back",
    )(scalars, q_t, own, other, o_t, do_t, lse)


VMEM_SPEC = pl.BlockSpec(memory_space=pltpu.VMEM)


def dispatch_kernel(me, x_ref, *outs):
    for dx, out in enumerate(outs):
        for dz in range(2):
            out[dz] = x_ref[jnp.bitwise_xor(me[0], 4 * dz + dx)]


def dispatch(me, x):
    return pl.pallas_call(
        dispatch_kernel,
        grid_spec=pltpu.PrefetchScalarGridSpec(
            num_scalar_prefetch=1,
            grid=(),
            in_specs=[VMEM_SPEC],
            out_specs=[VMEM_SPEC] * 4,
        ),
        out_shape=[jax.ShapeDtypeStruct((2,) + x.shape[1:], BF16)] * 4,
        compiler_params=pltpu.CompilerParams(vmem_limit_bytes=40 * 2**20),
        name="dispatch",
    )(me, x)


def across(x, d):
    return lax.ppermute(x, "fsdp", [(i, i ^ d) for i in range(FSDP)])


def send_parts(me, x):
    parts = dispatch(me, x.reshape(FSDP, -1, x.shape[1]))
    return [parts[0]] + [across(parts[dx], dx) for dx in range(1, 4)]


def sum_parts(parts):
    total = sum(p.astype(F32) for p in parts)
    return (total[0] + across(total[1].astype(BF16), 4).astype(F32)).astype(BF16)


UNITS = FF // FSDP // 2


def unpack_kernel(sc, *refs):
    mlp0, mlp0_p, mlp1, mlp1_p, qkv, qkv_p, qkv_ref, out_ref, gu_ref = refs

    def write(order):
        for layer, pair in enumerate(((mlp0, mlp0_p), (mlp1, mlp1_p))):
            for half, mlp in enumerate(pair[::order]):
                for k in range(2):
                    for i in range(FSDP):
                        src = k * HALF + i * UNITS
                        dst = k * FF + i * 2 * UNITS + half * UNITS
                        gu_ref[layer, :, dst : dst + UNITS] = mlp[:, src : src + UNITS].astype(F32)
                cut = D // 2
                out_ref[layer, :, half * cut : (half + 1) * cut] = (
                    mlp[:, FF + HALF : FF + HALF + cut].astype(F32)
                )
        for layer, src in enumerate((qkv, qkv_p)[::order]):
            qkv_ref[layer] = src[:, : Q_ROWS + KV_ROWS].astype(F32)

    @pl.when(sc[0] == 0)
    def _():
        write(1)

    @pl.when(sc[0] != 0)
    def _():
        write(-1)


def unpack(core, *shares):
    return pl.pallas_call(
        unpack_kernel,
        grid_spec=pltpu.PrefetchScalarGridSpec(
            num_scalar_prefetch=1,
            grid=(),
            in_specs=[VMEM_SPEC] * 6,
            out_specs=[VMEM_SPEC] * 3,
        ),
        out_shape=[
            jax.ShapeDtypeStruct((LAYERS, SHARD, Q_ROWS + KV_ROWS), F32),
            jax.ShapeDtypeStruct((LAYERS, SHARD, D), F32),
            jax.ShapeDtypeStruct((LAYERS, SHARD, 2 * FF), F32),
        ],
        compiler_params=pltpu.CompilerParams(vmem_limit_bytes=40 * 2**20),
        name="unpack",
    )(core, *shares)


def rotate(x, cosine, sine):
    half = HEAD_DIM // 2
    first, second = x[:, :half], x[:, half:]
    return jnp.concatenate([first * cosine - second * sine, second * cosine + first * sine], 1)


def normed(hidden):
    inv_rms = lax.rsqrt(jnp.mean(hidden * hidden, -1, keepdims=True) + EPS)
    return hidden * inv_rms, inv_rms


def norm_back(d_unit, unit, inv_rms):
    return inv_rms * (d_unit - unit * jnp.mean(d_unit * unit, -1, keepdims=True))


def mm(a, b):
    return jnp.dot(a, b, preferred_element_type=F32)


def ein(spec, a, b):
    return jnp.einsum(spec, a, b, preferred_element_type=F32)


def local(tokens, block_order, doc_ids, norm_gains, w_qkv, w_out, w_gate_up, w_down, cotangent):
    place = lax.axis_index("ctx")
    core = jnp.bitwise_and(place, 1)
    first_core = core == 0
    me = lax.axis_index("fsdp").reshape(1)

    def my_half(left, right):
        return jnp.where(first_core, left, right)

    def in_order(own, other):
        return my_half(own, other), my_half(other, own)

    gain_cols = jnp.transpose(norm_gains.reshape(2 * LAYERS, SHARD))
    cut = (Q_ROWS + KV_ROWS + D) // 2

    def wgu_pack(layer):
        wgu = w_gate_up[layer].reshape(SHARD, 2, FSDP, 2, UNITS)
        return my_half(wgu[..., 0, :], wgu[..., 1, :]).reshape(SHARD, FF)

    def wd_pack(layer):
        return my_half(w_down[layer, :UNITS], w_down[layer, UNITS:]).reshape(SHARD, HALF)

    def proj_pack(layer):
        proj = jnp.concatenate([w_qkv[layer], w_out[layer]], 1)
        return my_half(proj[:, :cut], proj[:, cut:])

    first = jnp.concatenate([proj_pack(0), gain_cols], 1)
    first = jnp.broadcast_to(first[None], (FSDP,) + first.shape)
    first, w_gate_up, w_down = lax.optimization_barrier((first, w_gate_up, w_down))
    first = over_fsdp(first).reshape(D, -1)
    pack0 = jnp.concatenate([wgu_pack(0), wd_pack(0)], 1)
    pack0 = lax.all_gather(pack0, "fsdp", axis=0, tiled=True)
    pack1 = lax.all_gather(wgu_pack(1), "fsdp", axis=0, tiled=True)
    gains = jnp.transpose(first[:, cut:].astype(F32)).reshape(LAYERS, 2, D)

    def whole_proj(own):
        return jnp.concatenate(in_order(own, to_partner(own)), 1)

    projs, mlps = [whole_proj(first[:, :cut])], []

    first_block = lax.dynamic_index_in_dim(block_order, 2 * place, 0, keepdims=False)
    low = jnp.minimum(first_block, NBLK - 1 - first_block)
    low_half = (first_block != low).astype(jnp.int32)
    starts = jnp.sum(
        (doc_ids[0][None, :] < jnp.arange(1, 5, dtype=jnp.int32)[:, None]).astype(jnp.int32), 1
    )
    scalars = jnp.concatenate([jnp.stack([low, low_half, core]), starts, block_order])
    lane = jnp.arange(ROWS, dtype=jnp.int32)
    pos = jnp.where(lane < BLK, first_block, NBLK - 2 - first_block) * BLK + lane
    inv_freq = THETA ** (-jnp.arange(HEAD_DIM // 2, dtype=F32) / (HEAD_DIM // 2))
    angles = pos.astype(F32)[None, :] * inv_freq[:, None]
    cosine, sine = jnp.cos(angles), jnp.sin(angles)

    hidden = tokens[0].astype(F32)
    saved = []
    for layer in range(LAYERS):
        wqkv, wout = projs[layer][:, : Q_ROWS + KV_ROWS], projs[layer][:, Q_ROWS + KV_ROWS :]
        unit_a, rms_a = normed(hidden)
        attn_in = (unit_a * gains[layer, 0]).astype(BF16)
        qkv_t = ein("de,td->et", wqkv, attn_in).reshape(-1, HEAD_DIM, ROWS)
        turned = rotate(qkv_t[: HEADS + KV_HEADS], cosine, sine)
        q_t = (turned[:HEADS] * HEAD_DIM**-0.5).astype(BF16)
        kv_t = jnp.concatenate([turned[HEADS:], qkv_t[HEADS + KV_HEADS :]], 0).astype(BF16)
        kv_t = kv_t.reshape(1, 2, KV_HEADS, HEAD_DIM, ROWS)
        kv_own = over_chips(jnp.broadcast_to(kv_t, (CTX // 2,) + kv_t.shape[1:]))
        if layer == 0:
            late = jnp.concatenate([proj_pack(1), wd_pack(1)], 1)
            kv_own, late = lax.optimization_barrier((kv_own, late))
            late = gather_fsdp(late)
        kv_other = to_partner(kv_own)
        o_t, lse = attention(scalars, q_t, kv_own, kv_other)
        if layer == 0:
            o_t, pack0 = lax.optimization_barrier((o_t, pack0))
            mlps.append((pack0[:, :FF], pack0[:, FF:].reshape(HALF, D)))
            projs.append(whole_proj(late[:, :cut]))
        else:
            o_t, pack1 = lax.optimization_barrier((o_t, pack1))
            mlps.append((pack1, late[:, cut:].reshape(HALF, D)))
        attn_out = o_t.astype(BF16).reshape(Q_ROWS, ROWS)
        mid = hidden + ein("at,ad->td", attn_out, wout)
        unit_m, rms_m = normed(mid)
        mlp_in = (unit_m * gains[layer, 1]).astype(BF16)
        wgu, wdown = mlps[layer]
        both_in = jnp.concatenate([mlp_in, to_partner(mlp_in)], 0)
        gate_up = mm(both_in, wgu)
        inner = (jax.nn.silu(gate_up[:, :HALF]) * gate_up[:, HALF:]).astype(BF16)
        part = mm(inner, wdown)
        hidden = mid + part[:ROWS] + to_partner(part[ROWS:].astype(BF16)).astype(F32)
        saved.append(
            (wqkv, wout, unit_a, rms_a, attn_in, q_t, kv_own, kv_other, o_t, lse, attn_out,
             unit_m, rms_m, both_in, gate_up, inner, wgu, wdown)
        )
    output = hidden.astype(BF16).reshape(1, ROWS, D)

    d_hidden = cotangent[0].astype(F32)
    gain_grads, qkv_grads = [None] * LAYERS, [None] * LAYERS
    for layer in reversed(range(LAYERS)):
        (wqkv, wout, unit_a, rms_a, attn_in, q_t, kv_own, kv_other, o_t, lse, attn_out,
         unit_m, rms_m, both_in, gate_up, inner, wgu, wdown) = saved[layer]
        grad_b = d_hidden.astype(BF16)
        both_grad = jnp.concatenate([grad_b, to_partner(grad_b)], 0)
        d_inner = ein("td,fd->tf", both_grad, wdown)
        gate, up = gate_up[:, :HALF], gate_up[:, HALF:]
        sig = jax.nn.sigmoid(gate)
        d_gate = d_inner * up * sig * (1.0 + gate * (1.0 - sig))
        d_up = d_inner * (gate * sig)
        d_gu = jnp.concatenate([d_gate, d_up], 1).astype(BF16)
        part = ein("tf,df->td", d_gu, wgu)
        d_norm = part[:ROWS] + to_partner(part[ROWS:].astype(BF16)).astype(F32)
        d_gain_m = jnp.sum(d_norm * unit_m, 0)
        d_hidden = d_hidden + norm_back(d_norm * gains[layer, 1], unit_m, rms_m)
        grad_b = d_hidden.astype(BF16)
        do_t = ein("ad,td->at", wout, grad_b).astype(BF16).reshape(HEADS, HEAD_DIM, ROWS)
        dq_t, dkv_own, dkv_other = attention_back(scalars, q_t, kv_own, kv_other, o_t, do_t, lse)
        dkv = (dkv_own.astype(F32) + to_partner(dkv_other).astype(F32)).astype(BF16)
        d_gu, late_in, late_grad, _ = lax.optimization_barrier((d_gu, both_in, grad_b, dkv))
        d_wgu = ein("td,tf->df", late_in, d_gu).astype(BF16)
        d_wdown = ein("tf,td->fd", inner, both_grad).astype(BF16)
        d_wout = mm(attn_out, late_grad).astype(BF16)
        wout_half = D // 2
        wout_mine = my_half(d_wout[:, :wout_half], d_wout[:, wout_half:])
        wout_theirs = my_half(d_wout[:, wout_half:], d_wout[:, :wout_half])
        d_mlp = [d_wgu, d_wdown.reshape(D, HALF), sum_pair(wout_mine, to_partner(wout_theirs))]
        d_mlp = jnp.concatenate(d_mlp, 1)
        dkv = jnp.sum(over_chips(dkv).astype(F32), 0)
        if layer == 1:
            dkv, d_mlp = lax.optimization_barrier((dkv, d_mlp))
            share1 = lax.psum_scatter(d_mlp, "fsdp", scatter_dimension=0, tiled=True)
        else:
            dkv, d_mlp, share1 = lax.optimization_barrier((dkv, d_mlp, share1))
            parts = send_parts(me, d_mlp)
            share1 = sum_chips(share1)
        turned = jnp.concatenate([dq_t, dkv[0]], 0)
        d_qkv = jnp.concatenate([rotate(turned, cosine, -sine), dkv[1]], 0)
        d_qkv = d_qkv.astype(BF16).reshape(Q_ROWS + KV_ROWS, ROWS)
        d_wqkv = ein("td,et->de", attn_in, d_qkv)
        d_norm = ein("et,de->td", d_qkv, wqkv)
        d_gain_a = jnp.sum(d_norm * unit_a, 0)
        d_hidden = d_hidden + norm_back(d_norm * gains[layer, 0], unit_a, rms_a)
        gain_grads[layer] = jnp.stack([d_gain_a, d_gain_m])
        qkv_grads[layer] = d_wqkv.astype(BF16)
    input_grad = d_hidden.reshape(1, ROWS, D)

    mine, theirs = in_order(*qkv_grads)
    d_gains = jnp.transpose(jnp.stack(gain_grads).reshape(2 * LAYERS, D)).astype(BF16)
    d_wqkv = jnp.concatenate([sum_pair(mine, to_partner(theirs)), d_gains], 1)
    share0 = sum_parts(lax.optimization_barrier((parts, d_wqkv))[0])
    qkv = sum_chips(scatter_fsdp(d_wqkv))
    qkv_p = to_partner(qkv)

    share0 = sum_chips(share0)
    mlp0, mlp0_p, mlp1, mlp1_p = share0, to_partner(share0), share1, to_partner(share1)
    half = Q_ROWS + KV_ROWS
    d_gain = qkv[:, half:].astype(F32) + qkv_p[:, half:].astype(F32)
    gain_grad = jnp.transpose(d_gain).reshape(LAYERS, 2, SHARD)
    qkv_grad, out_proj_grad, gate_up_grad = unpack(
        core.reshape(1), mlp0, mlp0_p, mlp1, mlp1_p, qkv, qkv_p
    )
    down_grad = []
    for own, theirs in ((mlp0, mlp0_p), (mlp1, mlp1_p)):
        rows = [x[:, FF : FF + HALF].reshape(UNITS, D) for x in in_order(own, theirs)]
        down_grad.append(jnp.concatenate(rows, 0))
    down_grad = jnp.stack(down_grad).astype(F32)
    return (output, input_grad, gain_grad, qkv_grad, out_proj_grad, gate_up_grad, down_grad)


def solution(mesh):
    in_specs = (
        P("fsdp", "ctx", None),
        P(),
        P("fsdp", None),
        P(None, None, "fsdp"),
        P(None, "fsdp", None),
        P(None, "fsdp", None),
        P(None, "fsdp", None),
        P(None, "fsdp", None),
        P("fsdp", "ctx", None),
    )
    out_specs = (
        P("fsdp", "ctx", None),
        P("fsdp", "ctx", None),
        P(None, None, "fsdp"),
        P(None, "fsdp", None),
        P(None, "fsdp", None),
        P(None, "fsdp", None),
        P(None, "fsdp", None),
    )
    return jax.shard_map(local, mesh=mesh, in_specs=in_specs, out_specs=out_specs, check_vma=False)
```

```python
import functools

import jax
import jax.numpy as jnp
from jax import lax
from jax.experimental import pallas as pl
from jax.experimental.pallas import tpu as pltpu
from jax.sharding import PartitionSpec as P

D = 576
HEADS = 9
KV_HEADS = 3
GROUP = 3
HEAD_DIM = 64
FF = 1536
LAYERS = 2
BLK = 128
NBLK = 32
EPS = 1e-05
THETA = 100000.0
NEG = -1e30
F32 = jnp.float32
BF16 = jnp.bfloat16
LANES = GROUP * BLK
CTX = 16
FSDP = 8
SHARD = D // FSDP
HALF = FF // 2
Q_ROWS = HEADS * HEAD_DIM
KV_ROWS = 2 * KV_HEADS * HEAD_DIM

PARTNER = [(i, i ^ 1) for i in range(CTX)]
SAME_CORE = [[2 * chip + core for chip in range(CTX // 2)] for core in range(2)]


def to_partner(x):
    return lax.ppermute(x, "ctx", PARTNER)


def over_chips(x):
    return lax.all_to_all(x, "ctx", 0, 0, axis_index_groups=SAME_CORE, tiled=True)


def over_fsdp(x):
    return lax.all_to_all(x, "fsdp", 0, 0, tiled=True)


def gather_fsdp(x):
    return over_fsdp(jnp.broadcast_to(x[None], (FSDP,) + x.shape)).reshape(-1, x.shape[1])


def scatter_fsdp(x):
    parts = over_fsdp(x.reshape(FSDP, -1, x.shape[1]))
    return jnp.sum(parts.astype(F32), 0).astype(BF16)


def sum_pair(a, b):
    return (a.astype(F32) + b.astype(F32)).astype(BF16)


def sum_chips(x):
    for bit in (2, 4, 8):
        x = sum_pair(x, lax.ppermute(x, "ctx", [(i, i ^ bit) for i in range(CTX)]))
    return x


def dot_tn(a, b):
    return lax.dot_general(a, b, (((0,), (0,)), ((), ())), preferred_element_type=F32)


def dot_nt(a, b):
    return lax.dot_general(a, b, (((1,), (1,)), ((), ())), preferred_element_type=F32)


UNROLL_F = 9
UNROLL_B = 3
CHUNK = 4
KEYS = CHUNK * BLK
CHUNKS = NBLK // CHUNK


def fill_keys(sc, own_ref, other_ref, kv_s):
    core = sc[2]
    for chip in range(CTX // 2):
        for half in range(2):
            lanes = slice(half * BLK, (half + 1) * BLK)
            block = sc[7 + 2 * (2 * chip + core) + half]
            kv_s[block] = own_ref[chip, :, 0, :, lanes]
            block = sc[7 + 2 * (2 * chip + 1 - core) + half]
            kv_s[block] = other_ref[chip, :, 0, :, lanes]


def fill_queries(sc, src_ref, dst):
    for half in range(2):
        lanes = slice(half * BLK, (half + 1) * BLK)
        which = jnp.bitwise_xor(half, sc[1])
        dst[which] = jnp.concatenate([src_ref[j, :, lanes] for j in range(GROUP)], axis=1)


def query_rows(sc, which):
    block = jnp.where(which == 0, sc[0], NBLK - 1 - sc[0])
    lane = lax.broadcasted_iota(jnp.int32, (1, LANES), 1)
    pos = block * BLK + jnp.bitwise_and(lane, BLK - 1)
    start = jnp.zeros((1, LANES), jnp.int32)
    for d in range(4):
        start = jnp.where(pos >= sc[3 + d], jnp.maximum(start, sc[3 + d]), start)
    return pos, start


def chunk_of(sc, t):
    high = (NBLK - sc[0] + CHUNK - 1) // CHUNK
    which = (t < high).astype(jnp.int32)
    return which, jnp.where(t < high, t, t - high)


def keys_of(kv_s, chunk, kind):
    return jnp.concatenate([kv_s[chunk * CHUNK + j, kind] for j in range(CHUNK)], axis=1)


def seen(pos_s, which, chunk):
    at = lax.broadcasted_iota(jnp.int32, (KEYS, LANES), 0)
    base = chunk * KEYS
    return (at >= pos_s[which, 1:2] - base) & (at <= pos_s[which, 0:1] - base)


def fill_rows(sc, pos_s):
    for which in range(2):
        pos, start = query_rows(sc, which)
        pos_s[which, 0:1] = pos
        pos_s[which, 1:2] = start


def forward_kernel(sc, q_ref, own_ref, other_ref, o_ref, lse_ref, kv_s, q_s, acc_s, m_s, l_s, pos_s):
    fill_keys(sc, own_ref, other_ref, kv_s)
    fill_queries(sc, q_ref, q_s)
    fill_rows(sc, pos_s)
    acc_s[...] = jnp.zeros_like(acc_s)
    m_s[...] = jnp.full_like(m_s, NEG)
    l_s[...] = jnp.zeros_like(l_s)

    def step(t, carry):
        which, chunk = chunk_of(sc, t)
        scores = dot_tn(keys_of(kv_s, chunk, 0), q_s[which])
        scores = jnp.where(seen(pos_s, which, chunk), scores, NEG)
        old = m_s[which]
        new = jnp.maximum(old, jnp.max(scores, axis=0, keepdims=True))
        prob = jnp.exp(scores - new)
        shrink = jnp.exp(old - new)
        m_s[which] = new
        l_s[which] = l_s[which] * shrink + jnp.sum(prob, axis=0, keepdims=True)
        acc_s[which] = acc_s[which] * shrink + jnp.dot(
            keys_of(kv_s, chunk, 1), prob.astype(BF16), preferred_element_type=F32
        )
        return carry

    lax.fori_loop(0, CHUNKS + 1, step, 0, unroll=UNROLL_F)
    for which in range(2):
        acc_s[which] = acc_s[which] / l_s[which]
        lse_ref[0, which] = m_s[which] + jnp.log(l_s[which])
    for half in range(2):
        mine = acc_s[jnp.bitwise_xor(half, sc[1])]
        for j in range(GROUP):
            o_ref[j, :, half * BLK : (half + 1) * BLK] = mine[:, j * BLK : (j + 1) * BLK]


def backward_kernel(
    sc, q_ref, own_ref, other_ref, o_ref, do_ref, lse_ref,
    dq_ref, down_ref, dother_ref,
    kv_s, q_s, do_s, dq_s, dkv_s, delta_s, pos_s,
):
    fill_keys(sc, own_ref, other_ref, kv_s)
    fill_queries(sc, q_ref, q_s)
    fill_queries(sc, do_ref, do_s)
    fill_queries(sc, o_ref, dq_s)
    fill_rows(sc, pos_s)
    for which in range(2):
        delta_s[which] = jnp.sum(dq_s[which] * do_s[which].astype(F32), axis=0, keepdims=True)
    dq_s[...] = jnp.zeros_like(dq_s)
    dkv_s[...] = jnp.zeros_like(dkv_s)

    def step(t, carry):
        which, chunk = chunk_of(sc, t)
        key_t, val_t, q_t, do_t = keys_of(kv_s, chunk, 0), keys_of(kv_s, chunk, 1), q_s[which], do_s[which]
        scores = dot_tn(key_t, q_t)
        prob = jnp.where(seen(pos_s, which, chunk), jnp.exp(scores - lse_ref[0, which]), 0.0)
        d_prob = dot_tn(val_t, do_t)
        d_score = (prob * (d_prob - delta_s[which])).astype(BF16)
        d_val = dot_nt(do_t, prob.astype(BF16))
        d_key = dot_nt(q_t, d_score)
        dq_s[which] = dq_s[which] + jnp.dot(key_t, d_score, preferred_element_type=F32)
        for j in range(CHUNK):
            lanes = slice(j * BLK, (j + 1) * BLK)
            dkv_s[chunk * CHUNK + j, 0] = dkv_s[chunk * CHUNK + j, 0] + d_key[:, lanes]
            dkv_s[chunk * CHUNK + j, 1] = dkv_s[chunk * CHUNK + j, 1] + d_val[:, lanes]
        return carry

    lax.fori_loop(0, CHUNKS + 1, step, 0, unroll=UNROLL_B)
    core = sc[2]
    scale = HEAD_DIM**-0.5
    for half in range(2):
        lanes = slice(half * BLK, (half + 1) * BLK)
        mine = dq_s[jnp.bitwise_xor(half, sc[1])] * scale
        for j in range(GROUP):
            dq_ref[j, :, lanes] = mine[:, j * BLK : (j + 1) * BLK]
        for chip in range(CTX // 2):
            block = sc[7 + 2 * (2 * chip + core) + half]
            down_ref[chip, :, 0, :, lanes] = dkv_s[block].astype(BF16)
            block = sc[7 + 2 * (2 * chip + 1 - core) + half]
            dother_ref[chip, :, 0, :, lanes] = dkv_s[block].astype(BF16)


ROWS = 2 * BLK
HEAD_SPEC = pl.BlockSpec((GROUP, HEAD_DIM, ROWS), lambda g, sc: (g, 0, 0))
KV_SPEC = pl.BlockSpec((CTX // 2, 2, 1, HEAD_DIM, ROWS), lambda g, sc: (0, 0, g, 0, 0))
LSE_SPEC = pl.BlockSpec((1, 2, 1, LANES), lambda g, sc: (g, 0, 0, 0))
HEAD_SHAPE = jax.ShapeDtypeStruct((HEADS, HEAD_DIM, ROWS), F32)
KV_SHAPE = jax.ShapeDtypeStruct((CTX // 2, 2, KV_HEADS, HEAD_DIM, ROWS), BF16)
LSE_SHAPE = jax.ShapeDtypeStruct((KV_HEADS, 2, 1, LANES), F32)
KERNEL_PARAMS = pltpu.CompilerParams(
    dimension_semantics=("arbitrary",), vmem_limit_bytes=40 * 2**20
)


def attention(scalars, q_t, own, other):
    return pl.pallas_call(
        forward_kernel,
        grid_spec=pltpu.PrefetchScalarGridSpec(
            num_scalar_prefetch=1,
            grid=(KV_HEADS,),
            in_specs=[HEAD_SPEC, KV_SPEC, KV_SPEC],
            out_specs=[HEAD_SPEC, LSE_SPEC],
            scratch_shapes=[
                pltpu.VMEM((NBLK, 2, HEAD_DIM, BLK), BF16),
                pltpu.VMEM((2, HEAD_DIM, LANES), BF16),
                pltpu.VMEM((2, HEAD_DIM, LANES), F32),
                pltpu.VMEM((2, 1, LANES), F32),
                pltpu.VMEM((2, 1, LANES), F32),
                pltpu.VMEM((2, 8, LANES), jnp.int32),
            ],
        ),
        out_shape=[HEAD_SHAPE, LSE_SHAPE],
        compiler_params=KERNEL_PARAMS,
        name="attention",
    )(scalars, q_t, own, other)


def attention_back(scalars, q_t, own, other, o_t, do_t, lse):
    return pl.pallas_call(
        backward_kernel,
        grid_spec=pltpu.PrefetchScalarGridSpec(
            num_scalar_prefetch=1,
            grid=(KV_HEADS,),
            in_specs=[HEAD_SPEC, KV_SPEC, KV_SPEC, HEAD_SPEC, HEAD_SPEC, LSE_SPEC],
            out_specs=[HEAD_SPEC, KV_SPEC, KV_SPEC],
            scratch_shapes=[
                pltpu.VMEM((NBLK, 2, HEAD_DIM, BLK), BF16),
                pltpu.VMEM((2, HEAD_DIM, LANES), BF16),
                pltpu.VMEM((2, HEAD_DIM, LANES), BF16),
                pltpu.VMEM((2, HEAD_DIM, LANES), F32),
                pltpu.VMEM((NBLK, 2, HEAD_DIM, BLK), F32),
                pltpu.VMEM((2, 1, LANES), F32),
                pltpu.VMEM((2, 8, LANES), jnp.int32),
            ],
        ),
        out_shape=[HEAD_SHAPE, KV_SHAPE, KV_SHAPE],
        compiler_params=KERNEL_PARAMS,
        name="attention_back",
    )(scalars, q_t, own, other, o_t, do_t, lse)


VMEM_SPEC = pl.BlockSpec(memory_space=pltpu.VMEM)


def dispatch_kernel(me, x_ref, *outs):
    for dx, out in enumerate(outs):
        for dz in range(2):
            out[dz] = x_ref[jnp.bitwise_xor(me[0], 4 * dz + dx)]


def dispatch(me, x):
    return pl.pallas_call(
        dispatch_kernel,
        grid_spec=pltpu.PrefetchScalarGridSpec(
            num_scalar_prefetch=1,
            grid=(),
            in_specs=[VMEM_SPEC],
            out_specs=[VMEM_SPEC] * 4,
        ),
        out_shape=[jax.ShapeDtypeStruct((2,) + x.shape[1:], BF16)] * 4,
        compiler_params=pltpu.CompilerParams(vmem_limit_bytes=40 * 2**20),
        name="dispatch",
    )(me, x)


def across(x, d):
    return lax.ppermute(x, "fsdp", [(i, i ^ d) for i in range(FSDP)])


def send_parts(me, x):
    parts = dispatch(me, x.reshape(FSDP, -1, x.shape[1]))
    return [parts[0]] + [across(parts[dx], dx) for dx in range(1, 4)]


def sum_parts(parts):
    total = sum(p.astype(F32) for p in parts)
    return (total[0] + across(total[1].astype(BF16), 4).astype(F32)).astype(BF16)


UNITS = FF // FSDP // 2


def unpack_kernel(sc, *refs):
    mlp0, mlp0_p, mlp1, mlp1_p, qkv, qkv_p, qkv_ref, out_ref, gu_ref = refs

    def write(order):
        for layer, pair in enumerate(((mlp0, mlp0_p), (mlp1, mlp1_p))):
            for half, mlp in enumerate(pair[::order]):
                for k in range(2):
                    for i in range(FSDP):
                        src = k * HALF + i * UNITS
                        dst = k * FF + i * 2 * UNITS + half * UNITS
                        gu_ref[layer, :, dst : dst + UNITS] = mlp[:, src : src + UNITS].astype(F32)
                cut = D // 2
                out_ref[layer, :, half * cut : (half + 1) * cut] = (
                    mlp[:, FF + HALF : FF + HALF + cut].astype(F32)
                )
        for layer, src in enumerate((qkv, qkv_p)[::order]):
            qkv_ref[layer] = src[:, : Q_ROWS + KV_ROWS].astype(F32)

    @pl.when(sc[0] == 0)
    def _():
        write(1)

    @pl.when(sc[0] != 0)
    def _():
        write(-1)


def unpack(core, *shares):
    return pl.pallas_call(
        unpack_kernel,
        grid_spec=pltpu.PrefetchScalarGridSpec(
            num_scalar_prefetch=1,
            grid=(),
            in_specs=[VMEM_SPEC] * 6,
            out_specs=[VMEM_SPEC] * 3,
        ),
        out_shape=[
            jax.ShapeDtypeStruct((LAYERS, SHARD, Q_ROWS + KV_ROWS), F32),
            jax.ShapeDtypeStruct((LAYERS, SHARD, D), F32),
            jax.ShapeDtypeStruct((LAYERS, SHARD, 2 * FF), F32),
        ],
        compiler_params=pltpu.CompilerParams(vmem_limit_bytes=40 * 2**20),
        name="unpack",
    )(core, *shares)


def rotate(x, cosine, sine):
    half = HEAD_DIM // 2
    first, second = x[:, :half], x[:, half:]
    return jnp.concatenate([first * cosine - second * sine, second * cosine + first * sine], 1)


def normed(hidden):
    inv_rms = lax.rsqrt(jnp.mean(hidden * hidden, -1, keepdims=True) + EPS)
    return hidden * inv_rms, inv_rms


def norm_back(d_unit, unit, inv_rms):
    return inv_rms * (d_unit - unit * jnp.mean(d_unit * unit, -1, keepdims=True))


def mm(a, b):
    return jnp.dot(a, b, preferred_element_type=F32)


def ein(spec, a, b):
    return jnp.einsum(spec, a, b, preferred_element_type=F32)


def local(tokens, block_order, doc_ids, norm_gains, w_qkv, w_out, w_gate_up, w_down, cotangent):
    place = lax.axis_index("ctx")
    core = jnp.bitwise_and(place, 1)
    first_core = core == 0
    me = lax.axis_index("fsdp").reshape(1)

    def my_half(left, right):
        return jnp.where(first_core, left, right)

    def in_order(own, other):
        return my_half(own, other), my_half(other, own)

    gain_cols = jnp.transpose(norm_gains.reshape(2 * LAYERS, SHARD))
    cut = (Q_ROWS + KV_ROWS + D) // 2

    def wgu_pack(layer):
        wgu = w_gate_up[layer].reshape(SHARD, 2, FSDP, 2, UNITS)
        return my_half(wgu[..., 0, :], wgu[..., 1, :]).reshape(SHARD, FF)

    def wd_pack(layer):
        return my_half(w_down[layer, :UNITS], w_down[layer, UNITS:]).reshape(SHARD, HALF)

    def proj_pack(layer):
        proj = jnp.concatenate([w_qkv[layer], w_out[layer]], 1)
        return my_half(proj[:, :cut], proj[:, cut:])

    first = jnp.concatenate([proj_pack(0), gain_cols], 1)
    first = jnp.broadcast_to(first[None], (FSDP,) + first.shape)
    first, w_gate_up, w_down = lax.optimization_barrier((first, w_gate_up, w_down))
    first = over_fsdp(first).reshape(D, -1)
    pack0 = jnp.concatenate([wgu_pack(0), wd_pack(0)], 1)
    pack0 = lax.all_gather(pack0, "fsdp", axis=0, tiled=True)
    pack1 = lax.all_gather(wgu_pack(1), "fsdp", axis=0, tiled=True)
    gains = jnp.transpose(first[:, cut:].astype(F32)).reshape(LAYERS, 2, D)

    def whole_proj(own):
        return jnp.concatenate(in_order(own, to_partner(own)), 1)

    projs, mlps = [whole_proj(first[:, :cut])], []

    first_block = lax.dynamic_index_in_dim(block_order, 2 * place, 0, keepdims=False)
    low = jnp.minimum(first_block, NBLK - 1 - first_block)
    low_half = (first_block != low).astype(jnp.int32)
    starts = jnp.sum(
        (doc_ids[0][None, :] < jnp.arange(1, 5, dtype=jnp.int32)[:, None]).astype(jnp.int32), 1
    )
    scalars = jnp.concatenate([jnp.stack([low, low_half, core]), starts, block_order])
    lane = jnp.arange(ROWS, dtype=jnp.int32)
    pos = jnp.where(lane < BLK, first_block, NBLK - 2 - first_block) * BLK + lane
    inv_freq = THETA ** (-jnp.arange(HEAD_DIM // 2, dtype=F32) / (HEAD_DIM // 2))
    angles = pos.astype(F32)[None, :] * inv_freq[:, None]
    cosine, sine = jnp.cos(angles), jnp.sin(angles)

    hidden = tokens[0].astype(F32)
    saved = []
    for layer in range(LAYERS):
        wqkv, wout = projs[layer][:, : Q_ROWS + KV_ROWS], projs[layer][:, Q_ROWS + KV_ROWS :]
        unit_a, rms_a = normed(hidden)
        attn_in = (unit_a * gains[layer, 0]).astype(BF16)
        qkv_t = ein("de,td->et", wqkv, attn_in).reshape(-1, HEAD_DIM, ROWS)
        turned = rotate(qkv_t[: HEADS + KV_HEADS], cosine, sine)
        q_t = (turned[:HEADS] * HEAD_DIM**-0.5).astype(BF16)
        kv_t = jnp.concatenate([turned[HEADS:], qkv_t[HEADS + KV_HEADS :]], 0).astype(BF16)
        kv_t = kv_t.reshape(1, 2, KV_HEADS, HEAD_DIM, ROWS)
        kv_own = over_chips(jnp.broadcast_to(kv_t, (CTX // 2,) + kv_t.shape[1:]))
        if layer == 0:
            late = jnp.concatenate([proj_pack(1), wd_pack(1)], 1)
            kv_own, late = lax.optimization_barrier((kv_own, late))
            late = gather_fsdp(late)
        kv_other = to_partner(kv_own)
        o_t, lse = attention(scalars, q_t, kv_own, kv_other)
        if layer == 0:
            o_t, pack0 = lax.optimization_barrier((o_t, pack0))
            mlps.append((pack0[:, :FF], pack0[:, FF:].reshape(HALF, D)))
            projs.append(whole_proj(late[:, :cut]))
        else:
            o_t, pack1 = lax.optimization_barrier((o_t, pack1))
            mlps.append((pack1, late[:, cut:].reshape(HALF, D)))
        attn_out = o_t.astype(BF16).reshape(Q_ROWS, ROWS)
        mid = hidden + ein("at,ad->td", attn_out, wout)
        unit_m, rms_m = normed(mid)
        mlp_in = (unit_m * gains[layer, 1]).astype(BF16)
        wgu, wdown = mlps[layer]
        both_in = jnp.concatenate([mlp_in, to_partner(mlp_in)], 0)
        gate_up = mm(both_in, wgu)
        inner = (jax.nn.silu(gate_up[:, :HALF]) * gate_up[:, HALF:]).astype(BF16)
        part = mm(inner, wdown)
        hidden = mid + part[:ROWS] + to_partner(part[ROWS:].astype(BF16)).astype(F32)
        saved.append(
            (wqkv, wout, unit_a, rms_a, attn_in, q_t, kv_own, kv_other, o_t, lse, attn_out,
             unit_m, rms_m, both_in, gate_up, inner, wgu, wdown)
        )
    output = hidden.astype(BF16).reshape(1, ROWS, D)

    d_hidden = cotangent[0].astype(F32)
    gain_grads, qkv_grads = [None] * LAYERS, [None] * LAYERS
    for layer in reversed(range(LAYERS)):
        (wqkv, wout, unit_a, rms_a, attn_in, q_t, kv_own, kv_other, o_t, lse, attn_out,
         unit_m, rms_m, both_in, gate_up, inner, wgu, wdown) = saved[layer]
        grad_b = d_hidden.astype(BF16)
        both_grad = jnp.concatenate([grad_b, to_partner(grad_b)], 0)
        d_inner = ein("td,fd->tf", both_grad, wdown)
        gate, up = gate_up[:, :HALF], gate_up[:, HALF:]
        sig = jax.nn.sigmoid(gate)
        d_gate = d_inner * up * sig * (1.0 + gate * (1.0 - sig))
        d_up = d_inner * (gate * sig)
        d_gu = jnp.concatenate([d_gate, d_up], 1).astype(BF16)
        part = ein("tf,df->td", d_gu, wgu)
        d_norm = part[:ROWS] + to_partner(part[ROWS:].astype(BF16)).astype(F32)
        d_gain_m = jnp.sum(d_norm * unit_m, 0)
        d_hidden = d_hidden + norm_back(d_norm * gains[layer, 1], unit_m, rms_m)
        grad_b = d_hidden.astype(BF16)
        do_t = ein("ad,td->at", wout, grad_b).astype(BF16).reshape(HEADS, HEAD_DIM, ROWS)
        dq_t, dkv_own, dkv_other = attention_back(scalars, q_t, kv_own, kv_other, o_t, do_t, lse)
        dkv = (dkv_own.astype(F32) + to_partner(dkv_other).astype(F32)).astype(BF16)
        d_gu, late_in, late_grad, _ = lax.optimization_barrier((d_gu, both_in, grad_b, dkv))
        d_wgu = ein("td,tf->df", late_in, d_gu).astype(BF16)
        d_wdown = ein("tf,td->fd", inner, both_grad).astype(BF16)
        d_wout = mm(attn_out, late_grad).astype(BF16)
        wout_half = D // 2
        wout_mine = my_half(d_wout[:, :wout_half], d_wout[:, wout_half:])
        wout_theirs = my_half(d_wout[:, wout_half:], d_wout[:, :wout_half])
        d_mlp = [d_wgu, d_wdown.reshape(D, HALF), sum_pair(wout_mine, to_partner(wout_theirs))]
        d_mlp = jnp.concatenate(d_mlp, 1)
        if layer == 0:
            share1 = sum_chips(sum_parts(lax.optimization_barrier((parts, dkv))[0]))
        dkv = jnp.sum(over_chips(dkv).astype(F32), 0)
        dkv, d_mlp = lax.optimization_barrier((dkv, d_mlp))
        parts = send_parts(me, d_mlp)
        turned = jnp.concatenate([dq_t, dkv[0]], 0)
        d_qkv = jnp.concatenate([rotate(turned, cosine, -sine), dkv[1]], 0)
        d_qkv = d_qkv.astype(BF16).reshape(Q_ROWS + KV_ROWS, ROWS)
        d_wqkv = ein("td,et->de", attn_in, d_qkv)
        d_norm = ein("et,de->td", d_qkv, wqkv)
        d_gain_a = jnp.sum(d_norm * unit_a, 0)
        d_hidden = d_hidden + norm_back(d_norm * gains[layer, 0], unit_a, rms_a)
        gain_grads[layer] = jnp.stack([d_gain_a, d_gain_m])
        qkv_grads[layer] = d_wqkv.astype(BF16)
    input_grad = d_hidden.reshape(1, ROWS, D)

    mine, theirs = in_order(*qkv_grads)
    d_gains = jnp.transpose(jnp.stack(gain_grads).reshape(2 * LAYERS, D)).astype(BF16)
    d_wqkv = jnp.concatenate([sum_pair(mine, to_partner(theirs)), d_gains], 1)
    qkv = scatter_fsdp(d_wqkv)
    share0 = sum_parts(lax.optimization_barrier((parts, qkv))[0])
    qkv = sum_chips(qkv)
    qkv_p = to_partner(qkv)

    share0 = sum_chips(share0)
    mlp0, mlp0_p, mlp1, mlp1_p = share0, to_partner(share0), share1, to_partner(share1)
    half = Q_ROWS + KV_ROWS
    d_gain = qkv[:, half:].astype(F32) + qkv_p[:, half:].astype(F32)
    gain_grad = jnp.transpose(d_gain).reshape(LAYERS, 2, SHARD)
    qkv_grad, out_proj_grad, gate_up_grad = unpack(
        core.reshape(1), mlp0, mlp0_p, mlp1, mlp1_p, qkv, qkv_p
    )
    down_grad = []
    for own, theirs in ((mlp0, mlp0_p), (mlp1, mlp1_p)):
        rows = [x[:, FF : FF + HALF].reshape(UNITS, D) for x in in_order(own, theirs)]
        down_grad.append(jnp.concatenate(rows, 0))
    down_grad = jnp.stack(down_grad).astype(F32)
    return (output, input_grad, gain_grad, qkv_grad, out_proj_grad, gate_up_grad, down_grad)


def solution(mesh):
    in_specs = (
        P("fsdp", "ctx", None),
        P(),
        P("fsdp", None),
        P(None, None, "fsdp"),
        P(None, "fsdp", None),
        P(None, "fsdp", None),
        P(None, "fsdp", None),
        P(None, "fsdp", None),
        P("fsdp", "ctx", None),
    )
    out_specs = (
        P("fsdp", "ctx", None),
        P("fsdp", "ctx", None),
        P(None, None, "fsdp"),
        P(None, "fsdp", None),
        P(None, "fsdp", None),
        P(None, "fsdp", None),
        P(None, "fsdp", None),
    )
    return jax.shard_map(local, mesh=mesh, in_specs=in_specs, out_specs=out_specs, check_vma=False)
```

```python
import functools

import jax
import jax.numpy as jnp
from jax import lax
from jax.experimental import pallas as pl
from jax.experimental.pallas import tpu as pltpu
from jax.sharding import PartitionSpec as P

D = 576
HEADS = 9
KV_HEADS = 3
GROUP = 3
HEAD_DIM = 64
FF = 1536
LAYERS = 2
BLK = 128
NBLK = 32
EPS = 1e-05
THETA = 100000.0
NEG = -1e30
F32 = jnp.float32
BF16 = jnp.bfloat16
LANES = GROUP * BLK
CTX = 16
FSDP = 8
SHARD = D // FSDP
HALF = FF // 2
Q_ROWS = HEADS * HEAD_DIM
KV_ROWS = 2 * KV_HEADS * HEAD_DIM

PARTNER = [(i, i ^ 1) for i in range(CTX)]
SAME_CORE = [[2 * chip + core for chip in range(CTX // 2)] for core in range(2)]


def to_partner(x):
    return lax.ppermute(x, "ctx", PARTNER)


def over_chips(x):
    return lax.all_to_all(x, "ctx", 0, 0, axis_index_groups=SAME_CORE, tiled=True)


def over_fsdp(x):
    return lax.all_to_all(x, "fsdp", 0, 0, tiled=True)


def gather_fsdp(x):
    return over_fsdp(jnp.broadcast_to(x[None], (FSDP,) + x.shape)).reshape(-1, x.shape[1])


def scatter_fsdp(x):
    parts = over_fsdp(x.reshape(FSDP, -1, x.shape[1]))
    return jnp.sum(parts.astype(F32), 0).astype(BF16)


def sum_pair(a, b):
    return (a.astype(F32) + b.astype(F32)).astype(BF16)


def sum_chips(x):
    for bit in (2, 4, 8):
        x = sum_pair(x, lax.ppermute(x, "ctx", [(i, i ^ bit) for i in range(CTX)]))
    return x


def dot_tn(a, b):
    return lax.dot_general(a, b, (((0,), (0,)), ((), ())), preferred_element_type=F32)


def dot_nt(a, b):
    return lax.dot_general(a, b, (((1,), (1,)), ((), ())), preferred_element_type=F32)


UNROLL_F = 9
UNROLL_B = 3
CHUNK = 4
KEYS = CHUNK * BLK
CHUNKS = NBLK // CHUNK


def fill_keys(sc, own_ref, other_ref, kv_s):
    core = sc[2]
    for chip in range(CTX // 2):
        for half in range(2):
            lanes = slice(half * BLK, (half + 1) * BLK)
            block = sc[7 + 2 * (2 * chip + core) + half]
            kv_s[block] = own_ref[chip, :, 0, :, lanes]
            block = sc[7 + 2 * (2 * chip + 1 - core) + half]
            kv_s[block] = other_ref[chip, :, 0, :, lanes]


def fill_queries(sc, src_ref, dst):
    for half in range(2):
        lanes = slice(half * BLK, (half + 1) * BLK)
        which = jnp.bitwise_xor(half, sc[1])
        dst[which] = jnp.concatenate([src_ref[j, :, lanes] for j in range(GROUP)], axis=1)


def query_rows(sc, which):
    block = jnp.where(which == 0, sc[0], NBLK - 1 - sc[0])
    lane = lax.broadcasted_iota(jnp.int32, (1, LANES), 1)
    pos = block * BLK + jnp.bitwise_and(lane, BLK - 1)
    start = jnp.zeros((1, LANES), jnp.int32)
    for d in range(4):
        start = jnp.where(pos >= sc[3 + d], jnp.maximum(start, sc[3 + d]), start)
    return pos, start


def chunk_of(sc, t):
    high = (NBLK - sc[0] + CHUNK - 1) // CHUNK
    which = (t < high).astype(jnp.int32)
    return which, jnp.where(t < high, t, t - high)


def keys_of(kv_s, chunk, kind):
    return jnp.concatenate([kv_s[chunk * CHUNK + j, kind] for j in range(CHUNK)], axis=1)


def seen(pos_s, which, chunk):
    at = lax.broadcasted_iota(jnp.int32, (KEYS, LANES), 0)
    base = chunk * KEYS
    return (at >= pos_s[which, 1:2] - base) & (at <= pos_s[which, 0:1] - base)


def fill_rows(sc, pos_s):
    for which in range(2):
        pos, start = query_rows(sc, which)
        pos_s[which, 0:1] = pos
        pos_s[which, 1:2] = start


def forward_kernel(sc, q_ref, own_ref, other_ref, o_ref, lse_ref, kv_s, q_s, acc_s, m_s, l_s, pos_s):
    fill_keys(sc, own_ref, other_ref, kv_s)
    fill_queries(sc, q_ref, q_s)
    fill_rows(sc, pos_s)
    acc_s[...] = jnp.zeros_like(acc_s)
    m_s[...] = jnp.full_like(m_s, NEG)
    l_s[...] = jnp.zeros_like(l_s)

    def step(t, carry):
        which, chunk = chunk_of(sc, t)
        scores = dot_tn(keys_of(kv_s, chunk, 0), q_s[which])
        scores = jnp.where(seen(pos_s, which, chunk), scores, NEG)
        old = m_s[which]
        new = jnp.maximum(old, jnp.max(scores, axis=0, keepdims=True))
        prob = jnp.exp(scores - new)
        shrink = jnp.exp(old - new)
        m_s[which] = new
        l_s[which] = l_s[which] * shrink + jnp.sum(prob, axis=0, keepdims=True)
        acc_s[which] = acc_s[which] * shrink + jnp.dot(
            keys_of(kv_s, chunk, 1), prob.astype(BF16), preferred_element_type=F32
        )
        return carry

    lax.fori_loop(0, CHUNKS + 1, step, 0, unroll=UNROLL_F)
    for which in range(2):
        acc_s[which] = acc_s[which] / l_s[which]
        lse_ref[0, which] = m_s[which] + jnp.log(l_s[which])
    for half in range(2):
        mine = acc_s[jnp.bitwise_xor(half, sc[1])]
        for j in range(GROUP):
            o_ref[j, :, half * BLK : (half + 1) * BLK] = mine[:, j * BLK : (j + 1) * BLK]


def backward_kernel(
    sc, q_ref, own_ref, other_ref, o_ref, do_ref, lse_ref,
    dq_ref, down_ref, dother_ref,
    kv_s, q_s, do_s, dq_s, dkv_s, delta_s, pos_s,
):
    fill_keys(sc, own_ref, other_ref, kv_s)
    fill_queries(sc, q_ref, q_s)
    fill_queries(sc, do_ref, do_s)
    fill_queries(sc, o_ref, dq_s)
    fill_rows(sc, pos_s)
    for which in range(2):
        delta_s[which] = jnp.sum(dq_s[which] * do_s[which].astype(F32), axis=0, keepdims=True)
    dq_s[...] = jnp.zeros_like(dq_s)
    dkv_s[...] = jnp.zeros_like(dkv_s)

    def step(t, carry):
        which, chunk = chunk_of(sc, t)
        key_t, val_t, q_t, do_t = keys_of(kv_s, chunk, 0), keys_of(kv_s, chunk, 1), q_s[which], do_s[which]
        scores = dot_tn(key_t, q_t)
        prob = jnp.where(seen(pos_s, which, chunk), jnp.exp(scores - lse_ref[0, which]), 0.0)
        d_prob = dot_tn(val_t, do_t)
        d_score = (prob * (d_prob - delta_s[which])).astype(BF16)
        d_val = dot_nt(do_t, prob.astype(BF16))
        d_key = dot_nt(q_t, d_score)
        dq_s[which] = dq_s[which] + jnp.dot(key_t, d_score, preferred_element_type=F32)
        for j in range(CHUNK):
            lanes = slice(j * BLK, (j + 1) * BLK)
            dkv_s[chunk * CHUNK + j, 0] = dkv_s[chunk * CHUNK + j, 0] + d_key[:, lanes]
            dkv_s[chunk * CHUNK + j, 1] = dkv_s[chunk * CHUNK + j, 1] + d_val[:, lanes]
        return carry

    lax.fori_loop(0, CHUNKS + 1, step, 0, unroll=UNROLL_B)
    core = sc[2]
    scale = HEAD_DIM**-0.5
    for half in range(2):
        lanes = slice(half * BLK, (half + 1) * BLK)
        mine = dq_s[jnp.bitwise_xor(half, sc[1])] * scale
        for j in range(GROUP):
            dq_ref[j, :, lanes] = mine[:, j * BLK : (j + 1) * BLK]
        for chip in range(CTX // 2):
            block = sc[7 + 2 * (2 * chip + core) + half]
            down_ref[chip, :, 0, :, lanes] = dkv_s[block].astype(BF16)
            block = sc[7 + 2 * (2 * chip + 1 - core) + half]
            dother_ref[chip, :, 0, :, lanes] = dkv_s[block].astype(BF16)


ROWS = 2 * BLK
HEAD_SPEC = pl.BlockSpec((GROUP, HEAD_DIM, ROWS), lambda g, sc: (g, 0, 0))
KV_SPEC = pl.BlockSpec((CTX // 2, 2, 1, HEAD_DIM, ROWS), lambda g, sc: (0, 0, g, 0, 0))
LSE_SPEC = pl.BlockSpec((1, 2, 1, LANES), lambda g, sc: (g, 0, 0, 0))
HEAD_SHAPE = jax.ShapeDtypeStruct((HEADS, HEAD_DIM, ROWS), F32)
KV_SHAPE = jax.ShapeDtypeStruct((CTX // 2, 2, KV_HEADS, HEAD_DIM, ROWS), BF16)
LSE_SHAPE = jax.ShapeDtypeStruct((KV_HEADS, 2, 1, LANES), F32)
KERNEL_PARAMS = pltpu.CompilerParams(
    dimension_semantics=("arbitrary",), vmem_limit_bytes=40 * 2**20
)


def attention(scalars, q_t, own, other):
    return pl.pallas_call(
        forward_kernel,
        grid_spec=pltpu.PrefetchScalarGridSpec(
            num_scalar_prefetch=1,
            grid=(KV_HEADS,),
            in_specs=[HEAD_SPEC, KV_SPEC, KV_SPEC],
            out_specs=[HEAD_SPEC, LSE_SPEC],
            scratch_shapes=[
                pltpu.VMEM((NBLK, 2, HEAD_DIM, BLK), BF16),
                pltpu.VMEM((2, HEAD_DIM, LANES), BF16),
                pltpu.VMEM((2, HEAD_DIM, LANES), F32),
                pltpu.VMEM((2, 1, LANES), F32),
                pltpu.VMEM((2, 1, LANES), F32),
                pltpu.VMEM((2, 8, LANES), jnp.int32),
            ],
        ),
        out_shape=[HEAD_SHAPE, LSE_SHAPE],
        compiler_params=KERNEL_PARAMS,
        name="attention",
    )(scalars, q_t, own, other)


def attention_back(scalars, q_t, own, other, o_t, do_t, lse):
    return pl.pallas_call(
        backward_kernel,
        grid_spec=pltpu.PrefetchScalarGridSpec(
            num_scalar_prefetch=1,
            grid=(KV_HEADS,),
            in_specs=[HEAD_SPEC, KV_SPEC, KV_SPEC, HEAD_SPEC, HEAD_SPEC, LSE_SPEC],
            out_specs=[HEAD_SPEC, KV_SPEC, KV_SPEC],
            scratch_shapes=[
                pltpu.VMEM((NBLK, 2, HEAD_DIM, BLK), BF16),
                pltpu.VMEM((2, HEAD_DIM, LANES), BF16),
                pltpu.VMEM((2, HEAD_DIM, LANES), BF16),
                pltpu.VMEM((2, HEAD_DIM, LANES), F32),
                pltpu.VMEM((NBLK, 2, HEAD_DIM, BLK), F32),
                pltpu.VMEM((2, 1, LANES), F32),
                pltpu.VMEM((2, 8, LANES), jnp.int32),
            ],
        ),
        out_shape=[HEAD_SHAPE, KV_SHAPE, KV_SHAPE],
        compiler_params=KERNEL_PARAMS,
        cost_estimate=pl.CostEstimate(
            flops=10 * 36 * BLK * HEADS * BLK * 256, transcendentals=36 * BLK * HEADS * BLK, bytes_accessed=75 * 10**6
        ),
        name="attention_back",
    )(scalars, q_t, own, other, o_t, do_t, lse)


VMEM_SPEC = pl.BlockSpec(memory_space=pltpu.VMEM)


def dispatch_kernel(me, x_ref, *outs):
    for dx, out in enumerate(outs):
        for dz in range(2):
            out[dz] = x_ref[jnp.bitwise_xor(me[0], 4 * dz + dx)]


def dispatch(me, x):
    return pl.pallas_call(
        dispatch_kernel,
        grid_spec=pltpu.PrefetchScalarGridSpec(
            num_scalar_prefetch=1,
            grid=(),
            in_specs=[VMEM_SPEC],
            out_specs=[VMEM_SPEC] * 4,
        ),
        out_shape=[jax.ShapeDtypeStruct((2,) + x.shape[1:], BF16)] * 4,
        compiler_params=pltpu.CompilerParams(vmem_limit_bytes=40 * 2**20),
        name="dispatch",
    )(me, x)


def across(x, d):
    return lax.ppermute(x, "fsdp", [(i, i ^ d) for i in range(FSDP)])


def send_parts(pieces):
    return [pieces[0]] + [across(pieces[dx], dx) for dx in range(1, 4)]


def sum_parts(parts):
    total = sum(p.astype(F32) for p in parts)
    return (total[0] + across(total[1].astype(BF16), 4).astype(F32)).astype(BF16)


UNITS = FF // FSDP // 2


def unpack_kernel(sc, *refs):
    mlp0, mlp0_p, mlp1, mlp1_p, qkv, qkv_p, qkv_ref, out_ref, gu_ref = refs

    def write(order):
        for layer, pair in enumerate(((mlp0, mlp0_p), (mlp1, mlp1_p))):
            for half, mlp in enumerate(pair[::order]):
                for k in range(2):
                    for i in range(FSDP):
                        src = k * HALF + i * UNITS
                        dst = k * FF + i * 2 * UNITS + half * UNITS
                        gu_ref[layer, :, dst : dst + UNITS] = mlp[:, src : src + UNITS].astype(F32)
                cut = D // 2
                out_ref[layer, :, half * cut : (half + 1) * cut] = (
                    mlp[:, FF + HALF : FF + HALF + cut].astype(F32)
                )
        for layer, src in enumerate((qkv, qkv_p)[::order]):
            qkv_ref[layer] = src[:, : Q_ROWS + KV_ROWS].astype(F32)

    @pl.when(sc[0] == 0)
    def _():
        write(1)

    @pl.when(sc[0] != 0)
    def _():
        write(-1)


def unpack(core, *shares):
    return pl.pallas_call(
        unpack_kernel,
        grid_spec=pltpu.PrefetchScalarGridSpec(
            num_scalar_prefetch=1,
            grid=(),
            in_specs=[VMEM_SPEC] * 6,
            out_specs=[VMEM_SPEC] * 3,
        ),
        out_shape=[
            jax.ShapeDtypeStruct((LAYERS, SHARD, Q_ROWS + KV_ROWS), F32),
            jax.ShapeDtypeStruct((LAYERS, SHARD, D), F32),
            jax.ShapeDtypeStruct((LAYERS, SHARD, 2 * FF), F32),
        ],
        compiler_params=pltpu.CompilerParams(vmem_limit_bytes=40 * 2**20),
        name="unpack",
    )(core, *shares)


def rotate(x, cosine, sine):
    half = HEAD_DIM // 2
    first, second = x[:, :half], x[:, half:]
    return jnp.concatenate([first * cosine - second * sine, second * cosine + first * sine], 1)


def normed(hidden):
    inv_rms = lax.rsqrt(jnp.mean(hidden * hidden, -1, keepdims=True) + EPS)
    return hidden * inv_rms, inv_rms


def norm_back(d_unit, unit, inv_rms):
    return inv_rms * (d_unit - unit * jnp.mean(d_unit * unit, -1, keepdims=True))


def mm(a, b):
    return jnp.dot(a, b, preferred_element_type=F32)


def ein(spec, a, b):
    return jnp.einsum(spec, a, b, preferred_element_type=F32)


def local(tokens, block_order, doc_ids, norm_gains, w_qkv, w_out, w_gate_up, w_down, cotangent):
    place = lax.axis_index("ctx")
    core = jnp.bitwise_and(place, 1)
    first_core = core == 0
    me = lax.axis_index("fsdp").reshape(1)

    def my_half(left, right):
        return jnp.where(first_core, left, right)

    def in_order(own, other):
        return my_half(own, other), my_half(other, own)

    gain_cols = jnp.transpose(norm_gains.reshape(2 * LAYERS, SHARD))
    cut = (Q_ROWS + KV_ROWS + D) // 2

    def wgu_pack(layer):
        wgu = w_gate_up[layer].reshape(SHARD, 2, FSDP, 2, UNITS)
        return my_half(wgu[..., 0, :], wgu[..., 1, :]).reshape(SHARD, FF)

    def wd_pack(layer):
        return my_half(w_down[layer, :UNITS], w_down[layer, UNITS:]).reshape(SHARD, HALF)

    def proj_pack(layer):
        proj = jnp.concatenate([w_qkv[layer], w_out[layer]], 1)
        return my_half(proj[:, :cut], proj[:, cut:])

    first = jnp.concatenate([proj_pack(0), gain_cols], 1)
    first = jnp.broadcast_to(first[None], (FSDP,) + first.shape)
    first, w_gate_up, w_down = lax.optimization_barrier((first, w_gate_up, w_down))
    first = over_fsdp(first).reshape(D, -1)
    pack0 = jnp.concatenate([wgu_pack(0), wd_pack(0)], 1)
    pack0 = lax.all_gather(pack0, "fsdp", axis=0, tiled=True)
    pack1 = lax.all_gather(wgu_pack(1), "fsdp", axis=0, tiled=True)
    gains = jnp.transpose(first[:, cut:].astype(F32)).reshape(LAYERS, 2, D)

    def whole_proj(own):
        return jnp.concatenate(in_order(own, to_partner(own)), 1)

    projs, mlps = [whole_proj(first[:, :cut])], []

    first_block = lax.dynamic_index_in_dim(block_order, 2 * place, 0, keepdims=False)
    low = jnp.minimum(first_block, NBLK - 1 - first_block)
    low_half = (first_block != low).astype(jnp.int32)
    starts = jnp.sum(
        (doc_ids[0][None, :] < jnp.arange(1, 5, dtype=jnp.int32)[:, None]).astype(jnp.int32), 1
    )
    scalars = jnp.concatenate([jnp.stack([low, low_half, core]), starts, block_order])
    lane = jnp.arange(ROWS, dtype=jnp.int32)
    pos = jnp.where(lane < BLK, first_block, NBLK - 2 - first_block) * BLK + lane
    inv_freq = THETA ** (-jnp.arange(HEAD_DIM // 2, dtype=F32) / (HEAD_DIM // 2))
    angles = pos.astype(F32)[None, :] * inv_freq[:, None]
    cosine, sine = jnp.cos(angles), jnp.sin(angles)

    hidden = tokens[0].astype(F32)
    saved = []
    for layer in range(LAYERS):
        wqkv, wout = projs[layer][:, : Q_ROWS + KV_ROWS], projs[layer][:, Q_ROWS + KV_ROWS :]
        unit_a, rms_a = normed(hidden)
        attn_in = (unit_a * gains[layer, 0]).astype(BF16)
        qkv_t = ein("de,td->et", wqkv, attn_in).reshape(-1, HEAD_DIM, ROWS)
        turned = rotate(qkv_t[: HEADS + KV_HEADS], cosine, sine)
        q_t = (turned[:HEADS] * HEAD_DIM**-0.5).astype(BF16)
        kv_t = jnp.concatenate([turned[HEADS:], qkv_t[HEADS + KV_HEADS :]], 0).astype(BF16)
        kv_t = kv_t.reshape(1, 2, KV_HEADS, HEAD_DIM, ROWS)
        kv_own = over_chips(jnp.broadcast_to(kv_t, (CTX // 2,) + kv_t.shape[1:]))
        if layer == 0:
            late = jnp.concatenate([proj_pack(1), wd_pack(1)], 1)
            kv_own, late = lax.optimization_barrier((kv_own, late))
            late = gather_fsdp(late)
        kv_other = to_partner(kv_own)
        o_t, lse = attention(scalars, q_t, kv_own, kv_other)
        if layer == 0:
            o_t, pack0 = lax.optimization_barrier((o_t, pack0))
            mlps.append((pack0[:, :FF], pack0[:, FF:].reshape(HALF, D)))
            projs.append(whole_proj(late[:, :cut]))
        else:
            o_t, pack1 = lax.optimization_barrier((o_t, pack1))
            mlps.append((pack1, late[:, cut:].reshape(HALF, D)))
        attn_out = o_t.astype(BF16).reshape(Q_ROWS, ROWS)
        mid = hidden + ein("at,ad->td", attn_out, wout)
        unit_m, rms_m = normed(mid)
        mlp_in = (unit_m * gains[layer, 1]).astype(BF16)
        wgu, wdown = mlps[layer]
        both_in = jnp.concatenate([mlp_in, to_partner(mlp_in)], 0)
        gate_up = mm(both_in, wgu)
        inner = (jax.nn.silu(gate_up[:, :HALF]) * gate_up[:, HALF:]).astype(BF16)
        part = mm(inner, wdown)
        hidden = mid + part[:ROWS] + to_partner(part[ROWS:].astype(BF16)).astype(F32)
        saved.append(
            (wqkv, wout, unit_a, rms_a, attn_in, q_t, kv_own, kv_other, o_t, lse, attn_out,
             unit_m, rms_m, both_in, gate_up, inner, wgu, wdown)
        )
    output = hidden.astype(BF16).reshape(1, ROWS, D)

    def weight_grads(d_gu, both_in, inner, both_grad, attn_out, grad_b):
        d_wgu = ein("td,tf->df", both_in, d_gu).astype(BF16)
        d_wdown = ein("tf,td->fd", inner, both_grad).astype(BF16)
        d_wout = mm(attn_out, grad_b).astype(BF16)
        left, right = d_wout[:, : D // 2], d_wout[:, D // 2 :]
        d_wout = sum_pair(my_half(left, right), to_partner(my_half(right, left)))
        grads = jnp.concatenate([d_wgu, d_wdown.reshape(D, HALF), d_wout], 1)
        return dispatch(me, grads.reshape(FSDP, SHARD, -1))

    d_hidden = cotangent[0].astype(F32)
    gain_grads, qkv_grads = [None] * LAYERS, [None] * LAYERS
    for layer in reversed(range(LAYERS)):
        (wqkv, wout, unit_a, rms_a, attn_in, q_t, kv_own, kv_other, o_t, lse, attn_out,
         unit_m, rms_m, both_in, gate_up, inner, wgu, wdown) = saved[layer]
        grad_b = d_hidden.astype(BF16)
        both_grad = jnp.concatenate([grad_b, to_partner(grad_b)], 0)
        d_inner = ein("td,fd->tf", both_grad, wdown)
        gate, up = gate_up[:, :HALF], gate_up[:, HALF:]
        sig = jax.nn.sigmoid(gate)
        d_gate = d_inner * up * sig * (1.0 + gate * (1.0 - sig))
        d_up = d_inner * (gate * sig)
        d_gu = jnp.concatenate([d_gate, d_up], 1).astype(BF16)
        part = ein("tf,df->td", d_gu, wgu)
        d_norm = part[:ROWS] + to_partner(part[ROWS:].astype(BF16)).astype(F32)
        d_gain_m = jnp.sum(d_norm * unit_m, 0)
        d_hidden = d_hidden + norm_back(d_norm * gains[layer, 1], unit_m, rms_m)
        grad_b = d_hidden.astype(BF16)
        do_t = ein("ad,td->at", wout, grad_b).astype(BF16).reshape(HEADS, HEAD_DIM, ROWS)
        if layer == 0:
            pieces = weight_grads(d_gu, both_in, inner, both_grad, attn_out, grad_b)
            share1 = sum_parts(parts)
            do_t, share1, pieces = lax.optimization_barrier((do_t, share1, pieces))
            parts = send_parts(pieces)
        dq_t, dkv_own, dkv_other = attention_back(scalars, q_t, kv_own, kv_other, o_t, do_t, lse)
        dkv = (dkv_own.astype(F32) + to_partner(dkv_other).astype(F32)).astype(BF16)
        if layer == 1:
            late = (d_gu, both_in, inner, both_grad, attn_out, grad_b)
            pieces = weight_grads(*lax.optimization_barrier((late, dkv))[0])
        else:
            share1 = sum_chips(lax.optimization_barrier((share1, dkv))[0])
        dkv = jnp.sum(over_chips(dkv).astype(F32), 0)
        if layer == 1:
            dkv, pieces = lax.optimization_barrier((dkv, pieces))
            parts = send_parts(pieces)
        else:
            share0 = sum_parts(lax.optimization_barrier((parts, dkv))[0])
        turned = jnp.concatenate([dq_t, dkv[0]], 0)
        d_qkv = jnp.concatenate([rotate(turned, cosine, -sine), dkv[1]], 0)
        d_qkv = d_qkv.astype(BF16).reshape(Q_ROWS + KV_ROWS, ROWS)
        d_wqkv = ein("td,et->de", attn_in, d_qkv)
        d_norm = ein("et,de->td", d_qkv, wqkv)
        d_gain_a = jnp.sum(d_norm * unit_a, 0)
        d_hidden = d_hidden + norm_back(d_norm * gains[layer, 0], unit_a, rms_a)
        gain_grads[layer] = jnp.stack([d_gain_a, d_gain_m])
        qkv_grads[layer] = d_wqkv.astype(BF16)
    input_grad = d_hidden.reshape(1, ROWS, D)

    mine, theirs = in_order(*qkv_grads)
    d_gains = jnp.transpose(jnp.stack(gain_grads).reshape(2 * LAYERS, D)).astype(BF16)
    d_wqkv = jnp.concatenate([sum_pair(mine, to_partner(theirs)), d_gains], 1)
    qkv = sum_chips(scatter_fsdp(d_wqkv))
    qkv_p = to_partner(qkv)

    share0 = sum_chips(share0)
    mlp0, mlp0_p, mlp1, mlp1_p = share0, to_partner(share0), share1, to_partner(share1)
    half = Q_ROWS + KV_ROWS
    d_gain = qkv[:, half:].astype(F32) + qkv_p[:, half:].astype(F32)
    gain_grad = jnp.transpose(d_gain).reshape(LAYERS, 2, SHARD)
    qkv_grad, out_proj_grad, gate_up_grad = unpack(
        core.reshape(1), mlp0, mlp0_p, mlp1, mlp1_p, qkv, qkv_p
    )
    down_grad = []
    for own, theirs in ((mlp0, mlp0_p), (mlp1, mlp1_p)):
        rows = [x[:, FF : FF + HALF].reshape(UNITS, D) for x in in_order(own, theirs)]
        down_grad.append(jnp.concatenate(rows, 0))
    down_grad = jnp.stack(down_grad).astype(F32)
    return (output, input_grad, gain_grad, qkv_grad, out_proj_grad, gate_up_grad, down_grad)


def solution(mesh):
    in_specs = (
        P("fsdp", "ctx", None),
        P(),
        P("fsdp", None),
        P(None, None, "fsdp"),
        P(None, "fsdp", None),
        P(None, "fsdp", None),
        P(None, "fsdp", None),
        P(None, "fsdp", None),
        P("fsdp", "ctx", None),
    )
    out_specs = (
        P("fsdp", "ctx", None),
        P("fsdp", "ctx", None),
        P(None, None, "fsdp"),
        P(None, "fsdp", None),
        P(None, "fsdp", None),
        P(None, "fsdp", None),
        P(None, "fsdp", None),
    )
    return jax.shard_map(local, mesh=mesh, in_specs=in_specs, out_specs=out_specs, check_vma=False)
```

```python
import functools

import jax
import jax.numpy as jnp
from jax import lax
from jax.experimental import pallas as pl
from jax.experimental.pallas import tpu as pltpu
from jax.sharding import PartitionSpec as P

D = 576
HEADS = 9
KV_HEADS = 3
GROUP = 3
HEAD_DIM = 64
FF = 1536
LAYERS = 2
BLK = 128
NBLK = 32
EPS = 1e-05
THETA = 100000.0
NEG = -1e30
F32 = jnp.float32
BF16 = jnp.bfloat16
LANES = GROUP * BLK
CTX = 16
FSDP = 8
SHARD = D // FSDP
HALF = FF // 2
Q_ROWS = HEADS * HEAD_DIM
KV_ROWS = 2 * KV_HEADS * HEAD_DIM

PARTNER = [(i, i ^ 1) for i in range(CTX)]
SAME_CORE = [[2 * chip + core for chip in range(CTX // 2)] for core in range(2)]


def to_partner(x):
    return lax.ppermute(x, "ctx", PARTNER)


def over_chips(x):
    return lax.all_to_all(x, "ctx", 0, 0, axis_index_groups=SAME_CORE, tiled=True)


def over_fsdp(x):
    return lax.all_to_all(x, "fsdp", 0, 0, tiled=True)


def gather_fsdp(x):
    return over_fsdp(jnp.broadcast_to(x[None], (FSDP,) + x.shape)).reshape(-1, x.shape[1])


def scatter_fsdp(x):
    parts = over_fsdp(x.reshape(FSDP, -1, x.shape[1]))
    return jnp.sum(parts.astype(F32), 0).astype(BF16)


def sum_pair(a, b):
    return (a.astype(F32) + b.astype(F32)).astype(BF16)


def sum_chips(x):
    for bit in (2, 4, 8):
        x = sum_pair(x, lax.ppermute(x, "ctx", [(i, i ^ bit) for i in range(CTX)]))
    return x


def dot_tn(a, b):
    return lax.dot_general(a, b, (((0,), (0,)), ((), ())), preferred_element_type=F32)


def dot_nt(a, b):
    return lax.dot_general(a, b, (((1,), (1,)), ((), ())), preferred_element_type=F32)


UNROLL_F = 9
UNROLL_B = 3
CHUNK = 4
KEYS = CHUNK * BLK
CHUNKS = NBLK // CHUNK


def fill_keys(sc, own_ref, other_ref, kv_s):
    core = sc[2]
    for chip in range(CTX // 2):
        for half in range(2):
            lanes = slice(half * BLK, (half + 1) * BLK)
            block = sc[7 + 2 * (2 * chip + core) + half]
            kv_s[block] = own_ref[chip, :, 0, :, lanes]
            block = sc[7 + 2 * (2 * chip + 1 - core) + half]
            kv_s[block] = other_ref[chip, :, 0, :, lanes]


def fill_queries(sc, src_ref, dst):
    for half in range(2):
        lanes = slice(half * BLK, (half + 1) * BLK)
        which = jnp.bitwise_xor(half, sc[1])
        dst[which] = jnp.concatenate([src_ref[j, :, lanes] for j in range(GROUP)], axis=1)


def query_rows(sc, which):
    block = jnp.where(which == 0, sc[0], NBLK - 1 - sc[0])
    lane = lax.broadcasted_iota(jnp.int32, (1, LANES), 1)
    pos = block * BLK + jnp.bitwise_and(lane, BLK - 1)
    start = jnp.zeros((1, LANES), jnp.int32)
    for d in range(4):
        start = jnp.where(pos >= sc[3 + d], jnp.maximum(start, sc[3 + d]), start)
    return pos, start


def chunk_of(sc, t):
    high = (NBLK - sc[0] + CHUNK - 1) // CHUNK
    which = (t < high).astype(jnp.int32)
    return which, jnp.where(t < high, t, t - high)


def keys_of(kv_s, chunk, kind):
    return jnp.concatenate([kv_s[chunk * CHUNK + j, kind] for j in range(CHUNK)], axis=1)


def seen(pos_s, which, chunk):
    at = lax.broadcasted_iota(jnp.int32, (KEYS, LANES), 0)
    base = chunk * KEYS
    return (at >= pos_s[which, 1:2] - base) & (at <= pos_s[which, 0:1] - base)


def fill_rows(sc, pos_s):
    for which in range(2):
        pos, start = query_rows(sc, which)
        pos_s[which, 0:1] = pos
        pos_s[which, 1:2] = start


def forward_kernel(sc, q_ref, own_ref, other_ref, o_ref, lse_ref, kv_s, q_s, acc_s, m_s, l_s, pos_s):
    fill_keys(sc, own_ref, other_ref, kv_s)
    fill_queries(sc, q_ref, q_s)
    fill_rows(sc, pos_s)
    acc_s[...] = jnp.zeros_like(acc_s)
    m_s[...] = jnp.full_like(m_s, NEG)
    l_s[...] = jnp.zeros_like(l_s)

    def step(t, carry):
        which, chunk = chunk_of(sc, t)
        scores = dot_tn(keys_of(kv_s, chunk, 0), q_s[which])
        scores = jnp.where(seen(pos_s, which, chunk), scores, NEG)
        old = m_s[which]
        new = jnp.maximum(old, jnp.max(scores, axis=0, keepdims=True))
        prob = jnp.exp(scores - new)
        shrink = jnp.exp(old - new)
        m_s[which] = new
        l_s[which] = l_s[which] * shrink + jnp.sum(prob, axis=0, keepdims=True)
        acc_s[which] = acc_s[which] * shrink + jnp.dot(
            keys_of(kv_s, chunk, 1), prob.astype(BF16), preferred_element_type=F32
        )
        return carry

    lax.fori_loop(0, CHUNKS + 1, step, 0, unroll=UNROLL_F)
    for which in range(2):
        acc_s[which] = acc_s[which] / l_s[which]
        lse_ref[0, which] = m_s[which] + jnp.log(l_s[which])
    for half in range(2):
        mine = acc_s[jnp.bitwise_xor(half, sc[1])]
        for j in range(GROUP):
            o_ref[j, :, half * BLK : (half + 1) * BLK] = mine[:, j * BLK : (j + 1) * BLK]


def backward_kernel(
    sc, q_ref, own_ref, other_ref, o_ref, do_ref, lse_ref,
    dq_ref, down_ref, dother_ref,
    kv_s, q_s, do_s, dq_s, dkv_s, delta_s, pos_s,
):
    fill_keys(sc, own_ref, other_ref, kv_s)
    fill_queries(sc, q_ref, q_s)
    fill_queries(sc, do_ref, do_s)
    fill_queries(sc, o_ref, dq_s)
    fill_rows(sc, pos_s)
    for which in range(2):
        delta_s[which] = jnp.sum(dq_s[which] * do_s[which].astype(F32), axis=0, keepdims=True)
    dq_s[...] = jnp.zeros_like(dq_s)
    dkv_s[...] = jnp.zeros_like(dkv_s)

    def step(t, carry):
        which, chunk = chunk_of(sc, t)
        key_t, val_t, q_t, do_t = keys_of(kv_s, chunk, 0), keys_of(kv_s, chunk, 1), q_s[which], do_s[which]
        scores = dot_tn(key_t, q_t)
        prob = jnp.where(seen(pos_s, which, chunk), jnp.exp(scores - lse_ref[0, which]), 0.0)
        d_prob = dot_tn(val_t, do_t)
        d_score = (prob * (d_prob - delta_s[which])).astype(BF16)
        d_val = dot_nt(do_t, prob.astype(BF16))
        d_key = dot_nt(q_t, d_score)
        dq_s[which] = dq_s[which] + jnp.dot(key_t, d_score, preferred_element_type=F32)
        for j in range(CHUNK):
            lanes = slice(j * BLK, (j + 1) * BLK)
            dkv_s[chunk * CHUNK + j, 0] = dkv_s[chunk * CHUNK + j, 0] + d_key[:, lanes]
            dkv_s[chunk * CHUNK + j, 1] = dkv_s[chunk * CHUNK + j, 1] + d_val[:, lanes]
        return carry

    lax.fori_loop(0, CHUNKS + 1, step, 0, unroll=UNROLL_B)
    core = sc[2]
    scale = HEAD_DIM**-0.5
    for half in range(2):
        lanes = slice(half * BLK, (half + 1) * BLK)
        mine = dq_s[jnp.bitwise_xor(half, sc[1])] * scale
        for j in range(GROUP):
            dq_ref[j, :, lanes] = mine[:, j * BLK : (j + 1) * BLK]
        for chip in range(CTX // 2):
            block = sc[7 + 2 * (2 * chip + core) + half]
            down_ref[chip, :, 0, :, lanes] = dkv_s[block].astype(BF16)
            block = sc[7 + 2 * (2 * chip + 1 - core) + half]
            dother_ref[chip, :, 0, :, lanes] = dkv_s[block].astype(BF16)


ROWS = 2 * BLK
HEAD_SPEC = pl.BlockSpec((GROUP, HEAD_DIM, ROWS), lambda g, sc: (g, 0, 0))
KV_SPEC = pl.BlockSpec((CTX // 2, 2, 1, HEAD_DIM, ROWS), lambda g, sc: (0, 0, g, 0, 0))
LSE_SPEC = pl.BlockSpec((1, 2, 1, LANES), lambda g, sc: (g, 0, 0, 0))
HEAD_SHAPE = jax.ShapeDtypeStruct((HEADS, HEAD_DIM, ROWS), F32)
KV_SHAPE = jax.ShapeDtypeStruct((CTX // 2, 2, KV_HEADS, HEAD_DIM, ROWS), BF16)
LSE_SHAPE = jax.ShapeDtypeStruct((KV_HEADS, 2, 1, LANES), F32)
KERNEL_PARAMS = pltpu.CompilerParams(
    dimension_semantics=("arbitrary",), vmem_limit_bytes=40 * 2**20
)


def attention(scalars, q_t, own, other):
    return pl.pallas_call(
        forward_kernel,
        grid_spec=pltpu.PrefetchScalarGridSpec(
            num_scalar_prefetch=1,
            grid=(KV_HEADS,),
            in_specs=[HEAD_SPEC, KV_SPEC, KV_SPEC],
            out_specs=[HEAD_SPEC, LSE_SPEC],
            scratch_shapes=[
                pltpu.VMEM((NBLK, 2, HEAD_DIM, BLK), BF16),
                pltpu.VMEM((2, HEAD_DIM, LANES), BF16),
                pltpu.VMEM((2, HEAD_DIM, LANES), F32),
                pltpu.VMEM((2, 1, LANES), F32),
                pltpu.VMEM((2, 1, LANES), F32),
                pltpu.VMEM((2, 8, LANES), jnp.int32),
            ],
        ),
        out_shape=[HEAD_SHAPE, LSE_SHAPE],
        compiler_params=KERNEL_PARAMS,
        name="attention",
    )(scalars, q_t, own, other)


def attention_back(scalars, q_t, own, other, o_t, do_t, lse):
    return pl.pallas_call(
        backward_kernel,
        grid_spec=pltpu.PrefetchScalarGridSpec(
            num_scalar_prefetch=1,
            grid=(KV_HEADS,),
            in_specs=[HEAD_SPEC, KV_SPEC, KV_SPEC, HEAD_SPEC, HEAD_SPEC, LSE_SPEC],
            out_specs=[HEAD_SPEC, KV_SPEC, KV_SPEC],
            scratch_shapes=[
                pltpu.VMEM((NBLK, 2, HEAD_DIM, BLK), BF16),
                pltpu.VMEM((2, HEAD_DIM, LANES), BF16),
                pltpu.VMEM((2, HEAD_DIM, LANES), BF16),
                pltpu.VMEM((2, HEAD_DIM, LANES), F32),
                pltpu.VMEM((NBLK, 2, HEAD_DIM, BLK), F32),
                pltpu.VMEM((2, 1, LANES), F32),
                pltpu.VMEM((2, 8, LANES), jnp.int32),
            ],
        ),
        out_shape=[HEAD_SHAPE, KV_SHAPE, KV_SHAPE],
        compiler_params=KERNEL_PARAMS,
        cost_estimate=pl.CostEstimate(
            flops=10 * 36 * BLK * HEADS * BLK * 256, transcendentals=36 * BLK * HEADS * BLK, bytes_accessed=75 * 10**6
        ),
        name="attention_back",
    )(scalars, q_t, own, other, o_t, do_t, lse)


VMEM_SPEC = pl.BlockSpec(memory_space=pltpu.VMEM)


def dispatch_kernel(me, x_ref, *outs):
    for dx, out in enumerate(outs):
        for dz in range(2):
            out[dz] = x_ref[jnp.bitwise_xor(me[0], 4 * dz + dx)]


def dispatch(me, x):
    return pl.pallas_call(
        dispatch_kernel,
        grid_spec=pltpu.PrefetchScalarGridSpec(
            num_scalar_prefetch=1,
            grid=(),
            in_specs=[VMEM_SPEC],
            out_specs=[VMEM_SPEC] * 4,
        ),
        out_shape=[jax.ShapeDtypeStruct((2,) + x.shape[1:], BF16)] * 4,
        compiler_params=pltpu.CompilerParams(vmem_limit_bytes=40 * 2**20),
        name="dispatch",
    )(me, x)


def across(x, d):
    return lax.ppermute(x, "fsdp", [(i, i ^ d) for i in range(FSDP)])


def send_parts(pieces):
    return [pieces[0]] + [across(pieces[dx], dx) for dx in range(1, 4)]


def sum_parts(parts):
    total = sum(p.astype(F32) for p in parts)
    return (total[0] + across(total[1].astype(BF16), 4).astype(F32)).astype(BF16)


UNITS = FF // FSDP // 2


def unpack_kernel(sc, *refs):
    mlp0, mlp0_p, mlp1, mlp1_p, qkv, qkv_p, qkv_ref, out_ref, gu_ref = refs

    def write(order):
        for layer, pair in enumerate(((mlp0, mlp0_p), (mlp1, mlp1_p))):
            for half, mlp in enumerate(pair[::order]):
                for k in range(2):
                    for i in range(FSDP):
                        src = k * HALF + i * UNITS
                        dst = k * FF + i * 2 * UNITS + half * UNITS
                        gu_ref[layer, :, dst : dst + UNITS] = mlp[:, src : src + UNITS].astype(F32)
                cut = D // 2
                out_ref[layer, :, half * cut : (half + 1) * cut] = (
                    mlp[:, FF + HALF : FF + HALF + cut].astype(F32)
                )
        for layer, src in enumerate((qkv, qkv_p)[::order]):
            qkv_ref[layer] = src[:, : Q_ROWS + KV_ROWS].astype(F32)

    @pl.when(sc[0] == 0)
    def _():
        write(1)

    @pl.when(sc[0] != 0)
    def _():
        write(-1)


def unpack(core, *shares):
    return pl.pallas_call(
        unpack_kernel,
        grid_spec=pltpu.PrefetchScalarGridSpec(
            num_scalar_prefetch=1,
            grid=(),
            in_specs=[VMEM_SPEC] * 6,
            out_specs=[VMEM_SPEC] * 3,
        ),
        out_shape=[
            jax.ShapeDtypeStruct((LAYERS, SHARD, Q_ROWS + KV_ROWS), F32),
            jax.ShapeDtypeStruct((LAYERS, SHARD, D), F32),
            jax.ShapeDtypeStruct((LAYERS, SHARD, 2 * FF), F32),
        ],
        compiler_params=pltpu.CompilerParams(vmem_limit_bytes=40 * 2**20),
        name="unpack",
    )(core, *shares)


def rotate(x, cosine, sine):
    half = HEAD_DIM // 2
    first, second = x[:, :half], x[:, half:]
    return jnp.concatenate([first * cosine - second * sine, second * cosine + first * sine], 1)


def normed(hidden):
    inv_rms = lax.rsqrt(jnp.mean(hidden * hidden, -1, keepdims=True) + EPS)
    return hidden * inv_rms, inv_rms


def norm_back(d_unit, unit, inv_rms):
    return inv_rms * (d_unit - unit * jnp.mean(d_unit * unit, -1, keepdims=True))


def mm(a, b):
    return jnp.dot(a, b, preferred_element_type=F32)


def ein(spec, a, b):
    return jnp.einsum(spec, a, b, preferred_element_type=F32)


def local(tokens, block_order, doc_ids, norm_gains, w_qkv, w_out, w_gate_up, w_down, cotangent):
    place = lax.axis_index("ctx")
    core = jnp.bitwise_and(place, 1)
    first_core = core == 0
    me = lax.axis_index("fsdp").reshape(1)

    def my_half(left, right):
        return jnp.where(first_core, left, right)

    def in_order(own, other):
        return my_half(own, other), my_half(other, own)

    gain_cols = jnp.transpose(norm_gains.reshape(2 * LAYERS, SHARD))
    cut = (Q_ROWS + KV_ROWS + D) // 2

    def wgu_pack(layer):
        wgu = w_gate_up[layer].reshape(SHARD, 2, FSDP, 2, UNITS)
        return my_half(wgu[..., 0, :], wgu[..., 1, :]).reshape(SHARD, FF)

    def wd_pack(layer):
        return my_half(w_down[layer, :UNITS], w_down[layer, UNITS:]).reshape(SHARD, HALF)

    def proj_pack(layer):
        proj = jnp.concatenate([w_qkv[layer], w_out[layer]], 1)
        return my_half(proj[:, :cut], proj[:, cut:])

    first = jnp.concatenate([proj_pack(0), gain_cols], 1)
    first = jnp.broadcast_to(first[None], (FSDP,) + first.shape)
    first, w_gate_up, w_down = lax.optimization_barrier((first, w_gate_up, w_down))
    first = over_fsdp(first).reshape(D, -1)
    pack0 = jnp.concatenate([wgu_pack(0), wd_pack(0)], 1)
    pack0 = lax.all_gather(pack0, "fsdp", axis=0, tiled=True)
    pack1 = lax.all_gather(wgu_pack(1), "fsdp", axis=0, tiled=True)
    gains = jnp.transpose(first[:, cut:].astype(F32)).reshape(LAYERS, 2, D)

    def whole_proj(own):
        return jnp.concatenate(in_order(own, to_partner(own)), 1)

    projs, mlps = [whole_proj(first[:, :cut])], []

    first_block = lax.dynamic_index_in_dim(block_order, 2 * place, 0, keepdims=False)
    low = jnp.minimum(first_block, NBLK - 1 - first_block)
    low_half = (first_block != low).astype(jnp.int32)
    starts = jnp.sum(
        (doc_ids[0][None, :] < jnp.arange(1, 5, dtype=jnp.int32)[:, None]).astype(jnp.int32), 1
    )
    scalars = jnp.concatenate([jnp.stack([low, low_half, core]), starts, block_order])
    lane = jnp.arange(ROWS, dtype=jnp.int32)
    pos = jnp.where(lane < BLK, first_block, NBLK - 2 - first_block) * BLK + lane
    inv_freq = THETA ** (-jnp.arange(HEAD_DIM // 2, dtype=F32) / (HEAD_DIM // 2))
    angles = pos.astype(F32)[None, :] * inv_freq[:, None]
    cosine, sine = jnp.cos(angles), jnp.sin(angles)

    hidden = tokens[0].astype(F32)
    saved = []
    for layer in range(LAYERS):
        wqkv, wout = projs[layer][:, : Q_ROWS + KV_ROWS], projs[layer][:, Q_ROWS + KV_ROWS :]
        unit_a, rms_a = normed(hidden)
        attn_in = (unit_a * gains[layer, 0]).astype(BF16)
        qkv_t = ein("de,td->et", wqkv, attn_in).reshape(-1, HEAD_DIM, ROWS)
        turned = rotate(qkv_t[: HEADS + KV_HEADS], cosine, sine)
        q_t = (turned[:HEADS] * HEAD_DIM**-0.5).astype(BF16)
        kv_t = jnp.concatenate([turned[HEADS:], qkv_t[HEADS + KV_HEADS :]], 0).astype(BF16)
        kv_t = kv_t.reshape(1, 2, KV_HEADS, HEAD_DIM, ROWS)
        kv_own = over_chips(jnp.broadcast_to(kv_t, (CTX // 2,) + kv_t.shape[1:]))
        if layer == 0:
            late = jnp.concatenate([proj_pack(1), wd_pack(1)], 1)
            kv_own, late = lax.optimization_barrier((kv_own, late))
            late = gather_fsdp(late)
        kv_other = to_partner(kv_own)
        o_t, lse = attention(scalars, q_t, kv_own, kv_other)
        if layer == 0:
            o_t, pack0 = lax.optimization_barrier((o_t, pack0))
            mlps.append((pack0[:, :FF], pack0[:, FF:].reshape(HALF, D)))
            projs.append(whole_proj(late[:, :cut]))
        else:
            o_t, pack1 = lax.optimization_barrier((o_t, pack1))
            mlps.append((pack1, late[:, cut:].reshape(HALF, D)))
        attn_out = o_t.astype(BF16).reshape(Q_ROWS, ROWS)
        mid = hidden + ein("at,ad->td", attn_out, wout)
        unit_m, rms_m = normed(mid)
        mlp_in = (unit_m * gains[layer, 1]).astype(BF16)
        wgu, wdown = mlps[layer]
        both_in = jnp.concatenate([mlp_in, to_partner(mlp_in)], 0)
        gate_up = mm(both_in, wgu)
        inner = (jax.nn.silu(gate_up[:, :HALF]) * gate_up[:, HALF:]).astype(BF16)
        part = mm(inner, wdown)
        hidden = mid + part[:ROWS] + to_partner(part[ROWS:].astype(BF16)).astype(F32)
        saved.append(
            (wqkv, wout, unit_a, rms_a, attn_in, q_t, kv_own, kv_other, o_t, lse, attn_out,
             unit_m, rms_m, both_in, gate_up, inner, wgu, wdown)
        )
    output = hidden.astype(BF16).reshape(1, ROWS, D)

    def weight_grads(d_gu, both_in, inner, both_grad, attn_out, grad_b):
        d_wgu = ein("td,tf->df", both_in, d_gu).astype(BF16)
        d_wdown = ein("tf,td->fd", inner, both_grad).astype(BF16)
        d_wout = mm(attn_out, grad_b).astype(BF16)
        left, right = d_wout[:, : D // 2], d_wout[:, D // 2 :]
        d_wout = sum_pair(my_half(left, right), to_partner(my_half(right, left)))
        grads = jnp.concatenate([d_wgu, d_wdown.reshape(D, HALF), d_wout], 1)
        return grads.reshape(FSDP, SHARD, -1)

    d_hidden = cotangent[0].astype(F32)
    gain_grads, qkv_grads = [None] * LAYERS, [None] * LAYERS
    for layer in reversed(range(LAYERS)):
        (wqkv, wout, unit_a, rms_a, attn_in, q_t, kv_own, kv_other, o_t, lse, attn_out,
         unit_m, rms_m, both_in, gate_up, inner, wgu, wdown) = saved[layer]
        grad_b = d_hidden.astype(BF16)
        both_grad = jnp.concatenate([grad_b, to_partner(grad_b)], 0)
        d_inner = ein("td,fd->tf", both_grad, wdown)
        gate, up = gate_up[:, :HALF], gate_up[:, HALF:]
        sig = jax.nn.sigmoid(gate)
        d_gate = d_inner * up * sig * (1.0 + gate * (1.0 - sig))
        d_up = d_inner * (gate * sig)
        d_gu = jnp.concatenate([d_gate, d_up], 1).astype(BF16)
        part = ein("tf,df->td", d_gu, wgu)
        d_norm = part[:ROWS] + to_partner(part[ROWS:].astype(BF16)).astype(F32)
        d_gain_m = jnp.sum(d_norm * unit_m, 0)
        d_hidden = d_hidden + norm_back(d_norm * gains[layer, 1], unit_m, rms_m)
        grad_b = d_hidden.astype(BF16)
        do_t = ein("ad,td->at", wout, grad_b).astype(BF16).reshape(HEADS, HEAD_DIM, ROWS)
        if layer == 0:
            pieces = dispatch(me, weight_grads(d_gu, both_in, inner, both_grad, attn_out, grad_b))
            do_t, pieces = lax.optimization_barrier((do_t, pieces))
            parts = send_parts(pieces)
        dq_t, dkv_own, dkv_other = attention_back(scalars, q_t, kv_own, kv_other, o_t, do_t, lse)
        dkv = (dkv_own.astype(F32) + to_partner(dkv_other).astype(F32)).astype(BF16)
        if layer == 1:
            late = (d_gu, both_in, inner, both_grad, attn_out, grad_b)
            grads = weight_grads(*lax.optimization_barrier((late, dkv))[0])
        else:
            dkv, parts = lax.optimization_barrier((dkv, parts))
            share0 = sum_parts(parts)
            share1 = sum_chips(lax.optimization_barrier((share1, dkv))[0])
        dkv = jnp.sum(over_chips(dkv).astype(F32), 0)
        if layer == 1:
            dkv, grads = lax.optimization_barrier((dkv, grads))
            share1 = lax.psum_scatter(grads.reshape(D, -1), "fsdp", scatter_dimension=0, tiled=True)
        turned = jnp.concatenate([dq_t, dkv[0]], 0)
        d_qkv = jnp.concatenate([rotate(turned, cosine, -sine), dkv[1]], 0)
        d_qkv = d_qkv.astype(BF16).reshape(Q_ROWS + KV_ROWS, ROWS)
        d_wqkv = ein("td,et->de", attn_in, d_qkv)
        d_norm = ein("et,de->td", d_qkv, wqkv)
        d_gain_a = jnp.sum(d_norm * unit_a, 0)
        d_hidden = d_hidden + norm_back(d_norm * gains[layer, 0], unit_a, rms_a)
        gain_grads[layer] = jnp.stack([d_gain_a, d_gain_m])
        qkv_grads[layer] = d_wqkv.astype(BF16)
    input_grad = d_hidden.reshape(1, ROWS, D)

    mine, theirs = in_order(*qkv_grads)
    d_gains = jnp.transpose(jnp.stack(gain_grads).reshape(2 * LAYERS, D)).astype(BF16)
    d_wqkv = jnp.concatenate([sum_pair(mine, to_partner(theirs)), d_gains], 1)
    qkv = sum_chips(scatter_fsdp(d_wqkv))
    qkv_p = to_partner(qkv)

    share0 = sum_chips(share0)
    mlp0, mlp0_p, mlp1, mlp1_p = share0, to_partner(share0), share1, to_partner(share1)
    half = Q_ROWS + KV_ROWS
    d_gain = qkv[:, half:].astype(F32) + qkv_p[:, half:].astype(F32)
    gain_grad = jnp.transpose(d_gain).reshape(LAYERS, 2, SHARD)
    qkv_grad, out_proj_grad, gate_up_grad = unpack(
        core.reshape(1), mlp0, mlp0_p, mlp1, mlp1_p, qkv, qkv_p
    )
    down_grad = []
    for own, theirs in ((mlp0, mlp0_p), (mlp1, mlp1_p)):
        rows = [x[:, FF : FF + HALF].reshape(UNITS, D) for x in in_order(own, theirs)]
        down_grad.append(jnp.concatenate(rows, 0))
    down_grad = jnp.stack(down_grad).astype(F32)
    return (output, input_grad, gain_grad, qkv_grad, out_proj_grad, gate_up_grad, down_grad)


def solution(mesh):
    in_specs = (
        P("fsdp", "ctx", None),
        P(),
        P("fsdp", None),
        P(None, None, "fsdp"),
        P(None, "fsdp", None),
        P(None, "fsdp", None),
        P(None, "fsdp", None),
        P(None, "fsdp", None),
        P("fsdp", "ctx", None),
    )
    out_specs = (
        P("fsdp", "ctx", None),
        P("fsdp", "ctx", None),
        P(None, None, "fsdp"),
        P(None, "fsdp", None),
        P(None, "fsdp", None),
        P(None, "fsdp", None),
        P(None, "fsdp", None),
    )
    return jax.shard_map(local, mesh=mesh, in_specs=in_specs, out_specs=out_specs, check_vma=False)
```

```python
import functools

import jax
import jax.numpy as jnp
from jax import lax
from jax.experimental import pallas as pl
from jax.experimental.pallas import tpu as pltpu
from jax.sharding import PartitionSpec as P

D = 576
HEADS = 9
KV_HEADS = 3
GROUP = 3
HEAD_DIM = 64
FF = 1536
LAYERS = 2
BLK = 128
NBLK = 32
EPS = 1e-05
THETA = 100000.0
NEG = -1e30
F32 = jnp.float32
BF16 = jnp.bfloat16
LANES = GROUP * BLK
CTX = 16
FSDP = 8
SHARD = D // FSDP
HALF = FF // 2
Q_ROWS = HEADS * HEAD_DIM
KV_ROWS = 2 * KV_HEADS * HEAD_DIM

PARTNER = [(i, i ^ 1) for i in range(CTX)]
SAME_CORE = [[2 * chip + core for chip in range(CTX // 2)] for core in range(2)]


def to_partner(x):
    return lax.ppermute(x, "ctx", PARTNER)


def over_chips(x):
    return lax.all_to_all(x, "ctx", 0, 0, axis_index_groups=SAME_CORE, tiled=True)


def over_fsdp(x):
    return lax.all_to_all(x, "fsdp", 0, 0, tiled=True)


def gather_fsdp(x):
    return over_fsdp(jnp.broadcast_to(x[None], (FSDP,) + x.shape)).reshape(-1, x.shape[1])


def scatter_fsdp(x):
    parts = over_fsdp(x.reshape(FSDP, -1, x.shape[1]))
    return jnp.sum(parts.astype(F32), 0).astype(BF16)


def sum_pair(a, b):
    return (a.astype(F32) + b.astype(F32)).astype(BF16)


def sum_chips(x):
    for bit in (2, 4, 8):
        x = sum_pair(x, lax.ppermute(x, "ctx", [(i, i ^ bit) for i in range(CTX)]))
    return x


def dot_tn(a, b):
    return lax.dot_general(a, b, (((0,), (0,)), ((), ())), preferred_element_type=F32)


def dot_nt(a, b):
    return lax.dot_general(a, b, (((1,), (1,)), ((), ())), preferred_element_type=F32)


UNROLL_F = 9
UNROLL_B = 3
CHUNK = 4
KEYS = CHUNK * BLK
CHUNKS = NBLK // CHUNK


def fill_keys(sc, own_ref, other_ref, kv_s):
    core = sc[2]
    for chip in range(CTX // 2):
        for half in range(2):
            lanes = slice(half * BLK, (half + 1) * BLK)
            block = sc[7 + 2 * (2 * chip + core) + half]
            kv_s[block] = own_ref[chip, :, 0, :, lanes]
            block = sc[7 + 2 * (2 * chip + 1 - core) + half]
            kv_s[block] = other_ref[chip, :, 0, :, lanes]


def fill_queries(sc, src_ref, dst):
    for half in range(2):
        lanes = slice(half * BLK, (half + 1) * BLK)
        which = jnp.bitwise_xor(half, sc[1])
        dst[which] = jnp.concatenate([src_ref[j, :, lanes] for j in range(GROUP)], axis=1)


def query_rows(sc, which):
    block = jnp.where(which == 0, sc[0], NBLK - 1 - sc[0])
    lane = lax.broadcasted_iota(jnp.int32, (1, LANES), 1)
    pos = block * BLK + jnp.bitwise_and(lane, BLK - 1)
    start = jnp.zeros((1, LANES), jnp.int32)
    for d in range(4):
        start = jnp.where(pos >= sc[3 + d], jnp.maximum(start, sc[3 + d]), start)
    return pos, start


def chunk_of(sc, t):
    high = (NBLK - sc[0] + CHUNK - 1) // CHUNK
    which = (t < high).astype(jnp.int32)
    return which, jnp.where(t < high, t, t - high)


def keys_of(kv_s, chunk, kind):
    return jnp.concatenate([kv_s[chunk * CHUNK + j, kind] for j in range(CHUNK)], axis=1)


def seen(pos_s, which, chunk):
    at = lax.broadcasted_iota(jnp.int32, (KEYS, LANES), 0)
    base = chunk * KEYS
    return (at >= pos_s[which, 1:2] - base) & (at <= pos_s[which, 0:1] - base)


def fill_rows(sc, pos_s):
    for which in range(2):
        pos, start = query_rows(sc, which)
        pos_s[which, 0:1] = pos
        pos_s[which, 1:2] = start


def forward_kernel(sc, q_ref, own_ref, other_ref, o_ref, lse_ref, kv_s, q_s, acc_s, m_s, l_s, pos_s):
    fill_keys(sc, own_ref, other_ref, kv_s)
    fill_queries(sc, q_ref, q_s)
    fill_rows(sc, pos_s)
    acc_s[...] = jnp.zeros_like(acc_s)
    m_s[...] = jnp.full_like(m_s, NEG)
    l_s[...] = jnp.zeros_like(l_s)

    def step(t, carry):
        which, chunk = chunk_of(sc, t)
        scores = dot_tn(keys_of(kv_s, chunk, 0), q_s[which])
        scores = jnp.where(seen(pos_s, which, chunk), scores, NEG)
        old = m_s[which]
        new = jnp.maximum(old, jnp.max(scores, axis=0, keepdims=True))
        prob = jnp.exp(scores - new)
        shrink = jnp.exp(old - new)
        m_s[which] = new
        l_s[which] = l_s[which] * shrink + jnp.sum(prob, axis=0, keepdims=True)
        acc_s[which] = acc_s[which] * shrink + jnp.dot(
            keys_of(kv_s, chunk, 1), prob.astype(BF16), preferred_element_type=F32
        )
        return carry

    lax.fori_loop(0, CHUNKS + 1, step, 0, unroll=UNROLL_F)
    for which in range(2):
        acc_s[which] = acc_s[which] / l_s[which]
        lse_ref[0, which] = m_s[which] + jnp.log(l_s[which])
    for half in range(2):
        mine = acc_s[jnp.bitwise_xor(half, sc[1])]
        for j in range(GROUP):
            o_ref[j, :, half * BLK : (half + 1) * BLK] = mine[:, j * BLK : (j + 1) * BLK]


def backward_kernel(
    sc, q_ref, own_ref, other_ref, o_ref, do_ref, lse_ref,
    dq_ref, down_ref, dother_ref,
    kv_s, q_s, do_s, dq_s, dkv_s, delta_s, pos_s,
):
    fill_keys(sc, own_ref, other_ref, kv_s)
    fill_queries(sc, q_ref, q_s)
    fill_queries(sc, do_ref, do_s)
    fill_queries(sc, o_ref, dq_s)
    fill_rows(sc, pos_s)
    for which in range(2):
        delta_s[which] = jnp.sum(dq_s[which] * do_s[which].astype(F32), axis=0, keepdims=True)
    dq_s[...] = jnp.zeros_like(dq_s)
    dkv_s[...] = jnp.zeros_like(dkv_s)

    def step(t, carry):
        which, chunk = chunk_of(sc, t)
        key_t, val_t, q_t, do_t = keys_of(kv_s, chunk, 0), keys_of(kv_s, chunk, 1), q_s[which], do_s[which]
        scores = dot_tn(key_t, q_t)
        prob = jnp.where(seen(pos_s, which, chunk), jnp.exp(scores - lse_ref[0, which]), 0.0)
        d_prob = dot_tn(val_t, do_t)
        d_score = (prob * (d_prob - delta_s[which])).astype(BF16)
        d_val = dot_nt(do_t, prob.astype(BF16))
        d_key = dot_nt(q_t, d_score)
        dq_s[which] = dq_s[which] + jnp.dot(key_t, d_score, preferred_element_type=F32)
        for j in range(CHUNK):
            lanes = slice(j * BLK, (j + 1) * BLK)
            dkv_s[chunk * CHUNK + j, 0] = dkv_s[chunk * CHUNK + j, 0] + d_key[:, lanes]
            dkv_s[chunk * CHUNK + j, 1] = dkv_s[chunk * CHUNK + j, 1] + d_val[:, lanes]
        return carry

    lax.fori_loop(0, CHUNKS + 1, step, 0, unroll=UNROLL_B)
    core = sc[2]
    scale = HEAD_DIM**-0.5
    for half in range(2):
        lanes = slice(half * BLK, (half + 1) * BLK)
        mine = dq_s[jnp.bitwise_xor(half, sc[1])] * scale
        for j in range(GROUP):
            dq_ref[j, :, lanes] = mine[:, j * BLK : (j + 1) * BLK]
        for chip in range(CTX // 2):
            block = sc[7 + 2 * (2 * chip + core) + half]
            down_ref[chip, :, 0, :, lanes] = dkv_s[block].astype(BF16)
            block = sc[7 + 2 * (2 * chip + 1 - core) + half]
            dother_ref[chip, :, 0, :, lanes] = dkv_s[block].astype(BF16)


ROWS = 2 * BLK
HEAD_SPEC = pl.BlockSpec((GROUP, HEAD_DIM, ROWS), lambda g, sc: (g, 0, 0))
KV_SPEC = pl.BlockSpec((CTX // 2, 2, 1, HEAD_DIM, ROWS), lambda g, sc: (0, 0, g, 0, 0))
LSE_SPEC = pl.BlockSpec((1, 2, 1, LANES), lambda g, sc: (g, 0, 0, 0))
HEAD_SHAPE = jax.ShapeDtypeStruct((HEADS, HEAD_DIM, ROWS), F32)
KV_SHAPE = jax.ShapeDtypeStruct((CTX // 2, 2, KV_HEADS, HEAD_DIM, ROWS), BF16)
LSE_SHAPE = jax.ShapeDtypeStruct((KV_HEADS, 2, 1, LANES), F32)
KERNEL_PARAMS = pltpu.CompilerParams(
    dimension_semantics=("arbitrary",), vmem_limit_bytes=40 * 2**20
)


def attention(scalars, q_t, own, other):
    return pl.pallas_call(
        forward_kernel,
        grid_spec=pltpu.PrefetchScalarGridSpec(
            num_scalar_prefetch=1,
            grid=(KV_HEADS,),
            in_specs=[HEAD_SPEC, KV_SPEC, KV_SPEC],
            out_specs=[HEAD_SPEC, LSE_SPEC],
            scratch_shapes=[
                pltpu.VMEM((NBLK, 2, HEAD_DIM, BLK), BF16),
                pltpu.VMEM((2, HEAD_DIM, LANES), BF16),
                pltpu.VMEM((2, HEAD_DIM, LANES), F32),
                pltpu.VMEM((2, 1, LANES), F32),
                pltpu.VMEM((2, 1, LANES), F32),
                pltpu.VMEM((2, 8, LANES), jnp.int32),
            ],
        ),
        out_shape=[HEAD_SHAPE, LSE_SHAPE],
        compiler_params=KERNEL_PARAMS,
        name="attention",
    )(scalars, q_t, own, other)


def attention_back(scalars, q_t, own, other, o_t, do_t, lse):
    return pl.pallas_call(
        backward_kernel,
        grid_spec=pltpu.PrefetchScalarGridSpec(
            num_scalar_prefetch=1,
            grid=(KV_HEADS,),
            in_specs=[HEAD_SPEC, KV_SPEC, KV_SPEC, HEAD_SPEC, HEAD_SPEC, LSE_SPEC],
            out_specs=[HEAD_SPEC, KV_SPEC, KV_SPEC],
            scratch_shapes=[
                pltpu.VMEM((NBLK, 2, HEAD_DIM, BLK), BF16),
                pltpu.VMEM((2, HEAD_DIM, LANES), BF16),
                pltpu.VMEM((2, HEAD_DIM, LANES), BF16),
                pltpu.VMEM((2, HEAD_DIM, LANES), F32),
                pltpu.VMEM((NBLK, 2, HEAD_DIM, BLK), F32),
                pltpu.VMEM((2, 1, LANES), F32),
                pltpu.VMEM((2, 8, LANES), jnp.int32),
            ],
        ),
        out_shape=[HEAD_SHAPE, KV_SHAPE, KV_SHAPE],
        compiler_params=KERNEL_PARAMS,
        name="attention_back",
    )(scalars, q_t, own, other, o_t, do_t, lse)


VMEM_SPEC = pl.BlockSpec(memory_space=pltpu.VMEM)


def dispatch_kernel(me, x_ref, *outs):
    for dx, out in enumerate(outs):
        for dz in range(2):
            out[dz] = x_ref[jnp.bitwise_xor(me[0], 4 * dz + dx)]


def dispatch(me, x):
    return pl.pallas_call(
        dispatch_kernel,
        grid_spec=pltpu.PrefetchScalarGridSpec(
            num_scalar_prefetch=1,
            grid=(),
            in_specs=[VMEM_SPEC],
            out_specs=[VMEM_SPEC] * 4,
        ),
        out_shape=[jax.ShapeDtypeStruct((2,) + x.shape[1:], BF16)] * 4,
        compiler_params=pltpu.CompilerParams(vmem_limit_bytes=40 * 2**20),
        name="dispatch",
    )(me, x)


def across(x, d):
    return lax.ppermute(x, "fsdp", [(i, i ^ d) for i in range(FSDP)])


def send_parts(pieces):
    return [pieces[0]] + [across(pieces[dx], dx) for dx in range(1, 4)]


def sum_parts(parts):
    total = sum(p.astype(F32) for p in parts)
    return (total[0] + across(total[1].astype(BF16), 4).astype(F32)).astype(BF16)


UNITS = FF // FSDP // 2


def unpack_kernel(sc, *refs):
    mlp0, mlp0_p, mlp1, mlp1_p, qkv, qkv_p, qkv_ref, out_ref, gu_ref = refs

    def write(order):
        for layer, pair in enumerate(((mlp0, mlp0_p), (mlp1, mlp1_p))):
            for half, mlp in enumerate(pair[::order]):
                for k in range(2):
                    for i in range(FSDP):
                        src = k * HALF + i * UNITS
                        dst = k * FF + i * 2 * UNITS + half * UNITS
                        gu_ref[layer, :, dst : dst + UNITS] = mlp[:, src : src + UNITS].astype(F32)
                cut = D // 2
                out_ref[layer, :, half * cut : (half + 1) * cut] = (
                    mlp[:, FF + HALF : FF + HALF + cut].astype(F32)
                )
        for layer, src in enumerate((qkv, qkv_p)[::order]):
            qkv_ref[layer] = src[:, : Q_ROWS + KV_ROWS].astype(F32)

    @pl.when(sc[0] == 0)
    def _():
        write(1)

    @pl.when(sc[0] != 0)
    def _():
        write(-1)


def unpack(core, *shares):
    return pl.pallas_call(
        unpack_kernel,
        grid_spec=pltpu.PrefetchScalarGridSpec(
            num_scalar_prefetch=1,
            grid=(),
            in_specs=[VMEM_SPEC] * 6,
            out_specs=[VMEM_SPEC] * 3,
        ),
        out_shape=[
            jax.ShapeDtypeStruct((LAYERS, SHARD, Q_ROWS + KV_ROWS), F32),
            jax.ShapeDtypeStruct((LAYERS, SHARD, D), F32),
            jax.ShapeDtypeStruct((LAYERS, SHARD, 2 * FF), F32),
        ],
        compiler_params=pltpu.CompilerParams(vmem_limit_bytes=40 * 2**20),
        name="unpack",
    )(core, *shares)


def rotate(x, cosine, sine):
    half = HEAD_DIM // 2
    first, second = x[:, :half], x[:, half:]
    return jnp.concatenate([first * cosine - second * sine, second * cosine + first * sine], 1)


def normed(hidden):
    inv_rms = lax.rsqrt(jnp.mean(hidden * hidden, -1, keepdims=True) + EPS)
    return hidden * inv_rms, inv_rms


def norm_back(d_unit, unit, inv_rms):
    return inv_rms * (d_unit - unit * jnp.mean(d_unit * unit, -1, keepdims=True))


def mm(a, b):
    return jnp.dot(a, b, preferred_element_type=F32)


def ein(spec, a, b):
    return jnp.einsum(spec, a, b, preferred_element_type=F32)


def local(tokens, block_order, doc_ids, norm_gains, w_qkv, w_out, w_gate_up, w_down, cotangent):
    place = lax.axis_index("ctx")
    core = jnp.bitwise_and(place, 1)
    first_core = core == 0
    me = lax.axis_index("fsdp").reshape(1)

    def my_half(left, right):
        return jnp.where(first_core, left, right)

    def in_order(own, other):
        return my_half(own, other), my_half(other, own)

    gain_cols = jnp.transpose(norm_gains.reshape(2 * LAYERS, SHARD))
    cut = (Q_ROWS + KV_ROWS + D) // 2

    def wgu_pack(layer):
        wgu = w_gate_up[layer].reshape(SHARD, 2, FSDP, 2, UNITS)
        return my_half(wgu[..., 0, :], wgu[..., 1, :]).reshape(SHARD, FF)

    def wd_pack(layer):
        return my_half(w_down[layer, :UNITS], w_down[layer, UNITS:]).reshape(SHARD, HALF)

    def proj_pack(layer):
        proj = jnp.concatenate([w_qkv[layer], w_out[layer]], 1)
        return my_half(proj[:, :cut], proj[:, cut:])

    first = jnp.concatenate([proj_pack(0), gain_cols], 1)
    first = jnp.broadcast_to(first[None], (FSDP,) + first.shape)
    first, w_gate_up, w_down = lax.optimization_barrier((first, w_gate_up, w_down))
    first = over_fsdp(first).reshape(D, -1)
    pack0 = jnp.concatenate([wgu_pack(0), wd_pack(0)], 1)
    pack0 = lax.all_gather(pack0, "fsdp", axis=0, tiled=True)
    pack1 = lax.all_gather(wgu_pack(1), "fsdp", axis=0, tiled=True)
    gains = jnp.transpose(first[:, cut:].astype(F32)).reshape(LAYERS, 2, D)

    def whole_proj(own):
        return jnp.concatenate(in_order(own, to_partner(own)), 1)

    projs, mlps = [whole_proj(first[:, :cut])], []

    first_block = lax.dynamic_index_in_dim(block_order, 2 * place, 0, keepdims=False)
    low = jnp.minimum(first_block, NBLK - 1 - first_block)
    low_half = (first_block != low).astype(jnp.int32)
    starts = jnp.sum(
        (doc_ids[0][None, :] < jnp.arange(1, 5, dtype=jnp.int32)[:, None]).astype(jnp.int32), 1
    )
    scalars = jnp.concatenate([jnp.stack([low, low_half, core]), starts, block_order])
    lane = jnp.arange(ROWS, dtype=jnp.int32)
    pos = jnp.where(lane < BLK, first_block, NBLK - 2 - first_block) * BLK + lane
    inv_freq = THETA ** (-jnp.arange(HEAD_DIM // 2, dtype=F32) / (HEAD_DIM // 2))
    angles = pos.astype(F32)[None, :] * inv_freq[:, None]
    cosine, sine = jnp.cos(angles), jnp.sin(angles)

    hidden = tokens[0].astype(F32)
    saved = []
    for layer in range(LAYERS):
        wqkv, wout = projs[layer][:, : Q_ROWS + KV_ROWS], projs[layer][:, Q_ROWS + KV_ROWS :]
        unit_a, rms_a = normed(hidden)
        attn_in = (unit_a * gains[layer, 0]).astype(BF16)
        qkv_t = ein("de,td->et", wqkv, attn_in).reshape(-1, HEAD_DIM, ROWS)
        turned = rotate(qkv_t[: HEADS + KV_HEADS], cosine, sine)
        q_t = (turned[:HEADS] * HEAD_DIM**-0.5).astype(BF16)
        kv_t = jnp.concatenate([turned[HEADS:], qkv_t[HEADS + KV_HEADS :]], 0).astype(BF16)
        kv_t = kv_t.reshape(1, 2, KV_HEADS, HEAD_DIM, ROWS)
        kv_own = over_chips(jnp.broadcast_to(kv_t, (CTX // 2,) + kv_t.shape[1:]))
        if layer == 0:
            late = jnp.concatenate([proj_pack(1), wd_pack(1)], 1)
            kv_own, late = lax.optimization_barrier((kv_own, late))
            late = gather_fsdp(late)
        kv_other = to_partner(kv_own)
        o_t, lse = attention(scalars, q_t, kv_own, kv_other)
        if layer == 0:
            o_t, pack0 = lax.optimization_barrier((o_t, pack0))
            mlps.append((pack0[:, :FF], pack0[:, FF:].reshape(HALF, D)))
            projs.append(whole_proj(late[:, :cut]))
        else:
            o_t, pack1 = lax.optimization_barrier((o_t, pack1))
            mlps.append((pack1, late[:, cut:].reshape(HALF, D)))
        attn_out = o_t.astype(BF16).reshape(Q_ROWS, ROWS)
        mid = hidden + ein("at,ad->td", attn_out, wout)
        unit_m, rms_m = normed(mid)
        mlp_in = (unit_m * gains[layer, 1]).astype(BF16)
        wgu, wdown = mlps[layer]
        both_in = jnp.concatenate([mlp_in, to_partner(mlp_in)], 0)
        gate_up = mm(both_in, wgu)
        inner = (jax.nn.silu(gate_up[:, :HALF]) * gate_up[:, HALF:]).astype(BF16)
        part = mm(inner, wdown)
        hidden = mid + part[:ROWS] + to_partner(part[ROWS:].astype(BF16)).astype(F32)
        saved.append(
            (wqkv, wout, unit_a, rms_a, attn_in, q_t, kv_own, kv_other, o_t, lse, attn_out,
             unit_m, rms_m, both_in, gate_up, inner, wgu, wdown)
        )
    output = hidden.astype(BF16).reshape(1, ROWS, D)

    def weight_grads(d_gu, both_in, inner, both_grad, attn_out, grad_b):
        d_wgu = ein("td,tf->df", both_in, d_gu).astype(BF16)
        d_wdown = ein("tf,td->fd", inner, both_grad).astype(BF16)
        d_wout = mm(attn_out, grad_b).astype(BF16)
        left, right = d_wout[:, : D // 2], d_wout[:, D // 2 :]
        d_wout = sum_pair(my_half(left, right), to_partner(my_half(right, left)))
        grads = jnp.concatenate([d_wgu, d_wdown.reshape(D, HALF), d_wout], 1)
        return grads.reshape(FSDP, SHARD, -1)

    d_hidden = cotangent[0].astype(F32)
    gain_grads, qkv_grads = [None] * LAYERS, [None] * LAYERS
    for layer in reversed(range(LAYERS)):
        (wqkv, wout, unit_a, rms_a, attn_in, q_t, kv_own, kv_other, o_t, lse, attn_out,
         unit_m, rms_m, both_in, gate_up, inner, wgu, wdown) = saved[layer]
        grad_b = d_hidden.astype(BF16)
        both_grad = jnp.concatenate([grad_b, to_partner(grad_b)], 0)
        d_inner = ein("td,fd->tf", both_grad, wdown)
        gate, up = gate_up[:, :HALF], gate_up[:, HALF:]
        sig = jax.nn.sigmoid(gate)
        d_gate = d_inner * up * sig * (1.0 + gate * (1.0 - sig))
        d_up = d_inner * (gate * sig)
        d_gu = jnp.concatenate([d_gate, d_up], 1).astype(BF16)
        part = ein("tf,df->td", d_gu, wgu)
        d_norm = part[:ROWS] + to_partner(part[ROWS:].astype(BF16)).astype(F32)
        d_gain_m = jnp.sum(d_norm * unit_m, 0)
        d_hidden = d_hidden + norm_back(d_norm * gains[layer, 1], unit_m, rms_m)
        grad_b = d_hidden.astype(BF16)
        do_t = ein("ad,td->at", wout, grad_b).astype(BF16).reshape(HEADS, HEAD_DIM, ROWS)
        dq_t, dkv_own, dkv_other = attention_back(scalars, q_t, kv_own, kv_other, o_t, do_t, lse)
        dkv = (dkv_own.astype(F32) + to_partner(dkv_other).astype(F32)).astype(BF16)
        late = (d_gu, both_in, inner, both_grad, attn_out, grad_b)
        grads = weight_grads(*lax.optimization_barrier((late, dkv))[0])
        if layer == 0:
            share1 = sum_chips(lax.optimization_barrier((share1, dkv))[0])
        dkv = jnp.sum(over_chips(dkv).astype(F32), 0)
        dkv, grads = lax.optimization_barrier((dkv, grads))
        if layer == 1:
            share1 = lax.psum_scatter(grads.reshape(D, -1), "fsdp", scatter_dimension=0, tiled=True)
        else:
            parts = send_parts(dispatch(me, grads))
        turned = jnp.concatenate([dq_t, dkv[0]], 0)
        d_qkv = jnp.concatenate([rotate(turned, cosine, -sine), dkv[1]], 0)
        d_qkv = d_qkv.astype(BF16).reshape(Q_ROWS + KV_ROWS, ROWS)
        d_wqkv = ein("td,et->de", attn_in, d_qkv)
        d_norm = ein("et,de->td", d_qkv, wqkv)
        d_gain_a = jnp.sum(d_norm * unit_a, 0)
        d_hidden = d_hidden + norm_back(d_norm * gains[layer, 0], unit_a, rms_a)
        gain_grads[layer] = jnp.stack([d_gain_a, d_gain_m])
        qkv_grads[layer] = d_wqkv.astype(BF16)
    input_grad = d_hidden.reshape(1, ROWS, D)

    mine, theirs = in_order(*qkv_grads)
    d_gains = jnp.transpose(jnp.stack(gain_grads).reshape(2 * LAYERS, D)).astype(BF16)
    d_wqkv = jnp.concatenate([sum_pair(mine, to_partner(theirs)), d_gains], 1)
    d_wqkv, parts[1], parts[3] = lax.optimization_barrier((d_wqkv, parts[1], parts[3]))
    qkv = scatter_fsdp(d_wqkv)
    parts[2] = lax.optimization_barrier((parts[2], qkv))[0]
    share0 = sum_parts(parts)
    qkv = sum_chips(qkv)
    qkv_p = to_partner(qkv)

    share0 = sum_chips(share0)
    mlp0, mlp0_p, mlp1, mlp1_p = share0, to_partner(share0), share1, to_partner(share1)
    half = Q_ROWS + KV_ROWS
    d_gain = qkv[:, half:].astype(F32) + qkv_p[:, half:].astype(F32)
    gain_grad = jnp.transpose(d_gain).reshape(LAYERS, 2, SHARD)
    qkv_grad, out_proj_grad, gate_up_grad = unpack(
        core.reshape(1), mlp0, mlp0_p, mlp1, mlp1_p, qkv, qkv_p
    )
    down_grad = []
    for own, theirs in ((mlp0, mlp0_p), (mlp1, mlp1_p)):
        rows = [x[:, FF : FF + HALF].reshape(UNITS, D) for x in in_order(own, theirs)]
        down_grad.append(jnp.concatenate(rows, 0))
    down_grad = jnp.stack(down_grad).astype(F32)
    return (output, input_grad, gain_grad, qkv_grad, out_proj_grad, gate_up_grad, down_grad)


def solution(mesh):
    in_specs = (
        P("fsdp", "ctx", None),
        P(),
        P("fsdp", None),
        P(None, None, "fsdp"),
        P(None, "fsdp", None),
        P(None, "fsdp", None),
        P(None, "fsdp", None),
        P(None, "fsdp", None),
        P("fsdp", "ctx", None),
    )
    out_specs = (
        P("fsdp", "ctx", None),
        P("fsdp", "ctx", None),
        P(None, None, "fsdp"),
        P(None, "fsdp", None),
        P(None, "fsdp", None),
        P(None, "fsdp", None),
        P(None, "fsdp", None),
    )
    return jax.shard_map(local, mesh=mesh, in_specs=in_specs, out_specs=out_specs, check_vma=False)
```

```python
import functools

import jax
import jax.numpy as jnp
from jax import lax
from jax.experimental import pallas as pl
from jax.experimental.pallas import tpu as pltpu
from jax.sharding import PartitionSpec as P

D = 576
HEADS = 9
KV_HEADS = 3
GROUP = 3
HEAD_DIM = 64
FF = 1536
LAYERS = 2
BLK = 128
NBLK = 32
EPS = 1e-05
THETA = 100000.0
NEG = -1e30
F32 = jnp.float32
BF16 = jnp.bfloat16
LANES = GROUP * BLK
CTX = 16
FSDP = 8
SHARD = D // FSDP
HALF = FF // 2
Q_ROWS = HEADS * HEAD_DIM
KV_ROWS = 2 * KV_HEADS * HEAD_DIM

PARTNER = [(i, i ^ 1) for i in range(CTX)]
SAME_CORE = [[2 * chip + core for chip in range(CTX // 2)] for core in range(2)]


def to_partner(x):
    return lax.ppermute(x, "ctx", PARTNER)


def over_chips(x):
    return lax.all_to_all(x, "ctx", 0, 0, axis_index_groups=SAME_CORE, tiled=True)


def over_fsdp(x):
    return lax.all_to_all(x, "fsdp", 0, 0, tiled=True)


def gather_fsdp(x):
    return over_fsdp(jnp.broadcast_to(x[None], (FSDP,) + x.shape)).reshape(-1, x.shape[1])


def scatter_fsdp(x):
    parts = over_fsdp(x.reshape(FSDP, -1, x.shape[1]))
    return jnp.sum(parts.astype(F32), 0).astype(BF16)


def sum_pair(a, b):
    return (a.astype(F32) + b.astype(F32)).astype(BF16)


def sum_chips(x):
    for bit in (2, 4, 8):
        x = sum_pair(x, lax.ppermute(x, "ctx", [(i, i ^ bit) for i in range(CTX)]))
    return x


def dot_tn(a, b):
    return lax.dot_general(a, b, (((0,), (0,)), ((), ())), preferred_element_type=F32)


def dot_nt(a, b):
    return lax.dot_general(a, b, (((1,), (1,)), ((), ())), preferred_element_type=F32)


UNROLL_F = 9
UNROLL_B = 9
CHUNK = 4
KEYS = CHUNK * BLK
CHUNKS = NBLK // CHUNK


def fill_keys(sc, own_ref, other_ref, kv_s):
    core = sc[2]
    for chip in range(CTX // 2):
        for half in range(2):
            lanes = slice(half * BLK, (half + 1) * BLK)
            block = sc[7 + 2 * (2 * chip + core) + half]
            kv_s[block] = own_ref[chip, :, 0, :, lanes]
            block = sc[7 + 2 * (2 * chip + 1 - core) + half]
            kv_s[block] = other_ref[chip, :, 0, :, lanes]


def fill_queries(sc, src_ref, dst):
    for half in range(2):
        lanes = slice(half * BLK, (half + 1) * BLK)
        which = jnp.bitwise_xor(half, sc[1])
        dst[which] = jnp.concatenate([src_ref[j, :, lanes] for j in range(GROUP)], axis=1)


def query_rows(sc, which):
    block = jnp.where(which == 0, sc[0], NBLK - 1 - sc[0])
    lane = lax.broadcasted_iota(jnp.int32, (1, LANES), 1)
    pos = block * BLK + jnp.bitwise_and(lane, BLK - 1)
    start = jnp.zeros((1, LANES), jnp.int32)
    for d in range(4):
        start = jnp.where(pos >= sc[3 + d], jnp.maximum(start, sc[3 + d]), start)
    return pos, start


def chunk_of(sc, t):
    high = (NBLK - sc[0] + CHUNK - 1) // CHUNK
    which = (t < high).astype(jnp.int32)
    return which, jnp.where(t < high, t, t - high)


def keys_of(kv_s, chunk, kind):
    return jnp.concatenate([kv_s[chunk * CHUNK + j, kind] for j in range(CHUNK)], axis=1)


def seen(pos_s, which, chunk):
    at = lax.broadcasted_iota(jnp.int32, (KEYS, LANES), 0)
    base = chunk * KEYS
    return (at >= pos_s[which, 1:2] - base) & (at <= pos_s[which, 0:1] - base)


def fill_rows(sc, pos_s):
    for which in range(2):
        pos, start = query_rows(sc, which)
        pos_s[which, 0:1] = pos
        pos_s[which, 1:2] = start


def forward_kernel(sc, q_ref, own_ref, other_ref, o_ref, lse_ref, kv_s, q_s, acc_s, m_s, l_s, pos_s):
    fill_keys(sc, own_ref, other_ref, kv_s)
    fill_queries(sc, q_ref, q_s)
    fill_rows(sc, pos_s)
    acc_s[...] = jnp.zeros_like(acc_s)
    m_s[...] = jnp.full_like(m_s, NEG)
    l_s[...] = jnp.zeros_like(l_s)

    def step(t, carry):
        which, chunk = chunk_of(sc, t)
        scores = dot_tn(keys_of(kv_s, chunk, 0), q_s[which])
        scores = jnp.where(seen(pos_s, which, chunk), scores, NEG)
        old = m_s[which]
        new = jnp.maximum(old, jnp.max(scores, axis=0, keepdims=True))
        prob = jnp.exp(scores - new)
        shrink = jnp.exp(old - new)
        m_s[which] = new
        l_s[which] = l_s[which] * shrink + jnp.sum(prob, axis=0, keepdims=True)
        acc_s[which] = acc_s[which] * shrink + jnp.dot(
            keys_of(kv_s, chunk, 1), prob.astype(BF16), preferred_element_type=F32
        )
        return carry

    lax.fori_loop(0, CHUNKS + 1, step, 0, unroll=UNROLL_F)
    for which in range(2):
        acc_s[which] = acc_s[which] / l_s[which]
        lse_ref[0, which] = m_s[which] + jnp.log(l_s[which])
    for half in range(2):
        mine = acc_s[jnp.bitwise_xor(half, sc[1])]
        for j in range(GROUP):
            o_ref[j, :, half * BLK : (half + 1) * BLK] = mine[:, j * BLK : (j + 1) * BLK]


def backward_kernel(
    sc, q_ref, own_ref, other_ref, o_ref, do_ref, lse_ref,
    dq_ref, down_ref, dother_ref,
    kv_s, q_s, do_s, dq_s, dkv_s, delta_s, pos_s,
):
    fill_keys(sc, own_ref, other_ref, kv_s)
    fill_queries(sc, q_ref, q_s)
    fill_queries(sc, do_ref, do_s)
    fill_queries(sc, o_ref, dq_s)
    fill_rows(sc, pos_s)
    for which in range(2):
        delta_s[which] = jnp.sum(dq_s[which] * do_s[which].astype(F32), axis=0, keepdims=True)
    dq_s[...] = jnp.zeros_like(dq_s)
    dkv_s[...] = jnp.zeros_like(dkv_s)

    def step(t, carry):
        which, chunk = chunk_of(sc, t)
        key_t, val_t, q_t, do_t = keys_of(kv_s, chunk, 0), keys_of(kv_s, chunk, 1), q_s[which], do_s[which]
        scores = dot_tn(key_t, q_t)
        prob = jnp.where(seen(pos_s, which, chunk), jnp.exp(scores - lse_ref[0, which]), 0.0)
        d_prob = dot_tn(val_t, do_t)
        d_score = (prob * (d_prob - delta_s[which])).astype(BF16)
        d_val = dot_nt(do_t, prob.astype(BF16))
        d_key = dot_nt(q_t, d_score)
        dq_s[which] = dq_s[which] + jnp.dot(key_t, d_score, preferred_element_type=F32)
        for j in range(CHUNK):
            lanes = slice(j * BLK, (j + 1) * BLK)
            dkv_s[chunk * CHUNK + j, 0] = dkv_s[chunk * CHUNK + j, 0] + d_key[:, lanes]
            dkv_s[chunk * CHUNK + j, 1] = dkv_s[chunk * CHUNK + j, 1] + d_val[:, lanes]
        return carry

    lax.fori_loop(0, CHUNKS + 1, step, 0, unroll=UNROLL_B)
    core = sc[2]
    scale = HEAD_DIM**-0.5
    for half in range(2):
        lanes = slice(half * BLK, (half + 1) * BLK)
        mine = dq_s[jnp.bitwise_xor(half, sc[1])] * scale
        for j in range(GROUP):
            dq_ref[j, :, lanes] = mine[:, j * BLK : (j + 1) * BLK]
        for chip in range(CTX // 2):
            block = sc[7 + 2 * (2 * chip + core) + half]
            down_ref[chip, :, 0, :, lanes] = dkv_s[block].astype(BF16)
            block = sc[7 + 2 * (2 * chip + 1 - core) + half]
            dother_ref[chip, :, 0, :, lanes] = dkv_s[block].astype(BF16)


ROWS = 2 * BLK
HEAD_SPEC = pl.BlockSpec((GROUP, HEAD_DIM, ROWS), lambda g, sc: (g, 0, 0))
KV_SPEC = pl.BlockSpec((CTX // 2, 2, 1, HEAD_DIM, ROWS), lambda g, sc: (0, 0, g, 0, 0))
LSE_SPEC = pl.BlockSpec((1, 2, 1, LANES), lambda g, sc: (g, 0, 0, 0))
HEAD_SHAPE = jax.ShapeDtypeStruct((HEADS, HEAD_DIM, ROWS), F32)
KV_SHAPE = jax.ShapeDtypeStruct((CTX // 2, 2, KV_HEADS, HEAD_DIM, ROWS), BF16)
LSE_SHAPE = jax.ShapeDtypeStruct((KV_HEADS, 2, 1, LANES), F32)
KERNEL_PARAMS = pltpu.CompilerParams(
    dimension_semantics=("arbitrary",), vmem_limit_bytes=40 * 2**20
)


def attention(scalars, q_t, own, other):
    return pl.pallas_call(
        forward_kernel,
        grid_spec=pltpu.PrefetchScalarGridSpec(
            num_scalar_prefetch=1,
            grid=(KV_HEADS,),
            in_specs=[HEAD_SPEC, KV_SPEC, KV_SPEC],
            out_specs=[HEAD_SPEC, LSE_SPEC],
            scratch_shapes=[
                pltpu.VMEM((NBLK, 2, HEAD_DIM, BLK), BF16),
                pltpu.VMEM((2, HEAD_DIM, LANES), BF16),
                pltpu.VMEM((2, HEAD_DIM, LANES), F32),
                pltpu.VMEM((2, 1, LANES), F32),
                pltpu.VMEM((2, 1, LANES), F32),
                pltpu.VMEM((2, 8, LANES), jnp.int32),
            ],
        ),
        out_shape=[HEAD_SHAPE, LSE_SHAPE],
        compiler_params=KERNEL_PARAMS,
        name="attention",
    )(scalars, q_t, own, other)


def attention_back(scalars, q_t, own, other, o_t, do_t, lse):
    return pl.pallas_call(
        backward_kernel,
        grid_spec=pltpu.PrefetchScalarGridSpec(
            num_scalar_prefetch=1,
            grid=(KV_HEADS,),
            in_specs=[HEAD_SPEC, KV_SPEC, KV_SPEC, HEAD_SPEC, HEAD_SPEC, LSE_SPEC],
            out_specs=[HEAD_SPEC, KV_SPEC, KV_SPEC],
            scratch_shapes=[
                pltpu.VMEM((NBLK, 2, HEAD_DIM, BLK), BF16),
                pltpu.VMEM((2, HEAD_DIM, LANES), BF16),
                pltpu.VMEM((2, HEAD_DIM, LANES), BF16),
                pltpu.VMEM((2, HEAD_DIM, LANES), F32),
                pltpu.VMEM((NBLK, 2, HEAD_DIM, BLK), F32),
                pltpu.VMEM((2, 1, LANES), F32),
                pltpu.VMEM((2, 8, LANES), jnp.int32),
            ],
        ),
        out_shape=[HEAD_SHAPE, KV_SHAPE, KV_SHAPE],
        compiler_params=KERNEL_PARAMS,
        name="attention_back",
    )(scalars, q_t, own, other, o_t, do_t, lse)


VMEM_SPEC = pl.BlockSpec(memory_space=pltpu.VMEM)


def dispatch_kernel(me, x_ref, *outs):
    for dx, out in enumerate(outs):
        for dz in range(2):
            out[dz] = x_ref[jnp.bitwise_xor(me[0], 4 * dz + dx)]


def dispatch(me, x):
    return pl.pallas_call(
        dispatch_kernel,
        grid_spec=pltpu.PrefetchScalarGridSpec(
            num_scalar_prefetch=1,
            grid=(),
            in_specs=[VMEM_SPEC],
            out_specs=[VMEM_SPEC] * 4,
        ),
        out_shape=[jax.ShapeDtypeStruct((2,) + x.shape[1:], BF16)] * 4,
        compiler_params=pltpu.CompilerParams(vmem_limit_bytes=40 * 2**20),
        name="dispatch",
    )(me, x)


def across(x, d):
    return lax.ppermute(x, "fsdp", [(i, i ^ d) for i in range(FSDP)])


def send_parts(pieces):
    return [pieces[0]] + [across(pieces[dx], dx) for dx in range(1, 4)]


def sum_parts(parts):
    total = sum(p.astype(F32) for p in parts)
    return (total[0] + across(total[1].astype(BF16), 4).astype(F32)).astype(BF16)


UNITS = FF // FSDP // 2


def unpack_kernel(sc, *refs):
    mlp0, mlp0_p, mlp1, mlp1_p, qkv, qkv_p, qkv_ref, out_ref, gu_ref = refs

    def write(order):
        for layer, pair in enumerate(((mlp0, mlp0_p), (mlp1, mlp1_p))):
            for half, mlp in enumerate(pair[::order]):
                for k in range(2):
                    for i in range(FSDP):
                        src = k * HALF + i * UNITS
                        dst = k * FF + i * 2 * UNITS + half * UNITS
                        gu_ref[layer, :, dst : dst + UNITS] = mlp[:, src : src + UNITS].astype(F32)
                cut = D // 2
                out_ref[layer, :, half * cut : (half + 1) * cut] = (
                    mlp[:, FF + HALF : FF + HALF + cut].astype(F32)
                )
        for layer, src in enumerate((qkv, qkv_p)[::order]):
            qkv_ref[layer] = src[:, : Q_ROWS + KV_ROWS].astype(F32)

    @pl.when(sc[0] == 0)
    def _():
        write(1)

    @pl.when(sc[0] != 0)
    def _():
        write(-1)


def unpack(core, *shares):
    return pl.pallas_call(
        unpack_kernel,
        grid_spec=pltpu.PrefetchScalarGridSpec(
            num_scalar_prefetch=1,
            grid=(),
            in_specs=[VMEM_SPEC] * 6,
            out_specs=[VMEM_SPEC] * 3,
        ),
        out_shape=[
            jax.ShapeDtypeStruct((LAYERS, SHARD, Q_ROWS + KV_ROWS), F32),
            jax.ShapeDtypeStruct((LAYERS, SHARD, D), F32),
            jax.ShapeDtypeStruct((LAYERS, SHARD, 2 * FF), F32),
        ],
        compiler_params=pltpu.CompilerParams(vmem_limit_bytes=40 * 2**20),
        name="unpack",
    )(core, *shares)


def rotate(x, cosine, sine):
    half = HEAD_DIM // 2
    first, second = x[:, :half], x[:, half:]
    return jnp.concatenate([first * cosine - second * sine, second * cosine + first * sine], 1)


def normed(hidden):
    inv_rms = lax.rsqrt(jnp.mean(hidden * hidden, -1, keepdims=True) + EPS)
    return hidden * inv_rms, inv_rms


def norm_back(d_unit, unit, inv_rms):
    return inv_rms * (d_unit - unit * jnp.mean(d_unit * unit, -1, keepdims=True))


def mm(a, b):
    return jnp.dot(a, b, preferred_element_type=F32)


def ein(spec, a, b):
    return jnp.einsum(spec, a, b, preferred_element_type=F32)


def local(tokens, block_order, doc_ids, norm_gains, w_qkv, w_out, w_gate_up, w_down, cotangent):
    place = lax.axis_index("ctx")
    core = jnp.bitwise_and(place, 1)
    first_core = core == 0
    me = lax.axis_index("fsdp").reshape(1)

    def my_half(left, right):
        return jnp.where(first_core, left, right)

    def in_order(own, other):
        return my_half(own, other), my_half(other, own)

    gain_cols = jnp.transpose(norm_gains.reshape(2 * LAYERS, SHARD))
    cut = (Q_ROWS + KV_ROWS + D) // 2

    def wgu_pack(layer):
        wgu = w_gate_up[layer].reshape(SHARD, 2, FSDP, 2, UNITS)
        return my_half(wgu[..., 0, :], wgu[..., 1, :]).reshape(SHARD, FF)

    def wd_pack(layer):
        return my_half(w_down[layer, :UNITS], w_down[layer, UNITS:]).reshape(SHARD, HALF)

    def proj_pack(layer):
        proj = jnp.concatenate([w_qkv[layer], w_out[layer]], 1)
        return my_half(proj[:, :cut], proj[:, cut:])

    first = jnp.concatenate([proj_pack(0), gain_cols], 1)
    first = jnp.broadcast_to(first[None], (FSDP,) + first.shape)
    first, w_gate_up, w_down = lax.optimization_barrier((first, w_gate_up, w_down))
    first = over_fsdp(first).reshape(D, -1)
    pack0 = jnp.concatenate([wgu_pack(0), wd_pack(0)], 1)
    pack0 = lax.all_gather(pack0, "fsdp", axis=0, tiled=True)
    pack1 = lax.all_gather(wgu_pack(1), "fsdp", axis=0, tiled=True)
    gains = jnp.transpose(first[:, cut:].astype(F32)).reshape(LAYERS, 2, D)

    def whole_proj(own):
        return jnp.concatenate(in_order(own, to_partner(own)), 1)

    projs, mlps = [whole_proj(first[:, :cut])], []

    first_block = lax.dynamic_index_in_dim(block_order, 2 * place, 0, keepdims=False)
    low = jnp.minimum(first_block, NBLK - 1 - first_block)
    low_half = (first_block != low).astype(jnp.int32)
    starts = jnp.sum(
        (doc_ids[0][None, :] < jnp.arange(1, 5, dtype=jnp.int32)[:, None]).astype(jnp.int32), 1
    )
    scalars = jnp.concatenate([jnp.stack([low, low_half, core]), starts, block_order])
    lane = jnp.arange(ROWS, dtype=jnp.int32)
    pos = jnp.where(lane < BLK, first_block, NBLK - 2 - first_block) * BLK + lane
    inv_freq = THETA ** (-jnp.arange(HEAD_DIM // 2, dtype=F32) / (HEAD_DIM // 2))
    angles = pos.astype(F32)[None, :] * inv_freq[:, None]
    cosine, sine = jnp.cos(angles), jnp.sin(angles)

    hidden = tokens[0].astype(F32)
    saved = []
    for layer in range(LAYERS):
        wqkv, wout = projs[layer][:, : Q_ROWS + KV_ROWS], projs[layer][:, Q_ROWS + KV_ROWS :]
        unit_a, rms_a = normed(hidden)
        attn_in = (unit_a * gains[layer, 0]).astype(BF16)
        qkv_t = ein("de,td->et", wqkv, attn_in).reshape(-1, HEAD_DIM, ROWS)
        turned = rotate(qkv_t[: HEADS + KV_HEADS], cosine, sine)
        q_t = (turned[:HEADS] * HEAD_DIM**-0.5).astype(BF16)
        kv_t = jnp.concatenate([turned[HEADS:], qkv_t[HEADS + KV_HEADS :]], 0).astype(BF16)
        kv_t = kv_t.reshape(1, 2, KV_HEADS, HEAD_DIM, ROWS)
        kv_own = over_chips(jnp.broadcast_to(kv_t, (CTX // 2,) + kv_t.shape[1:]))
        if layer == 0:
            late = jnp.concatenate([proj_pack(1), wd_pack(1)], 1)
            kv_own, late = lax.optimization_barrier((kv_own, late))
            late = gather_fsdp(late)
        kv_other = to_partner(kv_own)
        o_t, lse = attention(scalars, q_t, kv_own, kv_other)
        if layer == 0:
            o_t, pack0 = lax.optimization_barrier((o_t, pack0))
            mlps.append((pack0[:, :FF], pack0[:, FF:].reshape(HALF, D)))
            projs.append(whole_proj(late[:, :cut]))
        else:
            o_t, pack1 = lax.optimization_barrier((o_t, pack1))
            mlps.append((pack1, late[:, cut:].reshape(HALF, D)))
        attn_out = o_t.astype(BF16).reshape(Q_ROWS, ROWS)
        mid = hidden + ein("at,ad->td", attn_out, wout)
        unit_m, rms_m = normed(mid)
        mlp_in = (unit_m * gains[layer, 1]).astype(BF16)
        wgu, wdown = mlps[layer]
        both_in = jnp.concatenate([mlp_in, to_partner(mlp_in)], 0)
        gate_up = mm(both_in, wgu)
        inner = (jax.nn.silu(gate_up[:, :HALF]) * gate_up[:, HALF:]).astype(BF16)
        part = mm(inner, wdown)
        hidden = mid + part[:ROWS] + to_partner(part[ROWS:].astype(BF16)).astype(F32)
        saved.append(
            (wqkv, wout, unit_a, rms_a, attn_in, q_t, kv_own, kv_other, o_t, lse, attn_out,
             unit_m, rms_m, both_in, gate_up, inner, wgu, wdown)
        )
    output = hidden.astype(BF16).reshape(1, ROWS, D)

    def weight_grads(d_gu, both_in, inner, both_grad, attn_out, grad_b):
        d_wgu = ein("td,tf->df", both_in, d_gu).astype(BF16)
        d_wdown = ein("tf,td->fd", inner, both_grad).astype(BF16)
        d_wout = mm(attn_out, grad_b).astype(BF16)
        left, right = d_wout[:, : D // 2], d_wout[:, D // 2 :]
        d_wout = sum_pair(my_half(left, right), to_partner(my_half(right, left)))
        grads = jnp.concatenate([d_wgu, d_wdown.reshape(D, HALF), d_wout], 1)
        return grads.reshape(FSDP, SHARD, -1)

    d_hidden = cotangent[0].astype(F32)
    gain_grads, qkv_grads = [None] * LAYERS, [None] * LAYERS
    for layer in reversed(range(LAYERS)):
        (wqkv, wout, unit_a, rms_a, attn_in, q_t, kv_own, kv_other, o_t, lse, attn_out,
         unit_m, rms_m, both_in, gate_up, inner, wgu, wdown) = saved[layer]
        grad_b = d_hidden.astype(BF16)
        both_grad = jnp.concatenate([grad_b, to_partner(grad_b)], 0)
        d_inner = ein("td,fd->tf", both_grad, wdown)
        gate, up = gate_up[:, :HALF], gate_up[:, HALF:]
        sig = jax.nn.sigmoid(gate)
        d_gate = d_inner * up * sig * (1.0 + gate * (1.0 - sig))
        d_up = d_inner * (gate * sig)
        d_gu = jnp.concatenate([d_gate, d_up], 1).astype(BF16)
        part = ein("tf,df->td", d_gu, wgu)
        d_norm = part[:ROWS] + to_partner(part[ROWS:].astype(BF16)).astype(F32)
        d_gain_m = jnp.sum(d_norm * unit_m, 0)
        d_hidden = d_hidden + norm_back(d_norm * gains[layer, 1], unit_m, rms_m)
        grad_b = d_hidden.astype(BF16)
        do_t = ein("ad,td->at", wout, grad_b).astype(BF16).reshape(HEADS, HEAD_DIM, ROWS)
        dq_t, dkv_own, dkv_other = attention_back(scalars, q_t, kv_own, kv_other, o_t, do_t, lse)
        dkv = (dkv_own.astype(F32) + to_partner(dkv_other).astype(F32)).astype(BF16)
        late = (d_gu, both_in, inner, both_grad, attn_out, grad_b)
        grads = weight_grads(*lax.optimization_barrier((late, dkv))[0])
        dkv = jnp.sum(over_chips(dkv).astype(F32), 0)
        dkv, grads = lax.optimization_barrier((dkv, grads))
        if layer == 1:
            share1 = lax.psum_scatter(grads.reshape(D, -1), "fsdp", scatter_dimension=0, tiled=True)
        else:
            parts = send_parts(dispatch(me, grads))
        turned = jnp.concatenate([dq_t, dkv[0]], 0)
        d_qkv = jnp.concatenate([rotate(turned, cosine, -sine), dkv[1]], 0)
        d_qkv = d_qkv.astype(BF16).reshape(Q_ROWS + KV_ROWS, ROWS)
        d_wqkv = ein("td,et->de", attn_in, d_qkv)
        d_norm = ein("et,de->td", d_qkv, wqkv)
        d_gain_a = jnp.sum(d_norm * unit_a, 0)
        d_hidden = d_hidden + norm_back(d_norm * gains[layer, 0], unit_a, rms_a)
        gain_grads[layer] = jnp.stack([d_gain_a, d_gain_m])
        qkv_grads[layer] = d_wqkv.astype(BF16)
    input_grad = d_hidden.reshape(1, ROWS, D)

    mine, theirs = in_order(*qkv_grads)
    d_gains = jnp.transpose(jnp.stack(gain_grads).reshape(2 * LAYERS, D)).astype(BF16)
    d_wqkv = jnp.concatenate([sum_pair(mine, to_partner(theirs)), d_gains], 1)
    qkv = scatter_fsdp(d_wqkv)
    parts, share1, _ = lax.optimization_barrier((parts, share1, qkv))
    share1 = sum_chips(share1)
    share0 = sum_parts(parts)
    qkv = sum_chips(qkv)
    qkv_p = to_partner(qkv)

    share0 = sum_chips(share0)
    mlp0, mlp0_p, mlp1, mlp1_p = share0, to_partner(share0), share1, to_partner(share1)
    half = Q_ROWS + KV_ROWS
    d_gain = qkv[:, half:].astype(F32) + qkv_p[:, half:].astype(F32)
    gain_grad = jnp.transpose(d_gain).reshape(LAYERS, 2, SHARD)
    qkv_grad, out_proj_grad, gate_up_grad = unpack(
        core.reshape(1), mlp0, mlp0_p, mlp1, mlp1_p, qkv, qkv_p
    )
    down_grad = []
    for own, theirs in ((mlp0, mlp0_p), (mlp1, mlp1_p)):
        rows = [x[:, FF : FF + HALF].reshape(UNITS, D) for x in in_order(own, theirs)]
        down_grad.append(jnp.concatenate(rows, 0))
    down_grad = jnp.stack(down_grad).astype(F32)
    return (output, input_grad, gain_grad, qkv_grad, out_proj_grad, gate_up_grad, down_grad)


def solution(mesh):
    in_specs = (
        P("fsdp", "ctx", None),
        P(),
        P("fsdp", None),
        P(None, None, "fsdp"),
        P(None, "fsdp", None),
        P(None, "fsdp", None),
        P(None, "fsdp", None),
        P(None, "fsdp", None),
        P("fsdp", "ctx", None),
    )
    out_specs = (
        P("fsdp", "ctx", None),
        P("fsdp", "ctx", None),
        P(None, None, "fsdp"),
        P(None, "fsdp", None),
        P(None, "fsdp", None),
        P(None, "fsdp", None),
        P(None, "fsdp", None),
    )
    return jax.shard_map(local, mesh=mesh, in_specs=in_specs, out_specs=out_specs, check_vma=False)
```

```python
import functools

import jax
import jax.numpy as jnp
from jax import lax
from jax.experimental import pallas as pl
from jax.experimental.pallas import tpu as pltpu
from jax.sharding import PartitionSpec as P

D = 576
HEADS = 9
KV_HEADS = 3
GROUP = 3
HEAD_DIM = 64
FF = 1536
LAYERS = 2
BLK = 128
NBLK = 32
EPS = 1e-05
THETA = 100000.0
NEG = -1e30
F32 = jnp.float32
BF16 = jnp.bfloat16
LANES = GROUP * BLK
CTX = 16
FSDP = 8
SHARD = D // FSDP
HALF = FF // 2
Q_ROWS = HEADS * HEAD_DIM
KV_ROWS = 2 * KV_HEADS * HEAD_DIM

PARTNER = [(i, i ^ 1) for i in range(CTX)]
SAME_CORE = [[2 * chip + core for chip in range(CTX // 2)] for core in range(2)]


def to_partner(x):
    return lax.ppermute(x, "ctx", PARTNER)


def over_chips(x):
    return lax.all_to_all(x, "ctx", 0, 0, axis_index_groups=SAME_CORE, tiled=True)


def over_fsdp(x):
    return lax.all_to_all(x, "fsdp", 0, 0, tiled=True)


def gather_fsdp(x):
    return over_fsdp(jnp.broadcast_to(x[None], (FSDP,) + x.shape)).reshape(-1, x.shape[1])


def scatter_fsdp(x):
    parts = over_fsdp(x.reshape(FSDP, -1, x.shape[1]))
    return jnp.sum(parts.astype(F32), 0).astype(BF16)


def sum_pair(a, b):
    return (a.astype(F32) + b.astype(F32)).astype(BF16)


def sum_chips(x):
    for bit in (2, 4, 8):
        x = sum_pair(x, lax.ppermute(x, "ctx", [(i, i ^ bit) for i in range(CTX)]))
    return x


def dot_tn(a, b):
    return lax.dot_general(a, b, (((0,), (0,)), ((), ())), preferred_element_type=F32)


def dot_nt(a, b):
    return lax.dot_general(a, b, (((1,), (1,)), ((), ())), preferred_element_type=F32)


UNROLL_F = 9
UNROLL_B = 9
CHUNK = 4
KEYS = CHUNK * BLK
CHUNKS = NBLK // CHUNK


def fill_keys(sc, own_ref, other_ref, kv_s):
    core = sc[2]
    for chip in range(CTX // 2):
        for half in range(2):
            lanes = slice(half * BLK, (half + 1) * BLK)
            block = sc[7 + 2 * (2 * chip + core) + half]
            kv_s[block] = own_ref[chip, :, 0, :, lanes]
            block = sc[7 + 2 * (2 * chip + 1 - core) + half]
            kv_s[block] = other_ref[chip, :, 0, :, lanes]


def fill_queries(sc, src_ref, dst):
    for half in range(2):
        lanes = slice(half * BLK, (half + 1) * BLK)
        which = jnp.bitwise_xor(half, sc[1])
        dst[which] = jnp.concatenate([src_ref[j, :, lanes] for j in range(GROUP)], axis=1)


def query_rows(sc, which):
    block = jnp.where(which == 0, sc[0], NBLK - 1 - sc[0])
    lane = lax.broadcasted_iota(jnp.int32, (1, LANES), 1)
    pos = block * BLK + jnp.bitwise_and(lane, BLK - 1)
    start = jnp.zeros((1, LANES), jnp.int32)
    for d in range(4):
        start = jnp.where(pos >= sc[3 + d], jnp.maximum(start, sc[3 + d]), start)
    return pos, start


def chunk_of(sc, t):
    high = (NBLK - sc[0] + CHUNK - 1) // CHUNK
    which = (t < high).astype(jnp.int32)
    return which, jnp.where(t < high, t, t - high)


def keys_of(kv_s, chunk, kind):
    return jnp.concatenate([kv_s[chunk * CHUNK + j, kind] for j in range(CHUNK)], axis=1)


def seen(pos_s, which, chunk):
    at = lax.broadcasted_iota(jnp.int32, (KEYS, LANES), 0)
    base = chunk * KEYS
    return (at >= pos_s[which, 1:2] - base) & (at <= pos_s[which, 0:1] - base)


def fill_rows(sc, pos_s):
    for which in range(2):
        pos, start = query_rows(sc, which)
        pos_s[which, 0:1] = pos
        pos_s[which, 1:2] = start


def forward_kernel(sc, q_ref, own_ref, other_ref, o_ref, lse_ref, kv_s, q_s, acc_s, m_s, l_s, pos_s):
    fill_keys(sc, own_ref, other_ref, kv_s)
    fill_queries(sc, q_ref, q_s)
    fill_rows(sc, pos_s)
    acc_s[...] = jnp.zeros_like(acc_s)
    m_s[...] = jnp.full_like(m_s, NEG)
    l_s[...] = jnp.zeros_like(l_s)

    def step(t, carry):
        which, chunk = chunk_of(sc, t)
        scores = dot_tn(keys_of(kv_s, chunk, 0), q_s[which])
        scores = jnp.where(seen(pos_s, which, chunk), scores, NEG)
        old = m_s[which]
        new = jnp.maximum(old, jnp.max(scores, axis=0, keepdims=True))
        prob = jnp.exp(scores - new)
        shrink = jnp.exp(old - new)
        m_s[which] = new
        l_s[which] = l_s[which] * shrink + jnp.sum(prob, axis=0, keepdims=True)
        acc_s[which] = acc_s[which] * shrink + jnp.dot(
            keys_of(kv_s, chunk, 1), prob.astype(BF16), preferred_element_type=F32
        )
        return carry

    lax.fori_loop(0, CHUNKS + 1, step, 0, unroll=UNROLL_F)
    for which in range(2):
        acc_s[which] = acc_s[which] / l_s[which]
        lse_ref[0, which] = m_s[which] + jnp.log(l_s[which])
    for half in range(2):
        mine = acc_s[jnp.bitwise_xor(half, sc[1])]
        for j in range(GROUP):
            o_ref[j, :, half * BLK : (half + 1) * BLK] = mine[:, j * BLK : (j + 1) * BLK]


def backward_kernel(
    sc, q_ref, own_ref, other_ref, o_ref, do_ref, lse_ref,
    dq_ref, down_ref, dother_ref,
    kv_s, q_s, do_s, dq_s, dkv_s, delta_s, pos_s,
):
    fill_keys(sc, own_ref, other_ref, kv_s)
    fill_queries(sc, q_ref, q_s)
    fill_queries(sc, do_ref, do_s)
    fill_queries(sc, o_ref, dq_s)
    fill_rows(sc, pos_s)
    for which in range(2):
        delta_s[which] = jnp.sum(dq_s[which] * do_s[which].astype(F32), axis=0, keepdims=True)
    dq_s[...] = jnp.zeros_like(dq_s)
    dkv_s[...] = jnp.zeros_like(dkv_s)

    def step(t, carry):
        which, chunk = chunk_of(sc, t)
        key_t, val_t, q_t, do_t = keys_of(kv_s, chunk, 0), keys_of(kv_s, chunk, 1), q_s[which], do_s[which]
        scores = dot_tn(key_t, q_t)
        prob = jnp.where(seen(pos_s, which, chunk), jnp.exp(scores - lse_ref[0, which]), 0.0)
        d_prob = dot_tn(val_t, do_t)
        d_score = (prob * (d_prob - delta_s[which])).astype(BF16)
        d_val = dot_nt(do_t, prob.astype(BF16))
        d_key = dot_nt(q_t, d_score)
        dq_s[which] = dq_s[which] + jnp.dot(key_t, d_score, preferred_element_type=F32)
        for j in range(CHUNK):
            lanes = slice(j * BLK, (j + 1) * BLK)
            dkv_s[chunk * CHUNK + j, 0] = dkv_s[chunk * CHUNK + j, 0] + d_key[:, lanes]
            dkv_s[chunk * CHUNK + j, 1] = dkv_s[chunk * CHUNK + j, 1] + d_val[:, lanes]
        return carry

    lax.fori_loop(0, CHUNKS + 1, step, 0, unroll=UNROLL_B)
    core = sc[2]
    scale = HEAD_DIM**-0.5
    for half in range(2):
        lanes = slice(half * BLK, (half + 1) * BLK)
        mine = dq_s[jnp.bitwise_xor(half, sc[1])] * scale
        for j in range(GROUP):
            dq_ref[j, :, lanes] = mine[:, j * BLK : (j + 1) * BLK]
        for chip in range(CTX // 2):
            block = sc[7 + 2 * (2 * chip + core) + half]
            down_ref[chip, :, 0, :, lanes] = dkv_s[block].astype(BF16)
            block = sc[7 + 2 * (2 * chip + 1 - core) + half]
            dother_ref[chip, :, 0, :, lanes] = dkv_s[block].astype(BF16)


ROWS = 2 * BLK
HEAD_SPEC = pl.BlockSpec((GROUP, HEAD_DIM, ROWS), lambda g, sc: (g, 0, 0))
KV_SPEC = pl.BlockSpec((CTX // 2, 2, 1, HEAD_DIM, ROWS), lambda g, sc: (0, 0, g, 0, 0))
LSE_SPEC = pl.BlockSpec((1, 2, 1, LANES), lambda g, sc: (g, 0, 0, 0))
HEAD_SHAPE = jax.ShapeDtypeStruct((HEADS, HEAD_DIM, ROWS), F32)
KV_SHAPE = jax.ShapeDtypeStruct((CTX // 2, 2, KV_HEADS, HEAD_DIM, ROWS), BF16)
LSE_SHAPE = jax.ShapeDtypeStruct((KV_HEADS, 2, 1, LANES), F32)
KERNEL_PARAMS = pltpu.CompilerParams(
    dimension_semantics=("arbitrary",), vmem_limit_bytes=40 * 2**20
)


def attention(scalars, q_t, own, other):
    return pl.pallas_call(
        forward_kernel,
        grid_spec=pltpu.PrefetchScalarGridSpec(
            num_scalar_prefetch=1,
            grid=(KV_HEADS,),
            in_specs=[HEAD_SPEC, KV_SPEC, KV_SPEC],
            out_specs=[HEAD_SPEC, LSE_SPEC],
            scratch_shapes=[
                pltpu.VMEM((NBLK, 2, HEAD_DIM, BLK), BF16),
                pltpu.VMEM((2, HEAD_DIM, LANES), BF16),
                pltpu.VMEM((2, HEAD_DIM, LANES), F32),
                pltpu.VMEM((2, 1, LANES), F32),
                pltpu.VMEM((2, 1, LANES), F32),
                pltpu.VMEM((2, 8, LANES), jnp.int32),
            ],
        ),
        out_shape=[HEAD_SHAPE, LSE_SHAPE],
        compiler_params=KERNEL_PARAMS,
        name="attention",
    )(scalars, q_t, own, other)


def attention_back(scalars, q_t, own, other, o_t, do_t, lse):
    return pl.pallas_call(
        backward_kernel,
        grid_spec=pltpu.PrefetchScalarGridSpec(
            num_scalar_prefetch=1,
            grid=(KV_HEADS,),
            in_specs=[HEAD_SPEC, KV_SPEC, KV_SPEC, HEAD_SPEC, HEAD_SPEC, LSE_SPEC],
            out_specs=[HEAD_SPEC, KV_SPEC, KV_SPEC],
            scratch_shapes=[
                pltpu.VMEM((NBLK, 2, HEAD_DIM, BLK), BF16),
                pltpu.VMEM((2, HEAD_DIM, LANES), BF16),
                pltpu.VMEM((2, HEAD_DIM, LANES), BF16),
                pltpu.VMEM((2, HEAD_DIM, LANES), F32),
                pltpu.VMEM((NBLK, 2, HEAD_DIM, BLK), F32),
                pltpu.VMEM((2, 1, LANES), F32),
                pltpu.VMEM((2, 8, LANES), jnp.int32),
            ],
        ),
        out_shape=[HEAD_SHAPE, KV_SHAPE, KV_SHAPE],
        compiler_params=KERNEL_PARAMS,
        name="attention_back",
    )(scalars, q_t, own, other, o_t, do_t, lse)


VMEM_SPEC = pl.BlockSpec(memory_space=pltpu.VMEM)


def dispatch_kernel(me, x_ref, *outs):
    for dx, out in enumerate(outs):
        for dz in range(2):
            out[dz] = x_ref[jnp.bitwise_xor(me[0], 4 * dz + dx)]


def dispatch(me, x):
    return pl.pallas_call(
        dispatch_kernel,
        grid_spec=pltpu.PrefetchScalarGridSpec(
            num_scalar_prefetch=1,
            grid=(),
            in_specs=[VMEM_SPEC],
            out_specs=[VMEM_SPEC] * 4,
        ),
        out_shape=[jax.ShapeDtypeStruct((2,) + x.shape[1:], BF16)] * 4,
        compiler_params=pltpu.CompilerParams(vmem_limit_bytes=40 * 2**20),
        name="dispatch",
    )(me, x)


def across(x, d):
    return lax.ppermute(x, "fsdp", [(i, i ^ d) for i in range(FSDP)])


def send_parts(pieces):
    return [pieces[0]] + [across(pieces[dx], dx) for dx in range(1, 4)]


def sum_parts(parts):
    total = sum(p.astype(F32) for p in parts)
    return (total[0] + across(total[1].astype(BF16), 4).astype(F32)).astype(BF16)


UNITS = FF // FSDP // 2


def unpack_kernel(sc, *refs):
    mlp0, mlp0_p, mlp1, mlp1_p, qkv, qkv_p, qkv_ref, out_ref, gu_ref = refs

    def write(order):
        for layer, pair in enumerate(((mlp0, mlp0_p), (mlp1, mlp1_p))):
            for half, mlp in enumerate(pair[::order]):
                for k in range(2):
                    for i in range(FSDP):
                        src = k * HALF + i * UNITS
                        dst = k * FF + i * 2 * UNITS + half * UNITS
                        gu_ref[layer, :, dst : dst + UNITS] = mlp[:, src : src + UNITS].astype(F32)
                cut = D // 2
                out_ref[layer, :, half * cut : (half + 1) * cut] = (
                    mlp[:, FF + HALF : FF + HALF + cut].astype(F32)
                )
        for layer, src in enumerate((qkv, qkv_p)[::order]):
            qkv_ref[layer] = src[:, : Q_ROWS + KV_ROWS].astype(F32)

    @pl.when(sc[0] == 0)
    def _():
        write(1)

    @pl.when(sc[0] != 0)
    def _():
        write(-1)


def unpack(core, *shares):
    return pl.pallas_call(
        unpack_kernel,
        grid_spec=pltpu.PrefetchScalarGridSpec(
            num_scalar_prefetch=1,
            grid=(),
            in_specs=[VMEM_SPEC] * 6,
            out_specs=[VMEM_SPEC] * 3,
        ),
        out_shape=[
            jax.ShapeDtypeStruct((LAYERS, SHARD, Q_ROWS + KV_ROWS), F32),
            jax.ShapeDtypeStruct((LAYERS, SHARD, D), F32),
            jax.ShapeDtypeStruct((LAYERS, SHARD, 2 * FF), F32),
        ],
        compiler_params=pltpu.CompilerParams(vmem_limit_bytes=40 * 2**20),
        name="unpack",
    )(core, *shares)


def rotate(x, cosine, sine):
    half = HEAD_DIM // 2
    first, second = x[:, :half], x[:, half:]
    return jnp.concatenate([first * cosine - second * sine, second * cosine + first * sine], 1)


def normed(hidden):
    inv_rms = lax.rsqrt(jnp.mean(hidden * hidden, -1, keepdims=True) + EPS)
    return hidden * inv_rms, inv_rms


def norm_back(d_unit, unit, inv_rms):
    return inv_rms * (d_unit - unit * jnp.mean(d_unit * unit, -1, keepdims=True))


def mm(a, b):
    return jnp.dot(a, b, preferred_element_type=F32)


def ein(spec, a, b):
    return jnp.einsum(spec, a, b, preferred_element_type=F32)


def local(tokens, block_order, doc_ids, norm_gains, w_qkv, w_out, w_gate_up, w_down, cotangent):
    place = lax.axis_index("ctx")
    core = jnp.bitwise_and(place, 1)
    first_core = core == 0
    me = lax.axis_index("fsdp").reshape(1)

    def my_half(left, right):
        return jnp.where(first_core, left, right)

    def in_order(own, other):
        return my_half(own, other), my_half(other, own)

    gain_cols = jnp.transpose(norm_gains.reshape(2 * LAYERS, SHARD))
    cut = (Q_ROWS + KV_ROWS + D) // 2

    def wgu_pack(layer):
        wgu = w_gate_up[layer].reshape(SHARD, 2, FSDP, 2, UNITS)
        return my_half(wgu[..., 0, :], wgu[..., 1, :]).reshape(SHARD, FF)

    def wd_pack(layer):
        return my_half(w_down[layer, :UNITS], w_down[layer, UNITS:]).reshape(SHARD, HALF)

    def proj_pack(layer):
        proj = jnp.concatenate([w_qkv[layer], w_out[layer]], 1)
        return my_half(proj[:, :cut], proj[:, cut:])

    first = jnp.concatenate([proj_pack(0), gain_cols], 1)
    first = jnp.broadcast_to(first[None], (FSDP,) + first.shape)
    first, w_gate_up, w_down = lax.optimization_barrier((first, w_gate_up, w_down))
    first = over_fsdp(first).reshape(D, -1)
    pack0 = jnp.concatenate([wgu_pack(0), wd_pack(0)], 1)
    pack0 = lax.all_gather(pack0, "fsdp", axis=0, tiled=True)
    pack1 = lax.all_gather(wgu_pack(1), "fsdp", axis=0, tiled=True)
    gains = jnp.transpose(first[:, cut:].astype(F32)).reshape(LAYERS, 2, D)

    def whole_proj(own):
        return jnp.concatenate(in_order(own, to_partner(own)), 1)

    projs, mlps = [whole_proj(first[:, :cut])], []

    first_block = lax.dynamic_index_in_dim(block_order, 2 * place, 0, keepdims=False)
    low = jnp.minimum(first_block, NBLK - 1 - first_block)
    low_half = (first_block != low).astype(jnp.int32)
    starts = jnp.sum(
        (doc_ids[0][None, :] < jnp.arange(1, 5, dtype=jnp.int32)[:, None]).astype(jnp.int32), 1
    )
    scalars = jnp.concatenate([jnp.stack([low, low_half, core]), starts, block_order])
    lane = jnp.arange(ROWS, dtype=jnp.int32)
    pos = jnp.where(lane < BLK, first_block, NBLK - 2 - first_block) * BLK + lane
    inv_freq = THETA ** (-jnp.arange(HEAD_DIM // 2, dtype=F32) / (HEAD_DIM // 2))
    angles = pos.astype(F32)[None, :] * inv_freq[:, None]
    cosine, sine = jnp.cos(angles), jnp.sin(angles)

    hidden = tokens[0].astype(F32)
    saved = []
    for layer in range(LAYERS):
        wqkv, wout = projs[layer][:, : Q_ROWS + KV_ROWS], projs[layer][:, Q_ROWS + KV_ROWS :]
        unit_a, rms_a = normed(hidden)
        attn_in = (unit_a * gains[layer, 0]).astype(BF16)
        qkv_t = ein("de,td->et", wqkv, attn_in).reshape(-1, HEAD_DIM, ROWS)
        turned = rotate(qkv_t[: HEADS + KV_HEADS], cosine, sine)
        q_t = (turned[:HEADS] * HEAD_DIM**-0.5).astype(BF16)
        kv_t = jnp.concatenate([turned[HEADS:], qkv_t[HEADS + KV_HEADS :]], 0).astype(BF16)
        kv_t = kv_t.reshape(1, 2, KV_HEADS, HEAD_DIM, ROWS)
        kv_own = over_chips(jnp.broadcast_to(kv_t, (CTX // 2,) + kv_t.shape[1:]))
        if layer == 0:
            late = jnp.concatenate([proj_pack(1), wd_pack(1)], 1)
            kv_own, late = lax.optimization_barrier((kv_own, late))
            late = gather_fsdp(late)
        kv_other = to_partner(kv_own)
        o_t, lse = attention(scalars, q_t, kv_own, kv_other)
        if layer == 0:
            o_t, pack0 = lax.optimization_barrier((o_t, pack0))
            mlps.append((pack0[:, :FF], pack0[:, FF:].reshape(HALF, D)))
            projs.append(whole_proj(late[:, :cut]))
        else:
            o_t, pack1 = lax.optimization_barrier((o_t, pack1))
            mlps.append((pack1, late[:, cut:].reshape(HALF, D)))
        attn_out = o_t.astype(BF16).reshape(Q_ROWS, ROWS)
        mid = hidden + ein("at,ad->td", attn_out, wout)
        unit_m, rms_m = normed(mid)
        mlp_in = (unit_m * gains[layer, 1]).astype(BF16)
        wgu, wdown = mlps[layer]
        both_in = jnp.concatenate([mlp_in, to_partner(mlp_in)], 0)
        gate_up = mm(both_in, wgu)
        inner = (jax.nn.silu(gate_up[:, :HALF]) * gate_up[:, HALF:]).astype(BF16)
        part = mm(inner, wdown)
        hidden = mid + part[:ROWS] + to_partner(part[ROWS:].astype(BF16)).astype(F32)
        saved.append(
            (wqkv, wout, unit_a, rms_a, attn_in, q_t, kv_own, kv_other, o_t, lse, attn_out,
             unit_m, rms_m, both_in, gate_up, inner, wgu, wdown)
        )
    output = hidden.astype(BF16).reshape(1, ROWS, D)

    def weight_grads(d_gu, both_in, inner, both_grad, attn_out, grad_b):
        d_wgu = ein("td,tf->df", both_in, d_gu).astype(BF16)
        d_wdown = ein("tf,td->fd", inner, both_grad).astype(BF16)
        d_wout = mm(attn_out, grad_b).astype(BF16)
        left, right = d_wout[:, : D // 2], d_wout[:, D // 2 :]
        d_wout = sum_pair(my_half(left, right), to_partner(my_half(right, left)))
        grads = jnp.concatenate([d_wgu, d_wdown.reshape(D, HALF), d_wout], 1)
        return grads.reshape(FSDP, SHARD, -1)

    d_hidden = cotangent[0].astype(F32)
    gain_grads, qkv_grads = [None] * LAYERS, [None] * LAYERS
    for layer in reversed(range(LAYERS)):
        (wqkv, wout, unit_a, rms_a, attn_in, q_t, kv_own, kv_other, o_t, lse, attn_out,
         unit_m, rms_m, both_in, gate_up, inner, wgu, wdown) = saved[layer]
        grad_b = d_hidden.astype(BF16)
        both_grad = jnp.concatenate([grad_b, to_partner(grad_b)], 0)
        d_inner = ein("td,fd->tf", both_grad, wdown)
        gate, up = gate_up[:, :HALF], gate_up[:, HALF:]
        sig = jax.nn.sigmoid(gate)
        d_gate = d_inner * up * sig * (1.0 + gate * (1.0 - sig))
        d_up = d_inner * (gate * sig)
        d_gu = jnp.concatenate([d_gate, d_up], 1).astype(BF16)
        part = ein("tf,df->td", d_gu, wgu)
        d_norm = part[:ROWS] + to_partner(part[ROWS:].astype(BF16)).astype(F32)
        d_gain_m = jnp.sum(d_norm * unit_m, 0)
        d_hidden = d_hidden + norm_back(d_norm * gains[layer, 1], unit_m, rms_m)
        grad_b = d_hidden.astype(BF16)
        do_t = ein("ad,td->at", wout, grad_b).astype(BF16).reshape(HEADS, HEAD_DIM, ROWS)
        dq_t, dkv_own, dkv_other = attention_back(scalars, q_t, kv_own, kv_other, o_t, do_t, lse)
        dkv = (dkv_own.astype(F32) + to_partner(dkv_other).astype(F32)).astype(BF16)
        late = (d_gu, both_in, inner, both_grad, attn_out, grad_b)
        grads = weight_grads(*lax.optimization_barrier((late, dkv))[0])
        if layer == 0:
            share1 = sum_chips(lax.optimization_barrier((share1, dkv))[0])
        dkv = jnp.sum(over_chips(dkv).astype(F32), 0)
        dkv, grads = lax.optimization_barrier((dkv, grads))
        if layer == 1:
            share1 = lax.psum_scatter(grads.reshape(D, -1), "fsdp", scatter_dimension=0, tiled=True)
        else:
            parts = send_parts(dispatch(me, grads))
        turned = jnp.concatenate([dq_t, dkv[0]], 0)
        d_qkv = jnp.concatenate([rotate(turned, cosine, -sine), dkv[1]], 0)
        d_qkv = d_qkv.astype(BF16).reshape(Q_ROWS + KV_ROWS, ROWS)
        d_wqkv = ein("td,et->de", attn_in, d_qkv)
        d_norm = ein("et,de->td", d_qkv, wqkv)
        d_gain_a = jnp.sum(d_norm * unit_a, 0)
        d_hidden = d_hidden + norm_back(d_norm * gains[layer, 0], unit_a, rms_a)
        gain_grads[layer] = jnp.stack([d_gain_a, d_gain_m])
        qkv_grads[layer] = d_wqkv.astype(BF16)
    input_grad = d_hidden.reshape(1, ROWS, D)

    mine, theirs = in_order(*qkv_grads)
    d_gains = jnp.transpose(jnp.stack(gain_grads).reshape(2 * LAYERS, D)).astype(BF16)
    d_wqkv = jnp.concatenate([sum_pair(mine, to_partner(theirs)), d_gains], 1)
    qkv = scatter_fsdp(d_wqkv)
    share0 = sum_parts(parts)
    qkv = sum_chips(qkv)
    qkv_p = to_partner(qkv)

    share0 = sum_chips(share0)
    mlp0, mlp0_p, mlp1, mlp1_p = share0, to_partner(share0), share1, to_partner(share1)
    half = Q_ROWS + KV_ROWS
    d_gain = qkv[:, half:].astype(F32) + qkv_p[:, half:].astype(F32)
    gain_grad = jnp.transpose(d_gain).reshape(LAYERS, 2, SHARD)
    qkv_grad, out_proj_grad, gate_up_grad = unpack(
        core.reshape(1), mlp0, mlp0_p, mlp1, mlp1_p, qkv, qkv_p
    )
    down_grad = []
    for own, theirs in ((mlp0, mlp0_p), (mlp1, mlp1_p)):
        rows = [x[:, FF : FF + HALF].reshape(UNITS, D) for x in in_order(own, theirs)]
        down_grad.append(jnp.concatenate(rows, 0))
    down_grad = jnp.stack(down_grad).astype(F32)
    return (output, input_grad, gain_grad, qkv_grad, out_proj_grad, gate_up_grad, down_grad)


def solution(mesh):
    in_specs = (
        P("fsdp", "ctx", None),
        P(),
        P("fsdp", None),
        P(None, None, "fsdp"),
        P(None, "fsdp", None),
        P(None, "fsdp", None),
        P(None, "fsdp", None),
        P(None, "fsdp", None),
        P("fsdp", "ctx", None),
    )
    out_specs = (
        P("fsdp", "ctx", None),
        P("fsdp", "ctx", None),
        P(None, None, "fsdp"),
        P(None, "fsdp", None),
        P(None, "fsdp", None),
        P(None, "fsdp", None),
        P(None, "fsdp", None),
    )
    return jax.shard_map(local, mesh=mesh, in_specs=in_specs, out_specs=out_specs, check_vma=False)
```

```python
import functools

import jax
import jax.numpy as jnp
from jax import lax
from jax.experimental import pallas as pl
from jax.experimental.pallas import tpu as pltpu
from jax.sharding import PartitionSpec as P

D = 576
HEADS = 9
KV_HEADS = 3
GROUP = 3
HEAD_DIM = 64
FF = 1536
LAYERS = 2
BLK = 128
NBLK = 32
EPS = 1e-05
THETA = 100000.0
NEG = -1e30
F32 = jnp.float32
BF16 = jnp.bfloat16
LANES = GROUP * BLK
CTX = 16
FSDP = 8
SHARD = D // FSDP
HALF = FF // 2
Q_ROWS = HEADS * HEAD_DIM
KV_ROWS = 2 * KV_HEADS * HEAD_DIM

PARTNER = [(i, i ^ 1) for i in range(CTX)]
SAME_CORE = [[2 * chip + core for chip in range(CTX // 2)] for core in range(2)]


def to_partner(x):
    return lax.ppermute(x, "ctx", PARTNER)


def over_chips(x):
    return lax.all_to_all(x, "ctx", 0, 0, axis_index_groups=SAME_CORE, tiled=True)


def over_fsdp(x):
    return lax.all_to_all(x, "fsdp", 0, 0, tiled=True)


def gather_fsdp(x):
    return over_fsdp(jnp.broadcast_to(x[None], (FSDP,) + x.shape)).reshape(-1, x.shape[1])


def scatter_fsdp(x):
    parts = over_fsdp(x.reshape(FSDP, -1, x.shape[1]))
    return jnp.sum(parts.astype(F32), 0).astype(BF16)


def sum_pair(a, b):
    return (a.astype(F32) + b.astype(F32)).astype(BF16)


def sum_chips(x):
    for bit in (2, 4, 8):
        x = sum_pair(x, lax.ppermute(x, "ctx", [(i, i ^ bit) for i in range(CTX)]))
    return x


def dot_tn(a, b):
    return lax.dot_general(a, b, (((0,), (0,)), ((), ())), preferred_element_type=F32)


def dot_nt(a, b):
    return lax.dot_general(a, b, (((1,), (1,)), ((), ())), preferred_element_type=F32)


UNROLL_F = 9
UNROLL_B = 9
CHUNK = 4
KEYS = CHUNK * BLK
CHUNKS = NBLK // CHUNK


def fill_keys(sc, own_ref, other_ref, kv_s):
    core = sc[2]
    for chip in range(CTX // 2):
        for half in range(2):
            lanes = slice(half * BLK, (half + 1) * BLK)
            block = sc[7 + 2 * (2 * chip + core) + half]
            kv_s[block] = own_ref[chip, :, 0, :, lanes]
            block = sc[7 + 2 * (2 * chip + 1 - core) + half]
            kv_s[block] = other_ref[chip, :, 0, :, lanes]


def fill_queries(sc, src_ref, dst):
    for half in range(2):
        lanes = slice(half * BLK, (half + 1) * BLK)
        which = jnp.bitwise_xor(half, sc[1])
        dst[which] = jnp.concatenate([src_ref[j, :, lanes] for j in range(GROUP)], axis=1)


def query_rows(sc, which):
    block = jnp.where(which == 0, sc[0], NBLK - 1 - sc[0])
    lane = lax.broadcasted_iota(jnp.int32, (1, LANES), 1)
    pos = block * BLK + jnp.bitwise_and(lane, BLK - 1)
    start = jnp.zeros((1, LANES), jnp.int32)
    for d in range(4):
        start = jnp.where(pos >= sc[3 + d], jnp.maximum(start, sc[3 + d]), start)
    return pos, start


def chunk_of(sc, t):
    high = (NBLK - sc[0] + CHUNK - 1) // CHUNK
    which = (t < high).astype(jnp.int32)
    return which, jnp.where(t < high, t, t - high)


def keys_of(kv_s, chunk, kind):
    return jnp.concatenate([kv_s[chunk * CHUNK + j, kind] for j in range(CHUNK)], axis=1)


def seen(pos_s, which, chunk):
    at = lax.broadcasted_iota(jnp.int32, (KEYS, LANES), 0)
    base = chunk * KEYS
    return (at >= pos_s[which, 1:2] - base) & (at <= pos_s[which, 0:1] - base)


def fill_rows(sc, pos_s):
    for which in range(2):
        pos, start = query_rows(sc, which)
        pos_s[which, 0:1] = pos
        pos_s[which, 1:2] = start


def forward_kernel(sc, q_ref, own_ref, other_ref, o_ref, lse_ref, kv_s, q_s, acc_s, m_s, l_s, pos_s):
    fill_keys(sc, own_ref, other_ref, kv_s)
    fill_queries(sc, q_ref, q_s)
    fill_rows(sc, pos_s)
    acc_s[...] = jnp.zeros_like(acc_s)
    m_s[...] = jnp.full_like(m_s, NEG)
    l_s[...] = jnp.zeros_like(l_s)

    def step(t, carry):
        which, chunk = chunk_of(sc, t)
        scores = dot_tn(keys_of(kv_s, chunk, 0), q_s[which])
        scores = jnp.where(seen(pos_s, which, chunk), scores, NEG)
        old = m_s[which]
        new = jnp.maximum(old, jnp.max(scores, axis=0, keepdims=True))
        prob = jnp.exp(scores - new)
        shrink = jnp.exp(old - new)
        m_s[which] = new
        l_s[which] = l_s[which] * shrink + jnp.sum(prob, axis=0, keepdims=True)
        acc_s[which] = acc_s[which] * shrink + jnp.dot(
            keys_of(kv_s, chunk, 1), prob.astype(BF16), preferred_element_type=F32
        )
        return carry

    lax.fori_loop(0, CHUNKS + 1, step, 0, unroll=UNROLL_F)
    for which in range(2):
        acc_s[which] = acc_s[which] / l_s[which]
        lse_ref[0, which] = m_s[which] + jnp.log(l_s[which])
    for half in range(2):
        mine = acc_s[jnp.bitwise_xor(half, sc[1])]
        for j in range(GROUP):
            o_ref[j, :, half * BLK : (half + 1) * BLK] = mine[:, j * BLK : (j + 1) * BLK]


def backward_kernel(
    sc, q_ref, own_ref, other_ref, o_ref, do_ref, lse_ref,
    dq_ref, down_ref, dother_ref,
    kv_s, q_s, do_s, dq_s, dkv_s, delta_s, pos_s,
):
    fill_keys(sc, own_ref, other_ref, kv_s)
    fill_queries(sc, q_ref, q_s)
    fill_queries(sc, do_ref, do_s)
    fill_queries(sc, o_ref, dq_s)
    fill_rows(sc, pos_s)
    for which in range(2):
        delta_s[which] = jnp.sum(dq_s[which] * do_s[which].astype(F32), axis=0, keepdims=True)
    dq_s[...] = jnp.zeros_like(dq_s)
    dkv_s[...] = jnp.zeros_like(dkv_s)

    def step(t, carry):
        which, chunk = chunk_of(sc, t)
        key_t, val_t, q_t, do_t = keys_of(kv_s, chunk, 0), keys_of(kv_s, chunk, 1), q_s[which], do_s[which]
        scores = dot_tn(key_t, q_t)
        prob = jnp.where(seen(pos_s, which, chunk), jnp.exp(scores - lse_ref[0, which]), 0.0)
        d_prob = dot_tn(val_t, do_t)
        d_score = (prob * (d_prob - delta_s[which])).astype(BF16)
        d_val = dot_nt(do_t, prob.astype(BF16))
        d_key = dot_nt(q_t, d_score)
        dq_s[which] = dq_s[which] + jnp.dot(key_t, d_score, preferred_element_type=F32)
        for j in range(CHUNK):
            lanes = slice(j * BLK, (j + 1) * BLK)
            dkv_s[chunk * CHUNK + j, 0] = dkv_s[chunk * CHUNK + j, 0] + d_key[:, lanes]
            dkv_s[chunk * CHUNK + j, 1] = dkv_s[chunk * CHUNK + j, 1] + d_val[:, lanes]
        return carry

    lax.fori_loop(0, CHUNKS + 1, step, 0, unroll=UNROLL_B)
    core = sc[2]
    scale = HEAD_DIM**-0.5
    for half in range(2):
        lanes = slice(half * BLK, (half + 1) * BLK)
        mine = dq_s[jnp.bitwise_xor(half, sc[1])] * scale
        for j in range(GROUP):
            dq_ref[j, :, lanes] = mine[:, j * BLK : (j + 1) * BLK]
        for chip in range(CTX // 2):
            block = sc[7 + 2 * (2 * chip + core) + half]
            down_ref[chip, :, 0, :, lanes] = dkv_s[block].astype(BF16)
            block = sc[7 + 2 * (2 * chip + 1 - core) + half]
            dother_ref[chip, :, 0, :, lanes] = dkv_s[block].astype(BF16)


ROWS = 2 * BLK
HEAD_SPEC = pl.BlockSpec((GROUP, HEAD_DIM, ROWS), lambda g, sc: (g, 0, 0))
KV_SPEC = pl.BlockSpec((CTX // 2, 2, 1, HEAD_DIM, ROWS), lambda g, sc: (0, 0, g, 0, 0))
LSE_SPEC = pl.BlockSpec((1, 2, 1, LANES), lambda g, sc: (g, 0, 0, 0))
HEAD_SHAPE = jax.ShapeDtypeStruct((HEADS, HEAD_DIM, ROWS), F32)
KV_SHAPE = jax.ShapeDtypeStruct((CTX // 2, 2, KV_HEADS, HEAD_DIM, ROWS), BF16)
LSE_SHAPE = jax.ShapeDtypeStruct((KV_HEADS, 2, 1, LANES), F32)
KERNEL_PARAMS = pltpu.CompilerParams(
    dimension_semantics=("arbitrary",), vmem_limit_bytes=40 * 2**20
)


def attention(scalars, q_t, own, other):
    return pl.pallas_call(
        forward_kernel,
        grid_spec=pltpu.PrefetchScalarGridSpec(
            num_scalar_prefetch=1,
            grid=(KV_HEADS,),
            in_specs=[HEAD_SPEC, KV_SPEC, KV_SPEC],
            out_specs=[HEAD_SPEC, LSE_SPEC],
            scratch_shapes=[
                pltpu.VMEM((NBLK, 2, HEAD_DIM, BLK), BF16),
                pltpu.VMEM((2, HEAD_DIM, LANES), BF16),
                pltpu.VMEM((2, HEAD_DIM, LANES), F32),
                pltpu.VMEM((2, 1, LANES), F32),
                pltpu.VMEM((2, 1, LANES), F32),
                pltpu.VMEM((2, 8, LANES), jnp.int32),
            ],
        ),
        out_shape=[HEAD_SHAPE, LSE_SHAPE],
        compiler_params=KERNEL_PARAMS,
        name="attention",
    )(scalars, q_t, own, other)


def attention_back(scalars, q_t, own, other, o_t, do_t, lse):
    return pl.pallas_call(
        backward_kernel,
        grid_spec=pltpu.PrefetchScalarGridSpec(
            num_scalar_prefetch=1,
            grid=(KV_HEADS,),
            in_specs=[HEAD_SPEC, KV_SPEC, KV_SPEC, HEAD_SPEC, HEAD_SPEC, LSE_SPEC],
            out_specs=[HEAD_SPEC, KV_SPEC, KV_SPEC],
            scratch_shapes=[
                pltpu.VMEM((NBLK, 2, HEAD_DIM, BLK), BF16),
                pltpu.VMEM((2, HEAD_DIM, LANES), BF16),
                pltpu.VMEM((2, HEAD_DIM, LANES), BF16),
                pltpu.VMEM((2, HEAD_DIM, LANES), F32),
                pltpu.VMEM((NBLK, 2, HEAD_DIM, BLK), F32),
                pltpu.VMEM((2, 1, LANES), F32),
                pltpu.VMEM((2, 8, LANES), jnp.int32),
            ],
        ),
        out_shape=[HEAD_SHAPE, KV_SHAPE, KV_SHAPE],
        compiler_params=KERNEL_PARAMS,
        name="attention_back",
    )(scalars, q_t, own, other, o_t, do_t, lse)


VMEM_SPEC = pl.BlockSpec(memory_space=pltpu.VMEM)


def dispatch_kernel(me, x_ref, *outs):
    for dx, out in enumerate(outs):
        for dz in range(2):
            out[dz] = x_ref[jnp.bitwise_xor(me[0], 4 * dz + dx)]


def dispatch(me, x):
    return pl.pallas_call(
        dispatch_kernel,
        grid_spec=pltpu.PrefetchScalarGridSpec(
            num_scalar_prefetch=1,
            grid=(),
            in_specs=[VMEM_SPEC],
            out_specs=[VMEM_SPEC] * 4,
        ),
        out_shape=[jax.ShapeDtypeStruct((2,) + x.shape[1:], BF16)] * 4,
        compiler_params=pltpu.CompilerParams(vmem_limit_bytes=40 * 2**20),
        name="dispatch",
    )(me, x)


def across(x, d):
    return lax.ppermute(x, "fsdp", [(i, i ^ d) for i in range(FSDP)])


def send_parts(pieces):
    return [pieces[0]] + [across(pieces[dx], dx) for dx in range(1, 4)]


def sum_parts(parts):
    total = sum(p.astype(F32) for p in parts)
    return (total[0] + across(total[1].astype(BF16), 4).astype(F32)).astype(BF16)


UNITS = FF // FSDP // 2


def unpack_kernel(sc, *refs):
    mlp0, mlp0_p, mlp1, mlp1_p, qkv, qkv_p, qkv_ref, out_ref, gu_ref = refs

    def write(order):
        for layer, pair in enumerate(((mlp0, mlp0_p), (mlp1, mlp1_p))):
            for half, mlp in enumerate(pair[::order]):
                for k in range(2):
                    for i in range(FSDP):
                        src = k * HALF + i * UNITS
                        dst = k * FF + i * 2 * UNITS + half * UNITS
                        gu_ref[layer, :, dst : dst + UNITS] = mlp[:, src : src + UNITS].astype(F32)
                cut = D // 2
                out_ref[layer, :, half * cut : (half + 1) * cut] = (
                    mlp[:, FF + HALF : FF + HALF + cut].astype(F32)
                )
        for layer, src in enumerate((qkv, qkv_p)[::order]):
            qkv_ref[layer] = src[:, : Q_ROWS + KV_ROWS].astype(F32)

    @pl.when(sc[0] == 0)
    def _():
        write(1)

    @pl.when(sc[0] != 0)
    def _():
        write(-1)


def unpack(core, *shares):
    return pl.pallas_call(
        unpack_kernel,
        grid_spec=pltpu.PrefetchScalarGridSpec(
            num_scalar_prefetch=1,
            grid=(),
            in_specs=[VMEM_SPEC] * 6,
            out_specs=[VMEM_SPEC] * 3,
        ),
        out_shape=[
            jax.ShapeDtypeStruct((LAYERS, SHARD, Q_ROWS + KV_ROWS), F32),
            jax.ShapeDtypeStruct((LAYERS, SHARD, D), F32),
            jax.ShapeDtypeStruct((LAYERS, SHARD, 2 * FF), F32),
        ],
        compiler_params=pltpu.CompilerParams(vmem_limit_bytes=40 * 2**20),
        name="unpack",
    )(core, *shares)


def rotate(x, cosine, sine):
    half = HEAD_DIM // 2
    first, second = x[:, :half], x[:, half:]
    return jnp.concatenate([first * cosine - second * sine, second * cosine + first * sine], 1)


def normed(hidden):
    inv_rms = lax.rsqrt(jnp.mean(hidden * hidden, -1, keepdims=True) + EPS)
    return hidden * inv_rms, inv_rms


def norm_back(d_unit, unit, inv_rms):
    return inv_rms * (d_unit - unit * jnp.mean(d_unit * unit, -1, keepdims=True))


def mm(a, b):
    return jnp.dot(a, b, preferred_element_type=F32)


def ein(spec, a, b):
    return jnp.einsum(spec, a, b, preferred_element_type=F32)


def local(tokens, block_order, doc_ids, norm_gains, w_qkv, w_out, w_gate_up, w_down, cotangent):
    place = lax.axis_index("ctx")
    core = jnp.bitwise_and(place, 1)
    first_core = core == 0
    me = lax.axis_index("fsdp").reshape(1)

    def my_half(left, right):
        return jnp.where(first_core, left, right)

    def in_order(own, other):
        return my_half(own, other), my_half(other, own)

    gain_cols = jnp.transpose(norm_gains.reshape(2 * LAYERS, SHARD))
    cut = (Q_ROWS + KV_ROWS + D) // 2

    def wgu_pack(layer):
        wgu = w_gate_up[layer].reshape(SHARD, 2, FSDP, 2, UNITS)
        return my_half(wgu[..., 0, :], wgu[..., 1, :]).reshape(SHARD, FF)

    def wd_pack(layer):
        return my_half(w_down[layer, :UNITS], w_down[layer, UNITS:]).reshape(SHARD, HALF)

    def proj_pack(layer):
        proj = jnp.concatenate([w_qkv[layer], w_out[layer]], 1)
        return my_half(proj[:, :cut], proj[:, cut:])

    first = jnp.concatenate([proj_pack(0), gain_cols], 1)
    first = jnp.broadcast_to(first[None], (FSDP,) + first.shape)
    first, w_gate_up, w_down = lax.optimization_barrier((first, w_gate_up, w_down))
    first = over_fsdp(first).reshape(D, -1)
    pack0 = jnp.concatenate([wgu_pack(0), wd_pack(0)], 1)
    pack0 = lax.all_gather(pack0, "fsdp", axis=0, tiled=True)
    pack1 = lax.all_gather(wgu_pack(1), "fsdp", axis=0, tiled=True)
    gains = jnp.transpose(first[:, cut:].astype(F32)).reshape(LAYERS, 2, D)

    def whole_proj(own):
        return jnp.concatenate(in_order(own, to_partner(own)), 1)

    projs, mlps = [whole_proj(first[:, :cut])], []

    first_block = lax.dynamic_index_in_dim(block_order, 2 * place, 0, keepdims=False)
    low = jnp.minimum(first_block, NBLK - 1 - first_block)
    low_half = (first_block != low).astype(jnp.int32)
    starts = jnp.sum(
        (doc_ids[0][None, :] < jnp.arange(1, 5, dtype=jnp.int32)[:, None]).astype(jnp.int32), 1
    )
    scalars = jnp.concatenate([jnp.stack([low, low_half, core]), starts, block_order])
    lane = jnp.arange(ROWS, dtype=jnp.int32)
    pos = jnp.where(lane < BLK, first_block, NBLK - 2 - first_block) * BLK + lane
    inv_freq = THETA ** (-jnp.arange(HEAD_DIM // 2, dtype=F32) / (HEAD_DIM // 2))
    angles = pos.astype(F32)[None, :] * inv_freq[:, None]
    cosine, sine = jnp.cos(angles), jnp.sin(angles)

    hidden = tokens[0].astype(F32)
    saved = []
    for layer in range(LAYERS):
        wqkv, wout = projs[layer][:, : Q_ROWS + KV_ROWS], projs[layer][:, Q_ROWS + KV_ROWS :]
        unit_a, rms_a = normed(hidden)
        attn_in = (unit_a * gains[layer, 0]).astype(BF16)
        qkv_t = ein("de,td->et", wqkv, attn_in).reshape(-1, HEAD_DIM, ROWS)
        turned = rotate(qkv_t[: HEADS + KV_HEADS], cosine, sine)
        q_t = (turned[:HEADS] * HEAD_DIM**-0.5).astype(BF16)
        kv_t = jnp.concatenate([turned[HEADS:], qkv_t[HEADS + KV_HEADS :]], 0).astype(BF16)
        kv_t = kv_t.reshape(1, 2, KV_HEADS, HEAD_DIM, ROWS)
        kv_own = over_chips(jnp.broadcast_to(kv_t, (CTX // 2,) + kv_t.shape[1:]))
        if layer == 0:
            late = jnp.concatenate([proj_pack(1), wd_pack(1)], 1)
            kv_own, late = lax.optimization_barrier((kv_own, late))
            late = gather_fsdp(late)
        kv_other = to_partner(kv_own)
        o_t, lse = attention(scalars, q_t, kv_own, kv_other)
        if layer == 0:
            o_t, pack0 = lax.optimization_barrier((o_t, pack0))
            mlps.append((pack0[:, :FF], pack0[:, FF:].reshape(HALF, D)))
            projs.append(whole_proj(late[:, :cut]))
        else:
            o_t, pack1 = lax.optimization_barrier((o_t, pack1))
            mlps.append((pack1, late[:, cut:].reshape(HALF, D)))
        attn_out = o_t.astype(BF16).reshape(Q_ROWS, ROWS)
        mid = hidden + ein("at,ad->td", attn_out, wout)
        unit_m, rms_m = normed(mid)
        mlp_in = (unit_m * gains[layer, 1]).astype(BF16)
        wgu, wdown = mlps[layer]
        both_in = jnp.concatenate([mlp_in, to_partner(mlp_in)], 0)
        gate_up = mm(both_in, wgu)
        inner = (jax.nn.silu(gate_up[:, :HALF]) * gate_up[:, HALF:]).astype(BF16)
        part = mm(inner, wdown)
        hidden = mid + part[:ROWS] + to_partner(part[ROWS:].astype(BF16)).astype(F32)
        saved.append(
            (wqkv, wout, unit_a, rms_a, attn_in, q_t, kv_own, kv_other, o_t, lse, attn_out,
             unit_m, rms_m, both_in, gate_up, inner, wgu, wdown)
        )
    output = hidden.astype(BF16).reshape(1, ROWS, D)

    def weight_grads(d_gu, both_in, inner, both_grad, attn_out, grad_b):
        d_wgu = ein("td,tf->df", both_in, d_gu).astype(BF16)
        d_wdown = ein("tf,td->fd", inner, both_grad).astype(BF16)
        d_wout = mm(attn_out, grad_b).astype(BF16)
        left, right = d_wout[:, : D // 2], d_wout[:, D // 2 :]
        d_wout = sum_pair(my_half(left, right), to_partner(my_half(right, left)))
        grads = jnp.concatenate([d_wgu, d_wdown.reshape(D, HALF), d_wout], 1)
        return grads.reshape(FSDP, SHARD, -1)

    d_hidden = cotangent[0].astype(F32)
    gain_grads, qkv_grads = [None] * LAYERS, [None] * LAYERS
    for layer in reversed(range(LAYERS)):
        (wqkv, wout, unit_a, rms_a, attn_in, q_t, kv_own, kv_other, o_t, lse, attn_out,
         unit_m, rms_m, both_in, gate_up, inner, wgu, wdown) = saved[layer]
        grad_b = d_hidden.astype(BF16)
        both_grad = jnp.concatenate([grad_b, to_partner(grad_b)], 0)
        d_inner = ein("td,fd->tf", both_grad, wdown)
        gate, up = gate_up[:, :HALF], gate_up[:, HALF:]
        sig = jax.nn.sigmoid(gate)
        d_gate = d_inner * up * sig * (1.0 + gate * (1.0 - sig))
        d_up = d_inner * (gate * sig)
        d_gu = jnp.concatenate([d_gate, d_up], 1).astype(BF16)
        part = ein("tf,df->td", d_gu, wgu)
        d_norm = part[:ROWS] + to_partner(part[ROWS:].astype(BF16)).astype(F32)
        d_gain_m = jnp.sum(d_norm * unit_m, 0)
        d_hidden = d_hidden + norm_back(d_norm * gains[layer, 1], unit_m, rms_m)
        grad_b = d_hidden.astype(BF16)
        do_t = ein("ad,td->at", wout, grad_b).astype(BF16).reshape(HEADS, HEAD_DIM, ROWS)
        dq_t, dkv_own, dkv_other = attention_back(scalars, q_t, kv_own, kv_other, o_t, do_t, lse)
        dkv = (dkv_own.astype(F32) + to_partner(dkv_other).astype(F32)).astype(BF16)
        late = (d_gu, both_in, inner, both_grad, attn_out, grad_b)
        grads = weight_grads(*lax.optimization_barrier((late, dkv))[0])
        if layer == 0:
            share1 = sum_chips(lax.optimization_barrier((share1, dkv))[0])
        dkv = jnp.sum(over_chips(dkv).astype(F32), 0)
        dkv, grads = lax.optimization_barrier((dkv, grads))
        if layer == 1:
            share1 = lax.psum_scatter(grads.reshape(D, -1), "fsdp", scatter_dimension=0, tiled=True)
        else:
            parts = send_parts(dispatch(me, grads))
        turned = jnp.concatenate([dq_t, dkv[0]], 0)
        d_qkv = jnp.concatenate([rotate(turned, cosine, -sine), dkv[1]], 0)
        d_qkv = d_qkv.astype(BF16).reshape(Q_ROWS + KV_ROWS, ROWS)
        d_wqkv = ein("td,et->de", attn_in, d_qkv)
        d_norm = ein("et,de->td", d_qkv, wqkv)
        d_gain_a = jnp.sum(d_norm * unit_a, 0)
        d_hidden = d_hidden + norm_back(d_norm * gains[layer, 0], unit_a, rms_a)
        gain_grads[layer] = jnp.stack([d_gain_a, d_gain_m])
        qkv_grads[layer] = d_wqkv.astype(BF16)
    input_grad = d_hidden.reshape(1, ROWS, D)

    mine, theirs = in_order(*qkv_grads)
    d_gains = jnp.transpose(jnp.stack(gain_grads).reshape(2 * LAYERS, D)).astype(BF16)
    d_wqkv = jnp.concatenate([sum_pair(mine, to_partner(theirs)), d_gains], 1)
    qkv, share1 = lax.optimization_barrier((scatter_fsdp(d_wqkv), share1))
    share0 = sum_parts(parts)
    qkv = sum_chips(qkv)
    qkv_p = to_partner(qkv)

    share0 = sum_chips(share0)
    mlp0, mlp0_p, mlp1, mlp1_p = share0, to_partner(share0), share1, to_partner(share1)
    half = Q_ROWS + KV_ROWS
    d_gain = qkv[:, half:].astype(F32) + qkv_p[:, half:].astype(F32)
    gain_grad = jnp.transpose(d_gain).reshape(LAYERS, 2, SHARD)
    qkv_grad, out_proj_grad, gate_up_grad = unpack(
        core.reshape(1), mlp0, mlp0_p, mlp1, mlp1_p, qkv, qkv_p
    )
    down_grad = []
    for own, theirs in ((mlp0, mlp0_p), (mlp1, mlp1_p)):
        rows = [x[:, FF : FF + HALF].reshape(UNITS, D) for x in in_order(own, theirs)]
        down_grad.append(jnp.concatenate(rows, 0))
    down_grad = jnp.stack(down_grad).astype(F32)
    return (output, input_grad, gain_grad, qkv_grad, out_proj_grad, gate_up_grad, down_grad)


def solution(mesh):
    in_specs = (
        P("fsdp", "ctx", None),
        P(),
        P("fsdp", None),
        P(None, None, "fsdp"),
        P(None, "fsdp", None),
        P(None, "fsdp", None),
        P(None, "fsdp", None),
        P(None, "fsdp", None),
        P("fsdp", "ctx", None),
    )
    out_specs = (
        P("fsdp", "ctx", None),
        P("fsdp", "ctx", None),
        P(None, None, "fsdp"),
        P(None, "fsdp", None),
        P(None, "fsdp", None),
        P(None, "fsdp", None),
        P(None, "fsdp", None),
    )
    return jax.shard_map(local, mesh=mesh, in_specs=in_specs, out_specs=out_specs, check_vma=False)
```
